32 devices in a mesh: blk: 4 (over z), grp: 8 (over y, x, core).
Axes of the slice: x: 2, y: 2, z: 4, core: 2. Of those that a mesh axis runs over, the one named last changes fastest.
Arguments:
- user_prior: float32 [16384, 128], P(('blk', 'grp')), may hold values from -6 to 6
- item_factors: bfloat16 [131072, 128], P(('blk', 'grp')), may hold values from -0.1875 to 0.1875
- user_tiles: int32 [2048], P(('blk', 'grp')), may hold values from 0 to 31
- item_tiles: int32 [2048], P(('blk', 'grp')), may hold values from 0 to 1023, as said below
- counts: int32 [2048, 128, 128], P(('blk', 'grp')), may hold values from 0 to 20, as said below
Outputs:
- user_factors: float32 [16384, 128], P(('blk', 'grp'))
The draws below stay inside these ranges and needn't reach their ends.
Inputs may be any that keep to these rules, and one draw needn't show every extreme that they name: `item_tiles`: item tile t is held by device t // 32 of blk+grp. The entries of one device name tiles of 32 different holders, exactly 2 entries for each holder that they name, in no particular order. In each device's 64 entries, those whose tile of counts has a nonzero value come before those whose tile is all zero; in every group along grp at least one device has all 64 entries of the first kind.
All inputs are finite; a program needn't handle non-finite values.
Results may differ from the reference program's by a relative error of at most 0.0003.
The reference program's roundings to bfloat16 on the way count: a program that leaves them out, or rounds other values in their place, can miss the bound.
Values may be sent and summed in bfloat16 or wider, within the bound.
No kernel may reach another device: no remote copies, remote signals or barrier semaphores. Data moves between devices by JAX's collectives and lax.ppermute only.
A program may use at most 128 MiB of HBM per device.

```python
import jax
import jax.numpy as jnp
from jax import lax

R = 128
TILE = 128
ITERS = 3
UTB = 32
PAIRS_DEV = 64
IT_DEV = 32
CAP = 2
PAIRS = 2048
ITEM_TILES = 1024
ITEMS = 131072
USERS = 16384
N_BLK = 4
N_GRP = 8


def draw_item_tiles(key, part):
    devices = N_BLK * N_GRP
    holders = PAIRS_DEV // CAP
    device_keys = jax.random.split(jax.random.fold_in(key, 11), devices)

    def one_device(device_key):
        order_key, slot_key, place_key = jax.random.split(device_key, 3)
        owners = jax.random.permutation(order_key, devices)[:holders]
        owner_of = jnp.repeat(owners, CAP, total_repeat_length=PAIRS_DEV)
        owner_of = owner_of[jax.random.permutation(place_key, PAIRS_DEV)]
        slots = jax.random.randint(slot_key, (PAIRS_DEV,), 0, IT_DEV)
        return (owner_of * IT_DEV + slots).astype(jnp.int32)
    return jax.vmap(one_device)(device_keys).reshape(-1)


def draw_counts(key, part):
    devices = N_BLK * N_GRP
    shift_key, full_key, value_key, first_key = jax.random.split(jax.random.fold_in(key, 23), 4)
    shifts = jax.random.randint(shift_key, (devices,), 0, 4)
    full_slot = jax.random.randint(full_key, (N_BLK,), 0, N_GRP)
    device_ids = jnp.arange(devices, dtype=jnp.int32)
    is_full = device_ids % N_GRP == full_slot[device_ids // N_GRP]
    live = jnp.where(is_full, PAIRS_DEV, jnp.right_shift(jnp.full((devices,), PAIRS_DEV, jnp.int32), shifts))
    position = jnp.arange(PAIRS_DEV, dtype=jnp.int32)
    live_mask = (position[None, :] < live[:, None]).astype(jnp.int32).reshape(-1)
    raw = jax.random.randint(value_key, (devices * PAIRS_DEV, TILE, TILE), 0, 4000)
    values = jnp.where(raw < 3980, 0, raw - 3979)
    first = jax.random.randint(first_key, (devices * PAIRS_DEV,), 1, 21)
    values = values.at[:, 0, 0].set(first)
    return (values * live_mask[:, None, None]).astype(jnp.int32)


def set_ends(values, rng, least, largest):
    extent = values.shape
    spot = [jax.random.randint(jax.random.fold_in(rng, axis), (), 0, extent[axis]) for axis in range(len(extent))]
    values = values.at[tuple(spot)].set(least)
    longest = extent.index(max(extent))
    spot[longest] = (spot[longest] + 1) % extent[longest]
    return values.at[tuple(spot)].set(largest)


def raised(values, rng, source, target, shards_of, factor):
    owner, partner = [(jnp.arange(values.shape[dim]) // (values.shape[dim] // shards_of)).reshape([-1 if axis == dim else 1 for axis in range(values.ndim)]) for dim in (source, target)]
    chosen = jax.random.permutation(rng, shards_of)[partner]
    strong = (owner == chosen) | (owner == (partner + shards_of // 2) % shards_of)
    return jnp.where(strong, factor * values, values)


def level_of(key, shape, cuts, least, largest):
    def one(dim, blocks):
        heights = jax.random.uniform(jax.random.fold_in(jax.random.fold_in(key, 6), dim), (blocks,), jnp.float32, least / len(cuts), largest / len(cuts))
        return jnp.repeat(jnp.exp(heights), shape[dim] // blocks).reshape((-1,) + (1,) * (len(shape) - dim - 1))

    factor_of = one(*cuts[0])
    for cut in cuts[1:]:
        factor_of = factor_of * one(*cut)
    return factor_of


def centred(own_key, shape, spread, reach, cuts=(), held_as=jnp.bfloat16):
    loudness = level_of(own_key, shape, cuts, -0.22, 0.18) if cuts else 1.0
    result = jax.random.normal(own_key, shape, jnp.float32) * spread * loudness
    return jnp.minimum(jnp.maximum(result, -reach), reach).astype(held_as)


def noise_with(key, extent, spread, reach, shards, heavy, kind=jnp.bfloat16):
    array = spread * jax.random.normal(key, extent, jnp.float32)
    if shards:
        array = array * level_of(key, extent, shards, -0.22, 0.18)
    return jnp.clip(raised(array, jax.random.fold_in(key, 3), *heavy), -reach, reach).astype(kind)


def setup_inputs(seed: int = 0) -> dict:
    seeds = jax.random.split(jax.random.key(seed), 6)
    user_prior = centred(seeds[0], (USERS, R), 1.0, 6.0, ((0, 32),), jnp.float32)
    item_factors = noise_with(seeds[1], (ITEMS, R), (32 * R) ** -0.5, 0.1875, ((0, 32),), (0, 1, 32, 2.75))
    user_tiles = set_ends(jax.random.randint(seeds[2], (PAIRS,), 0, UTB), jax.random.fold_in(seeds[2], 1), 0, UTB - 1).astype(jnp.int32)
    item_tiles = draw_item_tiles(jax.random.fold_in(seeds[5], 71), 0)
    counts = draw_counts(jax.random.fold_in(seeds[5], 71), 0)
    return dict(user_prior=user_prior, item_factors=item_factors, user_tiles=user_tiles, item_tiles=item_tiles, counts=counts)


ALPHA = 40.0
REG = 32.0
EPS = 1e-6


def pair_products(low_tiles, factor_tiles, user_ids, item_ids, count_sets, with_rhs):
    def step(totals, inputs):
        users, items, counted = inputs
        factors = factor_tiles[items].astype(jnp.float32)
        counted = counted.astype(jnp.float32)
        if with_rhs:
            weights = jnp.where(counted > 0, 1.0 + ALPHA * counted, 0.0).astype(jnp.bfloat16)
        else:
            users_low = low_tiles[users].astype(jnp.float32)
            scores = jnp.einsum("bur,bir->bui", users_low, factors)
            weights = (ALPHA * counted * scores).astype(jnp.bfloat16)
        weights = lax.optimization_barrier(weights).astype(jnp.float32)
        back = jnp.einsum("bui,bir->bur", weights, factors)
        return totals.at[users].add(back), None

    start = jnp.zeros((UTB * N_BLK, TILE, R), jnp.float32)
    totals, _ = lax.scan(step, start, (user_ids, item_ids, count_sets))
    return totals.reshape(USERS, R)


def reference(user_prior, item_factors, user_tiles, item_tiles, counts):
    devices = N_BLK * N_GRP
    gram = lax.dot_general(item_factors, item_factors, (((0,), (0,)), ((), ())), preferred_element_type=jnp.float32)
    factor_tiles = item_factors.reshape(ITEM_TILES, TILE, R)
    offsets = (jnp.arange(devices, dtype=jnp.int32) // N_GRP) * UTB
    user_ids = user_tiles.reshape(devices, PAIRS_DEV) + offsets[:, None]
    item_ids = item_tiles.reshape(devices, PAIRS_DEV)
    count_sets = counts.reshape(devices, PAIRS_DEV, TILE, TILE)

    def operate(vectors):
        low_tiles = vectors.astype(jnp.bfloat16).reshape(UTB * N_BLK, TILE, R)
        pairs = pair_products(low_tiles, factor_tiles, user_ids, item_ids, count_sets, False)
        return jnp.dot(vectors, gram, precision=lax.Precision.HIGHEST) + REG * vectors + pairs

    rhs = pair_products(None, factor_tiles, user_ids, item_ids, count_sets, True)
    solution = user_prior
    residual = rhs - operate(solution)
    direction = residual
    norm_now = jnp.sum(residual * residual, axis=1, keepdims=True)
    for step in range(ITERS):
        image = operate(direction)
        alpha = norm_now / (jnp.sum(direction * image, axis=1, keepdims=True) + EPS)
        solution = solution + alpha * direction
        residual = residual - alpha * image
        fresh = jnp.sum(residual * residual, axis=1, keepdims=True)
        direction = residual + (fresh / (norm_now + EPS)) * direction
        norm_now = fresh
    return solution
```

```python
import functools

import jax
import jax.numpy as jnp
from jax import lax
from jax.experimental import pallas as pl
from jax.experimental.pallas import tpu as pltpu
from jax.sharding import PartitionSpec as P

ITERS = 3

ALPHA = 40.0
REG = 32.0
EPS = 1e-06

COUNT_CAP = 20
TILE_CAP = 16
LOAD_CAP = 32
SPAN = 2


def fetch_tiles(item_factors, item_tiles, pairs, tile, rank):
    n_all = lax.axis_size(("blk", "grp"))
    tiles_held = item_factors.shape[0] // tile
    slots_each = max(2, pairs // n_all)
    owner = item_tiles // tiles_held
    local_slot = item_tiles % tiles_held
    position = jnp.arange(pairs, dtype=jnp.int32)
    earlier = (owner[None, :] == owner[:, None]) & (position[None, :] < position[:, None])
    order = jnp.sum(earlier.astype(jnp.int32), axis=1)
    requests = jnp.full((n_all, slots_each), -1, jnp.int32).at[owner, order].set(local_slot)
    wanted = lax.all_to_all(requests, ("blk", "grp"), split_axis=0, concat_axis=0, tiled=True)
    held = item_factors.reshape(tiles_held, tile, rank)
    picked = jnp.take(held, jnp.maximum(wanted, 0), axis=0)
    picked = jnp.where((wanted >= 0)[:, :, None, None], picked, jnp.zeros((), picked.dtype))
    arrived = lax.all_to_all(picked, ("blk", "grp"), split_axis=0, concat_axis=0, tiled=True)
    return arrived[owner, order]


def row_sum(left, right):
    return jnp.sum(left * right, axis=1, keepdims=True)


def sweep_in_place(user_prior, item_factors, user_tiles, item_tiles, counts, live, gram_local):
    pairs = counts.shape[0]
    tile = counts.shape[1]
    rank = item_factors.shape[1]
    n_grp = lax.axis_size("grp")
    own_rows = user_prior.shape[0]
    block_rows = own_rows * n_grp
    user_blocks = block_rows // tile
    span = min(32, pairs)
    gram = lax.psum(gram_local, ("blk", "grp"))
    pair_tiles = fetch_tiles(item_factors, item_tiles, pairs, tile, rank)
    rounds = (jnp.sum(live.astype(jnp.int32)) + span - 1) // span
    tile_ids = jnp.arange(user_blocks, dtype=jnp.int32)

    def accumulate(low_tiles, with_rhs):

        def one_round(index, totals):
            start = index * span
            users = lax.dynamic_slice_in_dim(user_tiles, start, span)
            factors = lax.dynamic_slice_in_dim(pair_tiles, start, span)
            counted = lax.dynamic_slice_in_dim(counts, start, span).astype(jnp.float32)
            selector = (tile_ids[:, None] == users[None, :]).astype(jnp.float32)
            users_low = jnp.take(low_tiles, users, axis=0)
            scores = jnp.einsum(
                "bur,bir->bui", users_low, factors, preferred_element_type=jnp.float32
            )
            scaled = (ALPHA * counted * scores).astype(jnp.bfloat16)
            back = jnp.einsum("bui,bir->bur", scaled, factors, preferred_element_type=jnp.float32)
            result = [
                totals[0]
                + jnp.einsum("tb,bur->tur", selector, back, precision=lax.Precision.HIGHEST)
            ]
            if with_rhs:
                confidence = jnp.where(counted > 0, 1.0 + ALPHA * counted, 0.0).astype(jnp.bfloat16)
                pulled = jnp.einsum(
                    "bui,bir->bur", confidence, factors, preferred_element_type=jnp.float32
                )
                result.append(
                    totals[1]
                    + jnp.einsum("tb,bur->tur", selector, pulled, precision=lax.Precision.HIGHEST)
                )
            return tuple(result)

        zeros = jnp.zeros((user_blocks, tile, rank), jnp.float32)
        start_state = (zeros, zeros) if with_rhs else (zeros,)
        totals = lax.fori_loop(0, rounds, one_round, start_state)
        return tuple((total.reshape(block_rows, rank) for total in totals))

    def gram_term(vectors):
        return jnp.dot(vectors, gram, precision=lax.Precision.HIGHEST) + REG * vectors

    low = lax.all_gather(user_prior.astype(jnp.bfloat16), "grp", axis=0, tiled=True)
    pair_part, rhs_part = accumulate(low.reshape(user_blocks, tile, rank), True)
    pair_share, rhs_share = (
        lax.psum_scatter(pair_part, "grp", scatter_dimension=0, tiled=True),
        lax.psum_scatter(rhs_part, "grp", scatter_dimension=0, tiled=True),
    )
    solution = user_prior
    residual = rhs_share - (gram_term(solution) + pair_share)
    direction = residual
    norm_now = row_sum(residual, residual)
    for step in range(ITERS):
        low = lax.all_gather(direction.astype(jnp.bfloat16), "grp", axis=0, tiled=True)
        (pair_part,) = accumulate(low.reshape(user_blocks, tile, rank), False)
        image = gram_term(direction) + lax.psum_scatter(
            pair_part, "grp", scatter_dimension=0, tiled=True
        )
        alpha = norm_now / (row_sum(direction, image) + EPS)
        solution = solution + alpha * direction
        residual = residual - alpha * image
        fresh = row_sum(residual, residual)
        direction = residual + fresh / (norm_now + EPS) * direction
        norm_now = fresh
    return solution


def sweep_kernel(
    n_tiles, load_ref, count_at, tile_at, prior_ref, gram_ref, counts_ref, items_ref, out_ref,
    weights, factors, low, image, residual, direction,
):
    tile, rank = items_ref.shape[1:]
    most = load_ref[0]
    for user in range(1, n_tiles):
        most = jnp.maximum(most, load_ref[user])
    rounds = (most + SPAN - 1) // SPAN

    def place(step, carry):
        for user in range(n_tiles):
            load = load_ref[user]
            for part in range(SPAN):
                entry = step * SPAN + part
                at = user * LOAD_CAP + entry
                tile_counts = counts_ref[count_at[at]]
                weights[step, user, :, part * tile:(part + 1) * tile] = jnp.where(
                    entry < load, tile_counts, jnp.zeros_like(tile_counts)
                )
                factors[step, user, part * tile:(part + 1) * tile, :] = items_ref[tile_at[at]]
        return carry

    lax.fori_loop(0, rounds, place, 0)

    def pair_images(with_rhs):
        image[...] = jnp.zeros_like(image)
        if with_rhs:
            residual[...] = jnp.zeros_like(residual)

        def one_round(step, carry):
            for user in range(n_tiles):
                rows = slice(user * tile, (user + 1) * tile)
                items = factors[step, user]
                scaled = weights[step, user].astype(jnp.float32)
                scores = lax.dot_general(
                    low[rows, :], items, (((1,), (1,)), ((), ())),
                    preferred_element_type=jnp.float32,
                )
                image[rows, :] += jnp.dot(
                    (scaled * scores).astype(jnp.bfloat16), items,
                    preferred_element_type=jnp.float32,
                )
                if with_rhs:
                    confidence = jnp.where(scaled > 0, 1.0 + scaled, 0.0).astype(jnp.bfloat16)
                    residual[rows, :] += jnp.dot(
                        confidence, items, preferred_element_type=jnp.float32
                    )
            return carry

        lax.fori_loop(0, rounds, one_round, 0)

    def gram_term(vectors):
        return jnp.dot(
            vectors, gram_ref[...], precision=lax.Precision.HIGHEST,
            preferred_element_type=jnp.float32,
        ) + REG * vectors

    prior = prior_ref[...]
    low[...] = prior.astype(jnp.bfloat16)
    pair_images(True)
    start = residual[...] - (gram_term(prior) + image[...])
    residual[...] = start
    direction[...] = start
    out_ref[...] = prior
    norm_now = row_sum(start, start)
    for step in range(ITERS):
        heading = direction[...]
        low[...] = heading.astype(jnp.bfloat16)
        pair_images(False)
        shown = gram_term(heading) + image[...]
        alpha = norm_now / (row_sum(heading, shown) + EPS)
        out_ref[...] += alpha * heading
        if step < ITERS - 1:
            left = residual[...] - alpha * shown
            residual[...] = left
            fresh = row_sum(left, left)
            direction[...] = left + (fresh / (norm_now + EPS)) * heading
            norm_now = fresh


def run_sweep(load, count_at, tile_at, user_prior, gram, counts_in, items_in):
    own_rows, rank = user_prior.shape
    tile = counts_in.shape[1]
    n_tiles = own_rows // tile
    steps = LOAD_CAP // SPAN
    smem = pl.BlockSpec(memory_space=pltpu.SMEM)
    vmem = pl.BlockSpec(memory_space=pltpu.VMEM)
    return pl.pallas_call(
        functools.partial(sweep_kernel, n_tiles),
        out_shape=jax.ShapeDtypeStruct((own_rows, rank), jnp.float32),
        in_specs=[smem] * 3 + [vmem] * 4,
        out_specs=vmem,
        scratch_shapes=[
            pltpu.VMEM((steps, n_tiles, tile, SPAN * tile), jnp.bfloat16),
            pltpu.VMEM((steps, n_tiles, SPAN * tile, rank), jnp.bfloat16),
            pltpu.VMEM((own_rows, rank), jnp.bfloat16),
            pltpu.VMEM((own_rows, rank), jnp.float32),
            pltpu.VMEM((own_rows, rank), jnp.float32),
            pltpu.VMEM((own_rows, rank), jnp.float32),
        ],
        compiler_params=pltpu.CompilerParams(vmem_limit_bytes=48 * 2**20),
        name="sweep",
    )(load, count_at, tile_at, user_prior, gram, counts_in, items_in)


def body(user_prior, item_factors, user_tiles, item_tiles, counts):
    pairs = counts.shape[0]
    tile = counts.shape[1]
    rank = item_factors.shape[1]
    n_blk = lax.axis_size("blk")
    n_grp = lax.axis_size("grp")
    n_all = n_blk * n_grp
    own_rows = user_prior.shape[0]
    own_tiles = own_rows // tile
    user_blocks = own_tiles * n_grp
    tiles_held = item_factors.shape[0] // tile
    slots_each = max(2, pairs // n_all)
    my_blk = lax.axis_index("blk")
    my_grp = lax.axis_index("grp")
    me = my_blk * n_grp + my_grp

    live = jnp.any(counts > 0, axis=(1, 2))
    gram_local = lax.dot_general(
        item_factors, item_factors, (((0,), (0,)), ((), ())), preferred_element_type=jnp.float32
    )

    holder = item_tiles // tiles_held
    position = jnp.arange(pairs, dtype=jnp.int32)
    earlier = (holder[None, :] == holder[:, None]) & (position[None, :] < position[:, None])
    order = jnp.sum(earlier.astype(jnp.int32), axis=1)
    packed = ((item_tiles * 2 + live.astype(jnp.int32)) * slots_each + order) * user_blocks + user_tiles
    every = lax.all_to_all(
        jnp.broadcast_to(packed, (n_all, pairs)), ("blk", "grp"),
        split_axis=0, concat_axis=0, tiled=True,
    )
    all_user = every % user_blocks
    rest = every // user_blocks
    all_order = rest % slots_each
    rest = rest // slots_each
    all_live = rest % 2 == 1
    all_item = rest // 2
    all_holder = all_item // tiles_held
    all_slot = all_item % tiles_held

    by_group = lambda x: x.reshape(n_blk, n_grp * pairs)
    g_user, g_live = by_group(all_user), by_group(all_live)
    g_owner = g_user // own_tiles
    g_column = by_group(all_holder) % n_grp
    g_source = jnp.broadcast_to(
        jnp.repeat(jnp.arange(n_grp, dtype=jnp.int32), pairs)[None], (n_blk, n_grp * pairs)
    )
    bins = jnp.arange(n_grp * n_grp, dtype=jnp.int32)
    users = jnp.arange(user_blocks, dtype=jnp.int32)

    def marks(keys, ids):
        return (keys[..., None] == ids) & g_live[..., None]

    count_marks = marks(g_source * n_grp + g_owner, bins)
    tile_marks = marks(g_column * n_grp + g_owner, bins)
    user_marks = marks(g_user, users)
    most = lambda m: jnp.max(jnp.sum(m.astype(jnp.int32), axis=1))
    fits = (
        (most(count_marks) <= COUNT_CAP) & (most(tile_marks) <= TILE_CAP)
        & (most(user_marks) <= LOAD_CAP)
    )

    def sweep_by_owner(user_prior, item_factors, user_tiles, item_tiles, counts, live, gram_local):
        gram = lax.psum(gram_local, ("blk", "grp"))
        mine = all_holder == me
        at = (jnp.arange(n_all, dtype=jnp.int32)[:, None] * slots_each + all_order).reshape(-1)
        slots = jnp.arange(n_all * slots_each, dtype=jnp.int32)
        wanted = jnp.sum(
            jnp.where(mine.reshape(-1) & (at == slots[:, None]), all_slot.reshape(-1), 0), axis=1
        )
        held = item_factors.reshape(tiles_held, tile, rank)
        asked = jnp.take(held, wanted, axis=0).reshape(n_blk, n_grp * slots_each, tile, rank)
        column = lax.all_to_all(asked, "blk", split_axis=0, concat_axis=0, tiled=True)
        column = column.reshape(n_blk * n_grp * slots_each, tile, rank)

        pick = lambda x: lax.dynamic_index_in_dim(x, my_blk, 0, keepdims=False)
        mark = jnp.concatenate(
            [pick(count_marks), pick(tile_marks), pick(user_marks)], axis=1
        ).astype(jnp.bfloat16)
        n_entries = n_grp * pairs
        index = jnp.arange(n_entries, dtype=jnp.int32)
        before = (index[None, :] < index[:, None]).astype(jnp.bfloat16)
        ahead = jnp.dot(before, mark, preferred_element_type=jnp.float32) * mark.astype(jnp.float32)
        n_bins = n_grp * n_grp
        rank_of = lambda lo, hi: jnp.sum(ahead[:, lo:hi], axis=1).astype(jnp.int32)
        count_rank = rank_of(0, n_bins)
        tile_rank = rank_of(n_bins, 2 * n_bins)
        user_rank = rank_of(2 * n_bins, 2 * n_bins + user_blocks)
        e_user, e_live, e_owner = pick(g_user), pick(g_live), pick(g_owner)
        e_column = pick(g_column)
        e_source = index // pairs
        e_holder = pick(by_group(all_holder))
        e_order = pick(by_group(all_order))

        cells = jnp.arange(n_grp * COUNT_CAP, dtype=jnp.int32)
        hit = e_live & (e_source == my_grp)
        chosen = jnp.sum(
            jnp.where(hit & (e_owner * COUNT_CAP + count_rank == cells[:, None]), index % pairs, 0),
            axis=1,
        )
        scaled = (ALPHA * counts.astype(jnp.float32)).astype(jnp.bfloat16)
        outgoing = jnp.take(scaled, chosen, axis=0).reshape(n_grp, COUNT_CAP, tile, tile)
        counts_in = lax.all_to_all(outgoing, "grp", split_axis=0, concat_axis=0, tiled=True)
        counts_in = counts_in.reshape(n_grp * COUNT_CAP, tile, tile)

        cells = jnp.arange(n_grp * TILE_CAP, dtype=jnp.int32)
        hit = e_live & (e_column == my_grp)
        where = (e_holder // n_grp * n_grp + e_source) * slots_each + e_order
        chosen = jnp.sum(
            jnp.where(hit & (e_owner * TILE_CAP + tile_rank == cells[:, None]), where, 0), axis=1
        )
        outgoing = jnp.take(column, chosen, axis=0).reshape(n_grp, TILE_CAP, tile, rank)
        items_in = lax.all_to_all(outgoing, "grp", split_axis=0, concat_axis=0, tiled=True)
        items_in = items_in.reshape(n_grp * TILE_CAP, tile, rank)

        cells = jnp.arange(own_tiles * LOAD_CAP, dtype=jnp.int32)
        hit = e_live & (e_owner == my_grp)
        match = hit & ((e_user % own_tiles) * LOAD_CAP + user_rank == cells[:, None])
        count_at = jnp.sum(jnp.where(match, e_source * COUNT_CAP + count_rank, 0), axis=1)
        tile_at = jnp.sum(jnp.where(match, e_column * TILE_CAP + tile_rank, 0), axis=1)
        load = jnp.sum(match.reshape(own_tiles, -1).astype(jnp.int32), axis=1)
        return run_sweep(load, count_at, tile_at, user_prior, gram, counts_in, items_in)

    return lax.cond(
        fits, sweep_by_owner, sweep_in_place,
        user_prior, item_factors, user_tiles, item_tiles, counts, live, gram_local,
    )


def solution(mesh):
    in_specs = (
        P(("blk", "grp"), None),
        P(("blk", "grp"), None),
        P(("blk", "grp")),
        P(("blk", "grp")),
        P(("blk", "grp"), None, None),
    )
    out_specs = P(("blk", "grp"), None)
    return jax.shard_map(body, mesh=mesh, in_specs=in_specs, out_specs=out_specs, check_vma=False)
```

```python
import functools

import jax
import jax.numpy as jnp
from jax import lax
from jax.experimental import pallas as pl
from jax.experimental.pallas import tpu as pltpu
from jax.sharding import PartitionSpec as P

ITERS = 3

ALPHA = 40.0
REG = 32.0
EPS = 1e-06

COUNT_CAP = 18
TILE_CAP = 14
LOAD_CAP = 32
SPAN = 2


def fetch_tiles(item_factors, item_tiles, pairs, tile, rank):
    n_all = lax.axis_size(("blk", "grp"))
    tiles_held = item_factors.shape[0] // tile
    slots_each = max(2, pairs // n_all)
    owner = item_tiles // tiles_held
    local_slot = item_tiles % tiles_held
    position = jnp.arange(pairs, dtype=jnp.int32)
    earlier = (owner[None, :] == owner[:, None]) & (position[None, :] < position[:, None])
    order = jnp.sum(earlier.astype(jnp.int32), axis=1)
    requests = jnp.full((n_all, slots_each), -1, jnp.int32).at[owner, order].set(local_slot)
    wanted = lax.all_to_all(requests, ("blk", "grp"), split_axis=0, concat_axis=0, tiled=True)
    held = item_factors.reshape(tiles_held, tile, rank)
    picked = jnp.take(held, jnp.maximum(wanted, 0), axis=0)
    picked = jnp.where((wanted >= 0)[:, :, None, None], picked, jnp.zeros((), picked.dtype))
    arrived = lax.all_to_all(picked, ("blk", "grp"), split_axis=0, concat_axis=0, tiled=True)
    return arrived[owner, order]


def row_sum(left, right):
    return jnp.sum(left * right, axis=1, keepdims=True)


def sweep_in_place(user_prior, item_factors, user_tiles, item_tiles, counts, live, gram_local):
    pairs = counts.shape[0]
    tile = counts.shape[1]
    rank = item_factors.shape[1]
    n_grp = lax.axis_size("grp")
    own_rows = user_prior.shape[0]
    block_rows = own_rows * n_grp
    user_blocks = block_rows // tile
    span = min(32, pairs)
    gram = lax.psum(gram_local, ("blk", "grp"))
    pair_tiles = fetch_tiles(item_factors, item_tiles, pairs, tile, rank)
    rounds = (jnp.sum(live.astype(jnp.int32)) + span - 1) // span
    tile_ids = jnp.arange(user_blocks, dtype=jnp.int32)

    def accumulate(low_tiles, with_rhs):

        def one_round(index, totals):
            start = index * span
            users = lax.dynamic_slice_in_dim(user_tiles, start, span)
            factors = lax.dynamic_slice_in_dim(pair_tiles, start, span)
            counted = lax.dynamic_slice_in_dim(counts, start, span).astype(jnp.float32)
            selector = (tile_ids[:, None] == users[None, :]).astype(jnp.float32)
            users_low = jnp.take(low_tiles, users, axis=0)
            scores = jnp.einsum(
                "bur,bir->bui", users_low, factors, preferred_element_type=jnp.float32
            )
            scaled = (ALPHA * counted * scores).astype(jnp.bfloat16)
            back = jnp.einsum("bui,bir->bur", scaled, factors, preferred_element_type=jnp.float32)
            result = [
                totals[0]
                + jnp.einsum("tb,bur->tur", selector, back, precision=lax.Precision.HIGHEST)
            ]
            if with_rhs:
                confidence = jnp.where(counted > 0, 1.0 + ALPHA * counted, 0.0).astype(jnp.bfloat16)
                pulled = jnp.einsum(
                    "bui,bir->bur", confidence, factors, preferred_element_type=jnp.float32
                )
                result.append(
                    totals[1]
                    + jnp.einsum("tb,bur->tur", selector, pulled, precision=lax.Precision.HIGHEST)
                )
            return tuple(result)

        zeros = jnp.zeros((user_blocks, tile, rank), jnp.float32)
        start_state = (zeros, zeros) if with_rhs else (zeros,)
        totals = lax.fori_loop(0, rounds, one_round, start_state)
        return tuple((total.reshape(block_rows, rank) for total in totals))

    def gram_term(vectors):
        return jnp.dot(vectors, gram, precision=lax.Precision.HIGHEST) + REG * vectors

    low = lax.all_gather(user_prior.astype(jnp.bfloat16), "grp", axis=0, tiled=True)
    pair_part, rhs_part = accumulate(low.reshape(user_blocks, tile, rank), True)
    pair_share, rhs_share = (
        lax.psum_scatter(pair_part, "grp", scatter_dimension=0, tiled=True),
        lax.psum_scatter(rhs_part, "grp", scatter_dimension=0, tiled=True),
    )
    solution = user_prior
    residual = rhs_share - (gram_term(solution) + pair_share)
    direction = residual
    norm_now = row_sum(residual, residual)
    for step in range(ITERS):
        low = lax.all_gather(direction.astype(jnp.bfloat16), "grp", axis=0, tiled=True)
        (pair_part,) = accumulate(low.reshape(user_blocks, tile, rank), False)
        image = gram_term(direction) + lax.psum_scatter(
            pair_part, "grp", scatter_dimension=0, tiled=True
        )
        alpha = norm_now / (row_sum(direction, image) + EPS)
        solution = solution + alpha * direction
        residual = residual - alpha * image
        fresh = row_sum(residual, residual)
        direction = residual + fresh / (norm_now + EPS) * direction
        norm_now = fresh
    return solution


def sweep_kernel(
    n_tiles, load_ref, count_at, tile_at, prior_ref, gram_ref, counts_ref, items_ref, out_ref,
    weights, factors, low, image, residual, direction,
):
    tile, rank = items_ref.shape[1:]
    most = load_ref[0]
    for user in range(1, n_tiles):
        most = jnp.maximum(most, load_ref[user])
    rounds = (most + SPAN - 1) // SPAN

    def place(step, carry):
        for user in range(n_tiles):
            load = load_ref[user]
            for part in range(SPAN):
                entry = step * SPAN + part
                at = user * LOAD_CAP + entry
                tile_counts = counts_ref[count_at[at]]
                weights[step, user, :, part * tile:(part + 1) * tile] = jnp.where(
                    entry < load, tile_counts, jnp.zeros_like(tile_counts)
                )
                factors[step, user, part * tile:(part + 1) * tile, :] = items_ref[tile_at[at]]
        return carry

    lax.fori_loop(0, rounds, place, 0)

    def pair_images(with_rhs):
        image[...] = jnp.zeros_like(image)
        if with_rhs:
            residual[...] = jnp.zeros_like(residual)

        def one_round(step, carry):
            for user in range(n_tiles):
                rows = slice(user * tile, (user + 1) * tile)
                items = factors[step, user]
                scaled = weights[step, user].astype(jnp.float32)
                scores = lax.dot_general(
                    low[rows, :], items, (((1,), (1,)), ((), ())),
                    preferred_element_type=jnp.float32,
                )
                image[rows, :] += jnp.dot(
                    (scaled * scores).astype(jnp.bfloat16), items,
                    preferred_element_type=jnp.float32,
                )
                if with_rhs:
                    confidence = jnp.where(scaled > 0, 1.0 + scaled, 0.0).astype(jnp.bfloat16)
                    residual[rows, :] += jnp.dot(
                        confidence, items, preferred_element_type=jnp.float32
                    )
            return carry

        lax.fori_loop(0, rounds, one_round, 0)

    def gram_term(vectors):
        return jnp.dot(
            vectors, gram_ref[...], precision=lax.Precision.HIGHEST,
            preferred_element_type=jnp.float32,
        ) + REG * vectors

    prior = prior_ref[...]
    low[...] = prior.astype(jnp.bfloat16)
    pair_images(True)
    start = residual[...] - (gram_term(prior) + image[...])
    residual[...] = start
    direction[...] = start
    out_ref[...] = prior
    norm_now = row_sum(start, start)
    for step in range(ITERS):
        heading = direction[...]
        low[...] = heading.astype(jnp.bfloat16)
        pair_images(False)
        shown = gram_term(heading) + image[...]
        alpha = norm_now / (row_sum(heading, shown) + EPS)
        out_ref[...] += alpha * heading
        if step < ITERS - 1:
            left = residual[...] - alpha * shown
            residual[...] = left
            fresh = row_sum(left, left)
            direction[...] = left + (fresh / (norm_now + EPS)) * heading
            norm_now = fresh


def run_sweep(load, count_at, tile_at, user_prior, gram, counts_in, items_in):
    own_rows, rank = user_prior.shape
    tile = counts_in.shape[1]
    n_tiles = own_rows // tile
    steps = LOAD_CAP // SPAN
    smem = pl.BlockSpec(memory_space=pltpu.SMEM)
    vmem = pl.BlockSpec(memory_space=pltpu.VMEM)
    return pl.pallas_call(
        functools.partial(sweep_kernel, n_tiles),
        out_shape=jax.ShapeDtypeStruct((own_rows, rank), jnp.float32),
        in_specs=[smem] * 3 + [vmem] * 4,
        out_specs=vmem,
        scratch_shapes=[
            pltpu.VMEM((steps, n_tiles, tile, SPAN * tile), jnp.bfloat16),
            pltpu.VMEM((steps, n_tiles, SPAN * tile, rank), jnp.bfloat16),
            pltpu.VMEM((own_rows, rank), jnp.bfloat16),
            pltpu.VMEM((own_rows, rank), jnp.float32),
            pltpu.VMEM((own_rows, rank), jnp.float32),
            pltpu.VMEM((own_rows, rank), jnp.float32),
        ],
        compiler_params=pltpu.CompilerParams(vmem_limit_bytes=48 * 2**20),
        name="sweep",
    )(load, count_at, tile_at, user_prior, gram, counts_in, items_in)


def take_tiles(tiles, chosen):
    return jnp.take(tiles, chosen, axis=0, mode="clip")


def sum_everywhere(value):
    for axis in ("grp", "blk"):
        size = lax.axis_size(axis)
        bit = 1
        while bit < size:
            value = value + lax.ppermute(value, axis, [(i, i ^ bit) for i in range(size)])
            bit *= 2
    return value


def body(user_prior, item_factors, user_tiles, item_tiles, counts):
    pairs = counts.shape[0]
    tile = counts.shape[1]
    rank = item_factors.shape[1]
    n_blk = lax.axis_size("blk")
    n_grp = lax.axis_size("grp")
    n_all = n_blk * n_grp
    own_rows = user_prior.shape[0]
    own_tiles = own_rows // tile
    user_blocks = own_tiles * n_grp
    tiles_held = item_factors.shape[0] // tile
    slots_each = max(2, pairs // n_all)
    my_blk = lax.axis_index("blk")
    my_grp = lax.axis_index("grp")
    me = my_blk * n_grp + my_grp

    holder = item_tiles // tiles_held
    position = jnp.arange(pairs, dtype=jnp.int32)
    earlier = (holder[None, :] == holder[:, None]) & (position[None, :] < position[:, None])
    order = jnp.sum(earlier.astype(jnp.int32), axis=1)
    packed = (item_tiles * slots_each + order) * user_blocks + user_tiles
    every = lax.all_to_all(
        jnp.broadcast_to(packed, (n_all, pairs)), ("blk", "grp"),
        split_axis=0, concat_axis=0, tiled=True,
    )
    all_user = every % user_blocks
    all_order = every // user_blocks % slots_each
    all_item = every // (user_blocks * slots_each)
    all_holder = all_item // tiles_held
    all_slot = all_item % tiles_held

    asks = n_grp * slots_each
    mine = (all_holder == me).reshape(n_blk, -1)
    at = (jnp.arange(n_grp * pairs, dtype=jnp.int32) // pairs) * slots_each
    at = at + all_order.reshape(n_blk, -1)
    slots = jnp.arange(asks, dtype=jnp.int32)
    wanted = jnp.sum(
        jnp.where(
            mine[:, None, :] & (at[:, None, :] == slots[:, None]),
            all_slot.reshape(n_blk, 1, -1), 0,
        ),
        axis=2,
    )
    held = item_factors.reshape(tiles_held, tile, rank)
    column = []
    for shift in range(n_blk):
        wanted_there = lax.dynamic_index_in_dim(wanted, (my_blk + shift) % n_blk, 0, keepdims=False)
        asked = take_tiles(held, wanted_there)
        if shift:
            asked = lax.ppermute(asked, "blk", [(i, (i + shift) % n_blk) for i in range(n_blk)])
        column.append(asked)
    column = jnp.concatenate(column, axis=0)

    owner = user_tiles // own_tiles
    earlier = (owner[None, :] == owner[:, None]) & (position[None, :] < position[:, None])
    place = owner * COUNT_CAP + jnp.sum(earlier.astype(jnp.int32), axis=1)
    place = jnp.where(place < (owner + 1) * COUNT_CAP, place, -1)
    cells = jnp.arange(n_grp * COUNT_CAP, dtype=jnp.int32)
    chosen = jnp.sum(jnp.where(place == cells[:, None], position, 0), axis=1)
    scaled = (ALPHA * counts.astype(jnp.float32)).astype(jnp.bfloat16)
    outgoing = take_tiles(scaled, chosen).reshape(n_grp, COUNT_CAP, tile, tile)
    counts_in = lax.all_to_all(outgoing, "grp", split_axis=0, concat_axis=0, tiled=True)
    counts_in = counts_in.reshape(n_grp * COUNT_CAP, tile, tile)

    live = jnp.any(counts > 0, axis=(1, 2))
    gram_local = lax.dot_general(
        item_factors, item_factors, (((0,), (0,)), ((), ())), preferred_element_type=jnp.float32
    )
    n_live = jnp.sum(live.astype(jnp.float32))
    note_rows = -(-n_all // (8 * rank)) * 8
    note = jnp.arange(note_rows * rank, dtype=jnp.int32).reshape(note_rows, rank)
    note = jnp.where(note == me, n_live, 0.0)
    shared = sum_everywhere(jnp.concatenate([gram_local, note], axis=0))
    gram = shared[:rank]
    lives = shared[rank:].reshape(-1)[:n_all].astype(jnp.int32)

    n_entries = n_grp * pairs
    all_live = (position < lives[:, None]).reshape(n_blk, n_entries)
    g_user = all_user.reshape(n_blk, n_entries)
    g_owner = g_user // own_tiles
    g_column = (all_holder % n_grp).reshape(n_blk, n_entries)
    index = jnp.arange(n_entries, dtype=jnp.int32)
    source = index // pairs
    bins = jnp.arange(n_grp * n_grp, dtype=jnp.int32)
    users = jnp.arange(user_blocks, dtype=jnp.int32)

    def marks(keys, ids):
        return (keys[..., None] == ids) & all_live[..., None]

    count_marks = marks(source * n_grp + g_owner, bins)
    tile_marks = marks(g_column * n_grp + g_owner, bins)
    user_marks = marks(g_user, users)
    most = lambda m: jnp.max(jnp.sum(m.astype(jnp.int32), axis=1))
    fits = (
        (most(count_marks) <= COUNT_CAP) & (most(tile_marks) <= TILE_CAP)
        & (most(user_marks) <= LOAD_CAP)
    )

    pick = lambda x: lax.dynamic_index_in_dim(x, my_blk, 0, keepdims=False)
    mark = jnp.concatenate(
        [pick(count_marks), pick(tile_marks), pick(user_marks)], axis=1
    ).astype(jnp.bfloat16)
    before = (index[None, :] < index[:, None]).astype(jnp.bfloat16)
    ahead = jnp.dot(before, mark, preferred_element_type=jnp.float32) * mark.astype(jnp.float32)
    n_bins = n_grp * n_grp
    rank_of = lambda lo, hi: jnp.sum(ahead[:, lo:hi], axis=1).astype(jnp.int32)
    count_rank = rank_of(0, n_bins)
    tile_rank = rank_of(n_bins, 2 * n_bins)
    user_rank = rank_of(2 * n_bins, 2 * n_bins + user_blocks)
    e_live, e_user, e_owner = pick(all_live), pick(g_user), pick(g_owner)
    e_column = pick(g_column)
    e_holder = pick(all_holder.reshape(n_blk, n_entries))
    e_order = pick(all_order.reshape(n_blk, n_entries))

    cells = jnp.arange(n_grp * TILE_CAP, dtype=jnp.int32)
    hit = e_live & (e_column == my_grp) & (tile_rank < TILE_CAP)
    from_blk = (my_blk - e_holder // n_grp) % n_blk
    where = (from_blk * n_grp + source) * slots_each + e_order
    chosen = jnp.sum(
        jnp.where(hit & (e_owner * TILE_CAP + tile_rank == cells[:, None]), where, 0), axis=1
    )
    outgoing = take_tiles(column, chosen).reshape(n_grp, TILE_CAP, tile, rank)
    items_in = lax.all_to_all(outgoing, "grp", split_axis=0, concat_axis=0, tiled=True)
    items_in = items_in.reshape(n_grp * TILE_CAP, tile, rank)

    cells = jnp.arange(own_tiles * LOAD_CAP, dtype=jnp.int32)
    hit = e_live & (e_owner == my_grp) & (user_rank < LOAD_CAP)
    hit = hit & (count_rank < COUNT_CAP) & (tile_rank < TILE_CAP)
    match = hit & ((e_user % own_tiles) * LOAD_CAP + user_rank == cells[:, None])
    count_at = jnp.sum(jnp.where(match, source * COUNT_CAP + count_rank, 0), axis=1)
    tile_at = jnp.sum(jnp.where(match, e_column * TILE_CAP + tile_rank, 0), axis=1)
    load = jnp.sum(match.reshape(own_tiles, -1).astype(jnp.int32), axis=1)
    by_owner = run_sweep(load, count_at, tile_at, user_prior, gram, counts_in, items_in)

    return lax.cond(
        fits, lambda done, *given: done, lambda done, *given: sweep_in_place(*given),
        by_owner, user_prior, item_factors, user_tiles, item_tiles, counts, live, gram_local,
    )


def solution(mesh):
    in_specs = (
        P(("blk", "grp"), None),
        P(("blk", "grp"), None),
        P(("blk", "grp")),
        P(("blk", "grp")),
        P(("blk", "grp"), None, None),
    )
    out_specs = P(("blk", "grp"), None)
    return jax.shard_map(body, mesh=mesh, in_specs=in_specs, out_specs=out_specs, check_vma=False)
```

```python
import functools

import jax
import jax.numpy as jnp
from jax import lax
from jax.experimental import pallas as pl
from jax.experimental.pallas import tpu as pltpu
from jax.sharding import PartitionSpec as P

ITERS = 3

ALPHA = 40.0
REG = 32.0
EPS = 1e-06

COUNT_CAP = 19
ITEM_CAPS = (13, 7)
LOADS = 128
SPAN = 2


def fetch_tiles(item_factors, item_tiles, pairs, tile, rank):
    n_all = lax.axis_size(("blk", "grp"))
    tiles_held = item_factors.shape[0] // tile
    slots_each = max(2, pairs // n_all)
    owner = item_tiles // tiles_held
    local_slot = item_tiles % tiles_held
    position = jnp.arange(pairs, dtype=jnp.int32)
    earlier = (owner[None, :] == owner[:, None]) & (position[None, :] < position[:, None])
    order = jnp.sum(earlier.astype(jnp.int32), axis=1)
    requests = jnp.full((n_all, slots_each), -1, jnp.int32).at[owner, order].set(local_slot)
    wanted = lax.all_to_all(requests, ("blk", "grp"), split_axis=0, concat_axis=0, tiled=True)
    held = item_factors.reshape(tiles_held, tile, rank)
    picked = jnp.take(held, jnp.maximum(wanted, 0), axis=0)
    picked = jnp.where((wanted >= 0)[:, :, None, None], picked, jnp.zeros((), picked.dtype))
    arrived = lax.all_to_all(picked, ("blk", "grp"), split_axis=0, concat_axis=0, tiled=True)
    return arrived[owner, order]


def row_sum(left, right):
    return jnp.sum(left * right, axis=1, keepdims=True)


def sweep_in_place(user_prior, item_factors, user_tiles, item_tiles, counts, live, gram_local):
    pairs = counts.shape[0]
    tile = counts.shape[1]
    rank = item_factors.shape[1]
    n_grp = lax.axis_size("grp")
    own_rows = user_prior.shape[0]
    block_rows = own_rows * n_grp
    user_blocks = block_rows // tile
    span = min(32, pairs)
    gram = lax.psum(gram_local, ("blk", "grp"))
    pair_tiles = fetch_tiles(item_factors, item_tiles, pairs, tile, rank)
    rounds = (jnp.sum(live.astype(jnp.int32)) + span - 1) // span
    tile_ids = jnp.arange(user_blocks, dtype=jnp.int32)

    def accumulate(low_tiles, with_rhs):

        def one_round(index, totals):
            start = index * span
            users = lax.dynamic_slice_in_dim(user_tiles, start, span)
            factors = lax.dynamic_slice_in_dim(pair_tiles, start, span)
            counted = lax.dynamic_slice_in_dim(counts, start, span).astype(jnp.float32)
            selector = (tile_ids[:, None] == users[None, :]).astype(jnp.float32)
            users_low = jnp.take(low_tiles, users, axis=0)
            scores = jnp.einsum(
                "bur,bir->bui", users_low, factors, preferred_element_type=jnp.float32
            )
            scaled = (ALPHA * counted * scores).astype(jnp.bfloat16)
            back = jnp.einsum("bui,bir->bur", scaled, factors, preferred_element_type=jnp.float32)
            result = [
                totals[0]
                + jnp.einsum("tb,bur->tur", selector, back, precision=lax.Precision.HIGHEST)
            ]
            if with_rhs:
                confidence = jnp.where(counted > 0, 1.0 + ALPHA * counted, 0.0).astype(jnp.bfloat16)
                pulled = jnp.einsum(
                    "bui,bir->bur", confidence, factors, preferred_element_type=jnp.float32
                )
                result.append(
                    totals[1]
                    + jnp.einsum("tb,bur->tur", selector, pulled, precision=lax.Precision.HIGHEST)
                )
            return tuple(result)

        zeros = jnp.zeros((user_blocks, tile, rank), jnp.float32)
        start_state = (zeros, zeros) if with_rhs else (zeros,)
        totals = lax.fori_loop(0, rounds, one_round, start_state)
        return tuple((total.reshape(block_rows, rank) for total in totals))

    def gram_term(vectors):
        return jnp.dot(vectors, gram, precision=lax.Precision.HIGHEST) + REG * vectors

    low = lax.all_gather(user_prior.astype(jnp.bfloat16), "grp", axis=0, tiled=True)
    pair_part, rhs_part = accumulate(low.reshape(user_blocks, tile, rank), True)
    pair_share, rhs_share = (
        lax.psum_scatter(pair_part, "grp", scatter_dimension=0, tiled=True),
        lax.psum_scatter(rhs_part, "grp", scatter_dimension=0, tiled=True),
    )
    solution = user_prior
    residual = rhs_share - (gram_term(solution) + pair_share)
    direction = residual
    norm_now = row_sum(residual, residual)
    for step in range(ITERS):
        low = lax.all_gather(direction.astype(jnp.bfloat16), "grp", axis=0, tiled=True)
        (pair_part,) = accumulate(low.reshape(user_blocks, tile, rank), False)
        image = gram_term(direction) + lax.psum_scatter(
            pair_part, "grp", scatter_dimension=0, tiled=True
        )
        alpha = norm_now / (row_sum(direction, image) + EPS)
        solution = solution + alpha * direction
        residual = residual - alpha * image
        fresh = row_sum(residual, residual)
        direction = residual + fresh / (norm_now + EPS) * direction
        norm_now = fresh
    return solution


def sweep_kernel(n_tiles, n_grp, item_caps, plan, prior_ref, gram_ref, *refs):
    n_pieces = n_grp * (1 + len(item_caps))
    pieces, out_ref = refs[:n_pieces], refs[n_pieces]
    weights, factors, low, image, residual, direction, sems = refs[n_pieces + 1:]
    tile, rank = factors.shape[1:]
    caps = [COUNT_CAP] * n_grp + [cap for cap in item_caps for _ in range(n_grp)]

    most = plan[0]
    total = plan[0]
    for user in range(1, n_tiles):
        most = jnp.maximum(most, plan[user])
        total = total + plan[user]
    rounds = (most + SPAN - 1) // SPAN

    start = n_tiles + n_pieces
    for piece, cap in enumerate(caps):
        kind = 0 if piece < n_grp else 1
        room = (weights, factors)[kind]

        def fetch(entry, carry, piece=piece, start=start, kind=kind, room=room):
            pltpu.make_async_copy(
                pieces[piece].at[entry], room.at[plan[start + entry]], sems.at[kind]
            ).start()
            return carry

        lax.fori_loop(0, plan[n_tiles + piece], fetch, 0)
        start += cap

    for user in range(n_tiles):

        def clear(entry, carry, user=user):
            at = ((entry // SPAN) * n_tiles + user) * SPAN + entry % SPAN
            weights[at] = jnp.zeros((tile, tile), weights.dtype)
            factors[at] = jnp.zeros((tile, rank), factors.dtype)
            return carry

        lax.fori_loop(plan[user], rounds * SPAN, clear, 0)

    def arrive(entry, carry):
        pltpu.make_async_copy(pieces[0].at[0], weights.at[0], sems.at[0]).wait()
        pltpu.make_async_copy(pieces[n_grp].at[0], factors.at[0], sems.at[1]).wait()
        return carry

    lax.fori_loop(0, total, arrive, 0)

    def pair_images(with_rhs):
        image[...] = jnp.zeros_like(image)
        if with_rhs:
            residual[...] = jnp.zeros_like(residual)

        def one_round(step, carry):
            for user in range(n_tiles):
                rows = slice(user * tile, (user + 1) * tile)
                at = (step * n_tiles + user) * SPAN
                items = factors[pl.ds(at, SPAN)].reshape(SPAN * tile, rank)
                scaled = jnp.concatenate(
                    [weights[at + part].astype(jnp.float32) for part in range(SPAN)], axis=1
                )
                scores = lax.dot_general(
                    low[rows, :], items, (((1,), (1,)), ((), ())),
                    preferred_element_type=jnp.float32,
                )
                image[rows, :] += jnp.dot(
                    (scaled * scores).astype(jnp.bfloat16), items,
                    preferred_element_type=jnp.float32,
                )
                if with_rhs:
                    confidence = jnp.where(scaled > 0, 1.0 + scaled, 0.0).astype(jnp.bfloat16)
                    residual[rows, :] += jnp.dot(
                        confidence, items, preferred_element_type=jnp.float32
                    )
            return carry

        lax.fori_loop(0, rounds, one_round, 0)

    def gram_term(vectors):
        return jnp.dot(
            vectors, gram_ref[...], precision=lax.Precision.HIGHEST,
            preferred_element_type=jnp.float32,
        ) + REG * vectors

    prior = prior_ref[...]
    low[...] = prior.astype(jnp.bfloat16)
    pair_images(True)
    first = residual[...] - (gram_term(prior) + image[...])
    residual[...] = first
    direction[...] = first
    out_ref[...] = prior
    norm_now = row_sum(first, first)
    for step in range(ITERS):
        heading = direction[...]
        low[...] = heading.astype(jnp.bfloat16)
        pair_images(False)
        shown = gram_term(heading) + image[...]
        alpha = norm_now / (row_sum(heading, shown) + EPS)
        out_ref[...] += alpha * heading
        if step < ITERS - 1:
            left = residual[...] - alpha * shown
            residual[...] = left
            fresh = row_sum(left, left)
            direction[...] = left + (fresh / (norm_now + EPS)) * heading
            norm_now = fresh


def run_sweep(plan, user_prior, gram, count_pieces, item_pieces, item_caps):
    own_rows, rank = user_prior.shape
    tile = count_pieces[0].shape[1]
    n_tiles = own_rows // tile
    room = LOADS // SPAN * SPAN
    smem = pl.BlockSpec(memory_space=pltpu.SMEM)
    vmem = pl.BlockSpec(memory_space=pltpu.VMEM)
    anywhere = pl.BlockSpec(memory_space=pl.ANY)
    pieces = [*count_pieces, *item_pieces]
    return pl.pallas_call(
        functools.partial(sweep_kernel, n_tiles, len(count_pieces), item_caps),
        out_shape=jax.ShapeDtypeStruct((own_rows, rank), jnp.float32),
        in_specs=[smem, vmem, vmem] + [anywhere] * len(pieces),
        out_specs=vmem,
        scratch_shapes=[
            pltpu.VMEM((room, tile, tile), jnp.bfloat16),
            pltpu.VMEM((room, tile, rank), jnp.bfloat16),
            pltpu.VMEM((own_rows, rank), jnp.bfloat16),
            pltpu.VMEM((own_rows, rank), jnp.float32),
            pltpu.VMEM((own_rows, rank), jnp.float32),
            pltpu.VMEM((own_rows, rank), jnp.float32),
            pltpu.SemaphoreType.DMA((2,)),
        ],
        compiler_params=pltpu.CompilerParams(vmem_limit_bytes=32 * 2**20),
        name="sweep",
    )(plan, user_prior, gram, *pieces)


def take_tiles(tiles, chosen):
    return jnp.take(tiles, chosen, axis=0, mode="clip")


def sum_everywhere(value):
    for axis in ("grp", "blk"):
        size = lax.axis_size(axis)
        bit = 1
        while bit < size:
            value = value + lax.ppermute(value, axis, [(i, i ^ bit) for i in range(size)])
            bit *= 2
    return value


def choose(keys, hit, cells, values):
    return jnp.sum(jnp.where(hit & (keys == cells[:, None]), values, 0), axis=1)


def body(user_prior, item_factors, user_tiles, item_tiles, counts):
    pairs = counts.shape[0]
    tile = counts.shape[1]
    rank = item_factors.shape[1]
    n_blk = lax.axis_size("blk")
    n_grp = lax.axis_size("grp")
    n_all = n_blk * n_grp
    own_rows = user_prior.shape[0]
    own_tiles = own_rows // tile
    load_cap = LOADS // own_tiles
    user_blocks = own_tiles * n_grp
    tiles_held = item_factors.shape[0] // tile
    slots_each = max(2, pairs // n_all)
    my_blk = lax.axis_index("blk")
    my_grp = lax.axis_index("grp")
    me = my_blk * n_grp + my_grp
    partners = [[(i, i ^ off) for i in range(n_grp)] for off in range(n_grp)]
    partner = my_grp ^ jnp.arange(n_grp, dtype=jnp.int32)

    live = jnp.any(counts > 0, axis=(1, 2))
    scaled = (ALPHA * counts.astype(jnp.float32)).astype(jnp.bfloat16)
    holder = item_tiles // tiles_held
    position = jnp.arange(pairs, dtype=jnp.int32)
    earlier = (holder[None, :] == holder[:, None]) & (position[None, :] < position[:, None])
    order = jnp.sum(earlier.astype(jnp.int32), axis=1)
    packed = ((item_tiles * 2 + live.astype(jnp.int32)) * slots_each + order) * user_blocks + user_tiles
    every = lax.all_to_all(
        jnp.broadcast_to(packed, (n_all, pairs)), ("blk", "grp"),
        split_axis=0, concat_axis=0, tiled=True,
    )

    owner = user_tiles // own_tiles
    earlier = (owner[None, :] == owner[:, None]) & (position[None, :] < position[:, None])
    place = jnp.sum(earlier.astype(jnp.int32), axis=1)
    place = jnp.where(place < COUNT_CAP, (owner ^ my_grp) * COUNT_CAP + place, -1)
    chosen = choose(place, True, jnp.arange(n_grp * COUNT_CAP, dtype=jnp.int32), position)
    count_pieces = []
    for off in range(n_grp):
        piece = take_tiles(scaled, chosen[off * COUNT_CAP:(off + 1) * COUNT_CAP])
        count_pieces.append(lax.ppermute(piece, "grp", partners[off]) if off else piece)

    n_entries = n_grp * pairs
    every = every.reshape(n_blk, n_entries)
    all_user = every % user_blocks
    every = every // user_blocks
    all_order = every % slots_each
    every = every // slots_each
    all_live = every % 2 == 1
    all_item = every // 2
    all_holder = all_item // tiles_held
    all_slot = all_item % tiles_held
    all_owner = all_user // own_tiles
    all_column = all_holder % n_grp
    blocks = jnp.arange(n_blk, dtype=jnp.int32)[:, None]
    all_shift = (blocks - all_holder // n_grp) % n_blk
    index = jnp.arange(n_entries, dtype=jnp.int32)
    source = index // pairs

    asks = n_grp * slots_each
    slots = jnp.arange(asks, dtype=jnp.int32)
    at = source * slots_each + all_order
    wanted = jnp.sum(
        jnp.where(
            (all_holder == me)[:, None, :] & (at[:, None, :] == slots[:, None]),
            all_slot[:, None, :], 0,
        ),
        axis=2,
    )
    held = item_factors.reshape(tiles_held, tile, rank)
    column = []
    for shift in range(n_blk):
        wanted_there = lax.dynamic_index_in_dim(wanted, (my_blk + shift) % n_blk, 0, keepdims=False)
        asked = take_tiles(held, wanted_there)
        if shift:
            asked = lax.ppermute(asked, "blk", [(i, (i + shift) % n_blk) for i in range(n_blk)])
        column.append(asked)

    gram_local = lax.dot_general(
        item_factors, item_factors, (((0,), (0,)), ((), ())), preferred_element_type=jnp.float32
    )
    gram = sum_everywhere(gram_local)

    far = n_blk // 2
    parts = [[shift for shift in range(n_blk) if shift != far], [far]]
    all_far = all_shift == far

    def most(keys, bins, counted):
        ids = jnp.arange(bins, dtype=jnp.int32)
        hits = (keys[:, None, :] == ids[:, None]) & counted[:, None, :]
        return jnp.max(jnp.sum(hits.astype(jnp.int32), axis=2))

    item_bins = all_column * n_grp + all_owner
    fits = (
        (most(source * n_grp + all_owner, n_grp * n_grp, all_live) <= COUNT_CAP)
        & (most(item_bins, n_grp * n_grp, all_live & ~all_far) <= ITEM_CAPS[0])
        & (most(item_bins, n_grp * n_grp, all_live & all_far) <= ITEM_CAPS[1])
        & (most(all_user, user_blocks, all_live) <= load_cap)
    )

    pick = lambda x: lax.dynamic_index_in_dim(x, my_blk, 0, keepdims=False)
    e_live, e_user, e_owner = pick(all_live), pick(all_user), pick(all_owner)
    e_column, e_order, e_far = pick(all_column), pick(all_order), pick(all_far)
    e_shift = pick(all_shift)
    to_me = e_live & (e_owner == my_grp)
    from_me = e_live & (e_column == my_grp)
    members = jnp.arange(n_grp, dtype=jnp.int32)[:, None]
    local_user = e_user % own_tiles
    marks = [
        to_me & (source == members),
        to_me & (local_user == jnp.arange(own_tiles, dtype=jnp.int32)[:, None]),
    ]
    for inside in (~e_far, e_far):
        marks.append(to_me & inside & (e_column == members))
        marks.append(from_me & inside & (e_owner == members))
    sizes = [mark.shape[0] for mark in marks]
    marks = jnp.concatenate(marks, axis=0).astype(jnp.bfloat16)
    before = (index[:, None] < index[None, :]).astype(jnp.bfloat16)
    ahead = jnp.dot(marks, before, preferred_element_type=jnp.float32) * marks.astype(jnp.float32)
    ranks, start = [], 0
    for size in sizes:
        ranks.append(jnp.sum(ahead[start:start + size], axis=0).astype(jnp.int32))
        start += size
    count_rank, user_rank = ranks[:2]

    hit = to_me & fits
    room_at = ((user_rank // SPAN) * own_tiles + local_user) * SPAN + user_rank % SPAN
    lengths = lambda keys: jnp.sum((hit & (keys == members)).astype(jnp.int32), axis=1)
    loads = jnp.sum(
        (hit & (local_user == jnp.arange(own_tiles, dtype=jnp.int32)[:, None])).astype(jnp.int32), axis=1
    )
    source_off = source ^ my_grp
    column_off = e_column ^ my_grp
    cells = jnp.arange(n_grp * COUNT_CAP, dtype=jnp.int32)
    sizes = [loads, lengths(source_off)]
    tables = [choose(source_off * COUNT_CAP + count_rank, hit, cells, room_at)]
    item_pieces = []
    for number, (shifts, inside) in enumerate(zip(parts, (~e_far, e_far))):
        cap = ITEM_CAPS[number]
        in_rank, out_rank = ranks[2 + 2 * number:4 + 2 * number]
        lies = jnp.zeros_like(e_shift)
        for spot, shift in enumerate(shifts):
            lies = jnp.where(e_shift == shift, spot, lies)
        lies = lies * asks + source * slots_each + e_order
        cells = jnp.arange(n_grp * cap, dtype=jnp.int32)
        keys = (e_owner ^ my_grp) * cap + out_rank
        chosen = choose(keys, from_me & inside & (out_rank < cap), cells, lies)
        tiles = jnp.concatenate([column[shift] for shift in shifts], axis=0)
        for off in range(n_grp):
            piece = take_tiles(tiles, chosen[off * cap:(off + 1) * cap])
            item_pieces.append(lax.ppermute(piece, "grp", partners[off]) if off else piece)
        sizes.append(jnp.sum((hit & inside & (column_off == members)).astype(jnp.int32), axis=1))
        tables.append(choose(column_off * cap + in_rank, hit & inside, cells, room_at))

    plan = jnp.concatenate(sizes + tables)
    by_owner = run_sweep(plan, user_prior, gram, count_pieces, item_pieces, ITEM_CAPS)

    return lax.cond(
        fits, lambda done, *given: done, lambda done, *given: sweep_in_place(*given),
        by_owner, user_prior, item_factors, user_tiles, item_tiles, counts, live, gram_local,
    )


def solution(mesh):
    in_specs = (
        P(("blk", "grp"), None),
        P(("blk", "grp"), None),
        P(("blk", "grp")),
        P(("blk", "grp")),
        P(("blk", "grp"), None, None),
    )
    out_specs = P(("blk", "grp"), None)
    return jax.shard_map(body, mesh=mesh, in_specs=in_specs, out_specs=out_specs, check_vma=False)
```

```python
import functools

import jax
import jax.numpy as jnp
from jax import lax
from jax.experimental import pallas as pl
from jax.experimental.pallas import tpu as pltpu
from jax.sharding import PartitionSpec as P

ITERS = 3

ALPHA = 40.0
REG = 32.0
EPS = 1e-06

FAR_CAP = 14
COUNT_CAP = 24
ITEM_CAP = 20
LOADS = 128
SPAN = 2


def fetch_tiles(item_factors, item_tiles, pairs, tile, rank):
    n_all = lax.axis_size(("blk", "grp"))
    tiles_held = item_factors.shape[0] // tile
    slots_each = max(2, pairs // n_all)
    owner = item_tiles // tiles_held
    local_slot = item_tiles % tiles_held
    position = jnp.arange(pairs, dtype=jnp.int32)
    earlier = (owner[None, :] == owner[:, None]) & (position[None, :] < position[:, None])
    order = jnp.sum(earlier.astype(jnp.int32), axis=1)
    requests = jnp.full((n_all, slots_each), -1, jnp.int32).at[owner, order].set(local_slot)
    wanted = lax.all_to_all(requests, ("blk", "grp"), split_axis=0, concat_axis=0, tiled=True)
    held = item_factors.reshape(tiles_held, tile, rank)
    picked = jnp.take(held, jnp.maximum(wanted, 0), axis=0)
    picked = jnp.where((wanted >= 0)[:, :, None, None], picked, jnp.zeros((), picked.dtype))
    arrived = lax.all_to_all(picked, ("blk", "grp"), split_axis=0, concat_axis=0, tiled=True)
    return arrived[owner, order]


def row_sum(left, right):
    return jnp.sum(left * right, axis=1, keepdims=True)


def sweep_in_place(user_prior, item_factors, user_tiles, item_tiles, counts, live, gram_local):
    pairs = counts.shape[0]
    tile = counts.shape[1]
    rank = item_factors.shape[1]
    n_grp = lax.axis_size("grp")
    own_rows = user_prior.shape[0]
    block_rows = own_rows * n_grp
    user_blocks = block_rows // tile
    span = min(32, pairs)
    gram = lax.psum(gram_local, ("blk", "grp"))
    pair_tiles = fetch_tiles(item_factors, item_tiles, pairs, tile, rank)
    rounds = (jnp.sum(live.astype(jnp.int32)) + span - 1) // span
    tile_ids = jnp.arange(user_blocks, dtype=jnp.int32)

    def accumulate(low_tiles, with_rhs):

        def one_round(index, totals):
            start = index * span
            users = lax.dynamic_slice_in_dim(user_tiles, start, span)
            factors = lax.dynamic_slice_in_dim(pair_tiles, start, span)
            counted = lax.dynamic_slice_in_dim(counts, start, span).astype(jnp.float32)
            selector = (tile_ids[:, None] == users[None, :]).astype(jnp.float32)
            users_low = jnp.take(low_tiles, users, axis=0)
            scores = jnp.einsum(
                "bur,bir->bui", users_low, factors, preferred_element_type=jnp.float32
            )
            scaled = (ALPHA * counted * scores).astype(jnp.bfloat16)
            back = jnp.einsum("bui,bir->bur", scaled, factors, preferred_element_type=jnp.float32)
            result = [
                totals[0]
                + jnp.einsum("tb,bur->tur", selector, back, precision=lax.Precision.HIGHEST)
            ]
            if with_rhs:
                confidence = jnp.where(counted > 0, 1.0 + ALPHA * counted, 0.0).astype(jnp.bfloat16)
                pulled = jnp.einsum(
                    "bui,bir->bur", confidence, factors, preferred_element_type=jnp.float32
                )
                result.append(
                    totals[1]
                    + jnp.einsum("tb,bur->tur", selector, pulled, precision=lax.Precision.HIGHEST)
                )
            return tuple(result)

        zeros = jnp.zeros((user_blocks, tile, rank), jnp.float32)
        start_state = (zeros, zeros) if with_rhs else (zeros,)
        totals = lax.fori_loop(0, rounds, one_round, start_state)
        return tuple((total.reshape(block_rows, rank) for total in totals))

    def gram_term(vectors):
        return jnp.dot(vectors, gram, precision=lax.Precision.HIGHEST) + REG * vectors

    low = lax.all_gather(user_prior.astype(jnp.bfloat16), "grp", axis=0, tiled=True)
    pair_part, rhs_part = accumulate(low.reshape(user_blocks, tile, rank), True)
    pair_share, rhs_share = (
        lax.psum_scatter(pair_part, "grp", scatter_dimension=0, tiled=True),
        lax.psum_scatter(rhs_part, "grp", scatter_dimension=0, tiled=True),
    )
    solution = user_prior
    residual = rhs_share - (gram_term(solution) + pair_share)
    direction = residual
    norm_now = row_sum(residual, residual)
    for step in range(ITERS):
        low = lax.all_gather(direction.astype(jnp.bfloat16), "grp", axis=0, tiled=True)
        (pair_part,) = accumulate(low.reshape(user_blocks, tile, rank), False)
        image = gram_term(direction) + lax.psum_scatter(
            pair_part, "grp", scatter_dimension=0, tiled=True
        )
        alpha = norm_now / (row_sum(direction, image) + EPS)
        solution = solution + alpha * direction
        residual = residual - alpha * image
        fresh = row_sum(residual, residual)
        direction = residual + fresh / (norm_now + EPS) * direction
        norm_now = fresh
    return solution


def sweep_kernel(
    n_tiles, plan, prior_ref, gram_ref, counts_own, counts_mate, items_own, items_mate, out_ref,
    weights, factors, low, image, residual, direction, sems,
):
    tile, rank = factors.shape[1:]
    most = plan[0]
    total = plan[0]
    for user in range(1, n_tiles):
        most = jnp.maximum(most, plan[user])
        total = total + plan[user]
    rounds = (most + SPAN - 1) // SPAN

    def fetch(room, sem, at, place, own, mate):
        @pl.when(at % 2 == 0)
        def _():
            pltpu.make_async_copy(own.at[at // 2], room.at[place], sem).start()

        @pl.when(at % 2 == 1)
        def _():
            pltpu.make_async_copy(mate.at[at // 2], room.at[place], sem).start()

    for user in range(n_tiles):

        def bring(entry, carry, user=user):
            place = ((entry // SPAN) * n_tiles + user) * SPAN + entry % SPAN
            fetch(weights, sems.at[0], plan[n_tiles + place], place, counts_own, counts_mate)
            fetch(factors, sems.at[1], plan[n_tiles + LOADS + place], place, items_own, items_mate)
            return carry

        def clear(entry, carry, user=user):
            place = ((entry // SPAN) * n_tiles + user) * SPAN + entry % SPAN
            weights[place] = jnp.zeros((tile, tile), weights.dtype)
            factors[place] = jnp.zeros((tile, rank), factors.dtype)
            return carry

        lax.fori_loop(0, plan[user], bring, 0)
        lax.fori_loop(plan[user], rounds * SPAN, clear, 0)

    def arrive(entry, carry):
        pltpu.make_async_copy(counts_own.at[0], weights.at[0], sems.at[0]).wait()
        pltpu.make_async_copy(items_own.at[0], factors.at[0], sems.at[1]).wait()
        return carry

    lax.fori_loop(0, total, arrive, 0)

    def pair_images(with_rhs):
        image[...] = jnp.zeros_like(image)
        if with_rhs:
            residual[...] = jnp.zeros_like(residual)

        def one_round(step, carry):
            for user in range(n_tiles):
                rows = slice(user * tile, (user + 1) * tile)
                at = (step * n_tiles + user) * SPAN
                items = factors[pl.ds(at, SPAN)].reshape(SPAN * tile, rank)
                scaled = jnp.concatenate(
                    [weights[at + part].astype(jnp.float32) for part in range(SPAN)], axis=1
                )
                scores = lax.dot_general(
                    low[rows, :], items, (((1,), (1,)), ((), ())),
                    preferred_element_type=jnp.float32,
                )
                image[rows, :] += jnp.dot(
                    (scaled * scores).astype(jnp.bfloat16), items,
                    preferred_element_type=jnp.float32,
                )
                if with_rhs:
                    confidence = jnp.where(scaled > 0, 1.0 + scaled, 0.0).astype(jnp.bfloat16)
                    residual[rows, :] += jnp.dot(
                        confidence, items, preferred_element_type=jnp.float32
                    )
            return carry

        lax.fori_loop(0, rounds, one_round, 0)

    def gram_term(vectors):
        return jnp.dot(
            vectors, gram_ref[...], precision=lax.Precision.HIGHEST,
            preferred_element_type=jnp.float32,
        ) + REG * vectors

    prior = prior_ref[...]
    low[...] = prior.astype(jnp.bfloat16)
    pair_images(True)
    first = residual[...] - (gram_term(prior) + image[...])
    residual[...] = first
    direction[...] = first
    out_ref[...] = prior
    norm_now = row_sum(first, first)
    for step in range(ITERS):
        heading = direction[...]
        low[...] = heading.astype(jnp.bfloat16)
        pair_images(False)
        shown = gram_term(heading) + image[...]
        alpha = norm_now / (row_sum(heading, shown) + EPS)
        out_ref[...] += alpha * heading
        if step < ITERS - 1:
            left = residual[...] - alpha * shown
            residual[...] = left
            fresh = row_sum(left, left)
            direction[...] = left + (fresh / (norm_now + EPS)) * heading
            norm_now = fresh


def run_sweep(plan, user_prior, gram, *pieces):
    own_rows, rank = user_prior.shape
    tile = pieces[0].shape[1]
    n_tiles = own_rows // tile
    vmem = pl.BlockSpec(memory_space=pltpu.VMEM)
    return pl.pallas_call(
        functools.partial(sweep_kernel, n_tiles),
        out_shape=jax.ShapeDtypeStruct((own_rows, rank), jnp.float32),
        in_specs=[pl.BlockSpec(memory_space=pltpu.SMEM), vmem, vmem]
        + [pl.BlockSpec(memory_space=pl.ANY)] * len(pieces),
        out_specs=vmem,
        scratch_shapes=[
            pltpu.VMEM((LOADS, tile, tile), jnp.bfloat16),
            pltpu.VMEM((LOADS, tile, rank), jnp.bfloat16),
            pltpu.VMEM((own_rows, rank), jnp.bfloat16),
            pltpu.VMEM((own_rows, rank), jnp.float32),
            pltpu.VMEM((own_rows, rank), jnp.float32),
            pltpu.VMEM((own_rows, rank), jnp.float32),
            pltpu.SemaphoreType.DMA((2,)),
        ],
        compiler_params=pltpu.CompilerParams(vmem_limit_bytes=32 * 2**20),
        name="sweep",
    )(plan, user_prior, gram, *pieces)


def pack_kernel(n_sources, lengths, chosen, *refs):
    sources, outs, sem = refs[:n_sources], refs[n_sources:-1], refs[-1]
    start = 0
    for out, length in zip(outs, lengths):

        def place(spot, carry, out=out, start=start):
            at = chosen[start + spot]
            for number, source in enumerate(sources):

                @pl.when(at % n_sources == number)
                def _(source=source):
                    pltpu.make_async_copy(source.at[at // n_sources], out.at[spot], sem).start()

            return carry

        lax.fori_loop(0, length, place, 0)
        start += length
    for out in outs:
        pltpu.make_async_copy(out, out, sem).wait()


def pack_tiles(name, sources, chosen, lengths):
    anywhere = pl.BlockSpec(memory_space=pl.ANY)
    shape = sources[0].shape[1:]
    return pl.pallas_call(
        functools.partial(pack_kernel, len(sources), lengths),
        out_shape=[jax.ShapeDtypeStruct((n, *shape), sources[0].dtype) for n in lengths],
        in_specs=[pl.BlockSpec(memory_space=pltpu.SMEM)] + [anywhere] * len(sources),
        out_specs=[anywhere] * len(lengths),
        scratch_shapes=[pltpu.SemaphoreType.DMA],
        name=name,
    )(chosen, *sources)


def sum_everywhere(value):
    for axis in ("grp", "blk"):
        size = lax.axis_size(axis)
        bit = 1
        while bit < size:
            value = value + lax.ppermute(value, axis, [(i, i ^ bit) for i in range(size)])
            bit *= 2
    return value


def choose(keys, hit, cells, values):
    return jnp.sum(jnp.where(hit & (keys == cells[:, None]), values, 0), axis=1)


def body(user_prior, item_factors, user_tiles, item_tiles, counts):
    pairs = counts.shape[0]
    tile = counts.shape[1]
    rank = item_factors.shape[1]
    n_blk = lax.axis_size("blk")
    n_grp = lax.axis_size("grp")
    n_all = n_blk * n_grp
    n_chips = n_grp // 2
    own_rows = user_prior.shape[0]
    own_tiles = own_rows // tile
    user_blocks = own_tiles * n_grp
    tiles_held = item_factors.shape[0] // tile
    my_blk = lax.axis_index("blk")
    my_grp = lax.axis_index("grp")
    my_chip = my_grp // 2
    my_core = my_grp % 2
    lanes = [[chip * 2 + core for chip in range(n_chips)] for core in range(2)]

    def swap(value):
        return lax.ppermute(value, "grp", [(i, i ^ 1) for i in range(n_grp)])

    def to_chips(value):
        return lax.all_to_all(
            value, "grp", split_axis=0, concat_axis=0, tiled=True, axis_index_groups=lanes
        )

    held = item_factors.reshape(tiles_held, tile, rank)
    held_mate = swap(held)
    live = jnp.any(counts > 0, axis=(1, 2))
    scaled = (ALPHA * counts.astype(jnp.float32)).astype(jnp.bfloat16)
    scaled_mate = swap(scaled)
    packed = (item_tiles * 2 + live.astype(jnp.int32)) * user_blocks + user_tiles
    every = lax.all_to_all(
        jnp.broadcast_to(packed, (n_all, pairs)), ("blk", "grp"),
        split_axis=0, concat_axis=0, tiled=True,
    )
    n_entries = n_grp * pairs
    every = every.reshape(n_blk, n_entries)
    all_user = every % user_blocks
    every = every // user_blocks
    all_live = every % 2 == 1
    all_item = every // 2
    all_owner = all_user // own_tiles
    all_chip = all_item // (2 * tiles_held)
    all_tile = all_item % (2 * tiles_held)
    index = jnp.arange(n_entries, dtype=jnp.int32)
    source = index // pairs

    ids = jnp.arange(2 * tiles_held, dtype=jnp.int32)
    chips = jnp.arange(n_blk * n_chips, dtype=jnp.int32)
    on_chip = ((all_chip[:, None, :] == chips[:, None]) & all_live[:, None, :]).astype(jnp.bfloat16)
    on_tile = (all_tile[:, :, None] == ids).astype(jnp.bfloat16)
    needed = jnp.einsum("bce,bet->bct", on_chip, on_tile, preferred_element_type=jnp.float32) > 0
    fewer = (ids[:, None] < ids[None, :]).astype(jnp.bfloat16)
    tiles_ahead = jnp.einsum(
        "bct,ts->bcs", needed.astype(jnp.bfloat16), fewer, preferred_element_type=jnp.float32
    ).astype(jnp.int32)

    here = my_blk * n_chips + my_chip
    at_chip = lambda x: lax.dynamic_index_in_dim(x, here, 1, keepdims=False)
    spots = 2 * jnp.arange(FAR_CAP, dtype=jnp.int32) + my_core
    asked = jnp.sum(
        jnp.where(
            at_chip(needed)[:, None, :] & (at_chip(tiles_ahead)[:, None, :] == spots[:, None]),
            ((ids // tiles_held) ^ my_core) + 2 * (ids % tiles_held), 0,
        ),
        axis=2,
    )
    asked = jnp.take(asked, (my_blk + jnp.arange(1, n_blk)) % n_blk, axis=0, mode="clip")
    outgoing = pack_tiles("pack_far", [held, held_mate], asked.reshape(-1), [FAR_CAP] * (n_blk - 1))
    far = [
        lax.ppermute(piece, "blk", [(i, (i + 1 + shift) % n_blk) for i in range(n_blk)])
        for shift, piece in enumerate(outgoing)
    ]
    far_mate = [swap(piece) for piece in far]

    gram_local = lax.dot_general(
        item_factors, item_factors, (((0,), (0,)), ((), ())), preferred_element_type=jnp.float32
    )
    gram = sum_everywhere(gram_local)

    def most(keys, bins):
        marks = (keys[:, None, :] == jnp.arange(bins, dtype=jnp.int32)[:, None]) & all_live[:, None, :]
        return jnp.max(jnp.sum(marks.astype(jnp.int32), axis=2))

    to_chip = all_owner // 2
    elsewhere = chips // n_chips != jnp.arange(n_blk, dtype=jnp.int32)[:, None]
    asks = jnp.sum(needed.astype(jnp.int32), axis=2)
    fits = (
        (jnp.max(jnp.where(elsewhere, asks, 0)) <= 2 * FAR_CAP)
        & (most(source // 2 * n_chips + to_chip, n_chips * n_chips) <= 2 * COUNT_CAP)
        & (most(all_chip % n_chips * n_chips + to_chip, n_chips * n_chips) <= 2 * ITEM_CAP)
        & (most(all_user, user_blocks) <= LOADS // own_tiles)
    )

    pick = lambda x: lax.dynamic_index_in_dim(x, my_blk, 0, keepdims=False)
    e_live, e_user, e_owner = pick(all_live), pick(all_user), pick(all_owner)
    e_chip, e_tile = pick(all_chip), pick(all_tile)
    e_blk, e_column = e_chip // n_chips, e_chip % n_chips
    e_to = e_owner // 2
    e_from = source // 2
    to_us = e_live & (e_to == my_chip)
    local_user = e_user % own_tiles
    members = jnp.arange(n_chips, dtype=jnp.int32)[:, None]
    marks = [
        e_live & (e_from == my_chip) & (e_to == members),
        to_us & (e_from == members),
        e_live & (e_column == my_chip) & (e_to == members),
        to_us & (e_column == members),
        e_live & (e_owner == my_grp) & (local_user == jnp.arange(own_tiles, dtype=jnp.int32)[:, None]),
    ]
    marks = jnp.concatenate(marks, axis=0).astype(jnp.bfloat16)
    before = (index[:, None] < index[None, :]).astype(jnp.bfloat16)
    ahead = jnp.dot(marks, before, preferred_element_type=jnp.float32) * marks.astype(jnp.float32)
    starts = [n_chips * n for n in range(5)] + [4 * n_chips + own_tiles]
    counts_out, counts_back, items_out, items_back, user_rank = [
        jnp.sum(ahead[lo:hi], axis=0).astype(jnp.int32) for lo, hi in zip(starts, starts[1:])
    ]

    mine = lambda place, cap: (place % 2 == my_core) & (place // 2 < cap)
    cells = jnp.arange(n_chips * COUNT_CAP, dtype=jnp.int32)
    chosen = choose(
        e_to * COUNT_CAP + counts_out // 2,
        e_live & (e_from == my_chip) & mine(counts_out, COUNT_CAP),
        cells, ((source % 2) ^ my_core) + 2 * (index % pairs),
    )
    (outgoing,) = pack_tiles("pack_counts", [scaled, scaled_mate], chosen, [n_chips * COUNT_CAP])
    counts_own = to_chips(outgoing)
    counts_mate = swap(counts_own)

    n_sources = 2 * n_blk
    own_chips = jnp.take(
        pick(tiles_ahead), jnp.arange(n_blk) * n_chips + my_chip, axis=0, mode="clip"
    ).reshape(-1)
    cells = jnp.arange(own_chips.shape[0], dtype=jnp.int32)[:, None]
    far_place = jnp.sum(
        jnp.where(e_blk * (2 * tiles_held) + e_tile == cells, own_chips[:, None], 0), axis=0
    )
    shift = (my_blk - e_blk) % n_blk
    near = shift == 0
    lane = jnp.where(near, e_tile // tiles_held, far_place % 2) ^ my_core
    row = jnp.where(near, e_tile % tiles_held, far_place // 2)
    cells = jnp.arange(n_chips * ITEM_CAP, dtype=jnp.int32)
    chosen = choose(
        e_to * ITEM_CAP + items_out // 2,
        fits & e_live & (e_column == my_chip) & mine(items_out, ITEM_CAP),
        cells, row * n_sources + lane * n_blk + shift,
    )
    (outgoing,) = pack_tiles(
        "pack_items", [held, *far, held_mate, *far_mate], chosen, [n_chips * ITEM_CAP]
    )
    outgoing, counts_own = lax.optimization_barrier((outgoing, counts_own))
    items_own = to_chips(outgoing)
    items_mate = swap(items_own)

    hit = fits & e_live & (e_owner == my_grp)
    room_at = ((user_rank // SPAN) * own_tiles + local_user) * SPAN + user_rank % SPAN
    loads = jnp.sum(
        (hit & (local_user == jnp.arange(own_tiles, dtype=jnp.int32)[:, None])).astype(jnp.int32), axis=1
    )
    cells = jnp.arange(LOADS, dtype=jnp.int32)
    count_at = ((counts_back % 2) ^ my_core) + 2 * (e_from * COUNT_CAP + counts_back // 2)
    item_at = ((items_back % 2) ^ my_core) + 2 * (e_column * ITEM_CAP + items_back // 2)
    plan = jnp.concatenate(
        [loads, choose(room_at, hit, cells, count_at), choose(room_at, hit, cells, item_at)]
    )
    by_owner = run_sweep(plan, user_prior, gram, counts_own, counts_mate, items_own, items_mate)

    return lax.cond(
        fits, lambda done, *given: done, lambda done, *given: sweep_in_place(*given),
        by_owner, user_prior, item_factors, user_tiles, item_tiles, counts, live, gram_local,
    )


def solution(mesh):
    in_specs = (
        P(("blk", "grp"), None),
        P(("blk", "grp"), None),
        P(("blk", "grp")),
        P(("blk", "grp")),
        P(("blk", "grp"), None, None),
    )
    out_specs = P(("blk", "grp"), None)
    return jax.shard_map(body, mesh=mesh, in_specs=in_specs, out_specs=out_specs, check_vma=False)
```

```python
import functools

import jax
import jax.numpy as jnp
from jax import lax
from jax.experimental import pallas as pl
from jax.experimental.pallas import tpu as pltpu
from jax.sharding import PartitionSpec as P

ITERS = 3

ALPHA = 40.0
REG = 32.0
EPS = 1e-06

FAR_CAP = 14
COUNT_CAP = 24
ITEM_CAP = 20
LOADS = 128
SPAN = 2


def fetch_tiles(item_factors, item_tiles, pairs, tile, rank):
    n_all = lax.axis_size(("blk", "grp"))
    tiles_held = item_factors.shape[0] // tile
    slots_each = max(2, pairs // n_all)
    owner = item_tiles // tiles_held
    local_slot = item_tiles % tiles_held
    position = jnp.arange(pairs, dtype=jnp.int32)
    earlier = (owner[None, :] == owner[:, None]) & (position[None, :] < position[:, None])
    order = jnp.sum(earlier.astype(jnp.int32), axis=1)
    requests = jnp.full((n_all, slots_each), -1, jnp.int32).at[owner, order].set(local_slot)
    wanted = lax.all_to_all(requests, ("blk", "grp"), split_axis=0, concat_axis=0, tiled=True)
    held = item_factors.reshape(tiles_held, tile, rank)
    picked = jnp.take(held, jnp.maximum(wanted, 0), axis=0)
    picked = jnp.where((wanted >= 0)[:, :, None, None], picked, jnp.zeros((), picked.dtype))
    arrived = lax.all_to_all(picked, ("blk", "grp"), split_axis=0, concat_axis=0, tiled=True)
    return arrived[owner, order]


def row_sum(left, right):
    return jnp.sum(left * right, axis=1, keepdims=True)


def sweep_in_place(user_prior, item_factors, user_tiles, item_tiles, counts, live, gram_local):
    pairs = counts.shape[0]
    tile = counts.shape[1]
    rank = item_factors.shape[1]
    n_grp = lax.axis_size("grp")
    own_rows = user_prior.shape[0]
    block_rows = own_rows * n_grp
    user_blocks = block_rows // tile
    span = min(32, pairs)
    gram = lax.psum(gram_local, ("blk", "grp"))
    pair_tiles = fetch_tiles(item_factors, item_tiles, pairs, tile, rank)
    rounds = (jnp.sum(live.astype(jnp.int32)) + span - 1) // span
    tile_ids = jnp.arange(user_blocks, dtype=jnp.int32)

    def accumulate(low_tiles, with_rhs):

        def one_round(index, totals):
            start = index * span
            users = lax.dynamic_slice_in_dim(user_tiles, start, span)
            factors = lax.dynamic_slice_in_dim(pair_tiles, start, span)
            counted = lax.dynamic_slice_in_dim(counts, start, span).astype(jnp.float32)
            selector = (tile_ids[:, None] == users[None, :]).astype(jnp.float32)
            users_low = jnp.take(low_tiles, users, axis=0)
            scores = jnp.einsum(
                "bur,bir->bui", users_low, factors, preferred_element_type=jnp.float32
            )
            scaled = (ALPHA * counted * scores).astype(jnp.bfloat16)
            back = jnp.einsum("bui,bir->bur", scaled, factors, preferred_element_type=jnp.float32)
            result = [
                totals[0]
                + jnp.einsum("tb,bur->tur", selector, back, precision=lax.Precision.HIGHEST)
            ]
            if with_rhs:
                confidence = jnp.where(counted > 0, 1.0 + ALPHA * counted, 0.0).astype(jnp.bfloat16)
                pulled = jnp.einsum(
                    "bui,bir->bur", confidence, factors, preferred_element_type=jnp.float32
                )
                result.append(
                    totals[1]
                    + jnp.einsum("tb,bur->tur", selector, pulled, precision=lax.Precision.HIGHEST)
                )
            return tuple(result)

        zeros = jnp.zeros((user_blocks, tile, rank), jnp.float32)
        start_state = (zeros, zeros) if with_rhs else (zeros,)
        totals = lax.fori_loop(0, rounds, one_round, start_state)
        return tuple((total.reshape(block_rows, rank) for total in totals))

    def gram_term(vectors):
        return jnp.dot(vectors, gram, precision=lax.Precision.HIGHEST) + REG * vectors

    low = lax.all_gather(user_prior.astype(jnp.bfloat16), "grp", axis=0, tiled=True)
    pair_part, rhs_part = accumulate(low.reshape(user_blocks, tile, rank), True)
    pair_share, rhs_share = (
        lax.psum_scatter(pair_part, "grp", scatter_dimension=0, tiled=True),
        lax.psum_scatter(rhs_part, "grp", scatter_dimension=0, tiled=True),
    )
    solution = user_prior
    residual = rhs_share - (gram_term(solution) + pair_share)
    direction = residual
    norm_now = row_sum(residual, residual)
    for step in range(ITERS):
        low = lax.all_gather(direction.astype(jnp.bfloat16), "grp", axis=0, tiled=True)
        (pair_part,) = accumulate(low.reshape(user_blocks, tile, rank), False)
        image = gram_term(direction) + lax.psum_scatter(
            pair_part, "grp", scatter_dimension=0, tiled=True
        )
        alpha = norm_now / (row_sum(direction, image) + EPS)
        solution = solution + alpha * direction
        residual = residual - alpha * image
        fresh = row_sum(residual, residual)
        direction = residual + fresh / (norm_now + EPS) * direction
        norm_now = fresh
    return solution


def sweep_kernel(
    n_tiles, plan, prior_ref, gram_ref, counts_own, counts_mate, items_own, items_mate, out_ref,
    weights, factors, low, image, residual, direction, sems,
):
    tile, rank = factors.shape[1:]
    most = plan[0]
    total = plan[0]
    for user in range(1, n_tiles):
        most = jnp.maximum(most, plan[user])
        total = total + plan[user]
    rounds = (most + SPAN - 1) // SPAN

    def fetch(room, sem, at, place, own, mate):
        @pl.when(at % 2 == 0)
        def _():
            pltpu.make_async_copy(own.at[at // 2], room.at[place], sem).start()

        @pl.when(at % 2 == 1)
        def _():
            pltpu.make_async_copy(mate.at[at // 2], room.at[place], sem).start()

    for user in range(n_tiles):

        def bring(entry, carry, user=user):
            place = ((entry // SPAN) * n_tiles + user) * SPAN + entry % SPAN
            fetch(weights, sems.at[0], plan[n_tiles + place], place, counts_own, counts_mate)
            fetch(factors, sems.at[1], plan[n_tiles + LOADS + place], place, items_own, items_mate)
            return carry

        def clear(entry, carry, user=user):
            place = ((entry // SPAN) * n_tiles + user) * SPAN + entry % SPAN
            weights[place] = jnp.zeros((tile, tile), weights.dtype)
            factors[place] = jnp.zeros((tile, rank), factors.dtype)
            return carry

        lax.fori_loop(0, plan[user], bring, 0)
        lax.fori_loop(plan[user], rounds * SPAN, clear, 0)

    def arrive(entry, carry):
        pltpu.make_async_copy(counts_own.at[0], weights.at[0], sems.at[0]).wait()
        pltpu.make_async_copy(items_own.at[0], factors.at[0], sems.at[1]).wait()
        return carry

    lax.fori_loop(0, total, arrive, 0)

    def pair_images(with_rhs):
        image[...] = jnp.zeros_like(image)
        if with_rhs:
            residual[...] = jnp.zeros_like(residual)

        def one_round(step, carry):
            for user in range(n_tiles):
                rows = slice(user * tile, (user + 1) * tile)
                at = (step * n_tiles + user) * SPAN
                items = factors[pl.ds(at, SPAN)].reshape(SPAN * tile, rank)
                scaled = jnp.concatenate(
                    [weights[at + part].astype(jnp.float32) for part in range(SPAN)], axis=1
                )
                scores = lax.dot_general(
                    low[rows, :], items, (((1,), (1,)), ((), ())),
                    preferred_element_type=jnp.float32,
                )
                image[rows, :] += jnp.dot(
                    (scaled * scores).astype(jnp.bfloat16), items,
                    preferred_element_type=jnp.float32,
                )
                if with_rhs:
                    confidence = jnp.where(scaled > 0, 1.0 + scaled, 0.0).astype(jnp.bfloat16)
                    residual[rows, :] += jnp.dot(
                        confidence, items, preferred_element_type=jnp.float32
                    )
            return carry

        lax.fori_loop(0, rounds, one_round, 0)

    def gram_term(vectors):
        return jnp.dot(
            vectors, gram_ref[...], precision=lax.Precision.HIGHEST,
            preferred_element_type=jnp.float32,
        ) + REG * vectors

    prior = prior_ref[...]
    low[...] = prior.astype(jnp.bfloat16)
    pair_images(True)
    first = residual[...] - (gram_term(prior) + image[...])
    residual[...] = first
    direction[...] = first
    out_ref[...] = prior
    norm_now = row_sum(first, first)
    for step in range(ITERS):
        heading = direction[...]
        low[...] = heading.astype(jnp.bfloat16)
        pair_images(False)
        shown = gram_term(heading) + image[...]
        alpha = norm_now / (row_sum(heading, shown) + EPS)
        out_ref[...] += alpha * heading
        if step < ITERS - 1:
            left = residual[...] - alpha * shown
            residual[...] = left
            fresh = row_sum(left, left)
            direction[...] = left + (fresh / (norm_now + EPS)) * heading
            norm_now = fresh


def run_sweep(plan, user_prior, gram, *pieces):
    own_rows, rank = user_prior.shape
    tile = pieces[0].shape[1]
    n_tiles = own_rows // tile
    vmem = pl.BlockSpec(memory_space=pltpu.VMEM)
    return pl.pallas_call(
        functools.partial(sweep_kernel, n_tiles),
        out_shape=jax.ShapeDtypeStruct((own_rows, rank), jnp.float32),
        in_specs=[pl.BlockSpec(memory_space=pltpu.SMEM), vmem, vmem]
        + [pl.BlockSpec(memory_space=pl.ANY)] * len(pieces),
        out_specs=vmem,
        scratch_shapes=[
            pltpu.VMEM((LOADS, tile, tile), jnp.bfloat16),
            pltpu.VMEM((LOADS, tile, rank), jnp.bfloat16),
            pltpu.VMEM((own_rows, rank), jnp.bfloat16),
            pltpu.VMEM((own_rows, rank), jnp.float32),
            pltpu.VMEM((own_rows, rank), jnp.float32),
            pltpu.VMEM((own_rows, rank), jnp.float32),
            pltpu.SemaphoreType.DMA((2,)),
        ],
        compiler_params=pltpu.CompilerParams(vmem_limit_bytes=32 * 2**20),
        name="sweep",
    )(plan, user_prior, gram, *pieces)


def pack_kernel(n_sources, lengths, chosen, *refs):
    sources, outs, sem = refs[:n_sources], refs[n_sources:-1], refs[-1]
    start = 0
    for out, length in zip(outs, lengths):

        def place(spot, carry, out=out, start=start):
            at = chosen[start + spot]
            for number, source in enumerate(sources):

                @pl.when(at % n_sources == number)
                def _(source=source):
                    pltpu.make_async_copy(source.at[at // n_sources], out.at[spot], sem).start()

            return carry

        lax.fori_loop(0, length, place, 0)
        start += length
    for out in outs:
        pltpu.make_async_copy(out, out, sem).wait()


def pack_tiles(name, sources, chosen, lengths):
    anywhere = pl.BlockSpec(memory_space=pl.ANY)
    shape = sources[0].shape[1:]
    return pl.pallas_call(
        functools.partial(pack_kernel, len(sources), lengths),
        out_shape=[jax.ShapeDtypeStruct((n, *shape), sources[0].dtype) for n in lengths],
        in_specs=[pl.BlockSpec(memory_space=pltpu.SMEM)] + [anywhere] * len(sources),
        out_specs=[pl.BlockSpec(memory_space=pltpu.VMEM)] * len(lengths),
        scratch_shapes=[pltpu.SemaphoreType.DMA],
        compiler_params=pltpu.CompilerParams(vmem_limit_bytes=32 * 2**20),
        name=name,
    )(chosen, *sources)


def sum_everywhere(value):
    for axis in ("grp", "blk"):
        size = lax.axis_size(axis)
        bit = 1
        while bit < size:
            value = value + lax.ppermute(value, axis, [(i, i ^ bit) for i in range(size)])
            bit *= 2
    return value


def choose(keys, hit, cells, values):
    return jnp.sum(jnp.where(hit & (keys == cells[:, None]), values, 0), axis=1)


def body(user_prior, item_factors, user_tiles, item_tiles, counts):
    pairs = counts.shape[0]
    tile = counts.shape[1]
    rank = item_factors.shape[1]
    n_blk = lax.axis_size("blk")
    n_grp = lax.axis_size("grp")
    n_all = n_blk * n_grp
    n_chips = n_grp // 2
    own_rows = user_prior.shape[0]
    own_tiles = own_rows // tile
    user_blocks = own_tiles * n_grp
    tiles_held = item_factors.shape[0] // tile
    my_blk = lax.axis_index("blk")
    my_grp = lax.axis_index("grp")
    my_chip = my_grp // 2
    my_core = my_grp % 2
    lanes = [[chip * 2 + core for chip in range(n_chips)] for core in range(2)]

    def swap(value):
        return lax.ppermute(value, "grp", [(i, i ^ 1) for i in range(n_grp)])

    def to_chips(value):
        return lax.all_to_all(
            value, "grp", split_axis=0, concat_axis=0, tiled=True, axis_index_groups=lanes
        )

    held = item_factors.reshape(tiles_held, tile, rank)
    held_mate = swap(held)
    live = jnp.any(counts > 0, axis=(1, 2))
    scaled = (ALPHA * counts.astype(jnp.float32)).astype(jnp.bfloat16)
    scaled_mate = swap(scaled)
    packed = (item_tiles * 2 + live.astype(jnp.int32)) * user_blocks + user_tiles
    every = lax.all_to_all(
        jnp.broadcast_to(packed, (n_all, pairs)), ("blk", "grp"),
        split_axis=0, concat_axis=0, tiled=True,
    )
    n_entries = n_grp * pairs
    every = every.reshape(n_blk, n_entries)
    all_user = every % user_blocks
    every = every // user_blocks
    all_live = every % 2 == 1
    all_item = every // 2
    all_owner = all_user // own_tiles
    all_chip = all_item // (2 * tiles_held)
    all_tile = all_item % (2 * tiles_held)
    index = jnp.arange(n_entries, dtype=jnp.int32)
    source = index // pairs

    ids = jnp.arange(2 * tiles_held, dtype=jnp.int32)
    chips = jnp.arange(n_blk * n_chips, dtype=jnp.int32)
    on_chip = ((all_chip[:, None, :] == chips[:, None]) & all_live[:, None, :]).astype(jnp.bfloat16)
    on_tile = (all_tile[:, :, None] == ids).astype(jnp.bfloat16)
    needed = jnp.einsum("bce,bet->bct", on_chip, on_tile, preferred_element_type=jnp.float32) > 0
    fewer = (ids[:, None] < ids[None, :]).astype(jnp.bfloat16)
    tiles_ahead = jnp.einsum(
        "bct,ts->bcs", needed.astype(jnp.bfloat16), fewer, preferred_element_type=jnp.float32
    ).astype(jnp.int32)

    here = my_blk * n_chips + my_chip
    at_chip = lambda x: lax.dynamic_index_in_dim(x, here, 1, keepdims=False)
    spots = 2 * jnp.arange(FAR_CAP, dtype=jnp.int32) + my_core
    asked = jnp.sum(
        jnp.where(
            at_chip(needed)[:, None, :] & (at_chip(tiles_ahead)[:, None, :] == spots[:, None]),
            ((ids // tiles_held) ^ my_core) + 2 * (ids % tiles_held), 0,
        ),
        axis=2,
    )
    asked = jnp.take(asked, (my_blk + jnp.arange(1, n_blk)) % n_blk, axis=0, mode="clip")
    outgoing = pack_tiles("pack_far", [held, held_mate], asked.reshape(-1), [FAR_CAP] * (n_blk - 1))
    far = [
        lax.ppermute(piece, "blk", [(i, (i + 1 + shift) % n_blk) for i in range(n_blk)])
        for shift, piece in enumerate(outgoing)
    ]
    far_mate = [swap(piece) for piece in far]

    gram_local = lax.dot_general(
        item_factors, item_factors, (((0,), (0,)), ((), ())), preferred_element_type=jnp.float32
    )
    gram = sum_everywhere(gram_local)

    def most(keys, bins):
        marks = (keys[:, None, :] == jnp.arange(bins, dtype=jnp.int32)[:, None]) & all_live[:, None, :]
        return jnp.max(jnp.sum(marks.astype(jnp.int32), axis=2))

    to_chip = all_owner // 2
    elsewhere = chips // n_chips != jnp.arange(n_blk, dtype=jnp.int32)[:, None]
    asks = jnp.sum(needed.astype(jnp.int32), axis=2)
    fits = (
        (jnp.max(jnp.where(elsewhere, asks, 0)) <= 2 * FAR_CAP)
        & (most(source // 2 * n_chips + to_chip, n_chips * n_chips) <= 2 * COUNT_CAP)
        & (most(all_chip % n_chips * n_chips + to_chip, n_chips * n_chips) <= 2 * ITEM_CAP)
        & (most(all_user, user_blocks) <= LOADS // own_tiles)
    )

    pick = lambda x: lax.dynamic_index_in_dim(x, my_blk, 0, keepdims=False)
    e_live, e_user, e_owner = pick(all_live), pick(all_user), pick(all_owner)
    e_chip, e_tile = pick(all_chip), pick(all_tile)
    e_blk, e_column = e_chip // n_chips, e_chip % n_chips
    e_to = e_owner // 2
    e_from = source // 2
    to_us = e_live & (e_to == my_chip)
    local_user = e_user % own_tiles
    members = jnp.arange(n_chips, dtype=jnp.int32)[:, None]
    marks = [
        e_live & (e_from == my_chip) & (e_to == members),
        to_us & (e_from == members),
        e_live & (e_column == my_chip) & (e_to == members),
        to_us & (e_column == members),
        e_live & (e_owner == my_grp) & (local_user == jnp.arange(own_tiles, dtype=jnp.int32)[:, None]),
    ]
    marks = jnp.concatenate(marks, axis=0).astype(jnp.bfloat16)
    before = (index[:, None] < index[None, :]).astype(jnp.bfloat16)
    ahead = jnp.dot(marks, before, preferred_element_type=jnp.float32) * marks.astype(jnp.float32)
    starts = [n_chips * n for n in range(5)] + [4 * n_chips + own_tiles]
    counts_out, counts_back, items_out, items_back, user_rank = [
        jnp.sum(ahead[lo:hi], axis=0).astype(jnp.int32) for lo, hi in zip(starts, starts[1:])
    ]

    mine = lambda place, cap: (place % 2 == my_core) & (place // 2 < cap)
    cells = jnp.arange(n_chips * COUNT_CAP, dtype=jnp.int32)
    chosen = choose(
        e_to * COUNT_CAP + counts_out // 2,
        e_live & (e_from == my_chip) & mine(counts_out, COUNT_CAP),
        cells, ((source % 2) ^ my_core) + 2 * (index % pairs),
    )
    (outgoing,) = pack_tiles("pack_counts", [scaled, scaled_mate], chosen, [n_chips * COUNT_CAP])
    counts_own = to_chips(outgoing)
    counts_mate = swap(counts_own)

    n_sources = 2 * n_blk
    own_chips = jnp.take(
        pick(tiles_ahead), jnp.arange(n_blk) * n_chips + my_chip, axis=0, mode="clip"
    ).reshape(-1)
    cells = jnp.arange(own_chips.shape[0], dtype=jnp.int32)[:, None]
    far_place = jnp.sum(
        jnp.where(e_blk * (2 * tiles_held) + e_tile == cells, own_chips[:, None], 0), axis=0
    )
    shift = (my_blk - e_blk) % n_blk
    near = shift == 0
    lane = jnp.where(near, e_tile // tiles_held, far_place % 2) ^ my_core
    row = jnp.where(near, e_tile % tiles_held, far_place // 2)
    cells = jnp.arange(n_chips * ITEM_CAP, dtype=jnp.int32)
    chosen = choose(
        e_to * ITEM_CAP + items_out // 2,
        fits & e_live & (e_column == my_chip) & mine(items_out, ITEM_CAP),
        cells, row * n_sources + lane * n_blk + shift,
    )
    (outgoing,) = pack_tiles(
        "pack_items", [held, *far, held_mate, *far_mate], chosen, [n_chips * ITEM_CAP]
    )
    outgoing, counts_own, gram = lax.optimization_barrier((outgoing, counts_own, gram))
    items_own = to_chips(outgoing)
    items_mate = swap(items_own)

    hit = fits & e_live & (e_owner == my_grp)
    room_at = ((user_rank // SPAN) * own_tiles + local_user) * SPAN + user_rank % SPAN
    loads = jnp.sum(
        (hit & (local_user == jnp.arange(own_tiles, dtype=jnp.int32)[:, None])).astype(jnp.int32), axis=1
    )
    cells = jnp.arange(LOADS, dtype=jnp.int32)
    count_at = ((counts_back % 2) ^ my_core) + 2 * (e_from * COUNT_CAP + counts_back // 2)
    item_at = ((items_back % 2) ^ my_core) + 2 * (e_column * ITEM_CAP + items_back // 2)
    plan = jnp.concatenate(
        [loads, choose(room_at, hit, cells, count_at), choose(room_at, hit, cells, item_at)]
    )
    by_owner = run_sweep(plan, user_prior, gram, counts_own, counts_mate, items_own, items_mate)

    return lax.cond(
        fits, lambda done, *given: done, lambda done, *given: sweep_in_place(*given),
        by_owner, user_prior, item_factors, user_tiles, item_tiles, counts, live, gram_local,
    )


def solution(mesh):
    in_specs = (
        P(("blk", "grp"), None),
        P(("blk", "grp"), None),
        P(("blk", "grp")),
        P(("blk", "grp")),
        P(("blk", "grp"), None, None),
    )
    out_specs = P(("blk", "grp"), None)
    return jax.shard_map(body, mesh=mesh, in_specs=in_specs, out_specs=out_specs, check_vma=False)
```

```python
import functools

import jax
import jax.numpy as jnp
from jax import lax
from jax.experimental import pallas as pl
from jax.experimental.pallas import tpu as pltpu
from jax.sharding import PartitionSpec as P

ITERS = 3

ALPHA = 40.0
REG = 32.0
EPS = 1e-06

FAR_CAP = 14
COUNT_CAP = 24
ITEM_CAP = 20
LOADS = 128
SPAN = 2


def fetch_tiles(item_factors, item_tiles, pairs, tile, rank):
    n_all = lax.axis_size(("blk", "grp"))
    tiles_held = item_factors.shape[0] // tile
    slots_each = max(2, pairs // n_all)
    owner = item_tiles // tiles_held
    local_slot = item_tiles % tiles_held
    position = jnp.arange(pairs, dtype=jnp.int32)
    earlier = (owner[None, :] == owner[:, None]) & (position[None, :] < position[:, None])
    order = jnp.sum(earlier.astype(jnp.int32), axis=1)
    requests = jnp.full((n_all, slots_each), -1, jnp.int32).at[owner, order].set(local_slot)
    wanted = lax.all_to_all(requests, ("blk", "grp"), split_axis=0, concat_axis=0, tiled=True)
    held = item_factors.reshape(tiles_held, tile, rank)
    picked = jnp.take(held, jnp.maximum(wanted, 0), axis=0)
    picked = jnp.where((wanted >= 0)[:, :, None, None], picked, jnp.zeros((), picked.dtype))
    arrived = lax.all_to_all(picked, ("blk", "grp"), split_axis=0, concat_axis=0, tiled=True)
    return arrived[owner, order]


def row_sum(left, right):
    return jnp.sum(left * right, axis=1, keepdims=True)


def sweep_in_place(user_prior, item_factors, user_tiles, item_tiles, counts, live, gram_local):
    pairs = counts.shape[0]
    tile = counts.shape[1]
    rank = item_factors.shape[1]
    n_grp = lax.axis_size("grp")
    own_rows = user_prior.shape[0]
    block_rows = own_rows * n_grp
    user_blocks = block_rows // tile
    span = min(32, pairs)
    gram = lax.psum(gram_local, ("blk", "grp"))
    pair_tiles = fetch_tiles(item_factors, item_tiles, pairs, tile, rank)
    rounds = (jnp.sum(live.astype(jnp.int32)) + span - 1) // span
    tile_ids = jnp.arange(user_blocks, dtype=jnp.int32)

    def accumulate(low_tiles, with_rhs):

        def one_round(index, totals):
            start = index * span
            users = lax.dynamic_slice_in_dim(user_tiles, start, span)
            factors = lax.dynamic_slice_in_dim(pair_tiles, start, span)
            counted = lax.dynamic_slice_in_dim(counts, start, span).astype(jnp.float32)
            selector = (tile_ids[:, None] == users[None, :]).astype(jnp.float32)
            users_low = jnp.take(low_tiles, users, axis=0)
            scores = jnp.einsum(
                "bur,bir->bui", users_low, factors, preferred_element_type=jnp.float32
            )
            scaled = (ALPHA * counted * scores).astype(jnp.bfloat16)
            back = jnp.einsum("bui,bir->bur", scaled, factors, preferred_element_type=jnp.float32)
            result = [
                totals[0]
                + jnp.einsum("tb,bur->tur", selector, back, precision=lax.Precision.HIGHEST)
            ]
            if with_rhs:
                confidence = jnp.where(counted > 0, 1.0 + ALPHA * counted, 0.0).astype(jnp.bfloat16)
                pulled = jnp.einsum(
                    "bui,bir->bur", confidence, factors, preferred_element_type=jnp.float32
                )
                result.append(
                    totals[1]
                    + jnp.einsum("tb,bur->tur", selector, pulled, precision=lax.Precision.HIGHEST)
                )
            return tuple(result)

        zeros = jnp.zeros((user_blocks, tile, rank), jnp.float32)
        start_state = (zeros, zeros) if with_rhs else (zeros,)
        totals = lax.fori_loop(0, rounds, one_round, start_state)
        return tuple((total.reshape(block_rows, rank) for total in totals))

    def gram_term(vectors):
        return jnp.dot(vectors, gram, precision=lax.Precision.HIGHEST) + REG * vectors

    low = lax.all_gather(user_prior.astype(jnp.bfloat16), "grp", axis=0, tiled=True)
    pair_part, rhs_part = accumulate(low.reshape(user_blocks, tile, rank), True)
    pair_share, rhs_share = (
        lax.psum_scatter(pair_part, "grp", scatter_dimension=0, tiled=True),
        lax.psum_scatter(rhs_part, "grp", scatter_dimension=0, tiled=True),
    )
    solution = user_prior
    residual = rhs_share - (gram_term(solution) + pair_share)
    direction = residual
    norm_now = row_sum(residual, residual)
    for step in range(ITERS):
        low = lax.all_gather(direction.astype(jnp.bfloat16), "grp", axis=0, tiled=True)
        (pair_part,) = accumulate(low.reshape(user_blocks, tile, rank), False)
        image = gram_term(direction) + lax.psum_scatter(
            pair_part, "grp", scatter_dimension=0, tiled=True
        )
        alpha = norm_now / (row_sum(direction, image) + EPS)
        solution = solution + alpha * direction
        residual = residual - alpha * image
        fresh = row_sum(residual, residual)
        direction = residual + fresh / (norm_now + EPS) * direction
        norm_now = fresh
    return solution


def bits_for(n):
    return (n - 1).bit_length()


def at_source(number, row, n_sources):
    return (row << bits_for(n_sources)) + number


def start_copy(sources, at, target, sem):
    bits = bits_for(len(sources))
    row = lax.shift_right_logical(at, bits)
    which = at & ((1 << bits) - 1)
    for number, source in enumerate(sources):

        @pl.when(which == number)
        def _(source=source):
            pltpu.make_async_copy(source.at[row], target, sem).start()


def sweep_kernel(n_tiles, n_counts, plan, prior_ref, gram_ref, *refs):
    weights, factors, low, image, residual, direction, sems = refs[-7:]
    count_pieces, item_pieces, out_ref = refs[:n_counts], refs[n_counts:-8], refs[-8]
    tile, rank = factors.shape[1:]
    most = plan[0]
    total = plan[0]
    for user in range(1, n_tiles):
        most = jnp.maximum(most, plan[user])
        total = total + plan[user]
    rounds = (most + SPAN - 1) // SPAN

    for user in range(n_tiles):

        def bring(entry, carry, user=user):
            place = ((entry // SPAN) * n_tiles + user) * SPAN + entry % SPAN
            start_copy(count_pieces, plan[n_tiles + place], weights.at[place], sems.at[0])
            start_copy(item_pieces, plan[n_tiles + LOADS + place], factors.at[place], sems.at[1])
            return carry

        def clear(entry, carry, user=user):
            place = ((entry // SPAN) * n_tiles + user) * SPAN + entry % SPAN
            weights[place] = jnp.zeros((tile, tile), weights.dtype)
            factors[place] = jnp.zeros((tile, rank), factors.dtype)
            return carry

        lax.fori_loop(0, plan[user], bring, 0)
        lax.fori_loop(plan[user], rounds * SPAN, clear, 0)

    def arrive(entry, carry):
        pltpu.make_async_copy(count_pieces[0].at[0], weights.at[0], sems.at[0]).wait()
        pltpu.make_async_copy(item_pieces[0].at[0], factors.at[0], sems.at[1]).wait()
        return carry

    lax.fori_loop(0, total, arrive, 0)

    def pair_images(with_rhs):
        image[...] = jnp.zeros_like(image)
        if with_rhs:
            residual[...] = jnp.zeros_like(residual)

        def one_round(step, carry):
            for user in range(n_tiles):
                rows = slice(user * tile, (user + 1) * tile)
                at = (step * n_tiles + user) * SPAN
                items = factors[pl.ds(at, SPAN)].reshape(SPAN * tile, rank)
                scaled = jnp.concatenate(
                    [weights[at + part].astype(jnp.float32) for part in range(SPAN)], axis=1
                )
                scores = lax.dot_general(
                    low[rows, :], items, (((1,), (1,)), ((), ())),
                    preferred_element_type=jnp.float32,
                )
                image[rows, :] += jnp.dot(
                    (scaled * scores).astype(jnp.bfloat16), items,
                    preferred_element_type=jnp.float32,
                )
                if with_rhs:
                    confidence = jnp.where(scaled > 0, 1.0 + scaled, 0.0).astype(jnp.bfloat16)
                    residual[rows, :] += jnp.dot(
                        confidence, items, preferred_element_type=jnp.float32
                    )
            return carry

        lax.fori_loop(0, rounds, one_round, 0)

    def gram_term(vectors):
        return jnp.dot(
            vectors, gram_ref[...], precision=lax.Precision.HIGHEST,
            preferred_element_type=jnp.float32,
        ) + REG * vectors

    prior = prior_ref[...]
    low[...] = prior.astype(jnp.bfloat16)
    pair_images(True)
    first = residual[...] - (gram_term(prior) + image[...])
    residual[...] = first
    direction[...] = first
    out_ref[...] = prior
    norm_now = row_sum(first, first)
    for step in range(ITERS):
        heading = direction[...]
        low[...] = heading.astype(jnp.bfloat16)
        pair_images(False)
        shown = gram_term(heading) + image[...]
        alpha = norm_now / (row_sum(heading, shown) + EPS)
        out_ref[...] += alpha * heading
        if step < ITERS - 1:
            left = residual[...] - alpha * shown
            residual[...] = left
            fresh = row_sum(left, left)
            direction[...] = left + (fresh / (norm_now + EPS)) * heading
            norm_now = fresh


def run_sweep(plan, user_prior, gram, count_pieces, item_pieces):
    own_rows, rank = user_prior.shape
    tile = count_pieces[0].shape[1]
    pieces = [*count_pieces, *item_pieces]
    n_tiles = own_rows // tile
    vmem = pl.BlockSpec(memory_space=pltpu.VMEM)
    return pl.pallas_call(
        functools.partial(sweep_kernel, n_tiles, len(count_pieces)),
        out_shape=jax.ShapeDtypeStruct((own_rows, rank), jnp.float32),
        in_specs=[pl.BlockSpec(memory_space=pltpu.SMEM), vmem, vmem]
        + [pl.BlockSpec(memory_space=pl.ANY)] * len(pieces),
        out_specs=vmem,
        scratch_shapes=[
            pltpu.VMEM((LOADS, tile, tile), jnp.bfloat16),
            pltpu.VMEM((LOADS, tile, rank), jnp.bfloat16),
            pltpu.VMEM((own_rows, rank), jnp.bfloat16),
            pltpu.VMEM((own_rows, rank), jnp.float32),
            pltpu.VMEM((own_rows, rank), jnp.float32),
            pltpu.VMEM((own_rows, rank), jnp.float32),
            pltpu.SemaphoreType.DMA((2,)),
        ],
        compiler_params=pltpu.CompilerParams(vmem_limit_bytes=32 * 2**20),
        name="sweep",
    )(plan, user_prior, gram, *pieces)


def pack_kernel(n_sources, lengths, chosen, *refs):
    sources, outs, sem = refs[:n_sources], refs[n_sources:-1], refs[-1]
    start = 0
    for out, length in zip(outs, lengths):

        def place(spot, carry, out=out, start=start):
            start_copy(sources, chosen[start + spot], out.at[spot], sem)
            return carry

        lax.fori_loop(0, length, place, 0)
        start += length
    for out in outs:
        pltpu.make_async_copy(out, out, sem).wait()


def pack_tiles(name, sources, chosen, lengths):
    anywhere = pl.BlockSpec(memory_space=pl.ANY)
    shape = sources[0].shape[1:]
    return pl.pallas_call(
        functools.partial(pack_kernel, len(sources), lengths),
        out_shape=[jax.ShapeDtypeStruct((n, *shape), sources[0].dtype) for n in lengths],
        in_specs=[pl.BlockSpec(memory_space=pltpu.SMEM)] + [anywhere] * len(sources),
        out_specs=[pl.BlockSpec(memory_space=pltpu.VMEM)] * len(lengths),
        scratch_shapes=[pltpu.SemaphoreType.DMA],
        compiler_params=pltpu.CompilerParams(vmem_limit_bytes=32 * 2**20),
        name=name,
    )(chosen, *sources)


def sum_everywhere(value):
    for axis in ("grp", "blk"):
        size = lax.axis_size(axis)
        bit = 1
        while bit < size:
            value = value + lax.ppermute(value, axis, [(i, i ^ bit) for i in range(size)])
            bit *= 2
    return value


def choose(keys, hit, cells, values):
    return jnp.sum(jnp.where(hit & (keys == cells[:, None]), values, 0), axis=1)


def body(user_prior, item_factors, user_tiles, item_tiles, counts):
    pairs = counts.shape[0]
    tile = counts.shape[1]
    rank = item_factors.shape[1]
    n_blk = lax.axis_size("blk")
    n_grp = lax.axis_size("grp")
    n_all = n_blk * n_grp
    n_chips = n_grp // 2
    own_rows = user_prior.shape[0]
    own_tiles = own_rows // tile
    user_blocks = own_tiles * n_grp
    tiles_held = item_factors.shape[0] // tile
    my_blk = lax.axis_index("blk")
    my_grp = lax.axis_index("grp")
    my_chip = my_grp // 2
    my_core = my_grp % 2
    lanes = [[chip * 2 + core for chip in range(n_chips)] for core in range(2)]

    def swap(value):
        return lax.ppermute(value, "grp", [(i, i ^ 1) for i in range(n_grp)])

    def to_chips(value):
        return lax.all_to_all(
            value, "grp", split_axis=0, concat_axis=0, tiled=True, axis_index_groups=lanes
        )

    gram_local = lax.dot_general(
        item_factors, item_factors, (((0,), (0,)), ((), ())), preferred_element_type=jnp.float32
    )
    gram = sum_everywhere(gram_local)

    held = item_factors.reshape(tiles_held, tile, rank)
    held_mate = swap(held)
    live = jnp.any(counts > 0, axis=(1, 2))
    scaled = (ALPHA * counts.astype(jnp.float32)).astype(jnp.bfloat16)
    scaled_mate = swap(scaled)
    packed = (item_tiles * 2 + live.astype(jnp.int32)) * user_blocks + user_tiles
    every = lax.all_to_all(
        jnp.broadcast_to(packed, (n_all, pairs)), ("blk", "grp"),
        split_axis=0, concat_axis=0, tiled=True,
    )
    n_entries = n_grp * pairs
    every = every.reshape(n_blk, n_entries)
    all_user = every % user_blocks
    every = every // user_blocks
    all_live = every % 2 == 1
    all_item = every // 2
    all_owner = all_user // own_tiles
    all_chip = all_item // (2 * tiles_held)
    all_tile = all_item % (2 * tiles_held)
    index = jnp.arange(n_entries, dtype=jnp.int32)
    source = index // pairs

    ids = jnp.arange(2 * tiles_held, dtype=jnp.int32)
    chips = jnp.arange(n_blk * n_chips, dtype=jnp.int32)
    on_chip = ((all_chip[:, None, :] == chips[:, None]) & all_live[:, None, :]).astype(jnp.bfloat16)
    on_tile = (all_tile[:, :, None] == ids).astype(jnp.bfloat16)
    needed = jnp.einsum("bce,bet->bct", on_chip, on_tile, preferred_element_type=jnp.float32) > 0
    fewer = (ids[:, None] < ids[None, :]).astype(jnp.bfloat16)
    tiles_ahead = jnp.einsum(
        "bct,ts->bcs", needed.astype(jnp.bfloat16), fewer, preferred_element_type=jnp.float32
    ).astype(jnp.int32)

    here = my_blk * n_chips + my_chip
    at_chip = lambda x: lax.dynamic_index_in_dim(x, here, 1, keepdims=False)
    spots = 2 * jnp.arange(FAR_CAP, dtype=jnp.int32) + my_core
    asked = jnp.sum(
        jnp.where(
            at_chip(needed)[:, None, :] & (at_chip(tiles_ahead)[:, None, :] == spots[:, None]),
            at_source((ids // tiles_held) ^ my_core, ids % tiles_held, 2), 0,
        ),
        axis=2,
    )
    asked = jnp.take(asked, (my_blk + jnp.arange(1, n_blk)) % n_blk, axis=0, mode="clip")
    asked, gram = lax.optimization_barrier((asked, gram))
    far_out = pack_tiles("pack_far", [held, held_mate], asked.reshape(-1), [FAR_CAP] * (n_blk - 1))
    far = [
        lax.ppermute(piece, "blk", [(i, (i + 1 + shift) % n_blk) for i in range(n_blk)])
        for shift, piece in enumerate(far_out)
    ]
    far_mate = [swap(piece) for piece in far]

    pick = lambda x: lax.dynamic_index_in_dim(x, my_blk, 0, keepdims=False)
    e_live, e_user, e_owner = pick(all_live), pick(all_user), pick(all_owner)
    e_chip, e_tile = pick(all_chip), pick(all_tile)
    e_blk, e_column = e_chip // n_chips, e_chip % n_chips
    e_to = e_owner // 2
    e_from = source // 2
    to_us = e_live & (e_to == my_chip)
    local_user = e_user % own_tiles
    members = jnp.arange(n_chips, dtype=jnp.int32)[:, None]
    marks = [
        e_live & (e_from == my_chip) & (e_to == members),
        to_us & (e_from == members),
        e_live & (e_column == my_chip) & (e_to == members),
        to_us & (e_column == members),
        e_live & (e_owner == my_grp) & (local_user == jnp.arange(own_tiles, dtype=jnp.int32)[:, None]),
    ]
    marks = jnp.concatenate(marks, axis=0).astype(jnp.bfloat16)
    before = (index[:, None] < index[None, :]).astype(jnp.bfloat16)
    ahead = jnp.dot(marks, before, preferred_element_type=jnp.float32) * marks.astype(jnp.float32)
    starts = [n_chips * n for n in range(5)] + [4 * n_chips + own_tiles]
    counts_out, counts_back, items_out, items_back, user_rank = [
        jnp.sum(ahead[lo:hi], axis=0).astype(jnp.int32) for lo, hi in zip(starts, starts[1:])
    ]

    mine = lambda place, cap: (place % 2 == my_core) & (place // 2 < cap)
    cells = jnp.arange(n_chips * COUNT_CAP, dtype=jnp.int32)
    chosen = choose(
        e_to * COUNT_CAP + counts_out // 2,
        e_live & (e_from == my_chip) & mine(counts_out, COUNT_CAP),
        cells, at_source((source % 2) ^ my_core, index % pairs, 2),
    )
    chosen, *far_out = lax.optimization_barrier((chosen, *far_out))
    (outgoing,) = pack_tiles("pack_counts", [scaled, scaled_mate], chosen, [n_chips * COUNT_CAP])
    counted, needed, outgoing = lax.optimization_barrier((all_live, needed, outgoing))

    def most(keys, bins):
        marks = (keys[:, None, :] == jnp.arange(bins, dtype=jnp.int32)[:, None]) & counted[:, None, :]
        return jnp.max(jnp.sum(marks.astype(jnp.int32), axis=2))

    to_chip = all_owner // 2
    elsewhere = chips // n_chips != jnp.arange(n_blk, dtype=jnp.int32)[:, None]
    asks = jnp.sum(needed.astype(jnp.int32), axis=2)
    fits = (
        (jnp.max(jnp.where(elsewhere, asks, 0)) <= 2 * FAR_CAP)
        & (most(source // 2 * n_chips + to_chip, n_chips * n_chips) <= 2 * COUNT_CAP)
        & (most(all_chip % n_chips * n_chips + to_chip, n_chips * n_chips) <= 2 * ITEM_CAP)
        & (most(all_user, user_blocks) <= LOADS // own_tiles)
    )

    counts_own = to_chips(outgoing)
    counts_mate = swap(counts_own)

    n_sources = 2 * n_blk
    own_chips = jnp.take(
        pick(tiles_ahead), jnp.arange(n_blk) * n_chips + my_chip, axis=0, mode="clip"
    ).reshape(-1)
    cells = jnp.arange(own_chips.shape[0], dtype=jnp.int32)[:, None]
    far_place = jnp.sum(
        jnp.where(e_blk * (2 * tiles_held) + e_tile == cells, own_chips[:, None], 0), axis=0
    )
    shift = (my_blk - e_blk) % n_blk
    near = shift == 0
    lane = jnp.where(near, e_tile // tiles_held, far_place % 2) ^ my_core
    row = jnp.where(near, e_tile % tiles_held, far_place // 2)
    cells = jnp.arange(n_chips * ITEM_CAP, dtype=jnp.int32)
    chosen = choose(
        (e_to ^ my_chip) * ITEM_CAP + items_out // 2,
        fits & e_live & (e_column == my_chip) & mine(items_out, ITEM_CAP),
        cells, at_source(lane * n_blk + shift, row, n_sources),
    )
    items_out = pack_tiles(
        "pack_items", [held, *far, held_mate, *far_mate], chosen, [ITEM_CAP] * n_chips
    )

    hit = fits & e_live & (e_owner == my_grp)
    room_at = ((user_rank // SPAN) * own_tiles + local_user) * SPAN + user_rank % SPAN
    loads = jnp.sum(
        (hit & (local_user == jnp.arange(own_tiles, dtype=jnp.int32)[:, None])).astype(jnp.int32), axis=1
    )
    cells = jnp.arange(LOADS, dtype=jnp.int32)
    count_at = at_source((counts_back % 2) ^ my_core, e_from * COUNT_CAP + counts_back // 2, 2)
    item_at = at_source(
        (e_column ^ my_chip) * 2 + ((items_back % 2) ^ my_core), items_back // 2, 2 * n_chips
    )
    plan = jnp.concatenate(
        [loads, choose(room_at, hit, cells, count_at), choose(room_at, hit, cells, item_at)]
    )
    plan, *items_out = lax.optimization_barrier((plan, *items_out))
    item_pieces = []
    for off, piece in enumerate(items_out):
        if off:
            piece = lax.ppermute(piece, "grp", [(i, i ^ (2 * off)) for i in range(n_grp)])
        item_pieces += [piece, swap(piece)]
    by_owner = run_sweep(plan, user_prior, gram, [counts_own, counts_mate], item_pieces)

    return lax.cond(
        fits, lambda done, *given: done, lambda done, *given: sweep_in_place(*given),
        by_owner, user_prior, item_factors, user_tiles, item_tiles, counts, live, gram_local,
    )


def solution(mesh):
    in_specs = (
        P(("blk", "grp"), None),
        P(("blk", "grp"), None),
        P(("blk", "grp")),
        P(("blk", "grp")),
        P(("blk", "grp"), None, None),
    )
    out_specs = P(("blk", "grp"), None)
    return jax.shard_map(body, mesh=mesh, in_specs=in_specs, out_specs=out_specs, check_vma=False)
```

```python
import functools

import jax
import jax.numpy as jnp
from jax import lax
from jax.experimental import pallas as pl
from jax.experimental.pallas import tpu as pltpu
from jax.sharding import PartitionSpec as P

ITERS = 3

ALPHA = 40.0
REG = 32.0
EPS = 1e-06

FAR_CAP = 14
COUNT_CAP = 24
ITEM_CAP = 20
LOADS = 128
SPAN = 2
TOGETHER = 4
PLAN_HEAD = 2 + LOADS // SPAN


def fetch_tiles(item_factors, item_tiles, pairs, tile, rank):
    n_all = lax.axis_size(("blk", "grp"))
    tiles_held = item_factors.shape[0] // tile
    slots_each = max(2, pairs // n_all)
    owner = item_tiles // tiles_held
    local_slot = item_tiles % tiles_held
    position = jnp.arange(pairs, dtype=jnp.int32)
    earlier = (owner[None, :] == owner[:, None]) & (position[None, :] < position[:, None])
    order = jnp.sum(earlier.astype(jnp.int32), axis=1)
    requests = jnp.full((n_all, slots_each), -1, jnp.int32).at[owner, order].set(local_slot)
    wanted = lax.all_to_all(requests, ("blk", "grp"), split_axis=0, concat_axis=0, tiled=True)
    held = item_factors.reshape(tiles_held, tile, rank)
    picked = jnp.take(held, jnp.maximum(wanted, 0), axis=0)
    picked = jnp.where((wanted >= 0)[:, :, None, None], picked, jnp.zeros((), picked.dtype))
    arrived = lax.all_to_all(picked, ("blk", "grp"), split_axis=0, concat_axis=0, tiled=True)
    return arrived[owner, order]


def row_sum(left, right):
    return jnp.sum(left * right, axis=1, keepdims=True)


def sweep_in_place(user_prior, item_factors, user_tiles, item_tiles, counts, live, gram_local):
    pairs = counts.shape[0]
    tile = counts.shape[1]
    rank = item_factors.shape[1]
    n_grp = lax.axis_size("grp")
    own_rows = user_prior.shape[0]
    block_rows = own_rows * n_grp
    user_blocks = block_rows // tile
    span = min(32, pairs)
    gram = lax.psum(gram_local, ("blk", "grp"))
    pair_tiles = fetch_tiles(item_factors, item_tiles, pairs, tile, rank)
    rounds = (jnp.sum(live.astype(jnp.int32)) + span - 1) // span
    tile_ids = jnp.arange(user_blocks, dtype=jnp.int32)

    def accumulate(low_tiles, with_rhs):

        def one_round(index, totals):
            start = index * span
            users = lax.dynamic_slice_in_dim(user_tiles, start, span)
            factors = lax.dynamic_slice_in_dim(pair_tiles, start, span)
            counted = lax.dynamic_slice_in_dim(counts, start, span).astype(jnp.float32)
            selector = (tile_ids[:, None] == users[None, :]).astype(jnp.float32)
            users_low = jnp.take(low_tiles, users, axis=0)
            scores = jnp.einsum(
                "bur,bir->bui", users_low, factors, preferred_element_type=jnp.float32
            )
            scaled = (ALPHA * counted * scores).astype(jnp.bfloat16)
            back = jnp.einsum("bui,bir->bur", scaled, factors, preferred_element_type=jnp.float32)
            result = [
                totals[0]
                + jnp.einsum("tb,bur->tur", selector, back, precision=lax.Precision.HIGHEST)
            ]
            if with_rhs:
                confidence = jnp.where(counted > 0, 1.0 + ALPHA * counted, 0.0).astype(jnp.bfloat16)
                pulled = jnp.einsum(
                    "bui,bir->bur", confidence, factors, preferred_element_type=jnp.float32
                )
                result.append(
                    totals[1]
                    + jnp.einsum("tb,bur->tur", selector, pulled, precision=lax.Precision.HIGHEST)
                )
            return tuple(result)

        zeros = jnp.zeros((user_blocks, tile, rank), jnp.float32)
        start_state = (zeros, zeros) if with_rhs else (zeros,)
        totals = lax.fori_loop(0, rounds, one_round, start_state)
        return tuple((total.reshape(block_rows, rank) for total in totals))

    def gram_term(vectors):
        return jnp.dot(vectors, gram, precision=lax.Precision.HIGHEST) + REG * vectors

    low = lax.all_gather(user_prior.astype(jnp.bfloat16), "grp", axis=0, tiled=True)
    pair_part, rhs_part = accumulate(low.reshape(user_blocks, tile, rank), True)
    pair_share, rhs_share = (
        lax.psum_scatter(pair_part, "grp", scatter_dimension=0, tiled=True),
        lax.psum_scatter(rhs_part, "grp", scatter_dimension=0, tiled=True),
    )
    solution = user_prior
    residual = rhs_share - (gram_term(solution) + pair_share)
    direction = residual
    norm_now = row_sum(residual, residual)
    for step in range(ITERS):
        low = lax.all_gather(direction.astype(jnp.bfloat16), "grp", axis=0, tiled=True)
        (pair_part,) = accumulate(low.reshape(user_blocks, tile, rank), False)
        image = gram_term(direction) + lax.psum_scatter(
            pair_part, "grp", scatter_dimension=0, tiled=True
        )
        alpha = norm_now / (row_sum(direction, image) + EPS)
        solution = solution + alpha * direction
        residual = residual - alpha * image
        fresh = row_sum(residual, residual)
        direction = residual + fresh / (norm_now + EPS) * direction
        norm_now = fresh
    return solution


def bits_for(n):
    return (n - 1).bit_length()


def at_source(number, row, n_sources):
    return (row << bits_for(n_sources)) + number


def start_copy(sources, at, target, sem):
    bits = bits_for(len(sources))
    row = lax.shift_right_logical(at, bits)
    which = at & ((1 << bits) - 1)
    for number, source in enumerate(sources):

        @pl.when(which == number)
        def _(source=source):
            pltpu.make_async_copy(source.at[row], target, sem).start()


def sweep_kernel(n_counts, plan, prior_ref, gram_ref, *refs):
    weights, factors, low, image, residual, direction, sems = refs[-7:]
    count_pieces, item_pieces, out_ref = refs[:n_counts], refs[n_counts:-8], refs[-8]
    tile, rank = factors.shape[1:]
    rounds = plan[0]

    def bring(place, carry):
        count_at = plan[PLAN_HEAD + place]
        item_at = plan[PLAN_HEAD + LOADS + place]

        @pl.when(count_at > 0)
        def _():
            start_copy(count_pieces, count_at - 1, weights.at[place], sems.at[0])
            start_copy(item_pieces, item_at, factors.at[place], sems.at[1])

        @pl.when(count_at == 0)
        def _():
            weights[place] = jnp.zeros((tile, tile), weights.dtype)
            factors[place] = jnp.zeros((tile, rank), factors.dtype)

        return carry

    lax.fori_loop(0, rounds * (TOGETHER * SPAN), bring, 0)

    def arrive(entry, carry):
        pltpu.make_async_copy(count_pieces[0].at[0], weights.at[0], sems.at[0]).wait()
        pltpu.make_async_copy(item_pieces[0].at[0], factors.at[0], sems.at[1]).wait()
        return carry

    lax.fori_loop(0, plan[1], arrive, 0)

    def pair_images(with_rhs):
        image[...] = jnp.zeros_like(image)
        if with_rhs:
            residual[...] = jnp.zeros_like(residual)

        def one_round(step, carry):
            shares = []
            for number in range(TOGETHER):
                chunk = step * TOGETHER + number
                rows = pl.ds(pl.multiple_of(plan[2 + chunk] * tile, tile), tile)
                items = factors[pl.ds(chunk * SPAN, SPAN)].reshape(SPAN * tile, rank)
                scaled = jnp.concatenate(
                    [weights[chunk * SPAN + part].astype(jnp.float32) for part in range(SPAN)],
                    axis=1,
                )
                scores = lax.dot_general(
                    low[rows, :], items, (((1,), (1,)), ((), ())),
                    preferred_element_type=jnp.float32,
                )
                back = jnp.dot(
                    (scaled * scores).astype(jnp.bfloat16), items,
                    preferred_element_type=jnp.float32,
                )
                pulled = None
                if with_rhs:
                    confidence = jnp.where(scaled > 0, 1.0 + scaled, 0.0).astype(jnp.bfloat16)
                    pulled = jnp.dot(confidence, items, preferred_element_type=jnp.float32)
                shares.append((rows, back, pulled))
            for rows, back, pulled in shares:
                image[rows, :] += back
                if with_rhs:
                    residual[rows, :] += pulled
            return carry

        lax.fori_loop(0, rounds, one_round, 0)

    def gram_term(vectors):
        return jnp.dot(
            vectors, gram_ref[...], precision=lax.Precision.HIGHEST,
            preferred_element_type=jnp.float32,
        ) + REG * vectors

    prior = prior_ref[...]
    low[...] = prior.astype(jnp.bfloat16)
    pair_images(True)
    first = residual[...] - (gram_term(prior) + image[...])
    residual[...] = first
    direction[...] = first
    out_ref[...] = prior
    norm_now = row_sum(first, first)
    for step in range(ITERS):
        heading = direction[...]
        low[...] = heading.astype(jnp.bfloat16)
        pair_images(False)
        shown = gram_term(heading) + image[...]
        alpha = norm_now / (row_sum(heading, shown) + EPS)
        out_ref[...] += alpha * heading
        if step < ITERS - 1:
            left = residual[...] - alpha * shown
            residual[...] = left
            fresh = row_sum(left, left)
            direction[...] = left + (fresh / (norm_now + EPS)) * heading
            norm_now = fresh


def run_sweep(plan, user_prior, gram, count_pieces, item_pieces):
    own_rows, rank = user_prior.shape
    tile = count_pieces[0].shape[1]
    pieces = [*count_pieces, *item_pieces]
    vmem = pl.BlockSpec(memory_space=pltpu.VMEM)
    return pl.pallas_call(
        functools.partial(sweep_kernel, len(count_pieces)),
        out_shape=jax.ShapeDtypeStruct((own_rows, rank), jnp.float32),
        in_specs=[pl.BlockSpec(memory_space=pltpu.SMEM), vmem, vmem]
        + [pl.BlockSpec(memory_space=pl.ANY)] * len(pieces),
        out_specs=vmem,
        scratch_shapes=[
            pltpu.VMEM((LOADS, tile, tile), jnp.bfloat16),
            pltpu.VMEM((LOADS, tile, rank), jnp.bfloat16),
            pltpu.VMEM((own_rows, rank), jnp.bfloat16),
            pltpu.VMEM((own_rows, rank), jnp.float32),
            pltpu.VMEM((own_rows, rank), jnp.float32),
            pltpu.VMEM((own_rows, rank), jnp.float32),
            pltpu.SemaphoreType.DMA((2,)),
        ],
        compiler_params=pltpu.CompilerParams(vmem_limit_bytes=32 * 2**20),
        name="sweep",
    )(plan, user_prior, gram, *pieces)


def pack_kernel(n_sources, lengths, chosen, *refs):
    sources, outs, sem = refs[:n_sources], refs[n_sources:-1], refs[-1]
    start = 0
    for out, length in zip(outs, lengths):

        def place(spot, carry, out=out, start=start):
            start_copy(sources, chosen[start + spot], out.at[spot], sem)
            return carry

        lax.fori_loop(0, length, place, 0)
        start += length
    for out in outs:
        pltpu.make_async_copy(out, out, sem).wait()


def pack_tiles(name, sources, chosen, lengths):
    anywhere = pl.BlockSpec(memory_space=pl.ANY)
    shape = sources[0].shape[1:]
    return pl.pallas_call(
        functools.partial(pack_kernel, len(sources), lengths),
        out_shape=[jax.ShapeDtypeStruct((n, *shape), sources[0].dtype) for n in lengths],
        in_specs=[pl.BlockSpec(memory_space=pltpu.SMEM)] + [anywhere] * len(sources),
        out_specs=[pl.BlockSpec(memory_space=pltpu.VMEM)] * len(lengths),
        scratch_shapes=[pltpu.SemaphoreType.DMA],
        compiler_params=pltpu.CompilerParams(vmem_limit_bytes=32 * 2**20),
        name=name,
    )(chosen, *sources)


def sum_everywhere(value):
    for axis in ("grp", "blk"):
        size = lax.axis_size(axis)
        bit = 1
        while bit < size:
            value = value + lax.ppermute(value, axis, [(i, i ^ bit) for i in range(size)])
            bit *= 2
    return value


def choose(keys, hit, cells, values):
    return jnp.sum(jnp.where(hit & (keys == cells[:, None]), values, 0), axis=1)


def body(user_prior, item_factors, user_tiles, item_tiles, counts):
    pairs = counts.shape[0]
    tile = counts.shape[1]
    rank = item_factors.shape[1]
    n_blk = lax.axis_size("blk")
    n_grp = lax.axis_size("grp")
    n_all = n_blk * n_grp
    n_chips = n_grp // 2
    own_rows = user_prior.shape[0]
    own_tiles = own_rows // tile
    user_blocks = own_tiles * n_grp
    tiles_held = item_factors.shape[0] // tile
    my_blk = lax.axis_index("blk")
    my_grp = lax.axis_index("grp")
    my_chip = my_grp // 2
    my_core = my_grp % 2
    lanes = [[chip * 2 + core for chip in range(n_chips)] for core in range(2)]

    def swap(value):
        return lax.ppermute(value, "grp", [(i, i ^ 1) for i in range(n_grp)])

    def to_chips(value):
        return lax.all_to_all(
            value, "grp", split_axis=0, concat_axis=0, tiled=True, axis_index_groups=lanes
        )

    gram_local = lax.dot_general(
        item_factors, item_factors, (((0,), (0,)), ((), ())), preferred_element_type=jnp.float32
    )
    gram = sum_everywhere(gram_local)

    held = item_factors.reshape(tiles_held, tile, rank)
    held_mate = swap(held)
    live = jnp.any(counts > 0, axis=(1, 2))
    scaled = (ALPHA * counts.astype(jnp.float32)).astype(jnp.bfloat16)
    scaled_mate = swap(scaled)
    packed = (item_tiles * 2 + live.astype(jnp.int32)) * user_blocks + user_tiles
    every = lax.all_to_all(
        jnp.broadcast_to(packed, (n_all, pairs)), ("blk", "grp"),
        split_axis=0, concat_axis=0, tiled=True,
    )
    n_entries = n_grp * pairs
    every = every.reshape(n_blk, n_entries)
    all_user = every % user_blocks
    every = every // user_blocks
    all_live = every % 2 == 1
    all_item = every // 2
    all_owner = all_user // own_tiles
    all_chip = all_item // (2 * tiles_held)
    all_tile = all_item % (2 * tiles_held)
    index = jnp.arange(n_entries, dtype=jnp.int32)
    source = index // pairs

    ids = jnp.arange(2 * tiles_held, dtype=jnp.int32)
    chips = jnp.arange(n_blk * n_chips, dtype=jnp.int32)
    on_chip = ((all_chip[:, None, :] == chips[:, None]) & all_live[:, None, :]).astype(jnp.bfloat16)
    on_tile = (all_tile[:, :, None] == ids).astype(jnp.bfloat16)
    needed = jnp.einsum("bce,bet->bct", on_chip, on_tile, preferred_element_type=jnp.float32) > 0
    fewer = (ids[:, None] < ids[None, :]).astype(jnp.bfloat16)
    tiles_ahead = jnp.einsum(
        "bct,ts->bcs", needed.astype(jnp.bfloat16), fewer, preferred_element_type=jnp.float32
    ).astype(jnp.int32)

    pick = lambda x: lax.dynamic_index_in_dim(x, my_blk, 0, keepdims=False)
    e_live, e_user, e_owner = pick(all_live), pick(all_user), pick(all_owner)
    e_chip, e_tile = pick(all_chip), pick(all_tile)
    e_blk, e_column = e_chip // n_chips, e_chip % n_chips
    e_to = e_owner // 2
    e_from = source // 2
    to_us = e_live & (e_to == my_chip)
    local_user = e_user % own_tiles
    members = jnp.arange(n_chips, dtype=jnp.int32)[:, None]
    marks = [
        e_live & (e_from == my_chip) & (e_to == members),
        to_us & (e_from == members),
        e_live & (e_column == my_chip) & (e_to == members),
        to_us & (e_column == members),
        e_live & (e_owner == my_grp) & (local_user == jnp.arange(own_tiles, dtype=jnp.int32)[:, None]),
    ]
    marks = jnp.concatenate(marks, axis=0).astype(jnp.bfloat16)
    before = (index[:, None] < index[None, :]).astype(jnp.bfloat16)
    ahead = jnp.dot(marks, before, preferred_element_type=jnp.float32) * marks.astype(jnp.float32)
    starts = [n_chips * n for n in range(5)] + [4 * n_chips + own_tiles]
    counts_out, counts_back, items_out, items_back, user_rank = [
        jnp.sum(ahead[lo:hi], axis=0).astype(jnp.int32) for lo, hi in zip(starts, starts[1:])
    ]

    mine = lambda place, cap: (place % 2 == my_core) & (place // 2 < cap)
    cells = jnp.arange(n_chips * COUNT_CAP, dtype=jnp.int32)
    chosen = choose(
        e_to * COUNT_CAP + counts_out // 2,
        e_live & (e_from == my_chip) & mine(counts_out, COUNT_CAP),
        cells, at_source((source % 2) ^ my_core, index % pairs, 2),
    )
    (outgoing,) = pack_tiles("pack_counts", [scaled, scaled_mate], chosen, [n_chips * COUNT_CAP])
    here = my_blk * n_chips + my_chip
    at_chip = lambda x: lax.dynamic_index_in_dim(x, here, 1, keepdims=False)
    spots = 2 * jnp.arange(FAR_CAP, dtype=jnp.int32) + my_core
    asked = jnp.sum(
        jnp.where(
            at_chip(needed)[:, None, :] & (at_chip(tiles_ahead)[:, None, :] == spots[:, None]),
            at_source((ids // tiles_held) ^ my_core, ids % tiles_held, 2), 0,
        ),
        axis=2,
    )
    asked = jnp.take(asked, (my_blk + jnp.arange(1, n_blk)) % n_blk, axis=0, mode="clip")
    asked, gram, outgoing = lax.optimization_barrier((asked, gram, outgoing))
    far_out = pack_tiles("pack_far", [held, held_mate], asked.reshape(-1), [FAR_CAP] * (n_blk - 1))
    far = [
        lax.ppermute(piece, "blk", [(i, (i + 1 + shift) % n_blk) for i in range(n_blk)])
        for shift, piece in enumerate(far_out)
    ]
    far_mate = [swap(piece) for piece in far]

    counts_own = to_chips(outgoing)
    counts_mate = swap(counts_own)

    n_sources = 2 * n_blk
    own_chips = jnp.take(
        pick(tiles_ahead), jnp.arange(n_blk) * n_chips + my_chip, axis=0, mode="clip"
    ).reshape(-1)
    cells = jnp.arange(own_chips.shape[0], dtype=jnp.int32)[:, None]
    far_place = jnp.sum(
        jnp.where(e_blk * (2 * tiles_held) + e_tile == cells, own_chips[:, None], 0), axis=0
    )
    far_place = jnp.minimum(far_place, 2 * FAR_CAP - 1)
    shift = (my_blk - e_blk) % n_blk
    near = shift == 0
    lane = jnp.where(near, e_tile // tiles_held, far_place % 2) ^ my_core
    row = jnp.where(near, e_tile % tiles_held, far_place // 2)
    cells = jnp.arange(n_chips * ITEM_CAP, dtype=jnp.int32)
    chosen = choose(
        (e_to ^ my_chip) * ITEM_CAP + items_out // 2,
        e_live & (e_column == my_chip) & mine(items_out, ITEM_CAP),
        cells, at_source(lane * n_blk + shift, row, n_sources),
    )
    items_out = pack_tiles(
        "pack_items", [held, *far, held_mate, *far_mate], chosen, [ITEM_CAP] * n_chips
    )

    hit = e_live & (e_owner == my_grp)
    tiles = jnp.arange(own_tiles, dtype=jnp.int32)
    in_tile = hit & (local_user == tiles[:, None])
    loads = jnp.sum(in_tile.astype(jnp.int32), axis=1)
    chunks = -(-loads // SPAN)
    ends = jnp.sum(jnp.where(tiles[:, None] <= tiles, chunks[:, None], 0), axis=0)
    firsts = ends - chunks
    room_at = jnp.sum(jnp.where(in_tile, firsts[:, None] * SPAN, 0), axis=0) + user_rank
    hit = hit & (room_at < LOADS)
    rounds = jnp.minimum(-(-ends[-1] // TOGETHER), LOADS // (SPAN * TOGETHER))
    chunk_tile = jnp.sum(
        (jnp.arange(LOADS // SPAN, dtype=jnp.int32)[:, None] >= ends[:-1]).astype(jnp.int32), axis=1
    )
    cells = jnp.arange(LOADS, dtype=jnp.int32)
    counts_row = jnp.minimum(counts_back // 2, COUNT_CAP - 1)
    items_row = jnp.minimum(items_back // 2, ITEM_CAP - 1)
    count_at = at_source((counts_back % 2) ^ my_core, e_from * COUNT_CAP + counts_row, 2)
    item_at = at_source(
        (e_column ^ my_chip) * 2 + ((items_back % 2) ^ my_core), items_row, 2 * n_chips
    )
    head = jnp.stack([rounds, jnp.sum(hit.astype(jnp.int32))])
    plan = jnp.concatenate(
        [
            head, chunk_tile,
            choose(room_at, hit, cells, count_at + 1), choose(room_at, hit, cells, item_at),
        ]
    )
    plan, *items_out = lax.optimization_barrier((plan, *items_out))
    item_pieces = []
    for off, piece in enumerate(items_out):
        if off:
            piece = lax.ppermute(piece, "grp", [(i, i ^ (2 * off)) for i in range(n_grp)])
        item_pieces += [piece, swap(piece)]
    by_owner = run_sweep(plan, user_prior, gram, [counts_own, counts_mate], item_pieces)

    def totals(keys, bins):
        marks = (keys[:, None, :] == jnp.arange(bins, dtype=jnp.int32)[:, None]) & all_live[:, None, :]
        return jnp.sum(marks.astype(jnp.int32), axis=2)

    def most(keys, bins):
        return jnp.max(totals(keys, bins))

    to_chip = all_owner // 2
    elsewhere = chips // n_chips != jnp.arange(n_blk, dtype=jnp.int32)[:, None]
    asks = jnp.sum(needed.astype(jnp.int32), axis=2)
    chunks = -(-totals(all_user, user_blocks) // SPAN)
    chunks = chunks.reshape(n_blk, n_grp, own_tiles)
    fits = (
        (jnp.max(jnp.where(elsewhere, asks, 0)) <= 2 * FAR_CAP)
        & (most(source // 2 * n_chips + to_chip, n_chips * n_chips) <= 2 * COUNT_CAP)
        & (most(all_chip % n_chips * n_chips + to_chip, n_chips * n_chips) <= 2 * ITEM_CAP)
        & (jnp.max(jnp.sum(chunks, axis=2)) * SPAN <= LOADS)
    )

    return lax.cond(
        fits, lambda done, *given: done, lambda done, *given: sweep_in_place(*given),
        by_owner, user_prior, item_factors, user_tiles, item_tiles, counts, live, gram_local,
    )


def solution(mesh):
    in_specs = (
        P(("blk", "grp"), None),
        P(("blk", "grp"), None),
        P(("blk", "grp")),
        P(("blk", "grp")),
        P(("blk", "grp"), None, None),
    )
    out_specs = P(("blk", "grp"), None)
    return jax.shard_map(body, mesh=mesh, in_specs=in_specs, out_specs=out_specs, check_vma=False)
```

```python
import functools

import jax
import jax.numpy as jnp
from jax import lax
from jax.experimental import pallas as pl
from jax.experimental.pallas import tpu as pltpu
from jax.sharding import PartitionSpec as P

ITERS = 3

ALPHA = 40.0
REG = 32.0
EPS = 1e-06

FAR_CAP = 14
COUNT_CAP = 24
ITEM_CAP = 20
LOADS = 128
SPAN = 2
TOGETHER = 4
PLAN_HEAD = 2 + LOADS // SPAN


def fetch_tiles(item_factors, item_tiles, pairs, tile, rank):
    n_all = lax.axis_size(("blk", "grp"))
    tiles_held = item_factors.shape[0] // tile
    slots_each = max(2, pairs // n_all)
    owner = item_tiles // tiles_held
    local_slot = item_tiles % tiles_held
    position = jnp.arange(pairs, dtype=jnp.int32)
    earlier = (owner[None, :] == owner[:, None]) & (position[None, :] < position[:, None])
    order = jnp.sum(earlier.astype(jnp.int32), axis=1)
    requests = jnp.full((n_all, slots_each), -1, jnp.int32).at[owner, order].set(local_slot)
    wanted = lax.all_to_all(requests, ("blk", "grp"), split_axis=0, concat_axis=0, tiled=True)
    held = item_factors.reshape(tiles_held, tile, rank)
    picked = jnp.take(held, jnp.maximum(wanted, 0), axis=0)
    picked = jnp.where((wanted >= 0)[:, :, None, None], picked, jnp.zeros((), picked.dtype))
    arrived = lax.all_to_all(picked, ("blk", "grp"), split_axis=0, concat_axis=0, tiled=True)
    return arrived[owner, order]


def row_sum(left, right):
    return jnp.sum(left * right, axis=1, keepdims=True)


def sweep_in_place(user_prior, item_factors, user_tiles, item_tiles, counts, live, gram_local):
    pairs = counts.shape[0]
    tile = counts.shape[1]
    rank = item_factors.shape[1]
    n_grp = lax.axis_size("grp")
    own_rows = user_prior.shape[0]
    block_rows = own_rows * n_grp
    user_blocks = block_rows // tile
    span = min(32, pairs)
    gram = lax.psum(gram_local, ("blk", "grp"))
    pair_tiles = fetch_tiles(item_factors, item_tiles, pairs, tile, rank)
    rounds = (jnp.sum(live.astype(jnp.int32)) + span - 1) // span
    tile_ids = jnp.arange(user_blocks, dtype=jnp.int32)

    def accumulate(low_tiles, with_rhs):

        def one_round(index, totals):
            start = index * span
            users = lax.dynamic_slice_in_dim(user_tiles, start, span)
            factors = lax.dynamic_slice_in_dim(pair_tiles, start, span)
            counted = lax.dynamic_slice_in_dim(counts, start, span).astype(jnp.float32)
            selector = (tile_ids[:, None] == users[None, :]).astype(jnp.float32)
            users_low = jnp.take(low_tiles, users, axis=0)
            scores = jnp.einsum(
                "bur,bir->bui", users_low, factors, preferred_element_type=jnp.float32
            )
            scaled = (ALPHA * counted * scores).astype(jnp.bfloat16)
            back = jnp.einsum("bui,bir->bur", scaled, factors, preferred_element_type=jnp.float32)
            result = [
                totals[0]
                + jnp.einsum("tb,bur->tur", selector, back, precision=lax.Precision.HIGHEST)
            ]
            if with_rhs:
                confidence = jnp.where(counted > 0, 1.0 + ALPHA * counted, 0.0).astype(jnp.bfloat16)
                pulled = jnp.einsum(
                    "bui,bir->bur", confidence, factors, preferred_element_type=jnp.float32
                )
                result.append(
                    totals[1]
                    + jnp.einsum("tb,bur->tur", selector, pulled, precision=lax.Precision.HIGHEST)
                )
            return tuple(result)

        zeros = jnp.zeros((user_blocks, tile, rank), jnp.float32)
        start_state = (zeros, zeros) if with_rhs else (zeros,)
        totals = lax.fori_loop(0, rounds, one_round, start_state)
        return tuple((total.reshape(block_rows, rank) for total in totals))

    def gram_term(vectors):
        return jnp.dot(vectors, gram, precision=lax.Precision.HIGHEST) + REG * vectors

    low = lax.all_gather(user_prior.astype(jnp.bfloat16), "grp", axis=0, tiled=True)
    pair_part, rhs_part = accumulate(low.reshape(user_blocks, tile, rank), True)
    pair_share, rhs_share = (
        lax.psum_scatter(pair_part, "grp", scatter_dimension=0, tiled=True),
        lax.psum_scatter(rhs_part, "grp", scatter_dimension=0, tiled=True),
    )
    solution = user_prior
    residual = rhs_share - (gram_term(solution) + pair_share)
    direction = residual
    norm_now = row_sum(residual, residual)
    for step in range(ITERS):
        low = lax.all_gather(direction.astype(jnp.bfloat16), "grp", axis=0, tiled=True)
        (pair_part,) = accumulate(low.reshape(user_blocks, tile, rank), False)
        image = gram_term(direction) + lax.psum_scatter(
            pair_part, "grp", scatter_dimension=0, tiled=True
        )
        alpha = norm_now / (row_sum(direction, image) + EPS)
        solution = solution + alpha * direction
        residual = residual - alpha * image
        fresh = row_sum(residual, residual)
        direction = residual + fresh / (norm_now + EPS) * direction
        norm_now = fresh
    return solution


def bits_for(n):
    return (n - 1).bit_length()


def at_source(number, row, n_sources):
    return (row << bits_for(n_sources)) + number


def start_copy(sources, at, target, sem):
    bits = bits_for(len(sources))
    row = lax.shift_right_logical(at, bits)
    which = at & ((1 << bits) - 1)
    for number, source in enumerate(sources):

        @pl.when(which == number)
        def _(source=source):
            pltpu.make_async_copy(source.at[row], target, sem).start()


def sweep_kernel(n_counts, plan, prior_ref, gram_ref, *refs):
    weights, factors, low, image, residual, direction, sems = refs[-7:]
    count_pieces, item_pieces, out_ref = refs[:n_counts], refs[n_counts:-8], refs[-8]
    tile, rank = factors.shape[1:]
    rounds = plan[0]

    def bring(place, carry):
        count_at = plan[PLAN_HEAD + place]
        item_at = plan[PLAN_HEAD + LOADS + place]

        @pl.when(count_at > 0)
        def _():
            start_copy(count_pieces, count_at - 1, weights.at[place], sems.at[0])
            start_copy(item_pieces, item_at, factors.at[place], sems.at[1])

        @pl.when(count_at == 0)
        def _():
            weights[place] = jnp.zeros((tile, tile), weights.dtype)
            factors[place] = jnp.zeros((tile, rank), factors.dtype)

        return carry

    lax.fori_loop(0, rounds * (TOGETHER * SPAN), bring, 0)

    def arrive(entry, carry):
        pltpu.make_async_copy(count_pieces[0].at[0], weights.at[0], sems.at[0]).wait()
        pltpu.make_async_copy(item_pieces[0].at[0], factors.at[0], sems.at[1]).wait()
        return carry

    lax.fori_loop(0, plan[1], arrive, 0)

    def pair_images(with_rhs):
        image[...] = jnp.zeros_like(image)
        if with_rhs:
            residual[...] = jnp.zeros_like(residual)

        def one_round(step, carry):
            shares = []
            for number in range(TOGETHER):
                chunk = step * TOGETHER + number
                rows = pl.ds(pl.multiple_of(plan[2 + chunk] * tile, tile), tile)
                items = factors[pl.ds(chunk * SPAN, SPAN)].reshape(SPAN * tile, rank)
                scaled = jnp.concatenate(
                    [weights[chunk * SPAN + part].astype(jnp.float32) for part in range(SPAN)],
                    axis=1,
                )
                scores = lax.dot_general(
                    low[rows, :], items, (((1,), (1,)), ((), ())),
                    preferred_element_type=jnp.float32,
                )
                back = jnp.dot(
                    (scaled * scores).astype(jnp.bfloat16), items,
                    preferred_element_type=jnp.float32,
                )
                pulled = None
                if with_rhs:
                    confidence = jnp.where(scaled > 0, 1.0 + scaled, 0.0).astype(jnp.bfloat16)
                    pulled = jnp.dot(confidence, items, preferred_element_type=jnp.float32)
                shares.append((rows, back, pulled))
            for rows, back, pulled in shares:
                image[rows, :] += back
                if with_rhs:
                    residual[rows, :] += pulled
            return carry

        lax.fori_loop(0, rounds, one_round, 0)

    def gram_term(vectors):
        return jnp.dot(
            vectors, gram_ref[...], precision=lax.Precision.HIGHEST,
            preferred_element_type=jnp.float32,
        ) + REG * vectors

    prior = prior_ref[...]
    low[...] = prior.astype(jnp.bfloat16)
    pair_images(True)
    first = residual[...] - (gram_term(prior) + image[...])
    residual[...] = first
    direction[...] = first
    out_ref[...] = prior
    norm_now = row_sum(first, first)
    for step in range(ITERS):
        heading = direction[...]
        low[...] = heading.astype(jnp.bfloat16)
        pair_images(False)
        shown = gram_term(heading) + image[...]
        alpha = norm_now / (row_sum(heading, shown) + EPS)
        out_ref[...] += alpha * heading
        if step < ITERS - 1:
            left = residual[...] - alpha * shown
            residual[...] = left
            fresh = row_sum(left, left)
            direction[...] = left + (fresh / (norm_now + EPS)) * heading
            norm_now = fresh


def run_sweep(plan, user_prior, gram, count_pieces, item_pieces):
    own_rows, rank = user_prior.shape
    tile = count_pieces[0].shape[1]
    pieces = [*count_pieces, *item_pieces]
    vmem = pl.BlockSpec(memory_space=pltpu.VMEM)
    return pl.pallas_call(
        functools.partial(sweep_kernel, len(count_pieces)),
        out_shape=jax.ShapeDtypeStruct((own_rows, rank), jnp.float32),
        in_specs=[pl.BlockSpec(memory_space=pltpu.SMEM), vmem, vmem]
        + [pl.BlockSpec(memory_space=pl.ANY)] * len(pieces),
        out_specs=vmem,
        scratch_shapes=[
            pltpu.VMEM((LOADS, tile, tile), jnp.bfloat16),
            pltpu.VMEM((LOADS, tile, rank), jnp.bfloat16),
            pltpu.VMEM((own_rows, rank), jnp.bfloat16),
            pltpu.VMEM((own_rows, rank), jnp.float32),
            pltpu.VMEM((own_rows, rank), jnp.float32),
            pltpu.VMEM((own_rows, rank), jnp.float32),
            pltpu.SemaphoreType.DMA((2,)),
        ],
        compiler_params=pltpu.CompilerParams(vmem_limit_bytes=32 * 2**20),
        name="sweep",
    )(plan, user_prior, gram, *pieces)


def pack_kernel(n_sources, lengths, chosen, *refs):
    sources, outs, sem = refs[:n_sources], refs[n_sources:-1], refs[-1]
    start = 0
    for out, length in zip(outs, lengths):

        def place(spot, carry, out=out, start=start):
            start_copy(sources, chosen[start + spot], out.at[spot], sem)
            return carry

        lax.fori_loop(0, length, place, 0)
        start += length
    for out in outs:
        pltpu.make_async_copy(out, out, sem).wait()


def pack_tiles(name, sources, chosen, lengths):
    anywhere = pl.BlockSpec(memory_space=pl.ANY)
    shape = sources[0].shape[1:]
    return pl.pallas_call(
        functools.partial(pack_kernel, len(sources), lengths),
        out_shape=[jax.ShapeDtypeStruct((n, *shape), sources[0].dtype) for n in lengths],
        in_specs=[pl.BlockSpec(memory_space=pltpu.SMEM)] + [anywhere] * len(sources),
        out_specs=[pl.BlockSpec(memory_space=pltpu.VMEM)] * len(lengths),
        scratch_shapes=[pltpu.SemaphoreType.DMA],
        compiler_params=pltpu.CompilerParams(vmem_limit_bytes=32 * 2**20),
        name=name,
    )(chosen, *sources)


def sum_with(value, axis, bit):
    size = lax.axis_size(axis)
    return value + lax.ppermute(value, axis, [(i, i ^ bit) for i in range(size)])


def choose(keys, hit, cells, values):
    return jnp.sum(jnp.where(hit & (keys == cells[:, None]), values, 0), axis=1)


def body(user_prior, item_factors, user_tiles, item_tiles, counts):
    pairs = counts.shape[0]
    tile = counts.shape[1]
    rank = item_factors.shape[1]
    n_blk = lax.axis_size("blk")
    n_grp = lax.axis_size("grp")
    n_all = n_blk * n_grp
    n_chips = n_grp // 2
    own_rows = user_prior.shape[0]
    own_tiles = own_rows // tile
    user_blocks = own_tiles * n_grp
    tiles_held = item_factors.shape[0] // tile
    my_blk = lax.axis_index("blk")
    my_grp = lax.axis_index("grp")
    my_chip = my_grp // 2
    my_core = my_grp % 2
    lanes = [[chip * 2 + core for chip in range(n_chips)] for core in range(2)]

    def swap(value):
        return lax.ppermute(value, "grp", [(i, i ^ 1) for i in range(n_grp)])

    def to_chips(value):
        return lax.all_to_all(
            value, "grp", split_axis=0, concat_axis=0, tiled=True, axis_index_groups=lanes
        )

    gram_local = lax.dot_general(
        item_factors, item_factors, (((0,), (0,)), ((), ())), preferred_element_type=jnp.float32
    )
    steps = [(axis, 1 << n) for axis in ("blk", "grp") for n in range(bits_for(lax.axis_size(axis)))]
    gram = sum_with(gram_local, *steps[0])

    held = item_factors.reshape(tiles_held, tile, rank)
    held_mate = swap(held)
    live = jnp.any(counts > 0, axis=(1, 2))
    scaled = (ALPHA * counts.astype(jnp.float32)).astype(jnp.bfloat16)
    scaled_mate = swap(scaled)
    packed = (item_tiles * 2 + live.astype(jnp.int32)) * user_blocks + user_tiles
    packed, gram = lax.optimization_barrier((packed, gram))
    every = lax.all_to_all(
        jnp.broadcast_to(packed, (n_all, pairs)), ("blk", "grp"),
        split_axis=0, concat_axis=0, tiled=True,
    )
    for step in steps[1:]:
        gram = sum_with(gram, *step)
    n_entries = n_grp * pairs
    every = every.reshape(n_blk, n_entries)
    all_user = every % user_blocks
    every = every // user_blocks
    all_live = every % 2 == 1
    all_item = every // 2
    all_owner = all_user // own_tiles
    all_chip = all_item // (2 * tiles_held)
    all_tile = all_item % (2 * tiles_held)
    index = jnp.arange(n_entries, dtype=jnp.int32)
    source = index // pairs

    ids = jnp.arange(2 * tiles_held, dtype=jnp.int32)
    chips = jnp.arange(n_blk * n_chips, dtype=jnp.int32)
    on_chip = ((all_chip[:, None, :] == chips[:, None]) & all_live[:, None, :]).astype(jnp.bfloat16)
    on_tile = (all_tile[:, :, None] == ids).astype(jnp.bfloat16)
    needed = jnp.einsum("bce,bet->bct", on_chip, on_tile, preferred_element_type=jnp.float32) > 0
    fewer = (ids[:, None] < ids[None, :]).astype(jnp.bfloat16)
    tiles_ahead = jnp.einsum(
        "bct,ts->bcs", needed.astype(jnp.bfloat16), fewer, preferred_element_type=jnp.float32
    ).astype(jnp.int32)

    pick = lambda x: lax.dynamic_index_in_dim(x, my_blk, 0, keepdims=False)
    e_live, e_user, e_owner = pick(all_live), pick(all_user), pick(all_owner)
    e_chip, e_tile = pick(all_chip), pick(all_tile)
    e_blk, e_column = e_chip // n_chips, e_chip % n_chips
    e_to = e_owner // 2
    e_from = source // 2
    to_us = e_live & (e_to == my_chip)
    local_user = e_user % own_tiles
    members = jnp.arange(n_chips, dtype=jnp.int32)[:, None]
    marks = [
        e_live & (e_from == my_chip) & (e_to == members),
        to_us & (e_from == members),
        e_live & (e_column == my_chip) & (e_to == members),
        to_us & (e_column == members),
        e_live & (e_owner == my_grp) & (local_user == jnp.arange(own_tiles, dtype=jnp.int32)[:, None]),
    ]
    marks = jnp.concatenate(marks, axis=0).astype(jnp.bfloat16)
    before = (index[:, None] < index[None, :]).astype(jnp.bfloat16)
    ahead = jnp.dot(marks, before, preferred_element_type=jnp.float32) * marks.astype(jnp.float32)
    starts = [n_chips * n for n in range(5)] + [4 * n_chips + own_tiles]
    counts_out, counts_back, items_out, items_back, user_rank = [
        jnp.sum(ahead[lo:hi], axis=0).astype(jnp.int32) for lo, hi in zip(starts, starts[1:])
    ]

    mine = lambda place, cap: (place % 2 == my_core) & (place // 2 < cap)
    cells = jnp.arange(n_chips * COUNT_CAP, dtype=jnp.int32)
    chosen = choose(
        e_to * COUNT_CAP + counts_out // 2,
        e_live & (e_from == my_chip) & mine(counts_out, COUNT_CAP),
        cells, at_source((source % 2) ^ my_core, index % pairs, 2),
    )
    (outgoing,) = pack_tiles("pack_counts", [scaled, scaled_mate], chosen, [n_chips * COUNT_CAP])
    here = my_blk * n_chips + my_chip
    at_chip = lambda x: lax.dynamic_index_in_dim(x, here, 1, keepdims=False)
    spots = 2 * jnp.arange(FAR_CAP, dtype=jnp.int32) + my_core
    asked = jnp.sum(
        jnp.where(
            at_chip(needed)[:, None, :] & (at_chip(tiles_ahead)[:, None, :] == spots[:, None]),
            at_source((ids // tiles_held) ^ my_core, ids % tiles_held, 2), 0,
        ),
        axis=2,
    )
    asked = jnp.take(asked, (my_blk + jnp.arange(1, n_blk)) % n_blk, axis=0, mode="clip")
    asked, gram, outgoing = lax.optimization_barrier((asked, gram, outgoing))
    far_out = pack_tiles("pack_far", [held, held_mate], asked.reshape(-1), [FAR_CAP] * (n_blk - 1))
    far = [
        lax.ppermute(piece, "blk", [(i, (i + 1 + shift) % n_blk) for i in range(n_blk)])
        for shift, piece in enumerate(far_out)
    ]

    counts_own = to_chips(outgoing)

    n_sources = 2 * n_blk
    own_chips = jnp.take(
        pick(tiles_ahead), jnp.arange(n_blk) * n_chips + my_chip, axis=0, mode="clip"
    ).reshape(-1)
    cells = jnp.arange(own_chips.shape[0], dtype=jnp.int32)[:, None]
    far_place = jnp.sum(
        jnp.where(e_blk * (2 * tiles_held) + e_tile == cells, own_chips[:, None], 0), axis=0
    )
    far_place = jnp.minimum(far_place, 2 * FAR_CAP - 1)
    shift = (my_blk - e_blk) % n_blk
    near = shift == 0
    lane = jnp.where(near, e_tile // tiles_held, far_place % 2) ^ my_core
    row = jnp.where(near, e_tile % tiles_held, far_place // 2)
    cells = jnp.arange(n_chips * ITEM_CAP, dtype=jnp.int32)
    chosen = choose(
        (e_to ^ my_chip) * ITEM_CAP + items_out // 2,
        e_live & (e_column == my_chip) & mine(items_out, ITEM_CAP),
        cells, at_source(lane * n_blk + shift, row, n_sources),
    )
    hit = e_live & (e_owner == my_grp)
    tiles = jnp.arange(own_tiles, dtype=jnp.int32)
    in_tile = hit & (local_user == tiles[:, None])
    loads = jnp.sum(in_tile.astype(jnp.int32), axis=1)
    chunks = -(-loads // SPAN)
    ends = jnp.sum(jnp.where(tiles[:, None] <= tiles, chunks[:, None], 0), axis=0)
    firsts = ends - chunks
    room_at = jnp.sum(jnp.where(in_tile, firsts[:, None] * SPAN, 0), axis=0) + user_rank
    hit = hit & (room_at < LOADS)
    rounds = jnp.minimum(-(-ends[-1] // TOGETHER), LOADS // (SPAN * TOGETHER))
    chunk_tile = jnp.sum(
        (jnp.arange(LOADS // SPAN, dtype=jnp.int32)[:, None] >= ends[:-1]).astype(jnp.int32), axis=1
    )
    cells = jnp.arange(LOADS, dtype=jnp.int32)
    counts_row = jnp.minimum(counts_back // 2, COUNT_CAP - 1)
    items_row = jnp.minimum(items_back // 2, ITEM_CAP - 1)
    count_at = at_source((counts_back % 2) ^ my_core, e_from * COUNT_CAP + counts_row, 2)
    item_at = at_source(
        (e_column ^ my_chip) * 2 + ((items_back % 2) ^ my_core), items_row, 2 * n_chips
    )
    head = jnp.stack([rounds, jnp.sum(hit.astype(jnp.int32))])
    plan = jnp.concatenate(
        [
            head, chunk_tile,
            choose(room_at, hit, cells, count_at + 1), choose(room_at, hit, cells, item_at),
        ]
    )
    def totals(keys, bins):
        marks = (keys[:, None, :] == jnp.arange(bins, dtype=jnp.int32)[:, None]) & all_live[:, None, :]
        return jnp.sum(marks.astype(jnp.int32), axis=2)

    def most(keys, bins):
        return jnp.max(totals(keys, bins))

    to_chip = all_owner // 2
    elsewhere = chips // n_chips != jnp.arange(n_blk, dtype=jnp.int32)[:, None]
    asks = jnp.sum(needed.astype(jnp.int32), axis=2)
    chunks = -(-totals(all_user, user_blocks) // SPAN)
    chunks = chunks.reshape(n_blk, n_grp, own_tiles)
    fits = (
        (jnp.max(jnp.where(elsewhere, asks, 0)) <= 2 * FAR_CAP)
        & (most(source // 2 * n_chips + to_chip, n_chips * n_chips) <= 2 * COUNT_CAP)
        & (most(all_chip % n_chips * n_chips + to_chip, n_chips * n_chips) <= 2 * ITEM_CAP)
        & (jnp.max(jnp.sum(chunks, axis=2)) * SPAN <= LOADS)
    )

    far[0], chosen, plan, fits = lax.optimization_barrier((far[0], chosen, plan, fits))
    far_mate = [swap(piece) for piece in far]
    items_out = pack_tiles(
        "pack_items", [held, *far, held_mate, *far_mate], chosen, [ITEM_CAP] * n_chips
    )

    counts_own, *items_out = lax.optimization_barrier((counts_own, *items_out))
    counts_mate = swap(counts_own)
    item_pieces = []
    for off, piece in enumerate(items_out):
        if off:
            piece = lax.ppermute(piece, "grp", [(i, i ^ (2 * off)) for i in range(n_grp)])
        item_pieces += [piece, swap(piece)]
    by_owner = run_sweep(plan, user_prior, gram, [counts_own, counts_mate], item_pieces)

    return lax.cond(
        fits, lambda done, *given: done, lambda done, *given: sweep_in_place(*given),
        by_owner, user_prior, item_factors, user_tiles, item_tiles, counts, live, gram_local,
    )


def solution(mesh):
    in_specs = (
        P(("blk", "grp"), None),
        P(("blk", "grp"), None),
        P(("blk", "grp")),
        P(("blk", "grp")),
        P(("blk", "grp"), None, None),
    )
    out_specs = P(("blk", "grp"), None)
    return jax.shard_map(body, mesh=mesh, in_specs=in_specs, out_specs=out_specs, check_vma=False)
```

```python
import functools

import jax
import jax.numpy as jnp
from jax import lax
from jax.experimental import pallas as pl
from jax.experimental.pallas import tpu as pltpu
from jax.sharding import PartitionSpec as P

ITERS = 3

ALPHA = 40.0
REG = 32.0
EPS = 1e-06

FAR_CAP = 14
COUNT_CAP = 24
ITEM_CAP = 20
LOADS = 128
SPAN = 2
TOGETHER = 4


def fetch_tiles(item_factors, item_tiles, pairs, tile, rank):
    n_all = lax.axis_size(("blk", "grp"))
    tiles_held = item_factors.shape[0] // tile
    slots_each = max(2, pairs // n_all)
    owner = item_tiles // tiles_held
    local_slot = item_tiles % tiles_held
    position = jnp.arange(pairs, dtype=jnp.int32)
    earlier = (owner[None, :] == owner[:, None]) & (position[None, :] < position[:, None])
    order = jnp.sum(earlier.astype(jnp.int32), axis=1)
    requests = jnp.full((n_all, slots_each), -1, jnp.int32).at[owner, order].set(local_slot)
    wanted = lax.all_to_all(requests, ("blk", "grp"), split_axis=0, concat_axis=0, tiled=True)
    held = item_factors.reshape(tiles_held, tile, rank)
    picked = jnp.take(held, jnp.maximum(wanted, 0), axis=0)
    picked = jnp.where((wanted >= 0)[:, :, None, None], picked, jnp.zeros((), picked.dtype))
    arrived = lax.all_to_all(picked, ("blk", "grp"), split_axis=0, concat_axis=0, tiled=True)
    return arrived[owner, order]


def row_sum(left, right):
    return jnp.sum(left * right, axis=1, keepdims=True)


def sweep_in_place(user_prior, item_factors, user_tiles, item_tiles, counts, live, gram_local):
    pairs = counts.shape[0]
    tile = counts.shape[1]
    rank = item_factors.shape[1]
    n_grp = lax.axis_size("grp")
    own_rows = user_prior.shape[0]
    block_rows = own_rows * n_grp
    user_blocks = block_rows // tile
    span = min(32, pairs)
    gram = lax.psum(gram_local, ("blk", "grp"))
    pair_tiles = fetch_tiles(item_factors, item_tiles, pairs, tile, rank)
    rounds = (jnp.sum(live.astype(jnp.int32)) + span - 1) // span
    tile_ids = jnp.arange(user_blocks, dtype=jnp.int32)

    def accumulate(low_tiles, with_rhs):

        def one_round(index, totals):
            start = index * span
            users = lax.dynamic_slice_in_dim(user_tiles, start, span)
            factors = lax.dynamic_slice_in_dim(pair_tiles, start, span)
            counted = lax.dynamic_slice_in_dim(counts, start, span).astype(jnp.float32)
            selector = (tile_ids[:, None] == users[None, :]).astype(jnp.float32)
            users_low = jnp.take(low_tiles, users, axis=0)
            scores = jnp.einsum(
                "bur,bir->bui", users_low, factors, preferred_element_type=jnp.float32
            )
            scaled = (ALPHA * counted * scores).astype(jnp.bfloat16)
            back = jnp.einsum("bui,bir->bur", scaled, factors, preferred_element_type=jnp.float32)
            result = [
                totals[0]
                + jnp.einsum("tb,bur->tur", selector, back, precision=lax.Precision.HIGHEST)
            ]
            if with_rhs:
                confidence = jnp.where(counted > 0, 1.0 + ALPHA * counted, 0.0).astype(jnp.bfloat16)
                pulled = jnp.einsum(
                    "bui,bir->bur", confidence, factors, preferred_element_type=jnp.float32
                )
                result.append(
                    totals[1]
                    + jnp.einsum("tb,bur->tur", selector, pulled, precision=lax.Precision.HIGHEST)
                )
            return tuple(result)

        zeros = jnp.zeros((user_blocks, tile, rank), jnp.float32)
        start_state = (zeros, zeros) if with_rhs else (zeros,)
        totals = lax.fori_loop(0, rounds, one_round, start_state)
        return tuple((total.reshape(block_rows, rank) for total in totals))

    def gram_term(vectors):
        return jnp.dot(vectors, gram, precision=lax.Precision.HIGHEST) + REG * vectors

    low = lax.all_gather(user_prior.astype(jnp.bfloat16), "grp", axis=0, tiled=True)
    pair_part, rhs_part = accumulate(low.reshape(user_blocks, tile, rank), True)
    pair_share, rhs_share = (
        lax.psum_scatter(pair_part, "grp", scatter_dimension=0, tiled=True),
        lax.psum_scatter(rhs_part, "grp", scatter_dimension=0, tiled=True),
    )
    solution = user_prior
    residual = rhs_share - (gram_term(solution) + pair_share)
    direction = residual
    norm_now = row_sum(residual, residual)
    for step in range(ITERS):
        low = lax.all_gather(direction.astype(jnp.bfloat16), "grp", axis=0, tiled=True)
        (pair_part,) = accumulate(low.reshape(user_blocks, tile, rank), False)
        image = gram_term(direction) + lax.psum_scatter(
            pair_part, "grp", scatter_dimension=0, tiled=True
        )
        alpha = norm_now / (row_sum(direction, image) + EPS)
        solution = solution + alpha * direction
        residual = residual - alpha * image
        fresh = row_sum(residual, residual)
        direction = residual + fresh / (norm_now + EPS) * direction
        norm_now = fresh
    return solution


def bits_for(n):
    return (n - 1).bit_length()


def at_source(number, row, n_sources):
    return (row << bits_for(n_sources)) + number


def start_copy(sources, at, target, sem):
    bits = bits_for(len(sources))
    row = lax.shift_right_logical(at, bits)
    which = at & ((1 << bits) - 1)
    for number, source in enumerate(sources):

        @pl.when(which == number)
        def _(source=source):
            pltpu.make_async_copy(source.at[row], target, sem).start()


def sweep_kernel(n_counts, plan, prior_ref, gram_ref, *refs):
    weights, factors, low, image, residual, direction, sems = refs[-7:]
    count_pieces, item_pieces, out_ref = refs[:n_counts], refs[n_counts:-8], refs[-8]
    tile, rank = factors.shape[1:]
    rounds = plan[6, 0]

    def bring(place, carry):
        count_at = plan[3, place]
        item_at = plan[4, place]

        @pl.when(count_at > 0)
        def _():
            start_copy(count_pieces, count_at - 1, weights.at[place], sems.at[0])
            start_copy(item_pieces, item_at, factors.at[place], sems.at[1])

        @pl.when(count_at == 0)
        def _():
            weights[place] = jnp.zeros((tile, tile), weights.dtype)
            factors[place] = jnp.zeros((tile, rank), factors.dtype)

        return carry

    lax.fori_loop(0, rounds * (TOGETHER * SPAN), bring, 0)

    def arrive(entry, carry):
        pltpu.make_async_copy(count_pieces[0].at[0], weights.at[0], sems.at[0]).wait()
        pltpu.make_async_copy(item_pieces[0].at[0], factors.at[0], sems.at[1]).wait()
        return carry

    lax.fori_loop(0, plan[6, 1], arrive, 0)

    def pair_images(with_rhs):
        image[...] = jnp.zeros_like(image)
        if with_rhs:
            residual[...] = jnp.zeros_like(residual)

        def one_round(step, carry):
            shares = []
            for number in range(TOGETHER):
                chunk = step * TOGETHER + number
                rows = pl.ds(pl.multiple_of(plan[5, chunk] * tile, tile), tile)
                items = factors[pl.ds(chunk * SPAN, SPAN)].reshape(SPAN * tile, rank)
                scaled = jnp.concatenate(
                    [weights[chunk * SPAN + part].astype(jnp.float32) for part in range(SPAN)],
                    axis=1,
                )
                scores = lax.dot_general(
                    low[rows, :], items, (((1,), (1,)), ((), ())),
                    preferred_element_type=jnp.float32,
                )
                back = jnp.dot(
                    (scaled * scores).astype(jnp.bfloat16), items,
                    preferred_element_type=jnp.float32,
                )
                pulled = None
                if with_rhs:
                    confidence = jnp.where(scaled > 0, 1.0 + scaled, 0.0).astype(jnp.bfloat16)
                    pulled = jnp.dot(confidence, items, preferred_element_type=jnp.float32)
                shares.append((rows, back, pulled))
            for rows, back, pulled in shares:
                image[rows, :] += back
                if with_rhs:
                    residual[rows, :] += pulled
            return carry

        lax.fori_loop(0, rounds, one_round, 0)

    def gram_term(vectors):
        return jnp.dot(
            vectors, gram_ref[...], precision=lax.Precision.HIGHEST,
            preferred_element_type=jnp.float32,
        ) + REG * vectors

    prior = prior_ref[...]
    low[...] = prior.astype(jnp.bfloat16)
    pair_images(True)
    first = residual[...] - (gram_term(prior) + image[...])
    residual[...] = first
    direction[...] = first
    out_ref[...] = prior
    norm_now = row_sum(first, first)
    for step in range(ITERS):
        heading = direction[...]
        low[...] = heading.astype(jnp.bfloat16)
        pair_images(False)
        shown = gram_term(heading) + image[...]
        alpha = norm_now / (row_sum(heading, shown) + EPS)
        out_ref[...] += alpha * heading
        if step < ITERS - 1:
            left = residual[...] - alpha * shown
            residual[...] = left
            fresh = row_sum(left, left)
            direction[...] = left + (fresh / (norm_now + EPS)) * heading
            norm_now = fresh


def run_sweep(plan, user_prior, gram, count_pieces, item_pieces):
    own_rows, rank = user_prior.shape
    tile = count_pieces[0].shape[1]
    pieces = [*count_pieces, *item_pieces]
    vmem = pl.BlockSpec(memory_space=pltpu.VMEM)
    return pl.pallas_call(
        functools.partial(sweep_kernel, len(count_pieces)),
        out_shape=jax.ShapeDtypeStruct((own_rows, rank), jnp.float32),
        in_specs=[pl.BlockSpec(memory_space=pltpu.SMEM), vmem, vmem]
        + [pl.BlockSpec(memory_space=pl.ANY)] * len(pieces),
        out_specs=vmem,
        scratch_shapes=[
            pltpu.VMEM((LOADS, tile, tile), jnp.bfloat16),
            pltpu.VMEM((LOADS, tile, rank), jnp.bfloat16),
            pltpu.VMEM((own_rows, rank), jnp.bfloat16),
            pltpu.VMEM((own_rows, rank), jnp.float32),
            pltpu.VMEM((own_rows, rank), jnp.float32),
            pltpu.VMEM((own_rows, rank), jnp.float32),
            pltpu.SemaphoreType.DMA((2,)),
        ],
        compiler_params=pltpu.CompilerParams(vmem_limit_bytes=32 * 2**20),
        name="sweep",
    )(plan, user_prior, gram, *pieces)


def pack_kernel(n_sources, jobs, table, *refs):
    sources, refs = refs[:n_sources], refs[n_sources:]
    outs, rooms, arrived, written = refs[:len(jobs)], refs[len(jobs):-2], refs[-2], refs[-1]
    for number, (lo, hi, row, start, length) in enumerate(jobs):

        def place(spot, carry, number=number, lo=lo, hi=hi, row=row, start=start):
            start_copy(
                sources[lo:hi], table[row, start + spot], rooms[number].at[spot], arrived.at[number]
            )
            return carry

        lax.fori_loop(0, length, place, 0)
    write = [
        pltpu.make_async_copy(room, out, written.at[number])
        for number, (room, out) in enumerate(zip(rooms, outs))
    ]
    for number, room in enumerate(rooms):
        pltpu.make_async_copy(room, room, arrived.at[number]).wait()
        write[number].start()
    for copy in write:
        copy.wait()


def pack_tiles(name, table, sources, jobs):
    anywhere = pl.BlockSpec(memory_space=pl.ANY)
    kinds = [((job[4], *sources[job[0]].shape[1:]), sources[job[0]].dtype) for job in jobs]
    return pl.pallas_call(
        functools.partial(pack_kernel, len(sources), jobs),
        out_shape=[jax.ShapeDtypeStruct(*kind) for kind in kinds],
        in_specs=[pl.BlockSpec(memory_space=pltpu.SMEM)] + [anywhere] * len(sources),
        out_specs=[anywhere] * len(jobs),
        scratch_shapes=[pltpu.VMEM(*kind) for kind in kinds]
        + [pltpu.SemaphoreType.DMA((len(jobs),))] * 2,
        compiler_params=pltpu.CompilerParams(vmem_limit_bytes=32 * 2**20),
        name=name,
    )(table, *sources)


def sum_with(value, axis, bit):
    size = lax.axis_size(axis)
    return value + lax.ppermute(value, axis, [(i, i ^ bit) for i in range(size)])


def iota(rows, columns, axis):
    return lax.broadcasted_iota(jnp.int32, (rows, columns), axis)


def dot_nt(left, right):
    return lax.dot_general(
        left.astype(jnp.bfloat16), right.astype(jnp.bfloat16), (((1,), (1,)), ((), ())),
        preferred_element_type=jnp.float32,
    )


def choose(key, hit, cells, *values):
    match = hit & (key == iota(cells, key.shape[1], 0))
    row = iota(8, key.shape[1], 0)
    digits = jnp.zeros((8, key.shape[1]), jnp.int32)
    for number, value in enumerate(values):
        digits = jnp.where(row == 2 * number, value & 31, digits)
        digits = jnp.where(row == 2 * number + 1, lax.shift_right_logical(value, 5), digits)
    found = dot_nt(digits.astype(jnp.float32), match.astype(jnp.float32)).astype(jnp.int32)
    return [
        found[2 * number:2 * number + 1] + 32 * found[2 * number + 1:2 * number + 2]
        for number in range(len(values))
    ]


def route_kernel(n_grp, pairs, own_tiles, tiles_held, spot, every_ref, out_ref):
    n_blk, n_entries = every_ref.shape
    width = out_ref.shape[1]
    n_chips = n_grp // 2
    user_blocks = n_grp * own_tiles
    all_chips = n_blk * n_chips
    pad = lambda n: -(-n // 8) * 8
    my_blk, my_grp = spot[0], spot[1]
    my_chip = lax.shift_right_logical(my_grp, 1)
    my_core = my_grp & 1
    index = iota(1, n_entries, 1)
    source = lax.shift_right_logical(index, bits_for(pairs))
    from_chip = lax.shift_right_logical(source, 1)
    one_hot = lambda key, n: key == iota(pad(n), n_entries, 0)

    def fields(packed):
        user = packed & (user_blocks - 1)
        packed = lax.shift_right_logical(packed, bits_for(user_blocks))
        live = (packed & 1) == 1
        item = lax.shift_right_logical(packed, 1)
        held = item & (2 * tiles_held - 1)
        chip = lax.shift_right_logical(item, bits_for(2 * tiles_held))
        return user, live, chip, held

    ids = iota(1, 2 * tiles_held, 1)
    fewer = iota(2 * tiles_held, 2 * tiles_held, 0) > iota(2 * tiles_held, 2 * tiles_held, 1)

    def needs(live, chip, held):
        on_chip = one_hot(chip, all_chips) & live
        on_tile = one_hot(held, 2 * tiles_held)
        needed = dot_nt(on_chip.astype(jnp.float32), on_tile.astype(jnp.float32)) > 0
        return on_chip, on_tile, needed, dot_nt(needed.astype(jnp.float32), fewer.astype(jnp.float32))

    excess = jnp.zeros((1, 1), jnp.float32)
    worst = lambda loads, room: jnp.max(loads, axis=(0, 1), keepdims=True) - room
    asked = jnp.zeros((1, width), jnp.int32)
    here = my_blk * n_chips + my_chip
    chip_row = iota(pad(all_chips), 2 * tiles_held, 0)
    for blk in range(n_blk):
        user, live, chip, held = fields(every_ref[blk:blk + 1, :])
        _, _, needed, ahead = needs(live, chip, held)
        away = lax.shift_right_logical(chip_row, bits_for(n_chips)) != blk
        asks = jnp.sum((needed & away).astype(jnp.float32), axis=1, keepdims=True)
        excess = jnp.maximum(excess, worst(asks, 2 * FAR_CAP))
        to_chip = lax.shift_right_logical(user, bits_for(own_tiles) + 1)
        to = one_hot(to_chip, n_chips).astype(jnp.float32)
        for key, cap in ((from_chip, COUNT_CAP), (chip & (n_chips - 1), ITEM_CAP)):
            loads = dot_nt((one_hot(key, n_chips) & live).astype(jnp.float32), to)
            excess = jnp.maximum(excess, worst(loads, 2 * cap))
        loads = jnp.sum(
            (one_hot(user, user_blocks) & live).astype(jnp.int32), axis=1, keepdims=True
        )
        chunks = lax.shift_right_logical(loads + SPAN - 1, bits_for(SPAN)).astype(jnp.float32)
        owners = iota(pad(n_grp), pad(user_blocks), 1)
        owners = lax.shift_right_logical(owners, bits_for(own_tiles)) == iota(*owners.shape, 0)
        loads = jnp.dot(
            owners.astype(jnp.float32), jnp.broadcast_to(chunks, (chunks.shape[0], 128)),
            precision=lax.Precision.HIGHEST, preferred_element_type=jnp.float32,
        )
        excess = jnp.maximum(excess, worst(loads, LOADS // SPAN))

        mine = chip_row == here
        present = jnp.sum((needed & mine).astype(jnp.int32), axis=0, keepdims=True)
        place = jnp.sum(jnp.where(mine, ahead, 0.0), axis=0, keepdims=True).astype(jnp.int32)
        shift = (blk + n_blk - my_blk) & (n_blk - 1)
        spot_at = lax.shift_right_logical(place, 1)
        hit = (present > 0) & ((place & 1) == my_core) & (spot_at < FAR_CAP) & (shift > 0)
        value = at_source(
            lax.shift_right_logical(ids, bits_for(tiles_held)) ^ my_core, ids & (tiles_held - 1), 2
        )
        (found,) = choose((shift - 1) * FAR_CAP + spot_at, hit, width, value)
        asked = asked + found

    user, live, chip, held = fields(every_ref[pl.ds(my_blk, 1), :])
    on_chip, on_tile, _, ahead = needs(live, chip, held)
    places = jnp.dot(
        ahead.astype(jnp.bfloat16), on_tile.astype(jnp.float32).astype(jnp.bfloat16),
        preferred_element_type=jnp.float32,
    )
    far_place = jnp.sum(jnp.where(on_chip, places, 0.0), axis=0, keepdims=True).astype(jnp.int32)
    far_place = jnp.minimum(far_place, 2 * FAR_CAP - 1)
    owner = lax.shift_right_logical(user, bits_for(own_tiles))
    local_user = user & (own_tiles - 1)
    to_chip = lax.shift_right_logical(owner, 1)
    column = chip & (n_chips - 1)
    to_me = live & (owner == my_grp)
    groups = [
        one_hot(to_chip, n_chips) & (live & (from_chip == my_chip)),
        one_hot(from_chip, n_chips) & (live & (to_chip == my_chip)),
        one_hot(to_chip, n_chips) & (live & (column == my_chip)),
        one_hot(column, n_chips) & (live & (to_chip == my_chip)),
        one_hot(local_user, own_tiles) & to_me,
    ]
    before = (iota(n_entries, n_entries, 0) < iota(n_entries, n_entries, 1)).astype(jnp.float32)
    before = before.astype(jnp.bfloat16)
    ranks = []
    for marks in groups:
        earlier = jnp.dot(
            marks.astype(jnp.float32).astype(jnp.bfloat16), before,
            preferred_element_type=jnp.float32,
        )
        earlier = jnp.sum(jnp.where(marks, earlier, 0.0), axis=0, keepdims=True)
        ranks.append(earlier.astype(jnp.int32))
    counts_out, counts_back, items_out, items_back, user_rank = ranks

    half = lambda rank: lax.shift_right_logical(rank, 1)
    sent = lambda rank, cap: live & ((rank & 1) == my_core) & (half(rank) < cap)
    (out_ref[0:1, :],) = choose(
        to_chip * COUNT_CAP + half(counts_out), sent(counts_out, COUNT_CAP) & (from_chip == my_chip),
        width, at_source((source & 1) ^ my_core, index & (pairs - 1), 2),
    )
    out_ref[1:2, :] = asked
    shift = (my_blk + n_blk - lax.shift_right_logical(chip, bits_for(n_chips))) & (n_blk - 1)
    near = shift == 0
    lane = jnp.where(near, lax.shift_right_logical(held, bits_for(tiles_held)), far_place & 1)
    row = jnp.where(near, held & (tiles_held - 1), half(far_place))
    (out_ref[2:3, :],) = choose(
        (to_chip ^ my_chip) * ITEM_CAP + half(items_out),
        sent(items_out, ITEM_CAP) & (column == my_chip),
        width, at_source((lane ^ my_core) * n_blk + shift, row, 2 * n_blk),
    )

    in_tile = groups[4]
    loads = jnp.sum(in_tile.astype(jnp.int32), axis=1, keepdims=True)
    chunks = lax.shift_right_logical(loads + SPAN - 1, bits_for(SPAN)).astype(jnp.float32)
    rows = chunks.shape[0]
    ends = jnp.dot(
        (iota(rows, rows, 0) >= iota(rows, rows, 1)).astype(jnp.float32),
        jnp.broadcast_to(chunks, (rows, 128)),
        precision=lax.Precision.HIGHEST, preferred_element_type=jnp.float32,
    )
    firsts = ends[:, :1] - chunks
    room_at = jnp.sum(jnp.where(in_tile, firsts * SPAN, 0.0), axis=0, keepdims=True)
    room_at = room_at.astype(jnp.int32) + user_rank
    hit = to_me & (room_at < LOADS)
    counts_row = jnp.minimum(half(counts_back), COUNT_CAP - 1)
    items_row = jnp.minimum(half(items_back), ITEM_CAP - 1)
    count_at = at_source((counts_back & 1) ^ my_core, from_chip * COUNT_CAP + counts_row, 2)
    item_at = at_source(
        (column ^ my_chip) * 2 + ((items_back & 1) ^ my_core), items_row, 2 * n_chips
    )
    out_ref[3:4, :], out_ref[4:5, :] = choose(room_at, hit, width, count_at + 1, item_at)
    passed = (iota(rows, width, 1).astype(jnp.float32) >= ends[:, :1]) & (
        iota(rows, width, 0) < own_tiles - 1
    )
    out_ref[5:6, :] = jnp.sum(passed.astype(jnp.int32), axis=0, keepdims=True)
    total = ends[own_tiles - 1:own_tiles, :1].astype(jnp.int32)
    rounds = lax.shift_right_logical(total + TOGETHER - 1, bits_for(TOGETHER))
    rounds = jnp.minimum(rounds, LOADS // (SPAN * TOGETHER))
    copies = jnp.sum(hit.astype(jnp.int32), axis=1, keepdims=True)
    at = iota(1, width, 1)
    fits = (excess <= 0.0).astype(jnp.int32)
    head = jnp.where(at == 0, rounds, jnp.where(at == 1, copies, jnp.where(at == 2, fits, 0)))
    out_ref[6:7, :] = head
    out_ref[7:8, :] = jnp.zeros((1, width), jnp.int32)


def route(every, my_blk, my_grp, n_grp, own_tiles, tiles_held):
    n_blk, n_entries = every.shape
    n_chips = n_grp // 2
    width = max(n_chips * COUNT_CAP, (n_blk - 1) * FAR_CAP, n_chips * ITEM_CAP, LOADS)
    width = -(-width // 128) * 128
    vmem = pl.BlockSpec(memory_space=pltpu.VMEM)
    return pl.pallas_call(
        functools.partial(route_kernel, n_grp, n_entries // n_grp, own_tiles, tiles_held),
        out_shape=jax.ShapeDtypeStruct((8, width), jnp.int32),
        in_specs=[pl.BlockSpec(memory_space=pltpu.SMEM), vmem],
        out_specs=vmem,
        compiler_params=pltpu.CompilerParams(vmem_limit_bytes=32 * 2**20),
        name="route",
    )(jnp.stack([my_blk, my_grp]).astype(jnp.int32), every)


def scan_kernel(counts_ref, scaled_ref, most_ref):
    counts = counts_ref[...]
    scaled_ref[...] = (ALPHA * counts.astype(jnp.float32)).astype(jnp.bfloat16)
    most_ref[...] = jnp.max(counts, axis=1)


def scan_counts(counts):
    pairs, tile, columns = counts.shape
    block = 8
    return pl.pallas_call(
        scan_kernel,
        grid=(pairs // block,),
        out_shape=[
            jax.ShapeDtypeStruct(counts.shape, jnp.bfloat16),
            jax.ShapeDtypeStruct((pairs, columns), jnp.int32),
        ],
        in_specs=[pl.BlockSpec((block, tile, columns), lambda i: (i, 0, 0))],
        out_specs=[
            pl.BlockSpec((block, tile, columns), lambda i: (i, 0, 0)),
            pl.BlockSpec((block, columns), lambda i: (i, 0)),
        ],
        compiler_params=pltpu.CompilerParams(vmem_limit_bytes=16 * 2**20),
        name="scan_counts",
    )(counts)


def body(user_prior, item_factors, user_tiles, item_tiles, counts):
    pairs = counts.shape[0]
    tile = counts.shape[1]
    rank = item_factors.shape[1]
    n_blk = lax.axis_size("blk")
    n_grp = lax.axis_size("grp")
    n_all = n_blk * n_grp
    n_chips = n_grp // 2
    own_rows = user_prior.shape[0]
    own_tiles = own_rows // tile
    user_blocks = own_tiles * n_grp
    tiles_held = item_factors.shape[0] // tile
    my_blk = lax.axis_index("blk")
    my_grp = lax.axis_index("grp")
    my_chip = my_grp // 2
    my_core = my_grp % 2
    lanes = [[chip * 2 + core for chip in range(n_chips)] for core in range(2)]

    def swap(value):
        return lax.ppermute(value, "grp", [(i, i ^ 1) for i in range(n_grp)])

    def to_chips(value):
        return lax.all_to_all(
            value, "grp", split_axis=0, concat_axis=0, tiled=True, axis_index_groups=lanes
        )

    gram_local = lax.dot_general(
        item_factors, item_factors, (((0,), (0,)), ((), ())), preferred_element_type=jnp.float32
    )
    grp_bits, blk_bits = [[1 << n for n in range(bits_for(size))] for size in (n_grp, n_blk)]
    gram = sum_with(gram_local, "grp", grp_bits[0])

    held = item_factors.reshape(tiles_held, tile, rank)
    held_mate = swap(held)
    scaled, column_most = scan_counts(counts)
    live = jnp.any(column_most > 0, axis=1)
    scaled_mate = swap(scaled)
    packed = (item_tiles * 2 + live.astype(jnp.int32)) * user_blocks + user_tiles
    packed, gram = lax.optimization_barrier((packed, gram))
    every = lax.all_to_all(
        jnp.broadcast_to(packed, (n_all, pairs)), ("blk", "grp"),
        split_axis=0, concat_axis=0, tiled=True,
    )
    table = route(every.reshape(n_blk, n_grp * pairs), my_blk, my_grp, n_grp, own_tiles, tiles_held)
    for bit in grp_bits[1:]:
        gram = sum_with(gram, "grp", bit)
    table, gram = lax.optimization_barrier((table, gram))

    jobs = [(0, 2, 1, shift * FAR_CAP, FAR_CAP) for shift in range(n_blk - 1)]
    jobs.append((2, 4, 0, 0, n_chips * COUNT_CAP))
    *far, counts_out = pack_tiles("pack_first", table, [held, held_mate, scaled, scaled_mate], jobs)
    far = [
        lax.ppermute(piece, "blk", [(i, (i + 1 + shift) % n_blk) for i in range(n_blk)])
        for shift, piece in enumerate(far)
    ]
    far_mate = [swap(piece) for piece in far]
    counts_own = to_chips(counts_out)

    jobs = [(0, 2 * n_blk, 2, off * ITEM_CAP, ITEM_CAP) for off in range(n_chips)]
    items_out = pack_tiles("pack_items", table, [held, *far, held_mate, *far_mate], jobs)
    counts_own, gram, *items_out = lax.optimization_barrier((counts_own, gram, *items_out))
    counts_mate = swap(counts_own)
    for bit in blk_bits:
        gram = sum_with(gram, "blk", bit)
    item_pieces = []
    for off, piece in enumerate(items_out):
        if off:
            piece = lax.ppermute(piece, "grp", [(i, i ^ (2 * off)) for i in range(n_grp)])
        if off == 1:
            piece, gram = lax.optimization_barrier((piece, gram))
        item_pieces += [piece, swap(piece)]
    by_owner = run_sweep(table, user_prior, gram, [counts_own, counts_mate], item_pieces)

    fits = table[6, 2] > 0
    return lax.cond(
        fits, lambda done, *given: done, lambda done, *given: sweep_in_place(*given),
        by_owner, user_prior, item_factors, user_tiles, item_tiles, counts, live, gram_local,
    )


def solution(mesh):
    in_specs = (
        P(("blk", "grp"), None),
        P(("blk", "grp"), None),
        P(("blk", "grp")),
        P(("blk", "grp")),
        P(("blk", "grp"), None, None),
    )
    out_specs = P(("blk", "grp"), None)
    return jax.shard_map(body, mesh=mesh, in_specs=in_specs, out_specs=out_specs, check_vma=False)
```

```python
import functools

import jax
import jax.numpy as jnp
from jax import lax
from jax.experimental import pallas as pl
from jax.experimental.pallas import tpu as pltpu
from jax.sharding import PartitionSpec as P

ITERS = 3

ALPHA = 40.0
REG = 32.0
EPS = 1e-06

FAR_CAP = 14
COUNT_CAP = 24
ITEM_CAPS = (16, 8)
LOADS = 128
SPAN = 2
TOGETHER = 4


def fetch_tiles(item_factors, item_tiles, pairs, tile, rank):
    n_all = lax.axis_size(("blk", "grp"))
    tiles_held = item_factors.shape[0] // tile
    slots_each = max(2, pairs // n_all)
    owner = item_tiles // tiles_held
    local_slot = item_tiles % tiles_held
    position = jnp.arange(pairs, dtype=jnp.int32)
    earlier = (owner[None, :] == owner[:, None]) & (position[None, :] < position[:, None])
    order = jnp.sum(earlier.astype(jnp.int32), axis=1)
    requests = jnp.full((n_all, slots_each), -1, jnp.int32).at[owner, order].set(local_slot)
    wanted = lax.all_to_all(requests, ("blk", "grp"), split_axis=0, concat_axis=0, tiled=True)
    held = item_factors.reshape(tiles_held, tile, rank)
    picked = jnp.take(held, jnp.maximum(wanted, 0), axis=0)
    picked = jnp.where((wanted >= 0)[:, :, None, None], picked, jnp.zeros((), picked.dtype))
    arrived = lax.all_to_all(picked, ("blk", "grp"), split_axis=0, concat_axis=0, tiled=True)
    return arrived[owner, order]


def row_sum(left, right):
    return jnp.sum(left * right, axis=1, keepdims=True)


def sweep_in_place(user_prior, item_factors, user_tiles, item_tiles, counts, live, gram_local):
    pairs = counts.shape[0]
    tile = counts.shape[1]
    rank = item_factors.shape[1]
    n_grp = lax.axis_size("grp")
    own_rows = user_prior.shape[0]
    block_rows = own_rows * n_grp
    user_blocks = block_rows // tile
    span = min(32, pairs)
    gram = lax.psum(gram_local, ("blk", "grp"))
    pair_tiles = fetch_tiles(item_factors, item_tiles, pairs, tile, rank)
    rounds = (jnp.sum(live.astype(jnp.int32)) + span - 1) // span
    tile_ids = jnp.arange(user_blocks, dtype=jnp.int32)

    def accumulate(low_tiles, with_rhs):

        def one_round(index, totals):
            start = index * span
            users = lax.dynamic_slice_in_dim(user_tiles, start, span)
            factors = lax.dynamic_slice_in_dim(pair_tiles, start, span)
            counted = lax.dynamic_slice_in_dim(counts, start, span).astype(jnp.float32)
            selector = (tile_ids[:, None] == users[None, :]).astype(jnp.float32)
            users_low = jnp.take(low_tiles, users, axis=0)
            scores = jnp.einsum(
                "bur,bir->bui", users_low, factors, preferred_element_type=jnp.float32
            )
            scaled = (ALPHA * counted * scores).astype(jnp.bfloat16)
            back = jnp.einsum("bui,bir->bur", scaled, factors, preferred_element_type=jnp.float32)
            result = [
                totals[0]
                + jnp.einsum("tb,bur->tur", selector, back, precision=lax.Precision.HIGHEST)
            ]
            if with_rhs:
                confidence = jnp.where(counted > 0, 1.0 + ALPHA * counted, 0.0).astype(jnp.bfloat16)
                pulled = jnp.einsum(
                    "bui,bir->bur", confidence, factors, preferred_element_type=jnp.float32
                )
                result.append(
                    totals[1]
                    + jnp.einsum("tb,bur->tur", selector, pulled, precision=lax.Precision.HIGHEST)
                )
            return tuple(result)

        zeros = jnp.zeros((user_blocks, tile, rank), jnp.float32)
        start_state = (zeros, zeros) if with_rhs else (zeros,)
        totals = lax.fori_loop(0, rounds, one_round, start_state)
        return tuple((total.reshape(block_rows, rank) for total in totals))

    def gram_term(vectors):
        return jnp.dot(vectors, gram, precision=lax.Precision.HIGHEST) + REG * vectors

    low = lax.all_gather(user_prior.astype(jnp.bfloat16), "grp", axis=0, tiled=True)
    pair_part, rhs_part = accumulate(low.reshape(user_blocks, tile, rank), True)
    pair_share, rhs_share = (
        lax.psum_scatter(pair_part, "grp", scatter_dimension=0, tiled=True),
        lax.psum_scatter(rhs_part, "grp", scatter_dimension=0, tiled=True),
    )
    solution = user_prior
    residual = rhs_share - (gram_term(solution) + pair_share)
    direction = residual
    norm_now = row_sum(residual, residual)
    for step in range(ITERS):
        low = lax.all_gather(direction.astype(jnp.bfloat16), "grp", axis=0, tiled=True)
        (pair_part,) = accumulate(low.reshape(user_blocks, tile, rank), False)
        image = gram_term(direction) + lax.psum_scatter(
            pair_part, "grp", scatter_dimension=0, tiled=True
        )
        alpha = norm_now / (row_sum(direction, image) + EPS)
        solution = solution + alpha * direction
        residual = residual - alpha * image
        fresh = row_sum(residual, residual)
        direction = residual + fresh / (norm_now + EPS) * direction
        norm_now = fresh
    return solution


def bits_for(n):
    return (n - 1).bit_length()


def at_source(number, row, n_sources):
    return (row << bits_for(n_sources)) + number


def start_copy(sources, at, target, sem):
    bits = bits_for(len(sources))
    row = lax.shift_right_logical(at, bits)
    which = at & ((1 << bits) - 1)

    def among(lo, hi):
        if hi - lo == 1:
            pltpu.make_async_copy(sources[lo].at[row], target, sem).start()
            return
        mid = (lo + hi) // 2
        pl.when(which < mid)(lambda: among(lo, mid))
        pl.when(which >= mid)(lambda: among(mid, hi))

    among(0, len(sources))


def sweep_kernel(n_counts, plan, prior_ref, gram_ref, *refs):
    weights, factors, low, image, residual, direction, sems = refs[-7:]
    count_pieces, item_pieces, out_ref = refs[:n_counts], refs[n_counts:-8], refs[-8]
    tile, rank = factors.shape[1:]
    rounds = plan[6, 0]

    def bring(place, carry):
        count_at = plan[3, place]
        item_at = plan[4, place]

        @pl.when(count_at > 0)
        def _():
            start_copy(count_pieces, count_at - 1, weights.at[place], sems.at[0])
            start_copy(item_pieces, item_at, factors.at[place], sems.at[1])

        @pl.when(count_at == 0)
        def _():
            weights[place] = jnp.zeros((tile, tile), weights.dtype)
            factors[place] = jnp.zeros((tile, rank), factors.dtype)

        return carry

    lax.fori_loop(0, rounds * (TOGETHER * SPAN), bring, 0)

    def arrive(entry, carry):
        pltpu.make_async_copy(count_pieces[0].at[0], weights.at[0], sems.at[0]).wait()
        pltpu.make_async_copy(item_pieces[0].at[0], factors.at[0], sems.at[1]).wait()
        return carry

    lax.fori_loop(0, plan[6, 1], arrive, 0)

    def pair_images(with_rhs):
        image[...] = jnp.zeros_like(image)
        if with_rhs:
            residual[...] = jnp.zeros_like(residual)

        def one_round(step, carry):
            shares = []
            for number in range(TOGETHER):
                chunk = step * TOGETHER + number
                rows = pl.ds(pl.multiple_of(plan[5, chunk] * tile, tile), tile)
                items = factors[pl.ds(chunk * SPAN, SPAN)].reshape(SPAN * tile, rank)
                scaled = jnp.concatenate(
                    [weights[chunk * SPAN + part].astype(jnp.float32) for part in range(SPAN)],
                    axis=1,
                )
                scores = lax.dot_general(
                    low[rows, :], items, (((1,), (1,)), ((), ())),
                    preferred_element_type=jnp.float32,
                )
                back = jnp.dot(
                    (scaled * scores).astype(jnp.bfloat16), items,
                    preferred_element_type=jnp.float32,
                )
                pulled = None
                if with_rhs:
                    confidence = jnp.where(scaled > 0, 1.0 + scaled, 0.0).astype(jnp.bfloat16)
                    pulled = jnp.dot(confidence, items, preferred_element_type=jnp.float32)
                shares.append((rows, back, pulled))
            for rows, back, pulled in shares:
                image[rows, :] += back
                if with_rhs:
                    residual[rows, :] += pulled
            return carry

        lax.fori_loop(0, rounds, one_round, 0)

    def gram_term(vectors):
        return jnp.dot(
            vectors, gram_ref[...], precision=lax.Precision.HIGHEST,
            preferred_element_type=jnp.float32,
        ) + REG * vectors

    prior = prior_ref[...]
    low[...] = prior.astype(jnp.bfloat16)
    pair_images(True)
    first = residual[...] - (gram_term(prior) + image[...])
    residual[...] = first
    direction[...] = first
    out_ref[...] = prior
    norm_now = row_sum(first, first)
    for step in range(ITERS):
        heading = direction[...]
        low[...] = heading.astype(jnp.bfloat16)
        pair_images(False)
        shown = gram_term(heading) + image[...]
        alpha = norm_now / (row_sum(heading, shown) + EPS)
        out_ref[...] += alpha * heading
        if step < ITERS - 1:
            left = residual[...] - alpha * shown
            residual[...] = left
            fresh = row_sum(left, left)
            direction[...] = left + (fresh / (norm_now + EPS)) * heading
            norm_now = fresh


def run_sweep(plan, user_prior, gram, count_pieces, item_pieces):
    own_rows, rank = user_prior.shape
    tile = count_pieces[0].shape[1]
    pieces = [*count_pieces, *item_pieces]
    vmem = pl.BlockSpec(memory_space=pltpu.VMEM)
    return pl.pallas_call(
        functools.partial(sweep_kernel, len(count_pieces)),
        out_shape=jax.ShapeDtypeStruct((own_rows, rank), jnp.float32),
        in_specs=[pl.BlockSpec(memory_space=pltpu.SMEM), vmem, vmem]
        + [pl.BlockSpec(memory_space=pltpu.HBM)] * len(pieces),
        out_specs=vmem,
        scratch_shapes=[
            pltpu.VMEM((LOADS, tile, tile), jnp.bfloat16),
            pltpu.VMEM((LOADS, tile, rank), jnp.bfloat16),
            pltpu.VMEM((own_rows, rank), jnp.bfloat16),
            pltpu.VMEM((own_rows, rank), jnp.float32),
            pltpu.VMEM((own_rows, rank), jnp.float32),
            pltpu.VMEM((own_rows, rank), jnp.float32),
            pltpu.SemaphoreType.DMA((2,)),
        ],
        compiler_params=pltpu.CompilerParams(vmem_limit_bytes=32 * 2**20),
        name="sweep",
    )(plan, user_prior, gram, *pieces)


def pack_kernel(n_sources, jobs, table, *refs):
    sources, refs = refs[:n_sources], refs[n_sources:]
    outs, rooms, arrived, written = refs[:len(jobs)], refs[len(jobs):-2], refs[-2], refs[-1]
    for number, (lo, hi, row, start, length) in enumerate(jobs):

        def place(spot, carry, number=number, lo=lo, hi=hi, row=row, start=start):
            start_copy(
                sources[lo:hi], table[row, start + spot], rooms[number].at[spot], arrived.at[number]
            )
            return carry

        lax.fori_loop(0, length, place, 0, unroll=2)
    write = [
        pltpu.make_async_copy(room, out, written.at[number])
        for number, (room, out) in enumerate(zip(rooms, outs))
    ]
    for number, room in enumerate(rooms):
        pltpu.make_async_copy(room, room, arrived.at[number]).wait()
        write[number].start()
    for copy in write:
        copy.wait()


def pack_tiles(name, table, sources, jobs):
    in_hbm = pl.BlockSpec(memory_space=pltpu.HBM)
    kinds = [((job[4], *sources[job[0]].shape[1:]), sources[job[0]].dtype) for job in jobs]
    return pl.pallas_call(
        functools.partial(pack_kernel, len(sources), jobs),
        out_shape=[jax.ShapeDtypeStruct(*kind) for kind in kinds],
        in_specs=[pl.BlockSpec(memory_space=pltpu.SMEM)] + [in_hbm] * len(sources),
        out_specs=[in_hbm] * len(jobs),
        scratch_shapes=[pltpu.VMEM(*kind) for kind in kinds]
        + [pltpu.SemaphoreType.DMA((len(jobs),))] * 2,
        compiler_params=pltpu.CompilerParams(vmem_limit_bytes=32 * 2**20),
        name=name,
    )(table, *sources)


def sum_with(value, axis, bit):
    size = lax.axis_size(axis)
    return value + lax.ppermute(value, axis, [(i, i ^ bit) for i in range(size)])


def iota(rows, columns, axis):
    return lax.broadcasted_iota(jnp.int32, (rows, columns), axis)


def dot_nt(left, right):
    return lax.dot_general(
        left.astype(jnp.bfloat16), right.astype(jnp.bfloat16), (((1,), (1,)), ((), ())),
        preferred_element_type=jnp.float32,
    )


def choose(key, hit, cells, *values):
    match = hit & (key == iota(cells, key.shape[1], 0))
    row = iota(8, key.shape[1], 0)
    digits = jnp.zeros((8, key.shape[1]), jnp.int32)
    for number, value in enumerate(values):
        digits = jnp.where(row == 2 * number, value & 31, digits)
        digits = jnp.where(row == 2 * number + 1, lax.shift_right_logical(value, 5), digits)
    found = dot_nt(digits.astype(jnp.float32), match.astype(jnp.float32)).astype(jnp.int32)
    return [
        found[2 * number:2 * number + 1] + 32 * found[2 * number + 1:2 * number + 2]
        for number in range(len(values))
    ]


def route_kernel(n_grp, pairs, own_tiles, tiles_held, spot, every_ref, out_ref):
    n_blk, n_entries = every_ref.shape
    width = out_ref.shape[1]
    n_chips = n_grp // 2
    user_blocks = n_grp * own_tiles
    all_chips = n_blk * n_chips
    pad = lambda n: -(-n // 8) * 8
    my_blk, my_grp = spot[0], spot[1]
    my_chip = lax.shift_right_logical(my_grp, 1)
    my_core = my_grp & 1
    index = iota(1, n_entries, 1)
    source = lax.shift_right_logical(index, bits_for(pairs))
    from_chip = lax.shift_right_logical(source, 1)
    one_hot = lambda key, n: key == iota(pad(n), n_entries, 0)

    def fields(packed):
        user = packed & (user_blocks - 1)
        packed = lax.shift_right_logical(packed, bits_for(user_blocks))
        live = (packed & 1) == 1
        item = lax.shift_right_logical(packed, 1)
        held = item & (2 * tiles_held - 1)
        chip = lax.shift_right_logical(item, bits_for(2 * tiles_held))
        return user, live, chip, held

    ids = iota(1, 2 * tiles_held, 1)
    fewer = iota(2 * tiles_held, 2 * tiles_held, 0) > iota(2 * tiles_held, 2 * tiles_held, 1)

    def needs(live, chip, held):
        on_chip = one_hot(chip, all_chips) & live
        on_tile = one_hot(held, 2 * tiles_held)
        needed = dot_nt(on_chip.astype(jnp.float32), on_tile.astype(jnp.float32)) > 0
        return on_chip, on_tile, needed, dot_nt(needed.astype(jnp.float32), fewer.astype(jnp.float32))

    excess = jnp.zeros((1, 1), jnp.float32)
    worst = lambda loads, room: jnp.max(loads, axis=(0, 1), keepdims=True) - room
    asked = jnp.zeros((1, width), jnp.int32)
    here = my_blk * n_chips + my_chip
    chip_row = iota(pad(all_chips), 2 * tiles_held, 0)
    for blk in range(n_blk):
        user, live, chip, held = fields(every_ref[blk:blk + 1, :])
        _, _, needed, ahead = needs(live, chip, held)
        away = lax.shift_right_logical(chip_row, bits_for(n_chips)) != blk
        asks = jnp.sum((needed & away).astype(jnp.float32), axis=1, keepdims=True)
        excess = jnp.maximum(excess, worst(asks, 2 * FAR_CAP))
        to_chip = lax.shift_right_logical(user, bits_for(own_tiles) + 1)
        to = one_hot(to_chip, n_chips).astype(jnp.float32)
        column = chip & (n_chips - 1)
        far = (blk + n_blk - lax.shift_right_logical(chip, bits_for(n_chips))) & (n_blk - 1)
        far = far == n_blk // 2
        for key, inside, cap in (
            (from_chip, live, COUNT_CAP),
            (column, live & ~far, ITEM_CAPS[0]),
            (column, live & far, ITEM_CAPS[1]),
        ):
            loads = dot_nt((one_hot(key, n_chips) & inside).astype(jnp.float32), to)
            excess = jnp.maximum(excess, worst(loads, 2 * cap))
        loads = jnp.sum(
            (one_hot(user, user_blocks) & live).astype(jnp.int32), axis=1, keepdims=True
        )
        chunks = lax.shift_right_logical(loads + SPAN - 1, bits_for(SPAN)).astype(jnp.float32)
        owners = iota(pad(n_grp), pad(user_blocks), 1)
        owners = lax.shift_right_logical(owners, bits_for(own_tiles)) == iota(*owners.shape, 0)
        loads = jnp.dot(
            owners.astype(jnp.float32), jnp.broadcast_to(chunks, (chunks.shape[0], 128)),
            precision=lax.Precision.HIGHEST, preferred_element_type=jnp.float32,
        )
        excess = jnp.maximum(excess, worst(loads, LOADS // SPAN))

        mine = chip_row == here
        present = jnp.sum((needed & mine).astype(jnp.int32), axis=0, keepdims=True)
        place = jnp.sum(jnp.where(mine, ahead, 0.0), axis=0, keepdims=True).astype(jnp.int32)
        shift = (blk + n_blk - my_blk) & (n_blk - 1)
        spot_at = lax.shift_right_logical(place, 1)
        hit = (present > 0) & ((place & 1) == my_core) & (spot_at < FAR_CAP) & (shift > 0)
        value = at_source(
            lax.shift_right_logical(ids, bits_for(tiles_held)) ^ my_core, ids & (tiles_held - 1), 2
        )
        (found,) = choose((shift - 1) * FAR_CAP + spot_at, hit, width, value)
        asked = asked + found

    user, live, chip, held = fields(every_ref[pl.ds(my_blk, 1), :])
    on_chip, on_tile, _, ahead = needs(live, chip, held)
    places = jnp.dot(
        ahead.astype(jnp.bfloat16), on_tile.astype(jnp.float32).astype(jnp.bfloat16),
        preferred_element_type=jnp.float32,
    )
    far_place = jnp.sum(jnp.where(on_chip, places, 0.0), axis=0, keepdims=True).astype(jnp.int32)
    far_place = jnp.minimum(far_place, 2 * FAR_CAP - 1)
    owner = lax.shift_right_logical(user, bits_for(own_tiles))
    local_user = user & (own_tiles - 1)
    to_chip = lax.shift_right_logical(owner, 1)
    column = chip & (n_chips - 1)
    to_me = live & (owner == my_grp)
    shift = (my_blk + n_blk - lax.shift_right_logical(chip, bits_for(n_chips))) & (n_blk - 1)
    parts = (live & (shift != n_blk // 2), live & (shift == n_blk // 2))
    in_tile = one_hot(local_user, own_tiles) & to_me
    groups = [
        one_hot(to_chip, n_chips) & (live & (from_chip == my_chip)),
        one_hot(from_chip, n_chips) & (live & (to_chip == my_chip)),
        in_tile,
    ]
    for part in parts:
        groups.append(one_hot(to_chip, n_chips) & (part & (column == my_chip)))
        groups.append(one_hot(column, n_chips) & (part & (to_chip == my_chip)))
    before = (iota(n_entries, n_entries, 0) < iota(n_entries, n_entries, 1)).astype(jnp.float32)
    before = before.astype(jnp.bfloat16)
    ranks = []
    for marks in groups:
        earlier = jnp.dot(
            marks.astype(jnp.float32).astype(jnp.bfloat16), before,
            preferred_element_type=jnp.float32,
        )
        earlier = jnp.sum(jnp.where(marks, earlier, 0.0), axis=0, keepdims=True)
        ranks.append(earlier.astype(jnp.int32))
    counts_out, counts_back, user_rank = ranks[:3]

    half = lambda rank: lax.shift_right_logical(rank, 1)
    sent = lambda rank, cap: ((rank & 1) == my_core) & (half(rank) < cap)
    (out_ref[0:1, :],) = choose(
        to_chip * COUNT_CAP + half(counts_out), live & (from_chip == my_chip) & sent(counts_out, COUNT_CAP),
        width, at_source((source & 1) ^ my_core, index & (pairs - 1), 2),
    )
    out_ref[1:2, :] = asked
    near = shift == 0
    lane = jnp.where(near, lax.shift_right_logical(held, bits_for(tiles_held)), far_place & 1)
    row = jnp.where(near, held & (tiles_held - 1), half(far_place))
    item_at = jnp.zeros((1, n_entries), jnp.int32)
    for number, (part, cap) in enumerate(zip(parts, ITEM_CAPS)):
        rank_out, rank_back = ranks[3 + 2 * number:5 + 2 * number]
        at = at_source(lane ^ my_core, row, 2) if number else at_source(
            (lane ^ my_core) * n_blk + shift, row, 2 * n_blk
        )
        out_row = 7 if number else 2
        (out_ref[out_row:out_row + 1, :],) = choose(
            (to_chip ^ my_chip) * cap + half(rank_out),
            part & (column == my_chip) & sent(rank_out, cap), width, at,
        )
        item_at = jnp.where(
            part,
            at_source(
                number * 2 * n_chips + (column ^ my_chip) * 2 + ((rank_back & 1) ^ my_core),
                jnp.minimum(half(rank_back), cap - 1), 4 * n_chips,
            ),
            item_at,
        )

    loads = jnp.sum(in_tile.astype(jnp.int32), axis=1, keepdims=True)
    chunks = lax.shift_right_logical(loads + SPAN - 1, bits_for(SPAN)).astype(jnp.float32)
    rows = chunks.shape[0]
    ends = jnp.dot(
        (iota(rows, rows, 0) >= iota(rows, rows, 1)).astype(jnp.float32),
        jnp.broadcast_to(chunks, (rows, 128)),
        precision=lax.Precision.HIGHEST, preferred_element_type=jnp.float32,
    )
    firsts = ends[:, :1] - chunks
    room_at = jnp.sum(jnp.where(in_tile, firsts * SPAN, 0.0), axis=0, keepdims=True)
    room_at = room_at.astype(jnp.int32) + user_rank
    hit = to_me & (room_at < LOADS)
    counts_row = jnp.minimum(half(counts_back), COUNT_CAP - 1)
    count_at = at_source((counts_back & 1) ^ my_core, from_chip * COUNT_CAP + counts_row, 2)
    out_ref[3:4, :], out_ref[4:5, :] = choose(room_at, hit, width, count_at + 1, item_at)
    passed = (iota(rows, width, 1).astype(jnp.float32) >= ends[:, :1]) & (
        iota(rows, width, 0) < own_tiles - 1
    )
    out_ref[5:6, :] = jnp.sum(passed.astype(jnp.int32), axis=0, keepdims=True)
    total = ends[own_tiles - 1:own_tiles, :1].astype(jnp.int32)
    rounds = lax.shift_right_logical(total + TOGETHER - 1, bits_for(TOGETHER))
    rounds = jnp.minimum(rounds, LOADS // (SPAN * TOGETHER))
    copies = jnp.sum(hit.astype(jnp.int32), axis=1, keepdims=True)
    at = iota(1, width, 1)
    fits = (excess <= 0.0).astype(jnp.int32)
    head = jnp.where(at == 0, rounds, jnp.where(at == 1, copies, jnp.where(at == 2, fits, 0)))
    out_ref[6:7, :] = head


def route(every, my_blk, my_grp, n_grp, own_tiles, tiles_held):
    n_blk, n_entries = every.shape
    n_chips = n_grp // 2
    width = max(n_chips * COUNT_CAP, (n_blk - 1) * FAR_CAP, n_chips * max(ITEM_CAPS), LOADS)
    width = -(-width // 128) * 128
    vmem = pl.BlockSpec(memory_space=pltpu.VMEM)
    return pl.pallas_call(
        functools.partial(route_kernel, n_grp, n_entries // n_grp, own_tiles, tiles_held),
        out_shape=jax.ShapeDtypeStruct((8, width), jnp.int32),
        in_specs=[pl.BlockSpec(memory_space=pltpu.SMEM), vmem],
        out_specs=vmem,
        compiler_params=pltpu.CompilerParams(vmem_limit_bytes=32 * 2**20),
        name="route",
    )(jnp.stack([my_blk, my_grp]).astype(jnp.int32), every)


def scan_kernel(counts_ref, scaled_ref, most_ref):
    counts = counts_ref[...]
    scaled_ref[...] = (ALPHA * counts.astype(jnp.float32)).astype(jnp.bfloat16)
    most_ref[...] = jnp.max(counts, axis=1)


def scan_counts(counts):
    pairs, tile, columns = counts.shape
    block = 16
    return pl.pallas_call(
        scan_kernel,
        grid=(pairs // block,),
        out_shape=[
            jax.ShapeDtypeStruct(counts.shape, jnp.bfloat16),
            jax.ShapeDtypeStruct((pairs, columns), jnp.int32),
        ],
        in_specs=[pl.BlockSpec((block, tile, columns), lambda i: (i, 0, 0))],
        out_specs=[
            pl.BlockSpec((block, tile, columns), lambda i: (i, 0, 0)),
            pl.BlockSpec((block, columns), lambda i: (i, 0)),
        ],
        compiler_params=pltpu.CompilerParams(vmem_limit_bytes=16 * 2**20),
        name="scan_counts",
    )(counts)


def body(user_prior, item_factors, user_tiles, item_tiles, counts):
    pairs = counts.shape[0]
    tile = counts.shape[1]
    rank = item_factors.shape[1]
    n_blk = lax.axis_size("blk")
    n_grp = lax.axis_size("grp")
    n_all = n_blk * n_grp
    n_chips = n_grp // 2
    own_rows = user_prior.shape[0]
    own_tiles = own_rows // tile
    user_blocks = own_tiles * n_grp
    tiles_held = item_factors.shape[0] // tile
    my_blk = lax.axis_index("blk")
    my_grp = lax.axis_index("grp")
    my_chip = my_grp // 2
    my_core = my_grp % 2
    lanes = [[chip * 2 + core for chip in range(n_chips)] for core in range(2)]

    def swap(value):
        return lax.ppermute(value, "grp", [(i, i ^ 1) for i in range(n_grp)])

    def to_chips(value):
        return lax.all_to_all(
            value, "grp", split_axis=0, concat_axis=0, tiled=True, axis_index_groups=lanes
        )

    gram_local = lax.dot_general(
        item_factors, item_factors, (((0,), (0,)), ((), ())), preferred_element_type=jnp.float32
    )
    grp_bits, blk_bits = [[1 << n for n in range(bits_for(size))] for size in (n_grp, n_blk)]
    held = item_factors.reshape(tiles_held, tile, rank)
    held_mate = swap(held)
    scaled, column_most = scan_counts(counts)
    live = jnp.any(column_most > 0, axis=1)
    scaled_mate = swap(scaled)
    packed = (item_tiles * 2 + live.astype(jnp.int32)) * user_blocks + user_tiles
    every = lax.all_to_all(
        jnp.broadcast_to(packed, (n_all, pairs)), ("blk", "grp"),
        split_axis=0, concat_axis=0, tiled=True,
    )
    table = route(every.reshape(n_blk, n_grp * pairs), my_blk, my_grp, n_grp, own_tiles, tiles_held)
    gram = gram_local
    for bit in grp_bits[:-1]:
        gram = sum_with(gram, "grp", bit)
    table, gram = lax.optimization_barrier((table, gram))

    jobs = [(0, 2, 1, shift * FAR_CAP, FAR_CAP) for shift in range(n_blk - 1)]
    jobs.append((2, 4, 0, 0, n_chips * COUNT_CAP))
    *far, counts_out = pack_tiles("pack_first", table, [held, held_mate, scaled, scaled_mate], jobs)
    far = [
        lax.ppermute(piece, "blk", [(i, (i + 1 + shift) % n_blk) for i in range(n_blk)])
        for shift, piece in enumerate(far)
    ]
    gram = sum_with(gram, "grp", grp_bits[-1])
    far[0], gram = lax.optimization_barrier((far[0], gram))
    far_mate = [swap(piece) for piece in far]
    counts_own = to_chips(counts_out)

    last = n_blk // 2 - 1
    jobs = [(0, 2 * n_blk, 2, off * ITEM_CAPS[0], ITEM_CAPS[0]) for off in range(n_chips)]
    sources = [held, *far, held_mate, *far_mate]
    sources[last + 1], sources[n_blk + last + 1] = held, held_mate
    first = pack_tiles("pack_near", table, sources, jobs)
    counts_own, gram, *first = lax.optimization_barrier((counts_own, gram, *first))
    counts_mate = swap(counts_own)
    jobs = [(0, 2, 7, off * ITEM_CAPS[1], ITEM_CAPS[1]) for off in range(n_chips)]
    second = pack_tiles("pack_far", table, [far[last], far_mate[last]], jobs)
    for bit in blk_bits:
        gram = sum_with(gram, "blk", bit)
    item_pieces = []
    for part in (first, second):
        for off, piece in enumerate(part):
            if off:
                piece = lax.ppermute(piece, "grp", [(i, i ^ (2 * off)) for i in range(n_grp)])
            if part is second and off == 1:
                piece, gram = lax.optimization_barrier((piece, gram))
            item_pieces += [piece, swap(piece)]
    by_owner = run_sweep(table, user_prior, gram, [counts_own, counts_mate], item_pieces)

    fits = table[6, 2] > 0
    return lax.cond(
        fits, lambda done, *given: done, lambda done, *given: sweep_in_place(*given),
        by_owner, user_prior, item_factors, user_tiles, item_tiles, counts, live, gram_local,
    )


def solution(mesh):
    in_specs = (
        P(("blk", "grp"), None),
        P(("blk", "grp"), None),
        P(("blk", "grp")),
        P(("blk", "grp")),
        P(("blk", "grp"), None, None),
    )
    out_specs = P(("blk", "grp"), None)
    return jax.shard_map(body, mesh=mesh, in_specs=in_specs, out_specs=out_specs, check_vma=False)
```

```python
import functools

import jax
import jax.numpy as jnp
from jax import lax
from jax.experimental import pallas as pl
from jax.experimental.pallas import tpu as pltpu
from jax.sharding import PartitionSpec as P

ITERS = 3

ALPHA = 40.0
REG = 32.0
EPS = 1e-06

FAR_CAP = 14
COUNT_CAP = 24
ITEM_CAP = 20
LOADS = 128
SPAN = 2
VMEM_GRANT = 60 * 2**20
TOGETHER = 8


def fetch_tiles(item_factors, item_tiles, pairs, tile, rank):
    n_all = lax.axis_size(("blk", "grp"))
    tiles_held = item_factors.shape[0] // tile
    slots_each = max(2, pairs // n_all)
    owner = item_tiles // tiles_held
    local_slot = item_tiles % tiles_held
    position = jnp.arange(pairs, dtype=jnp.int32)
    earlier = (owner[None, :] == owner[:, None]) & (position[None, :] < position[:, None])
    order = jnp.sum(earlier.astype(jnp.int32), axis=1)
    requests = jnp.full((n_all, slots_each), -1, jnp.int32).at[owner, order].set(local_slot)
    wanted = lax.all_to_all(requests, ("blk", "grp"), split_axis=0, concat_axis=0, tiled=True)
    held = item_factors.reshape(tiles_held, tile, rank)
    picked = jnp.take(held, jnp.maximum(wanted, 0), axis=0)
    picked = jnp.where((wanted >= 0)[:, :, None, None], picked, jnp.zeros((), picked.dtype))
    arrived = lax.all_to_all(picked, ("blk", "grp"), split_axis=0, concat_axis=0, tiled=True)
    return arrived[owner, order]


def row_sum(left, right):
    return jnp.sum(left * right, axis=1, keepdims=True)


def sweep_in_place(user_prior, item_factors, user_tiles, item_tiles, counts, live, gram_local):
    pairs = counts.shape[0]
    tile = counts.shape[1]
    rank = item_factors.shape[1]
    n_grp = lax.axis_size("grp")
    own_rows = user_prior.shape[0]
    block_rows = own_rows * n_grp
    user_blocks = block_rows // tile
    span = min(32, pairs)
    gram = lax.psum(gram_local, ("blk", "grp"))
    pair_tiles = fetch_tiles(item_factors, item_tiles, pairs, tile, rank)
    rounds = (jnp.sum(live.astype(jnp.int32)) + span - 1) // span
    tile_ids = jnp.arange(user_blocks, dtype=jnp.int32)

    def accumulate(low_tiles, with_rhs):

        def one_round(index, totals):
            start = index * span
            users = lax.dynamic_slice_in_dim(user_tiles, start, span)
            factors = lax.dynamic_slice_in_dim(pair_tiles, start, span)
            counted = lax.dynamic_slice_in_dim(counts, start, span).astype(jnp.float32)
            selector = (tile_ids[:, None] == users[None, :]).astype(jnp.float32)
            users_low = jnp.take(low_tiles, users, axis=0)
            scores = jnp.einsum(
                "bur,bir->bui", users_low, factors, preferred_element_type=jnp.float32
            )
            scaled = (ALPHA * counted * scores).astype(jnp.bfloat16)
            back = jnp.einsum("bui,bir->bur", scaled, factors, preferred_element_type=jnp.float32)
            result = [
                totals[0]
                + jnp.einsum("tb,bur->tur", selector, back, precision=lax.Precision.HIGHEST)
            ]
            if with_rhs:
                confidence = jnp.where(counted > 0, 1.0 + ALPHA * counted, 0.0).astype(jnp.bfloat16)
                pulled = jnp.einsum(
                    "bui,bir->bur", confidence, factors, preferred_element_type=jnp.float32
                )
                result.append(
                    totals[1]
                    + jnp.einsum("tb,bur->tur", selector, pulled, precision=lax.Precision.HIGHEST)
                )
            return tuple(result)

        zeros = jnp.zeros((user_blocks, tile, rank), jnp.float32)
        start_state = (zeros, zeros) if with_rhs else (zeros,)
        totals = lax.fori_loop(0, rounds, one_round, start_state)
        return tuple((total.reshape(block_rows, rank) for total in totals))

    def gram_term(vectors):
        return jnp.dot(vectors, gram, precision=lax.Precision.HIGHEST) + REG * vectors

    low = lax.all_gather(user_prior.astype(jnp.bfloat16), "grp", axis=0, tiled=True)
    pair_part, rhs_part = accumulate(low.reshape(user_blocks, tile, rank), True)
    pair_share, rhs_share = (
        lax.psum_scatter(pair_part, "grp", scatter_dimension=0, tiled=True),
        lax.psum_scatter(rhs_part, "grp", scatter_dimension=0, tiled=True),
    )
    solution = user_prior
    residual = rhs_share - (gram_term(solution) + pair_share)
    direction = residual
    norm_now = row_sum(residual, residual)
    for step in range(ITERS):
        low = lax.all_gather(direction.astype(jnp.bfloat16), "grp", axis=0, tiled=True)
        (pair_part,) = accumulate(low.reshape(user_blocks, tile, rank), False)
        image = gram_term(direction) + lax.psum_scatter(
            pair_part, "grp", scatter_dimension=0, tiled=True
        )
        alpha = norm_now / (row_sum(direction, image) + EPS)
        solution = solution + alpha * direction
        residual = residual - alpha * image
        fresh = row_sum(residual, residual)
        direction = residual + fresh / (norm_now + EPS) * direction
        norm_now = fresh
    return solution


def bits_for(n):
    return (n - 1).bit_length()


def at_source(number, row, n_sources):
    return (row << bits_for(n_sources)) + number


def start_copy(sources, at, target, sem):
    bits = bits_for(len(sources))
    row = lax.shift_right_logical(at, bits)
    which = at & ((1 << bits) - 1)

    def among(lo, hi):
        if hi - lo == 1:
            pltpu.make_async_copy(sources[lo].at[row], target, sem).start()
            return
        mid = (lo + hi) // 2
        pl.when(which < mid)(lambda: among(lo, mid))
        pl.when(which >= mid)(lambda: among(mid, hi))

    among(0, len(sources))


def sweep_kernel(n_counts, plan, prior_ref, gram_ref, *refs):
    weights, factors, low, image, residual, direction, sems = refs[-7:]
    count_pieces, item_pieces, out_ref = refs[:n_counts], refs[n_counts:-8], refs[-8]
    tile, rank = factors.shape[1:]
    rounds = plan[6, 0]

    def bring(place, carry):
        count_at = plan[3, place]
        item_at = plan[4, place]

        @pl.when(count_at > 0)
        def _():
            start_copy(count_pieces, count_at - 1, weights.at[place], sems.at[0])
            start_copy(item_pieces, item_at, factors.at[place], sems.at[1])

        @pl.when(count_at == 0)
        def _():
            weights[place] = jnp.zeros((tile, tile), weights.dtype)
            factors[place] = jnp.zeros((tile, rank), factors.dtype)

        return carry

    lax.fori_loop(0, rounds * (TOGETHER * SPAN), bring, 0)

    def arrive(entry, carry):
        pltpu.make_async_copy(count_pieces[0].at[0], weights.at[0], sems.at[0]).wait()
        pltpu.make_async_copy(item_pieces[0].at[0], factors.at[0], sems.at[1]).wait()
        return carry

    lax.fori_loop(0, plan[6, 1], arrive, 0)

    def pair_images(with_rhs):
        image[...] = jnp.zeros_like(image)
        if with_rhs:
            residual[...] = jnp.zeros_like(residual)

        def one_round(step, carry):
            shares = []
            for number in range(TOGETHER):
                chunk = step * TOGETHER + number
                rows = pl.ds(pl.multiple_of(plan[5, chunk] * tile, tile), tile)
                items = factors[pl.ds(chunk * SPAN, SPAN)].reshape(SPAN * tile, rank)
                scaled = jnp.concatenate(
                    [weights[chunk * SPAN + part].astype(jnp.float32) for part in range(SPAN)],
                    axis=1,
                )
                scores = lax.dot_general(
                    low[rows, :], items, (((1,), (1,)), ((), ())),
                    preferred_element_type=jnp.float32,
                )
                back = jnp.dot(
                    (scaled * scores).astype(jnp.bfloat16), items,
                    preferred_element_type=jnp.float32,
                )
                pulled = None
                if with_rhs:
                    confidence = jnp.where(scaled > 0, 1.0 + scaled, 0.0).astype(jnp.bfloat16)
                    pulled = jnp.dot(confidence, items, preferred_element_type=jnp.float32)
                shares.append((rows, back, pulled))
            for rows, back, pulled in shares:
                image[rows, :] += back
                if with_rhs:
                    residual[rows, :] += pulled
            return carry

        lax.fori_loop(0, rounds, one_round, 0)

    def gram_term(vectors):
        return jnp.dot(
            vectors, gram_ref[...], precision=lax.Precision.HIGHEST,
            preferred_element_type=jnp.float32,
        ) + REG * vectors

    prior = prior_ref[...]
    low[...] = prior.astype(jnp.bfloat16)
    pair_images(True)
    first = residual[...] - (gram_term(prior) + image[...])
    residual[...] = first
    direction[...] = first
    out_ref[...] = prior
    norm_now = row_sum(first, first)
    for step in range(ITERS):
        heading = direction[...]
        low[...] = heading.astype(jnp.bfloat16)
        pair_images(False)
        shown = gram_term(heading) + image[...]
        alpha = norm_now / (row_sum(heading, shown) + EPS)
        out_ref[...] += alpha * heading
        if step < ITERS - 1:
            left = residual[...] - alpha * shown
            residual[...] = left
            fresh = row_sum(left, left)
            direction[...] = left + (fresh / (norm_now + EPS)) * heading
            norm_now = fresh


def run_sweep(plan, user_prior, gram, count_pieces, item_pieces):
    own_rows, rank = user_prior.shape
    tile = count_pieces[0].shape[1]
    pieces = [*count_pieces, *item_pieces]
    vmem = pl.BlockSpec(memory_space=pltpu.VMEM)
    return pl.pallas_call(
        functools.partial(sweep_kernel, len(count_pieces)),
        out_shape=jax.ShapeDtypeStruct((own_rows, rank), jnp.float32),
        in_specs=[pl.BlockSpec(memory_space=pltpu.SMEM), vmem, vmem]
        + [pl.BlockSpec(memory_space=pl.ANY)] * len(pieces),
        out_specs=vmem,
        scratch_shapes=[
            pltpu.VMEM((LOADS, tile, tile), jnp.bfloat16),
            pltpu.VMEM((LOADS, tile, rank), jnp.bfloat16),
            pltpu.VMEM((own_rows, rank), jnp.bfloat16),
            pltpu.VMEM((own_rows, rank), jnp.float32),
            pltpu.VMEM((own_rows, rank), jnp.float32),
            pltpu.VMEM((own_rows, rank), jnp.float32),
            pltpu.SemaphoreType.DMA((2,)),
        ],
        compiler_params=pltpu.CompilerParams(vmem_limit_bytes=VMEM_GRANT),
        name="sweep",
    )(plan, user_prior, gram, *pieces)


def pack_kernel(n_sources, jobs, table, *refs):
    sources, refs = refs[:n_sources], refs[n_sources:]
    outs, rooms, arrived, written = refs[:len(jobs)], refs[len(jobs):-2], refs[-2], refs[-1]
    for number, (lo, hi, row, start, length) in enumerate(jobs):

        def place(spot, carry, number=number, lo=lo, hi=hi, row=row, start=start):
            start_copy(
                sources[lo:hi], table[row, start + spot], rooms[number].at[spot], arrived.at[number]
            )
            return carry

        lax.fori_loop(0, length, place, 0, unroll=2)
    write = [
        pltpu.make_async_copy(room, out, written.at[number])
        for number, (room, out) in enumerate(zip(rooms, outs))
    ]
    for number, room in enumerate(rooms):
        pltpu.make_async_copy(room, room, arrived.at[number]).wait()
        write[number].start()
    for copy in write:
        copy.wait()


def pack_tiles(name, table, sources, jobs):
    anywhere = pl.BlockSpec(memory_space=pl.ANY)
    kinds = [((job[4], *sources[job[0]].shape[1:]), sources[job[0]].dtype) for job in jobs]
    return pl.pallas_call(
        functools.partial(pack_kernel, len(sources), jobs),
        out_shape=[jax.ShapeDtypeStruct(*kind) for kind in kinds],
        in_specs=[pl.BlockSpec(memory_space=pltpu.SMEM)] + [anywhere] * len(sources),
        out_specs=[anywhere] * len(jobs),
        scratch_shapes=[pltpu.VMEM(*kind) for kind in kinds]
        + [pltpu.SemaphoreType.DMA((len(jobs),))] * 2,
        compiler_params=pltpu.CompilerParams(vmem_limit_bytes=VMEM_GRANT),
        name=name,
    )(table, *sources)


def sum_with(value, axis, bit):
    size = lax.axis_size(axis)
    return value + lax.ppermute(value, axis, [(i, i ^ bit) for i in range(size)])


def iota(rows, columns, axis):
    return lax.broadcasted_iota(jnp.int32, (rows, columns), axis)


def dot_nt(left, right):
    return lax.dot_general(
        left.astype(jnp.bfloat16), right.astype(jnp.bfloat16), (((1,), (1,)), ((), ())),
        preferred_element_type=jnp.float32,
    )


def choose(key, hit, cells, *values):
    match = hit & (key == iota(cells, key.shape[1], 0))
    row = iota(8, key.shape[1], 0)
    digits = jnp.zeros((8, key.shape[1]), jnp.int32)
    for number, value in enumerate(values):
        digits = jnp.where(row == 2 * number, value & 31, digits)
        digits = jnp.where(row == 2 * number + 1, lax.shift_right_logical(value, 5), digits)
    found = dot_nt(digits.astype(jnp.float32), match.astype(jnp.float32)).astype(jnp.int32)
    return [
        found[2 * number:2 * number + 1] + 32 * found[2 * number + 1:2 * number + 2]
        for number in range(len(values))
    ]


def route_kernel(n_grp, pairs, own_tiles, tiles_held, spot, every_ref, out_ref):
    n_blk, n_entries = every_ref.shape
    width = out_ref.shape[1]
    n_chips = n_grp // 2
    user_blocks = n_grp * own_tiles
    all_chips = n_blk * n_chips
    pad = lambda n: -(-n // 8) * 8
    my_blk, my_grp = spot[0], spot[1]
    my_chip = lax.shift_right_logical(my_grp, 1)
    my_core = my_grp & 1
    index = iota(1, n_entries, 1)
    source = lax.shift_right_logical(index, bits_for(pairs))
    from_chip = lax.shift_right_logical(source, 1)
    one_hot = lambda key, n: key == iota(pad(n), n_entries, 0)

    def fields(packed):
        user = packed & (user_blocks - 1)
        packed = lax.shift_right_logical(packed, bits_for(user_blocks))
        live = (packed & 1) == 1
        item = lax.shift_right_logical(packed, 1)
        held = item & (2 * tiles_held - 1)
        chip = lax.shift_right_logical(item, bits_for(2 * tiles_held))
        return user, live, chip, held

    ids = iota(1, 2 * tiles_held, 1)
    fewer = iota(2 * tiles_held, 2 * tiles_held, 0) > iota(2 * tiles_held, 2 * tiles_held, 1)

    def needs(live, chip, held):
        on_chip = one_hot(chip, all_chips) & live
        on_tile = one_hot(held, 2 * tiles_held)
        needed = dot_nt(on_chip.astype(jnp.float32), on_tile.astype(jnp.float32)) > 0
        return on_chip, on_tile, needed, dot_nt(needed.astype(jnp.float32), fewer.astype(jnp.float32))

    excess = jnp.zeros((1, 1), jnp.float32)
    worst = lambda loads, room: jnp.max(loads, axis=(0, 1), keepdims=True) - room
    asked = jnp.zeros((1, width), jnp.int32)
    here = my_blk * n_chips + my_chip
    chip_row = iota(pad(all_chips), 2 * tiles_held, 0)
    for blk in range(n_blk):
        user, live, chip, held = fields(every_ref[blk:blk + 1, :])
        _, _, needed, ahead = needs(live, chip, held)
        away = lax.shift_right_logical(chip_row, bits_for(n_chips)) != blk
        asks = jnp.sum((needed & away).astype(jnp.float32), axis=1, keepdims=True)
        excess = jnp.maximum(excess, worst(asks, 2 * FAR_CAP))
        to_chip = lax.shift_right_logical(user, bits_for(own_tiles) + 1)
        to = one_hot(to_chip, n_chips).astype(jnp.float32)
        for key, cap in ((from_chip, COUNT_CAP), (chip & (n_chips - 1), ITEM_CAP)):
            loads = dot_nt((one_hot(key, n_chips) & live).astype(jnp.float32), to)
            excess = jnp.maximum(excess, worst(loads, 2 * cap))
        loads = jnp.sum(
            (one_hot(user, user_blocks) & live).astype(jnp.int32), axis=1, keepdims=True
        )
        chunks = lax.shift_right_logical(loads + SPAN - 1, bits_for(SPAN)).astype(jnp.float32)
        owners = iota(pad(n_grp), pad(user_blocks), 1)
        owners = lax.shift_right_logical(owners, bits_for(own_tiles)) == iota(*owners.shape, 0)
        loads = jnp.dot(
            owners.astype(jnp.float32), jnp.broadcast_to(chunks, (chunks.shape[0], 128)),
            precision=lax.Precision.HIGHEST, preferred_element_type=jnp.float32,
        )
        excess = jnp.maximum(excess, worst(loads, LOADS // SPAN))

        mine = chip_row == here
        present = jnp.sum((needed & mine).astype(jnp.int32), axis=0, keepdims=True)
        place = jnp.sum(jnp.where(mine, ahead, 0.0), axis=0, keepdims=True).astype(jnp.int32)
        shift = (blk + n_blk - my_blk) & (n_blk - 1)
        spot_at = lax.shift_right_logical(place, 1)
        hit = (present > 0) & ((place & 1) == my_core) & (spot_at < FAR_CAP) & (shift > 0)
        value = at_source(
            lax.shift_right_logical(ids, bits_for(tiles_held)) ^ my_core, ids & (tiles_held - 1), 2
        )
        (found,) = choose((shift - 1) * FAR_CAP + spot_at, hit, width, value)
        asked = asked + found

    user, live, chip, held = fields(every_ref[pl.ds(my_blk, 1), :])
    on_chip, on_tile, _, ahead = needs(live, chip, held)
    places = jnp.dot(
        ahead.astype(jnp.bfloat16), on_tile.astype(jnp.float32).astype(jnp.bfloat16),
        preferred_element_type=jnp.float32,
    )
    far_place = jnp.sum(jnp.where(on_chip, places, 0.0), axis=0, keepdims=True).astype(jnp.int32)
    far_place = jnp.minimum(far_place, 2 * FAR_CAP - 1)
    owner = lax.shift_right_logical(user, bits_for(own_tiles))
    local_user = user & (own_tiles - 1)
    to_chip = lax.shift_right_logical(owner, 1)
    column = chip & (n_chips - 1)
    to_me = live & (owner == my_grp)
    groups = [
        one_hot(to_chip, n_chips) & (live & (from_chip == my_chip)),
        one_hot(from_chip, n_chips) & (live & (to_chip == my_chip)),
        one_hot(to_chip, n_chips) & (live & (column == my_chip)),
        one_hot(column, n_chips) & (live & (to_chip == my_chip)),
        one_hot(local_user, own_tiles) & to_me,
    ]
    before = (iota(n_entries, n_entries, 0) < iota(n_entries, n_entries, 1)).astype(jnp.float32)
    before = before.astype(jnp.bfloat16)
    ranks = []
    for marks in groups:
        earlier = jnp.dot(
            marks.astype(jnp.float32).astype(jnp.bfloat16), before,
            preferred_element_type=jnp.float32,
        )
        earlier = jnp.sum(jnp.where(marks, earlier, 0.0), axis=0, keepdims=True)
        ranks.append(earlier.astype(jnp.int32))
    counts_out, counts_back, items_out, items_back, user_rank = ranks

    half = lambda rank: lax.shift_right_logical(rank, 1)
    sent = lambda rank, cap: live & ((rank & 1) == my_core) & (half(rank) < cap)
    (out_ref[0:1, :],) = choose(
        to_chip * COUNT_CAP + half(counts_out), sent(counts_out, COUNT_CAP) & (from_chip == my_chip),
        width, at_source((source & 1) ^ my_core, index & (pairs - 1), 2),
    )
    out_ref[1:2, :] = asked
    shift = (my_blk + n_blk - lax.shift_right_logical(chip, bits_for(n_chips))) & (n_blk - 1)
    near = shift == 0
    lane = jnp.where(near, lax.shift_right_logical(held, bits_for(tiles_held)), far_place & 1)
    row = jnp.where(near, held & (tiles_held - 1), half(far_place))
    (out_ref[2:3, :],) = choose(
        (to_chip ^ my_chip) * ITEM_CAP + half(items_out),
        sent(items_out, ITEM_CAP) & (column == my_chip),
        width, at_source((lane ^ my_core) * n_blk + shift, row, 2 * n_blk),
    )

    in_tile = groups[4]
    loads = jnp.sum(in_tile.astype(jnp.int32), axis=1, keepdims=True)
    chunks = lax.shift_right_logical(loads + SPAN - 1, bits_for(SPAN)).astype(jnp.float32)
    rows = chunks.shape[0]
    ends = jnp.dot(
        (iota(rows, rows, 0) >= iota(rows, rows, 1)).astype(jnp.float32),
        jnp.broadcast_to(chunks, (rows, 128)),
        precision=lax.Precision.HIGHEST, preferred_element_type=jnp.float32,
    )
    firsts = ends[:, :1] - chunks
    room_at = jnp.sum(jnp.where(in_tile, firsts * SPAN, 0.0), axis=0, keepdims=True)
    room_at = room_at.astype(jnp.int32) + user_rank
    hit = to_me & (room_at < LOADS)
    counts_row = jnp.minimum(half(counts_back), COUNT_CAP - 1)
    items_row = jnp.minimum(half(items_back), ITEM_CAP - 1)
    count_at = at_source((counts_back & 1) ^ my_core, from_chip * COUNT_CAP + counts_row, 2)
    item_at = at_source(
        (column ^ my_chip) * 2 + ((items_back & 1) ^ my_core), items_row, 2 * n_chips
    )
    out_ref[3:4, :], out_ref[4:5, :] = choose(room_at, hit, width, count_at + 1, item_at)
    passed = (iota(rows, width, 1).astype(jnp.float32) >= ends[:, :1]) & (
        iota(rows, width, 0) < own_tiles - 1
    )
    out_ref[5:6, :] = jnp.sum(passed.astype(jnp.int32), axis=0, keepdims=True)
    total = ends[own_tiles - 1:own_tiles, :1].astype(jnp.int32)
    rounds = lax.shift_right_logical(total + TOGETHER - 1, bits_for(TOGETHER))
    rounds = jnp.minimum(rounds, LOADS // (SPAN * TOGETHER))
    copies = jnp.sum(hit.astype(jnp.int32), axis=1, keepdims=True)
    at = iota(1, width, 1)
    fits = (excess <= 0.0).astype(jnp.int32)
    head = jnp.where(at == 0, rounds, jnp.where(at == 1, copies, jnp.where(at == 2, fits, 0)))
    out_ref[6:7, :] = head
    out_ref[7:8, :] = jnp.zeros((1, width), jnp.int32)


def route(every, my_blk, my_grp, n_grp, own_tiles, tiles_held):
    n_blk, n_entries = every.shape
    n_chips = n_grp // 2
    width = max(n_chips * COUNT_CAP, (n_blk - 1) * FAR_CAP, n_chips * ITEM_CAP, LOADS)
    width = -(-width // 128) * 128
    vmem = pl.BlockSpec(memory_space=pltpu.VMEM)
    return pl.pallas_call(
        functools.partial(route_kernel, n_grp, n_entries // n_grp, own_tiles, tiles_held),
        out_shape=jax.ShapeDtypeStruct((8, width), jnp.int32),
        in_specs=[pl.BlockSpec(memory_space=pltpu.SMEM), vmem],
        out_specs=vmem,
        compiler_params=pltpu.CompilerParams(vmem_limit_bytes=16 * 2**20),
        name="route",
    )(jnp.stack([my_blk, my_grp]).astype(jnp.int32), every)


def scan_kernel(counts_ref, scaled_ref, most_ref):
    counts = counts_ref[...]
    scaled_ref[...] = (ALPHA * counts.astype(jnp.float32)).astype(jnp.bfloat16)
    most_ref[...] = jnp.max(counts, axis=1)


def scan_counts(counts):
    pairs, tile, columns = counts.shape
    block = 16
    return pl.pallas_call(
        scan_kernel,
        grid=(pairs // block,),
        out_shape=[
            jax.ShapeDtypeStruct(counts.shape, jnp.bfloat16),
            jax.ShapeDtypeStruct((pairs, columns), jnp.int32),
        ],
        in_specs=[pl.BlockSpec((block, tile, columns), lambda i: (i, 0, 0))],
        out_specs=[
            pl.BlockSpec((block, tile, columns), lambda i: (i, 0, 0)),
            pl.BlockSpec((block, columns), lambda i: (i, 0)),
        ],
        compiler_params=pltpu.CompilerParams(vmem_limit_bytes=16 * 2**20),
        name="scan_counts",
    )(counts)


def body(user_prior, item_factors, user_tiles, item_tiles, counts):
    pairs = counts.shape[0]
    tile = counts.shape[1]
    rank = item_factors.shape[1]
    n_blk = lax.axis_size("blk")
    n_grp = lax.axis_size("grp")
    n_all = n_blk * n_grp
    n_chips = n_grp // 2
    own_rows = user_prior.shape[0]
    own_tiles = own_rows // tile
    user_blocks = own_tiles * n_grp
    tiles_held = item_factors.shape[0] // tile
    my_blk = lax.axis_index("blk")
    my_grp = lax.axis_index("grp")
    my_chip = my_grp // 2
    my_core = my_grp % 2
    lanes = [[chip * 2 + core for chip in range(n_chips)] for core in range(2)]

    def swap(value):
        return lax.ppermute(value, "grp", [(i, i ^ 1) for i in range(n_grp)])

    def to_chips(value):
        return lax.all_to_all(
            value, "grp", split_axis=0, concat_axis=0, tiled=True, axis_index_groups=lanes
        )

    gram_local = lax.dot_general(
        item_factors, item_factors, (((0,), (0,)), ((), ())), preferred_element_type=jnp.float32
    )
    grp_bits, blk_bits = [[1 << n for n in range(bits_for(size))] for size in (n_grp, n_blk)]
    held = item_factors.reshape(tiles_held, tile, rank)
    held_mate = swap(held)
    scaled, column_most = scan_counts(counts)
    live = jnp.any(column_most > 0, axis=1)
    scaled_mate = swap(scaled)
    packed = (item_tiles * 2 + live.astype(jnp.int32)) * user_blocks + user_tiles
    every = lax.all_to_all(
        jnp.broadcast_to(packed, (n_all, pairs)), ("blk", "grp"),
        split_axis=0, concat_axis=0, tiled=True,
    )
    table = route(every.reshape(n_blk, n_grp * pairs), my_blk, my_grp, n_grp, own_tiles, tiles_held)
    gram = gram_local
    for bit in grp_bits:
        gram = sum_with(gram, "grp", bit)
    table, gram = lax.optimization_barrier((table, gram))

    jobs = [(0, 2, 1, shift * FAR_CAP, FAR_CAP) for shift in range(n_blk - 1)]
    jobs.append((2, 4, 0, 0, n_chips * COUNT_CAP))
    *far, counts_out = pack_tiles("pack_first", table, [held, held_mate, scaled, scaled_mate], jobs)
    far = [
        lax.ppermute(piece, "blk", [(i, (i + 1 + shift) % n_blk) for i in range(n_blk)])
        for shift, piece in enumerate(far)
    ]
    far_mate = [swap(piece) for piece in far]
    counts_own = to_chips(counts_out)

    jobs = [(0, 2 * n_blk, 2, off * ITEM_CAP, ITEM_CAP) for off in range(n_chips)]
    items_out = pack_tiles("pack_items", table, [held, *far, held_mate, *far_mate], jobs)
    counts_own, gram, *items_out = lax.optimization_barrier((counts_own, gram, *items_out))
    counts_mate = swap(counts_own)
    for bit in blk_bits:
        gram = sum_with(gram, "blk", bit)
    item_pieces = []
    for off, piece in enumerate(items_out):
        if off:
            piece = lax.ppermute(piece, "grp", [(i, i ^ (2 * off)) for i in range(n_grp)])
        if off == n_chips - 1:
            piece, gram = lax.optimization_barrier((piece, gram))
        item_pieces += [piece, swap(piece)]
    by_owner = run_sweep(table, user_prior, gram, [counts_own, counts_mate], item_pieces)

    fits = table[6, 2] > 0
    return lax.cond(
        fits, lambda done, *given: done, lambda done, *given: sweep_in_place(*given),
        by_owner, user_prior, item_factors, user_tiles, item_tiles, counts, live, gram_local,
    )


def solution(mesh):
    in_specs = (
        P(("blk", "grp"), None),
        P(("blk", "grp"), None),
        P(("blk", "grp")),
        P(("blk", "grp")),
        P(("blk", "grp"), None, None),
    )
    out_specs = P(("blk", "grp"), None)
    return jax.shard_map(body, mesh=mesh, in_specs=in_specs, out_specs=out_specs, check_vma=False)
```

```python
import functools

import jax
import jax.numpy as jnp
from jax import lax
from jax.experimental import pallas as pl
from jax.experimental.pallas import tpu as pltpu
from jax.sharding import PartitionSpec as P

ITERS = 3

ALPHA = 40.0
REG = 32.0
EPS = 1e-06

FAR_CAP = 14
COUNT_CAP = 24
ITEM_CAP = 20
LOADS = 128
SPAN = 2
VMEM_GRANT = 60 * 2**20
TOGETHER = 8


def fetch_tiles(item_factors, item_tiles, pairs, tile, rank):
    n_all = lax.axis_size(("blk", "grp"))
    tiles_held = item_factors.shape[0] // tile
    slots_each = max(2, pairs // n_all)
    owner = item_tiles // tiles_held
    local_slot = item_tiles % tiles_held
    position = jnp.arange(pairs, dtype=jnp.int32)
    earlier = (owner[None, :] == owner[:, None]) & (position[None, :] < position[:, None])
    order = jnp.sum(earlier.astype(jnp.int32), axis=1)
    requests = jnp.full((n_all, slots_each), -1, jnp.int32).at[owner, order].set(local_slot)
    wanted = lax.all_to_all(requests, ("blk", "grp"), split_axis=0, concat_axis=0, tiled=True)
    held = item_factors.reshape(tiles_held, tile, rank)
    picked = jnp.take(held, jnp.maximum(wanted, 0), axis=0)
    picked = jnp.where((wanted >= 0)[:, :, None, None], picked, jnp.zeros((), picked.dtype))
    arrived = lax.all_to_all(picked, ("blk", "grp"), split_axis=0, concat_axis=0, tiled=True)
    return arrived[owner, order]


def row_sum(left, right):
    return jnp.sum(left * right, axis=1, keepdims=True)


def sweep_in_place(user_prior, item_factors, user_tiles, item_tiles, counts, live, gram_local):
    pairs = counts.shape[0]
    tile = counts.shape[1]
    rank = item_factors.shape[1]
    n_grp = lax.axis_size("grp")
    own_rows = user_prior.shape[0]
    block_rows = own_rows * n_grp
    user_blocks = block_rows // tile
    span = min(32, pairs)
    gram = lax.psum(gram_local, ("blk", "grp"))
    pair_tiles = fetch_tiles(item_factors, item_tiles, pairs, tile, rank)
    rounds = (jnp.sum(live.astype(jnp.int32)) + span - 1) // span
    tile_ids = jnp.arange(user_blocks, dtype=jnp.int32)

    def accumulate(low_tiles, with_rhs):

        def one_round(index, totals):
            start = index * span
            users = lax.dynamic_slice_in_dim(user_tiles, start, span)
            factors = lax.dynamic_slice_in_dim(pair_tiles, start, span)
            counted = lax.dynamic_slice_in_dim(counts, start, span).astype(jnp.float32)
            selector = (tile_ids[:, None] == users[None, :]).astype(jnp.float32)
            users_low = jnp.take(low_tiles, users, axis=0)
            scores = jnp.einsum(
                "bur,bir->bui", users_low, factors, preferred_element_type=jnp.float32
            )
            scaled = (ALPHA * counted * scores).astype(jnp.bfloat16)
            back = jnp.einsum("bui,bir->bur", scaled, factors, preferred_element_type=jnp.float32)
            result = [
                totals[0]
                + jnp.einsum("tb,bur->tur", selector, back, precision=lax.Precision.HIGHEST)
            ]
            if with_rhs:
                confidence = jnp.where(counted > 0, 1.0 + ALPHA * counted, 0.0).astype(jnp.bfloat16)
                pulled = jnp.einsum(
                    "bui,bir->bur", confidence, factors, preferred_element_type=jnp.float32
                )
                result.append(
                    totals[1]
                    + jnp.einsum("tb,bur->tur", selector, pulled, precision=lax.Precision.HIGHEST)
                )
            return tuple(result)

        zeros = jnp.zeros((user_blocks, tile, rank), jnp.float32)
        start_state = (zeros, zeros) if with_rhs else (zeros,)
        totals = lax.fori_loop(0, rounds, one_round, start_state)
        return tuple((total.reshape(block_rows, rank) for total in totals))

    def gram_term(vectors):
        return jnp.dot(vectors, gram, precision=lax.Precision.HIGHEST) + REG * vectors

    low = lax.all_gather(user_prior.astype(jnp.bfloat16), "grp", axis=0, tiled=True)
    pair_part, rhs_part = accumulate(low.reshape(user_blocks, tile, rank), True)
    pair_share, rhs_share = (
        lax.psum_scatter(pair_part, "grp", scatter_dimension=0, tiled=True),
        lax.psum_scatter(rhs_part, "grp", scatter_dimension=0, tiled=True),
    )
    solution = user_prior
    residual = rhs_share - (gram_term(solution) + pair_share)
    direction = residual
    norm_now = row_sum(residual, residual)
    for step in range(ITERS):
        low = lax.all_gather(direction.astype(jnp.bfloat16), "grp", axis=0, tiled=True)
        (pair_part,) = accumulate(low.reshape(user_blocks, tile, rank), False)
        image = gram_term(direction) + lax.psum_scatter(
            pair_part, "grp", scatter_dimension=0, tiled=True
        )
        alpha = norm_now / (row_sum(direction, image) + EPS)
        solution = solution + alpha * direction
        residual = residual - alpha * image
        fresh = row_sum(residual, residual)
        direction = residual + fresh / (norm_now + EPS) * direction
        norm_now = fresh
    return solution


def bits_for(n):
    return (n - 1).bit_length()


def at_source(number, row, n_sources):
    return (row << bits_for(n_sources)) + number


def move_tile(sources, at, room, place):
    bits = bits_for(len(sources))
    row = lax.shift_right_logical(at, bits)
    which = at & ((1 << bits) - 1)

    def among(lo, hi):
        if hi - lo == 1:
            room[place] = sources[lo][row]
            return
        mid = (lo + hi) // 2
        pl.when(which < mid)(lambda: among(lo, mid))
        pl.when(which >= mid)(lambda: among(mid, hi))

    among(0, len(sources))


def sweep_kernel(n_counts, plan, prior_ref, gram_ref, *refs):
    weights, factors, low, image, residual, direction = refs[-6:]
    count_pieces, item_pieces, out_ref = refs[:n_counts], refs[n_counts:-7], refs[-7]
    tile, rank = factors.shape[1:]
    rounds = plan[6, 0]

    def bring(place, carry):
        count_at = plan[3, place]
        item_at = plan[4, place]

        @pl.when(count_at > 0)
        def _():
            move_tile(count_pieces, count_at - 1, weights, place)
            move_tile(item_pieces, item_at, factors, place)

        @pl.when(count_at == 0)
        def _():
            weights[place] = jnp.zeros((tile, tile), weights.dtype)
            factors[place] = jnp.zeros((tile, rank), factors.dtype)

        return carry

    lax.fori_loop(0, rounds * (TOGETHER * SPAN), bring, 0)

    def pair_images(with_rhs):
        image[...] = jnp.zeros_like(image)
        if with_rhs:
            residual[...] = jnp.zeros_like(residual)

        def one_round(step, carry):
            shares = []
            for number in range(TOGETHER):
                chunk = step * TOGETHER + number
                rows = pl.ds(pl.multiple_of(plan[5, chunk] * tile, tile), tile)
                items = factors[pl.ds(chunk * SPAN, SPAN)].reshape(SPAN * tile, rank)
                scaled = jnp.concatenate(
                    [weights[chunk * SPAN + part].astype(jnp.float32) for part in range(SPAN)],
                    axis=1,
                )
                scores = lax.dot_general(
                    low[rows, :], items, (((1,), (1,)), ((), ())),
                    preferred_element_type=jnp.float32,
                )
                back = jnp.dot(
                    (scaled * scores).astype(jnp.bfloat16), items,
                    preferred_element_type=jnp.float32,
                )
                pulled = None
                if with_rhs:
                    confidence = jnp.where(scaled > 0, 1.0 + scaled, 0.0).astype(jnp.bfloat16)
                    pulled = jnp.dot(confidence, items, preferred_element_type=jnp.float32)
                shares.append((rows, back, pulled))
            for rows, back, pulled in shares:
                image[rows, :] += back
                if with_rhs:
                    residual[rows, :] += pulled
            return carry

        lax.fori_loop(0, rounds, one_round, 0)

    def gram_term(vectors):
        return jnp.dot(
            vectors, gram_ref[...], precision=lax.Precision.HIGHEST,
            preferred_element_type=jnp.float32,
        ) + REG * vectors

    prior = prior_ref[...]
    low[...] = prior.astype(jnp.bfloat16)
    pair_images(True)
    first = residual[...] - (gram_term(prior) + image[...])
    residual[...] = first
    direction[...] = first
    out_ref[...] = prior
    norm_now = row_sum(first, first)
    for step in range(ITERS):
        heading = direction[...]
        low[...] = heading.astype(jnp.bfloat16)
        pair_images(False)
        shown = gram_term(heading) + image[...]
        alpha = norm_now / (row_sum(heading, shown) + EPS)
        out_ref[...] += alpha * heading
        if step < ITERS - 1:
            left = residual[...] - alpha * shown
            residual[...] = left
            fresh = row_sum(left, left)
            direction[...] = left + (fresh / (norm_now + EPS)) * heading
            norm_now = fresh


def run_sweep(plan, user_prior, gram, count_pieces, item_pieces):
    own_rows, rank = user_prior.shape
    tile = count_pieces[0].shape[1]
    pieces = [*count_pieces, *item_pieces]
    vmem = pl.BlockSpec(memory_space=pltpu.VMEM)
    return pl.pallas_call(
        functools.partial(sweep_kernel, len(count_pieces)),
        out_shape=jax.ShapeDtypeStruct((own_rows, rank), jnp.float32),
        in_specs=[pl.BlockSpec(memory_space=pltpu.SMEM)] + [vmem] * (2 + len(pieces)),
        out_specs=vmem,
        scratch_shapes=[
            pltpu.VMEM((LOADS, tile, tile), jnp.bfloat16),
            pltpu.VMEM((LOADS, tile, rank), jnp.bfloat16),
            pltpu.VMEM((own_rows, rank), jnp.bfloat16),
            pltpu.VMEM((own_rows, rank), jnp.float32),
            pltpu.VMEM((own_rows, rank), jnp.float32),
            pltpu.VMEM((own_rows, rank), jnp.float32),
        ],
        compiler_params=pltpu.CompilerParams(vmem_limit_bytes=32 * 2**20),
        name="sweep",
    )(plan, user_prior, gram, *pieces)


def pack_kernel(n_sources, n_outs, jobs, table, *refs):
    sources, refs = refs[:n_sources], refs[n_sources:]
    outs, rooms, written = refs[:n_outs], refs[n_outs:-1], refs[-1]
    copies = []
    for number, (lo, hi, row, start, length, out, first) in enumerate(jobs):

        def place(spot, carry, number=number, lo=lo, hi=hi, row=row, start=start):
            move_tile(sources[lo:hi], table[row, start + spot], rooms[number], spot)
            return carry

        lax.fori_loop(0, length, place, 0, unroll=2)
        target = outs[out].at[pl.ds(first, length)]
        copies.append(pltpu.make_async_copy(rooms[number], target, written.at[number]))
        copies[-1].start()
    for copy in copies:
        copy.wait()


def pack_tiles(name, table, sources, lengths, jobs):
    anywhere = pl.BlockSpec(memory_space=pl.ANY)
    kind = sources[0].dtype
    shape = sources[0].shape[1:]
    return pl.pallas_call(
        functools.partial(pack_kernel, len(sources), len(lengths), jobs),
        out_shape=[jax.ShapeDtypeStruct((n, *shape), kind) for n in lengths],
        in_specs=[pl.BlockSpec(memory_space=pltpu.SMEM)]
        + [pl.BlockSpec(memory_space=pltpu.VMEM)] * len(sources),
        out_specs=[anywhere] * len(lengths),
        scratch_shapes=[pltpu.VMEM((job[4], *shape), kind) for job in jobs]
        + [pltpu.SemaphoreType.DMA((len(jobs),))],
        compiler_params=pltpu.CompilerParams(vmem_limit_bytes=VMEM_GRANT),
        name=name,
    )(table, *sources)


def sum_with(value, axis, bit):
    size = lax.axis_size(axis)
    return value + lax.ppermute(value, axis, [(i, i ^ bit) for i in range(size)])


def iota(rows, columns, axis):
    return lax.broadcasted_iota(jnp.int32, (rows, columns), axis)


def dot_nt(left, right):
    return lax.dot_general(
        left.astype(jnp.bfloat16), right.astype(jnp.bfloat16), (((1,), (1,)), ((), ())),
        preferred_element_type=jnp.float32,
    )


def choose(key, hit, cells, *values):
    match = hit & (key == iota(cells, key.shape[1], 0))
    row = iota(8, key.shape[1], 0)
    digits = jnp.zeros((8, key.shape[1]), jnp.int32)
    for number, value in enumerate(values):
        digits = jnp.where(row == 2 * number, value & 31, digits)
        digits = jnp.where(row == 2 * number + 1, lax.shift_right_logical(value, 5), digits)
    found = dot_nt(digits.astype(jnp.float32), match.astype(jnp.float32)).astype(jnp.int32)
    return [
        found[2 * number:2 * number + 1] + 32 * found[2 * number + 1:2 * number + 2]
        for number in range(len(values))
    ]


def route_kernel(n_grp, pairs, own_tiles, tiles_held, spot, every_ref, out_ref):
    n_blk, n_entries = every_ref.shape
    width = out_ref.shape[1]
    n_chips = n_grp // 2
    user_blocks = n_grp * own_tiles
    all_chips = n_blk * n_chips
    pad = lambda n: -(-n // 8) * 8
    my_blk, my_grp = spot[0], spot[1]
    my_chip = lax.shift_right_logical(my_grp, 1)
    my_core = my_grp & 1
    index = iota(1, n_entries, 1)
    source = lax.shift_right_logical(index, bits_for(pairs))
    from_chip = lax.shift_right_logical(source, 1)
    one_hot = lambda key, n: key == iota(pad(n), n_entries, 0)

    def fields(packed):
        user = packed & (user_blocks - 1)
        packed = lax.shift_right_logical(packed, bits_for(user_blocks))
        live = (packed & 1) == 1
        item = lax.shift_right_logical(packed, 1)
        held = item & (2 * tiles_held - 1)
        chip = lax.shift_right_logical(item, bits_for(2 * tiles_held))
        return user, live, chip, held

    ids = iota(1, 2 * tiles_held, 1)
    fewer = iota(2 * tiles_held, 2 * tiles_held, 0) > iota(2 * tiles_held, 2 * tiles_held, 1)

    def needs(live, chip, held):
        on_chip = one_hot(chip, all_chips) & live
        on_tile = one_hot(held, 2 * tiles_held)
        needed = dot_nt(on_chip.astype(jnp.float32), on_tile.astype(jnp.float32)) > 0
        return on_chip, on_tile, needed, dot_nt(needed.astype(jnp.float32), fewer.astype(jnp.float32))

    excess = jnp.zeros((1, 1), jnp.float32)
    worst = lambda loads, room: jnp.max(loads, axis=(0, 1), keepdims=True) - room
    asked = jnp.zeros((1, width), jnp.int32)
    here = my_blk * n_chips + my_chip
    chip_row = iota(pad(all_chips), 2 * tiles_held, 0)
    for blk in range(n_blk):
        user, live, chip, held = fields(every_ref[blk:blk + 1, :])
        _, _, needed, ahead = needs(live, chip, held)
        away = lax.shift_right_logical(chip_row, bits_for(n_chips)) != blk
        asks = jnp.sum((needed & away).astype(jnp.float32), axis=1, keepdims=True)
        excess = jnp.maximum(excess, worst(asks, 2 * FAR_CAP))
        to_chip = lax.shift_right_logical(user, bits_for(own_tiles) + 1)
        to = one_hot(to_chip, n_chips).astype(jnp.float32)
        for key, cap in ((from_chip, COUNT_CAP), (chip & (n_chips - 1), ITEM_CAP)):
            loads = dot_nt((one_hot(key, n_chips) & live).astype(jnp.float32), to)
            excess = jnp.maximum(excess, worst(loads, 2 * cap))
        loads = jnp.sum(
            (one_hot(user, user_blocks) & live).astype(jnp.int32), axis=1, keepdims=True
        )
        chunks = lax.shift_right_logical(loads + SPAN - 1, bits_for(SPAN)).astype(jnp.float32)
        owners = iota(pad(n_grp), pad(user_blocks), 1)
        owners = lax.shift_right_logical(owners, bits_for(own_tiles)) == iota(*owners.shape, 0)
        loads = jnp.dot(
            owners.astype(jnp.float32), jnp.broadcast_to(chunks, (chunks.shape[0], 128)),
            precision=lax.Precision.HIGHEST, preferred_element_type=jnp.float32,
        )
        excess = jnp.maximum(excess, worst(loads, LOADS // SPAN))

        mine = chip_row == here
        present = jnp.sum((needed & mine).astype(jnp.int32), axis=0, keepdims=True)
        place = jnp.sum(jnp.where(mine, ahead, 0.0), axis=0, keepdims=True).astype(jnp.int32)
        shift = (blk + n_blk - my_blk) & (n_blk - 1)
        spot_at = lax.shift_right_logical(place, 1)
        hit = (present > 0) & ((place & 1) == my_core) & (spot_at < FAR_CAP) & (shift > 0)
        value = at_source(
            lax.shift_right_logical(ids, bits_for(tiles_held)) ^ my_core, ids & (tiles_held - 1), 2
        )
        (found,) = choose((shift - 1) * FAR_CAP + spot_at, hit, width, value)
        asked = asked + found

    user, live, chip, held = fields(every_ref[pl.ds(my_blk, 1), :])
    on_chip, on_tile, _, ahead = needs(live, chip, held)
    places = jnp.dot(
        ahead.astype(jnp.bfloat16), on_tile.astype(jnp.float32).astype(jnp.bfloat16),
        preferred_element_type=jnp.float32,
    )
    far_place = jnp.sum(jnp.where(on_chip, places, 0.0), axis=0, keepdims=True).astype(jnp.int32)
    far_place = jnp.minimum(far_place, 2 * FAR_CAP - 1)
    owner = lax.shift_right_logical(user, bits_for(own_tiles))
    local_user = user & (own_tiles - 1)
    to_chip = lax.shift_right_logical(owner, 1)
    column = chip & (n_chips - 1)
    to_me = live & (owner == my_grp)
    groups = [
        one_hot(to_chip, n_chips) & (live & (from_chip == my_chip)),
        one_hot(from_chip, n_chips) & (live & (to_chip == my_chip)),
        one_hot(to_chip, n_chips) & (live & (column == my_chip)),
        one_hot(column, n_chips) & (live & (to_chip == my_chip)),
        one_hot(local_user, own_tiles) & to_me,
    ]
    before = (iota(n_entries, n_entries, 0) < iota(n_entries, n_entries, 1)).astype(jnp.float32)
    before = before.astype(jnp.bfloat16)
    ranks = []
    for marks in groups:
        earlier = jnp.dot(
            marks.astype(jnp.float32).astype(jnp.bfloat16), before,
            preferred_element_type=jnp.float32,
        )
        earlier = jnp.sum(jnp.where(marks, earlier, 0.0), axis=0, keepdims=True)
        ranks.append(earlier.astype(jnp.int32))
    counts_out, counts_back, items_out, items_back, user_rank = ranks

    half = lambda rank: lax.shift_right_logical(rank, 1)
    sent = lambda rank, cap: live & ((rank & 1) == my_core) & (half(rank) < cap)
    (out_ref[0:1, :],) = choose(
        to_chip * COUNT_CAP + half(counts_out), sent(counts_out, COUNT_CAP) & (from_chip == my_chip),
        width, at_source((source & 1) ^ my_core, index & (pairs - 1), 2),
    )
    out_ref[1:2, :] = asked
    shift = (my_blk + n_blk - lax.shift_right_logical(chip, bits_for(n_chips))) & (n_blk - 1)
    near = shift == 0
    lane = jnp.where(near, lax.shift_right_logical(held, bits_for(tiles_held)), far_place & 1)
    row = jnp.where(near, held & (tiles_held - 1), half(far_place))
    (out_ref[2:3, :],) = choose(
        (to_chip ^ my_chip) * ITEM_CAP + half(items_out),
        sent(items_out, ITEM_CAP) & (column == my_chip),
        width, at_source((lane ^ my_core) * n_blk + shift, row, 2 * n_blk),
    )

    in_tile = groups[4]
    loads = jnp.sum(in_tile.astype(jnp.int32), axis=1, keepdims=True)
    chunks = lax.shift_right_logical(loads + SPAN - 1, bits_for(SPAN)).astype(jnp.float32)
    rows = chunks.shape[0]
    ends = jnp.dot(
        (iota(rows, rows, 0) >= iota(rows, rows, 1)).astype(jnp.float32),
        jnp.broadcast_to(chunks, (rows, 128)),
        precision=lax.Precision.HIGHEST, preferred_element_type=jnp.float32,
    )
    firsts = ends[:, :1] - chunks
    room_at = jnp.sum(jnp.where(in_tile, firsts * SPAN, 0.0), axis=0, keepdims=True)
    room_at = room_at.astype(jnp.int32) + user_rank
    hit = to_me & (room_at < LOADS)
    counts_row = jnp.minimum(half(counts_back), COUNT_CAP - 1)
    items_row = jnp.minimum(half(items_back), ITEM_CAP - 1)
    count_at = at_source((counts_back & 1) ^ my_core, from_chip * COUNT_CAP + counts_row, 2)
    item_at = at_source(
        (column ^ my_chip) * 2 + ((items_back & 1) ^ my_core), items_row, 2 * n_chips
    )
    out_ref[3:4, :], out_ref[4:5, :] = choose(room_at, hit, width, count_at + 1, item_at)
    passed = (iota(rows, width, 1).astype(jnp.float32) >= ends[:, :1]) & (
        iota(rows, width, 0) < own_tiles - 1
    )
    out_ref[5:6, :] = jnp.sum(passed.astype(jnp.int32), axis=0, keepdims=True)
    total = ends[own_tiles - 1:own_tiles, :1].astype(jnp.int32)
    rounds = lax.shift_right_logical(total + TOGETHER - 1, bits_for(TOGETHER))
    rounds = jnp.minimum(rounds, LOADS // (SPAN * TOGETHER))
    copies = jnp.sum(hit.astype(jnp.int32), axis=1, keepdims=True)
    at = iota(1, width, 1)
    fits = (excess <= 0.0).astype(jnp.int32)
    head = jnp.where(at == 0, rounds, jnp.where(at == 1, copies, jnp.where(at == 2, fits, 0)))
    out_ref[6:7, :] = head
    out_ref[7:8, :] = jnp.zeros((1, width), jnp.int32)


def route(every, my_blk, my_grp, n_grp, own_tiles, tiles_held):
    n_blk, n_entries = every.shape
    n_chips = n_grp // 2
    width = max(n_chips * COUNT_CAP, (n_blk - 1) * FAR_CAP, n_chips * ITEM_CAP, LOADS)
    width = -(-width // 128) * 128
    vmem = pl.BlockSpec(memory_space=pltpu.VMEM)
    return pl.pallas_call(
        functools.partial(route_kernel, n_grp, n_entries // n_grp, own_tiles, tiles_held),
        out_shape=jax.ShapeDtypeStruct((8, width), jnp.int32),
        in_specs=[pl.BlockSpec(memory_space=pltpu.SMEM), vmem],
        out_specs=vmem,
        compiler_params=pltpu.CompilerParams(vmem_limit_bytes=16 * 2**20),
        name="route",
    )(jnp.stack([my_blk, my_grp]).astype(jnp.int32), every)


def scan_kernel(counts_ref, scaled_ref, most_ref):
    counts = counts_ref[...]
    scaled_ref[...] = (ALPHA * counts.astype(jnp.float32)).astype(jnp.bfloat16)
    most_ref[...] = jnp.max(counts, axis=1)


def scan_counts(counts):
    pairs, tile, columns = counts.shape
    block = 16
    return pl.pallas_call(
        scan_kernel,
        grid=(pairs // block,),
        out_shape=[
            jax.ShapeDtypeStruct(counts.shape, jnp.bfloat16),
            jax.ShapeDtypeStruct((pairs, columns), jnp.int32),
        ],
        in_specs=[pl.BlockSpec((block, tile, columns), lambda i: (i, 0, 0))],
        out_specs=[
            pl.BlockSpec((block, tile, columns), lambda i: (i, 0, 0)),
            pl.BlockSpec((block, columns), lambda i: (i, 0)),
        ],
        compiler_params=pltpu.CompilerParams(vmem_limit_bytes=16 * 2**20),
        name="scan_counts",
    )(counts)


def body(user_prior, item_factors, user_tiles, item_tiles, counts):
    pairs = counts.shape[0]
    tile = counts.shape[1]
    rank = item_factors.shape[1]
    n_blk = lax.axis_size("blk")
    n_grp = lax.axis_size("grp")
    n_all = n_blk * n_grp
    n_chips = n_grp // 2
    own_rows = user_prior.shape[0]
    own_tiles = own_rows // tile
    user_blocks = own_tiles * n_grp
    tiles_held = item_factors.shape[0] // tile
    my_blk = lax.axis_index("blk")
    my_grp = lax.axis_index("grp")
    my_chip = my_grp // 2
    my_core = my_grp % 2
    lanes = [[chip * 2 + core for chip in range(n_chips)] for core in range(2)]

    def swap(value):
        return lax.ppermute(value, "grp", [(i, i ^ 1) for i in range(n_grp)])

    def to_chips(value):
        return lax.all_to_all(
            value, "grp", split_axis=0, concat_axis=0, tiled=True, axis_index_groups=lanes
        )

    gram_local = lax.dot_general(
        item_factors, item_factors, (((0,), (0,)), ((), ())), preferred_element_type=jnp.float32
    )
    grp_bits, blk_bits = [[1 << n for n in range(bits_for(size))] for size in (n_grp, n_blk)]
    held = item_factors.reshape(tiles_held, tile, rank)
    held_mate = swap(held)
    scaled, column_most = scan_counts(counts)
    live = jnp.any(column_most > 0, axis=1)
    scaled_mate = swap(scaled)
    packed = (item_tiles * 2 + live.astype(jnp.int32)) * user_blocks + user_tiles
    every = lax.all_to_all(
        jnp.broadcast_to(packed, (n_all, pairs)), ("blk", "grp"),
        split_axis=0, concat_axis=0, tiled=True,
    )
    table = route(every.reshape(n_blk, n_grp * pairs), my_blk, my_grp, n_grp, own_tiles, tiles_held)
    gram = gram_local
    for bit in grp_bits[1:]:
        gram = sum_with(gram, "grp", bit)
    table, gram = lax.optimization_barrier((table, gram))

    jobs = [(0, 2, 1, shift * FAR_CAP, FAR_CAP, shift, 0) for shift in range(n_blk - 1)]
    for chip in range(n_chips):
        jobs.append((2, 4, 0, chip * COUNT_CAP, COUNT_CAP, n_blk - 1, chip * COUNT_CAP))
    lengths = [FAR_CAP] * (n_blk - 1) + [n_chips * COUNT_CAP]
    *far, counts_out = pack_tiles(
        "pack_first", table, [held, held_mate, scaled, scaled_mate], lengths, jobs
    )
    far = [
        lax.ppermute(piece, "blk", [(i, (i + 1 + shift) % n_blk) for i in range(n_blk)])
        for shift, piece in enumerate(far)
    ]
    far_mate = [swap(piece) for piece in far]
    counts_own = to_chips(counts_out)

    jobs = [(0, 2 * n_blk, 2, off * ITEM_CAP, ITEM_CAP, off, 0) for off in range(n_chips)]
    items_out = pack_tiles(
        "pack_items", table, [held, *far, held_mate, *far_mate], [ITEM_CAP] * n_chips, jobs
    )
    counts_own, gram, *items_out = lax.optimization_barrier((counts_own, gram, *items_out))
    counts_mate = swap(counts_own)
    gram = sum_with(gram, "grp", grp_bits[0])
    for bit in blk_bits:
        gram = sum_with(gram, "blk", bit)
    item_pieces = []
    for off, piece in enumerate(items_out):
        if off:
            piece = lax.ppermute(piece, "grp", [(i, i ^ (2 * off)) for i in range(n_grp)])
        if off == n_chips - 1:
            piece, gram = lax.optimization_barrier((piece, gram))
        item_pieces += [piece, swap(piece)]
    by_owner = run_sweep(table, user_prior, gram, [counts_own, counts_mate], item_pieces)

    fits = table[6, 2] > 0
    return lax.cond(
        fits, lambda done, *given: done, lambda done, *given: sweep_in_place(*given),
        by_owner, user_prior, item_factors, user_tiles, item_tiles, counts, live, gram_local,
    )


def solution(mesh):
    in_specs = (
        P(("blk", "grp"), None),
        P(("blk", "grp"), None),
        P(("blk", "grp")),
        P(("blk", "grp")),
        P(("blk", "grp"), None, None),
    )
    out_specs = P(("blk", "grp"), None)
    return jax.shard_map(body, mesh=mesh, in_specs=in_specs, out_specs=out_specs, check_vma=False)
```

```python
import functools

import jax
import jax.numpy as jnp
from jax import lax
from jax.experimental import pallas as pl
from jax.experimental.pallas import tpu as pltpu
from jax.sharding import PartitionSpec as P

ITERS = 3

ALPHA = 40.0
REG = 32.0
EPS = 1e-06

FAR_CAP = 14
COUNT_CAP = 24
NEAR_CAP = 8
ITEM_CAP = 16
RIDE = COUNT_CAP + NEAR_CAP
LOADS = 128
SPAN = 2
VMEM_GRANT = 60 * 2**20
TOGETHER = 8


def fetch_tiles(item_factors, item_tiles, pairs, tile, rank):
    n_all = lax.axis_size(("blk", "grp"))
    tiles_held = item_factors.shape[0] // tile
    slots_each = max(2, pairs // n_all)
    owner = item_tiles // tiles_held
    local_slot = item_tiles % tiles_held
    position = jnp.arange(pairs, dtype=jnp.int32)
    earlier = (owner[None, :] == owner[:, None]) & (position[None, :] < position[:, None])
    order = jnp.sum(earlier.astype(jnp.int32), axis=1)
    requests = jnp.full((n_all, slots_each), -1, jnp.int32).at[owner, order].set(local_slot)
    wanted = lax.all_to_all(requests, ("blk", "grp"), split_axis=0, concat_axis=0, tiled=True)
    held = item_factors.reshape(tiles_held, tile, rank)
    picked = jnp.take(held, jnp.maximum(wanted, 0), axis=0)
    picked = jnp.where((wanted >= 0)[:, :, None, None], picked, jnp.zeros((), picked.dtype))
    arrived = lax.all_to_all(picked, ("blk", "grp"), split_axis=0, concat_axis=0, tiled=True)
    return arrived[owner, order]


def row_sum(left, right):
    return jnp.sum(left * right, axis=1, keepdims=True)


def sweep_in_place(user_prior, item_factors, user_tiles, item_tiles, counts, live, gram_local):
    pairs = counts.shape[0]
    tile = counts.shape[1]
    rank = item_factors.shape[1]
    n_grp = lax.axis_size("grp")
    own_rows = user_prior.shape[0]
    block_rows = own_rows * n_grp
    user_blocks = block_rows // tile
    span = min(32, pairs)
    gram = lax.psum(gram_local, ("blk", "grp"))
    pair_tiles = fetch_tiles(item_factors, item_tiles, pairs, tile, rank)
    rounds = (jnp.sum(live.astype(jnp.int32)) + span - 1) // span
    tile_ids = jnp.arange(user_blocks, dtype=jnp.int32)

    def accumulate(low_tiles, with_rhs):

        def one_round(index, totals):
            start = index * span
            users = lax.dynamic_slice_in_dim(user_tiles, start, span)
            factors = lax.dynamic_slice_in_dim(pair_tiles, start, span)
            counted = lax.dynamic_slice_in_dim(counts, start, span).astype(jnp.float32)
            selector = (tile_ids[:, None] == users[None, :]).astype(jnp.float32)
            users_low = jnp.take(low_tiles, users, axis=0)
            scores = jnp.einsum(
                "bur,bir->bui", users_low, factors, preferred_element_type=jnp.float32
            )
            scaled = (ALPHA * counted * scores).astype(jnp.bfloat16)
            back = jnp.einsum("bui,bir->bur", scaled, factors, preferred_element_type=jnp.float32)
            result = [
                totals[0]
                + jnp.einsum("tb,bur->tur", selector, back, precision=lax.Precision.HIGHEST)
            ]
            if with_rhs:
                confidence = jnp.where(counted > 0, 1.0 + ALPHA * counted, 0.0).astype(jnp.bfloat16)
                pulled = jnp.einsum(
                    "bui,bir->bur", confidence, factors, preferred_element_type=jnp.float32
                )
                result.append(
                    totals[1]
                    + jnp.einsum("tb,bur->tur", selector, pulled, precision=lax.Precision.HIGHEST)
                )
            return tuple(result)

        zeros = jnp.zeros((user_blocks, tile, rank), jnp.float32)
        start_state = (zeros, zeros) if with_rhs else (zeros,)
        totals = lax.fori_loop(0, rounds, one_round, start_state)
        return tuple((total.reshape(block_rows, rank) for total in totals))

    def gram_term(vectors):
        return jnp.dot(vectors, gram, precision=lax.Precision.HIGHEST) + REG * vectors

    low = lax.all_gather(user_prior.astype(jnp.bfloat16), "grp", axis=0, tiled=True)
    pair_part, rhs_part = accumulate(low.reshape(user_blocks, tile, rank), True)
    pair_share, rhs_share = (
        lax.psum_scatter(pair_part, "grp", scatter_dimension=0, tiled=True),
        lax.psum_scatter(rhs_part, "grp", scatter_dimension=0, tiled=True),
    )
    solution = user_prior
    residual = rhs_share - (gram_term(solution) + pair_share)
    direction = residual
    norm_now = row_sum(residual, residual)
    for step in range(ITERS):
        low = lax.all_gather(direction.astype(jnp.bfloat16), "grp", axis=0, tiled=True)
        (pair_part,) = accumulate(low.reshape(user_blocks, tile, rank), False)
        image = gram_term(direction) + lax.psum_scatter(
            pair_part, "grp", scatter_dimension=0, tiled=True
        )
        alpha = norm_now / (row_sum(direction, image) + EPS)
        solution = solution + alpha * direction
        residual = residual - alpha * image
        fresh = row_sum(residual, residual)
        direction = residual + fresh / (norm_now + EPS) * direction
        norm_now = fresh
    return solution


def bits_for(n):
    return (n - 1).bit_length()


def at_source(number, row, n_sources):
    return (row << bits_for(n_sources)) + number


def move_tile(sources, at, room, place):
    bits = bits_for(len(sources))
    row = lax.shift_right_logical(at, bits)
    which = at & ((1 << bits) - 1)

    def among(lo, hi):
        if hi - lo == 1:
            room[place] = sources[lo][row]
            return
        mid = (lo + hi) // 2
        pl.when(which < mid)(lambda: among(lo, mid))
        pl.when(which >= mid)(lambda: among(mid, hi))

    among(0, len(sources))


def sweep_kernel(plan, prior_ref, gram_ref, *refs):
    weights, factors, low, image, residual, direction = refs[-6:]
    item_pieces, out_ref = refs[:-7], refs[-7]
    count_pieces = item_pieces[:2]
    tile, rank = factors.shape[1:]
    n_chunks = plan[6, 0]
    halves = (n_chunks + TOGETHER // 2 - 1) // (TOGETHER // 2)
    rounds = halves // 2

    def bring(place, carry):
        count_at = plan[3, place]
        item_at = plan[4, place]

        @pl.when(count_at > 0)
        def _():
            move_tile(count_pieces, count_at - 1, weights, place)
            move_tile(item_pieces, item_at, factors, place)

        @pl.when(count_at == 0)
        def _():
            weights[place] = jnp.zeros((tile, tile), weights.dtype)
            factors[place] = jnp.zeros((tile, rank), factors.dtype)

        return carry

    lax.fori_loop(0, halves * (TOGETHER // 2 * SPAN), bring, 0)

    def pair_images(with_rhs):
        image[...] = jnp.zeros_like(image)
        if with_rhs:
            residual[...] = jnp.zeros_like(residual)

        def some(first, n):
            shares = []
            for number in range(n):
                chunk = first + number
                rows = pl.ds(pl.multiple_of(plan[5, chunk] * tile, tile), tile)
                items = factors[pl.ds(chunk * SPAN, SPAN)].reshape(SPAN * tile, rank)
                scaled = jnp.concatenate(
                    [weights[chunk * SPAN + part].astype(jnp.float32) for part in range(SPAN)],
                    axis=1,
                )
                scores = lax.dot_general(
                    low[rows, :], items, (((1,), (1,)), ((), ())),
                    preferred_element_type=jnp.float32,
                )
                back = jnp.dot(
                    (scaled * scores).astype(jnp.bfloat16), items,
                    preferred_element_type=jnp.float32,
                )
                pulled = None
                if with_rhs:
                    confidence = jnp.where(scaled > 0, 1.0 + scaled, 0.0).astype(jnp.bfloat16)
                    pulled = jnp.dot(confidence, items, preferred_element_type=jnp.float32)
                shares.append((rows, back, pulled))
            for rows, back, pulled in shares:
                image[rows, :] += back
                if with_rhs:
                    residual[rows, :] += pulled

        def one_round(step, carry):
            some(step * TOGETHER, TOGETHER)
            return carry

        lax.fori_loop(0, rounds, one_round, 0)
        pl.when(halves % 2 == 1)(lambda: some(rounds * TOGETHER, TOGETHER // 2))

    def gram_term(vectors):
        return jnp.dot(
            vectors, gram_ref[...], precision=lax.Precision.HIGHEST,
            preferred_element_type=jnp.float32,
        ) + REG * vectors

    prior = prior_ref[...]
    low[...] = prior.astype(jnp.bfloat16)
    pair_images(True)
    first = residual[...] - (gram_term(prior) + image[...])
    residual[...] = first
    direction[...] = first
    out_ref[...] = prior
    norm_now = row_sum(first, first)
    for step in range(ITERS):
        heading = direction[...]
        low[...] = heading.astype(jnp.bfloat16)
        pair_images(False)
        shown = gram_term(heading) + image[...]
        alpha = norm_now / (row_sum(heading, shown) + EPS)
        out_ref[...] += alpha * heading
        if step < ITERS - 1:
            left = residual[...] - alpha * shown
            residual[...] = left
            fresh = row_sum(left, left)
            direction[...] = left + (fresh / (norm_now + EPS)) * heading
            norm_now = fresh


def run_sweep(plan, user_prior, gram, pieces):
    own_rows, rank = user_prior.shape
    tile = pieces[0].shape[1]
    vmem = pl.BlockSpec(memory_space=pltpu.VMEM)
    return pl.pallas_call(
        sweep_kernel,
        out_shape=jax.ShapeDtypeStruct((own_rows, rank), jnp.float32),
        in_specs=[pl.BlockSpec(memory_space=pltpu.SMEM)] + [vmem] * (2 + len(pieces)),
        out_specs=vmem,
        scratch_shapes=[
            pltpu.VMEM((LOADS, tile, tile), jnp.bfloat16),
            pltpu.VMEM((LOADS, tile, rank), jnp.bfloat16),
            pltpu.VMEM((own_rows, rank), jnp.bfloat16),
            pltpu.VMEM((own_rows, rank), jnp.float32),
            pltpu.VMEM((own_rows, rank), jnp.float32),
            pltpu.VMEM((own_rows, rank), jnp.float32),
        ],
        compiler_params=pltpu.CompilerParams(vmem_limit_bytes=32 * 2**20),
        name="sweep",
    )(plan, user_prior, gram, *pieces)


def pack_kernel(n_sources, n_outs, jobs, table, *refs):
    sources, refs = refs[:n_sources], refs[n_sources:]
    outs, rooms, written = refs[:n_outs], refs[n_outs:-1], refs[-1]
    copies = []
    for number, (lo, hi, row, start, length, out, first) in enumerate(jobs):

        def place(spot, carry, number=number, lo=lo, hi=hi, row=row, start=start):
            move_tile(sources[lo:hi], table[row, start + spot], rooms[number], spot)
            return carry

        lax.fori_loop(0, length, place, 0, unroll=2)
        target = outs[out].at[pl.ds(first, length)]
        copies.append(pltpu.make_async_copy(rooms[number], target, written.at[number]))
        copies[-1].start()
    for copy in copies:
        copy.wait()


def pack_tiles(name, table, sources, lengths, jobs):
    anywhere = pl.BlockSpec(memory_space=pl.ANY)
    kind = sources[0].dtype
    shape = sources[0].shape[1:]
    return pl.pallas_call(
        functools.partial(pack_kernel, len(sources), len(lengths), jobs),
        out_shape=[jax.ShapeDtypeStruct((n, *shape), kind) for n in lengths],
        in_specs=[pl.BlockSpec(memory_space=pltpu.SMEM)]
        + [pl.BlockSpec(memory_space=pltpu.VMEM)] * len(sources),
        out_specs=[anywhere] * len(lengths),
        scratch_shapes=[pltpu.VMEM((job[4], *shape), kind) for job in jobs]
        + [pltpu.SemaphoreType.DMA((len(jobs),))],
        compiler_params=pltpu.CompilerParams(vmem_limit_bytes=VMEM_GRANT),
        name=name,
    )(table, *sources)


def sum_with(value, axis, bit):
    size = lax.axis_size(axis)
    return value + lax.ppermute(value, axis, [(i, i ^ bit) for i in range(size)])


def iota(rows, columns, axis):
    return lax.broadcasted_iota(jnp.int32, (rows, columns), axis)


def dot_nt(left, right):
    return lax.dot_general(
        left.astype(jnp.bfloat16), right.astype(jnp.bfloat16), (((1,), (1,)), ((), ())),
        preferred_element_type=jnp.float32,
    )


def choose(key, hit, cells, *values):
    match = hit & (key == iota(cells, key.shape[1], 0))
    row = iota(8, key.shape[1], 0)
    digits = jnp.zeros((8, key.shape[1]), jnp.int32)
    for number, value in enumerate(values):
        digits = jnp.where(row == 2 * number, value & 31, digits)
        digits = jnp.where(row == 2 * number + 1, lax.shift_right_logical(value, 5), digits)
    found = dot_nt(digits.astype(jnp.float32), match.astype(jnp.float32)).astype(jnp.int32)
    return [
        found[2 * number:2 * number + 1] + 32 * found[2 * number + 1:2 * number + 2]
        for number in range(len(values))
    ]


def route_kernel(n_grp, pairs, own_tiles, tiles_held, spot, every_ref, out_ref):
    n_blk, n_entries = every_ref.shape
    width = out_ref.shape[1]
    n_chips = n_grp // 2
    user_blocks = n_grp * own_tiles
    all_chips = n_blk * n_chips
    pad = lambda n: -(-n // 8) * 8
    my_blk, my_grp = spot[0], spot[1]
    my_chip = lax.shift_right_logical(my_grp, 1)
    my_core = my_grp & 1
    index = iota(1, n_entries, 1)
    source = lax.shift_right_logical(index, bits_for(pairs))
    from_chip = lax.shift_right_logical(source, 1)
    one_hot = lambda key, n: key == iota(pad(n), n_entries, 0)

    def fields(packed):
        user = packed & (user_blocks - 1)
        packed = lax.shift_right_logical(packed, bits_for(user_blocks))
        live = (packed & 1) == 1
        item = lax.shift_right_logical(packed, 1)
        held = item & (2 * tiles_held - 1)
        chip = lax.shift_right_logical(item, bits_for(2 * tiles_held))
        return user, live, chip, held

    ids = iota(1, 2 * tiles_held, 1)
    fewer = iota(2 * tiles_held, 2 * tiles_held, 0) > iota(2 * tiles_held, 2 * tiles_held, 1)

    def needs(live, chip, held):
        on_chip = one_hot(chip, all_chips) & live
        on_tile = one_hot(held, 2 * tiles_held)
        needed = dot_nt(on_chip.astype(jnp.float32), on_tile.astype(jnp.float32)) > 0
        return on_chip, on_tile, needed, dot_nt(needed.astype(jnp.float32), fewer.astype(jnp.float32))

    excess = jnp.zeros((1, 1), jnp.float32)
    worst = lambda loads, room: jnp.max(loads, axis=(0, 1), keepdims=True) - room
    asked = jnp.zeros((1, width), jnp.int32)
    here = my_blk * n_chips + my_chip
    chip_row = iota(pad(all_chips), 2 * tiles_held, 0)
    for blk in range(n_blk):
        user, live, chip, held = fields(every_ref[blk:blk + 1, :])
        _, _, needed, ahead = needs(live, chip, held)
        away = lax.shift_right_logical(chip_row, bits_for(n_chips)) != blk
        asks = jnp.sum((needed & away).astype(jnp.float32), axis=1, keepdims=True)
        excess = jnp.maximum(excess, worst(asks, 2 * FAR_CAP))
        to_chip = lax.shift_right_logical(user, bits_for(own_tiles) + 1)
        to = one_hot(to_chip, n_chips).astype(jnp.float32)
        column = chip & (n_chips - 1)
        near = lax.shift_right_logical(chip, bits_for(n_chips)) == blk
        for key, inside, cap in (
            (from_chip, live, COUNT_CAP),
            (column, live & near, NEAR_CAP),
            (column, live & ~near, ITEM_CAP),
        ):
            loads = dot_nt((one_hot(key, n_chips) & inside).astype(jnp.float32), to)
            excess = jnp.maximum(excess, worst(loads, 2 * cap))
        loads = jnp.sum(
            (one_hot(user, user_blocks) & live).astype(jnp.int32), axis=1, keepdims=True
        )
        chunks = lax.shift_right_logical(loads + SPAN - 1, bits_for(SPAN)).astype(jnp.float32)
        owners = iota(pad(n_grp), pad(user_blocks), 1)
        owners = lax.shift_right_logical(owners, bits_for(own_tiles)) == iota(*owners.shape, 0)
        loads = jnp.dot(
            owners.astype(jnp.float32), jnp.broadcast_to(chunks, (chunks.shape[0], 128)),
            precision=lax.Precision.HIGHEST, preferred_element_type=jnp.float32,
        )
        excess = jnp.maximum(excess, worst(loads, LOADS // SPAN))

        mine = chip_row == here
        present = jnp.sum((needed & mine).astype(jnp.int32), axis=0, keepdims=True)
        place = jnp.sum(jnp.where(mine, ahead, 0.0), axis=0, keepdims=True).astype(jnp.int32)
        shift = (blk + n_blk - my_blk) & (n_blk - 1)
        spot_at = lax.shift_right_logical(place, 1)
        hit = (present > 0) & ((place & 1) == my_core) & (spot_at < FAR_CAP) & (shift > 0)
        value = at_source(
            lax.shift_right_logical(ids, bits_for(tiles_held)) ^ my_core, ids & (tiles_held - 1), 2
        )
        (found,) = choose((shift - 1) * FAR_CAP + spot_at, hit, width, value)
        asked = asked + found

    user, live, chip, held = fields(every_ref[pl.ds(my_blk, 1), :])
    on_chip, on_tile, _, ahead = needs(live, chip, held)
    places = jnp.dot(
        ahead.astype(jnp.bfloat16), on_tile.astype(jnp.float32).astype(jnp.bfloat16),
        preferred_element_type=jnp.float32,
    )
    far_place = jnp.sum(jnp.where(on_chip, places, 0.0), axis=0, keepdims=True).astype(jnp.int32)
    far_place = jnp.minimum(far_place, 2 * FAR_CAP - 1)
    owner = lax.shift_right_logical(user, bits_for(own_tiles))
    local_user = user & (own_tiles - 1)
    to_chip = lax.shift_right_logical(owner, 1)
    column = chip & (n_chips - 1)
    to_me = live & (owner == my_grp)
    shift = (my_blk + n_blk - lax.shift_right_logical(chip, bits_for(n_chips))) & (n_blk - 1)
    near, far = live & (shift == 0), live & (shift > 0)
    in_tile = one_hot(local_user, own_tiles) & to_me
    groups = [
        one_hot(to_chip, n_chips) & (live & (from_chip == my_chip)),
        one_hot(from_chip, n_chips) & (live & (to_chip == my_chip)),
        one_hot(to_chip, n_chips) & (near & (column == my_chip)),
        one_hot(column, n_chips) & (near & (to_chip == my_chip)),
        one_hot(to_chip, n_chips) & (far & (column == my_chip)),
        one_hot(column, n_chips) & (far & (to_chip == my_chip)),
        in_tile,
    ]
    before = (iota(n_entries, n_entries, 0) < iota(n_entries, n_entries, 1)).astype(jnp.float32)
    before = before.astype(jnp.bfloat16)
    ranks = []
    for marks in groups:
        earlier = jnp.dot(
            marks.astype(jnp.float32).astype(jnp.bfloat16), before,
            preferred_element_type=jnp.float32,
        )
        earlier = jnp.sum(jnp.where(marks, earlier, 0.0), axis=0, keepdims=True)
        ranks.append(earlier.astype(jnp.int32))
    counts_out, counts_back, near_out, near_back, far_out, far_back, user_rank = ranks

    half = lambda rank: lax.shift_right_logical(rank, 1)
    sent = lambda rank, cap: live & ((rank & 1) == my_core) & (half(rank) < cap)
    back = lambda rank, cap: jnp.minimum(half(rank), cap - 1)
    core = lambda rank: (rank & 1) ^ my_core
    (out_ref[0:1, :],) = choose(
        to_chip * COUNT_CAP + half(counts_out), sent(counts_out, COUNT_CAP) & (from_chip == my_chip),
        width, at_source((source & 1) ^ my_core, index & (pairs - 1), 2),
    )
    out_ref[1:2, :] = asked
    (out_ref[7:8, :],) = choose(
        to_chip * NEAR_CAP + half(near_out), near & (column == my_chip) & sent(near_out, NEAR_CAP),
        width,
        at_source(
            lax.shift_right_logical(held, bits_for(tiles_held)) ^ my_core, held & (tiles_held - 1), 2
        ),
    )
    (out_ref[2:3, :],) = choose(
        (to_chip ^ my_chip) * ITEM_CAP + half(far_out),
        far & (column == my_chip) & sent(far_out, ITEM_CAP), width,
        at_source(
            core(far_place) * (n_blk - 1) + shift - 1, half(far_place), 2 * (n_blk - 1)
        ),
    )

    loads = jnp.sum(in_tile.astype(jnp.int32), axis=1, keepdims=True)
    chunks = lax.shift_right_logical(loads + SPAN - 1, bits_for(SPAN)).astype(jnp.float32)
    rows = chunks.shape[0]
    ends = jnp.dot(
        (iota(rows, rows, 0) >= iota(rows, rows, 1)).astype(jnp.float32),
        jnp.broadcast_to(chunks, (rows, 128)),
        precision=lax.Precision.HIGHEST, preferred_element_type=jnp.float32,
    )
    firsts = ends[:, :1] - chunks
    room_at = jnp.sum(jnp.where(in_tile, firsts * SPAN, 0.0), axis=0, keepdims=True)
    room_at = room_at.astype(jnp.int32) + user_rank
    hit = to_me & (room_at < LOADS)
    count_at = at_source(
        core(counts_back), from_chip * RIDE + back(counts_back, COUNT_CAP), 2
    )
    n_sources = 2 + 2 * n_chips
    item_at = jnp.where(
        shift == 0,
        at_source(
            core(near_back), column * RIDE + COUNT_CAP + back(near_back, NEAR_CAP), n_sources
        ),
        at_source(
            2 + (column ^ my_chip) * 2 + core(far_back), back(far_back, ITEM_CAP), n_sources
        ),
    )
    out_ref[3:4, :], out_ref[4:5, :] = choose(room_at, hit, width, count_at + 1, item_at)
    passed = (iota(rows, width, 1).astype(jnp.float32) >= ends[:, :1]) & (
        iota(rows, width, 0) < own_tiles - 1
    )
    out_ref[5:6, :] = jnp.sum(passed.astype(jnp.int32), axis=0, keepdims=True)
    total = ends[own_tiles - 1:own_tiles, :1].astype(jnp.int32)
    total = jnp.minimum(total, LOADS // SPAN)
    copies = jnp.sum(hit.astype(jnp.int32), axis=1, keepdims=True)
    at = iota(1, width, 1)
    fits = (excess <= 0.0).astype(jnp.int32)
    head = jnp.where(at == 0, total, jnp.where(at == 1, copies, jnp.where(at == 2, fits, 0)))
    out_ref[6:7, :] = head


def route(every, my_blk, my_grp, n_grp, own_tiles, tiles_held):
    n_blk, n_entries = every.shape
    n_chips = n_grp // 2
    width = max(n_chips * COUNT_CAP, (n_blk - 1) * FAR_CAP, n_chips * ITEM_CAP, LOADS)
    width = -(-width // 128) * 128
    vmem = pl.BlockSpec(memory_space=pltpu.VMEM)
    return pl.pallas_call(
        functools.partial(route_kernel, n_grp, n_entries // n_grp, own_tiles, tiles_held),
        out_shape=jax.ShapeDtypeStruct((8, width), jnp.int32),
        in_specs=[pl.BlockSpec(memory_space=pltpu.SMEM), vmem],
        out_specs=vmem,
        compiler_params=pltpu.CompilerParams(vmem_limit_bytes=16 * 2**20),
        name="route",
    )(jnp.stack([my_blk, my_grp]).astype(jnp.int32), every)


def scan_kernel(counts_ref, scaled_ref, most_ref):
    counts = counts_ref[...]
    scaled_ref[...] = (ALPHA * counts.astype(jnp.float32)).astype(jnp.bfloat16)
    most_ref[...] = jnp.max(counts, axis=1)


def scan_counts(counts):
    pairs, tile, columns = counts.shape
    block = 16
    return pl.pallas_call(
        scan_kernel,
        grid=(pairs // block,),
        out_shape=[
            jax.ShapeDtypeStruct(counts.shape, jnp.bfloat16),
            jax.ShapeDtypeStruct((pairs, columns), jnp.int32),
        ],
        in_specs=[pl.BlockSpec((block, tile, columns), lambda i: (i, 0, 0))],
        out_specs=[
            pl.BlockSpec((block, tile, columns), lambda i: (i, 0, 0)),
            pl.BlockSpec((block, columns), lambda i: (i, 0)),
        ],
        compiler_params=pltpu.CompilerParams(vmem_limit_bytes=16 * 2**20),
        name="scan_counts",
    )(counts)


def body(user_prior, item_factors, user_tiles, item_tiles, counts):
    pairs = counts.shape[0]
    tile = counts.shape[1]
    rank = item_factors.shape[1]
    n_blk = lax.axis_size("blk")
    n_grp = lax.axis_size("grp")
    n_all = n_blk * n_grp
    n_chips = n_grp // 2
    own_rows = user_prior.shape[0]
    own_tiles = own_rows // tile
    user_blocks = own_tiles * n_grp
    tiles_held = item_factors.shape[0] // tile
    my_blk = lax.axis_index("blk")
    my_grp = lax.axis_index("grp")
    my_chip = my_grp // 2
    my_core = my_grp % 2
    lanes = [[chip * 2 + core for chip in range(n_chips)] for core in range(2)]

    def swap(value):
        return lax.ppermute(value, "grp", [(i, i ^ 1) for i in range(n_grp)])

    def to_chips(value):
        return lax.all_to_all(
            value, "grp", split_axis=0, concat_axis=0, tiled=True, axis_index_groups=lanes
        )

    gram_local = lax.dot_general(
        item_factors, item_factors, (((0,), (0,)), ((), ())), preferred_element_type=jnp.float32
    )
    grp_bits, blk_bits = [[1 << n for n in range(bits_for(size))] for size in (n_grp, n_blk)]
    held = item_factors.reshape(tiles_held, tile, rank)
    held_mate = swap(held)
    scaled, column_most = scan_counts(counts)
    live = jnp.any(column_most > 0, axis=1)
    scaled_mate = swap(scaled)
    packed = (item_tiles * 2 + live.astype(jnp.int32)) * user_blocks + user_tiles
    every = lax.all_to_all(
        jnp.broadcast_to(packed, (n_all, pairs)), ("blk", "grp"), split_axis=0, concat_axis=0
    )
    table = route(every.reshape(n_blk, n_grp * pairs), my_blk, my_grp, n_grp, own_tiles, tiles_held)
    gram = gram_local
    for bit in grp_bits[1:]:
        gram = sum_with(gram, "grp", bit)
    table, gram = lax.optimization_barrier((table, gram))

    jobs = [(0, 2, 1, shift * FAR_CAP, FAR_CAP, shift, 0) for shift in range(n_blk - 1)]
    for chip in range(n_chips):
        ride = chip * RIDE
        jobs.append((2, 4, 0, chip * COUNT_CAP, COUNT_CAP, n_blk - 1, ride))
        jobs.append((0, 2, 7, chip * NEAR_CAP, NEAR_CAP, n_blk - 1, ride + COUNT_CAP))
    lengths = [FAR_CAP] * (n_blk - 1) + [n_chips * RIDE]
    *far, counts_out = pack_tiles(
        "pack_first", table, [held, held_mate, scaled, scaled_mate], lengths, jobs
    )
    far = [
        lax.ppermute(piece, "blk", [(i, (i + 1 + shift) % n_blk) for i in range(n_blk)])
        for shift, piece in enumerate(far)
    ]
    far_mate = [swap(piece) for piece in far]
    counts_own = to_chips(counts_out)

    jobs = [(0, 2 * (n_blk - 1), 2, off * ITEM_CAP, ITEM_CAP, off, 0) for off in range(n_chips)]
    items_out = pack_tiles(
        "pack_items", table, [*far, *far_mate], [ITEM_CAP] * n_chips, jobs
    )
    counts_own, gram, *items_out = lax.optimization_barrier((counts_own, gram, *items_out))
    counts_mate = swap(counts_own)
    gram = sum_with(gram, "grp", grp_bits[0])
    for bit in blk_bits:
        gram = sum_with(gram, "blk", bit)
    item_pieces = [counts_own, counts_mate]
    for off, piece in enumerate(items_out):
        if off:
            piece = lax.ppermute(piece, "grp", [(i, i ^ (2 * off)) for i in range(n_grp)])
        if off == n_chips - 1:
            piece, gram = lax.optimization_barrier((piece, gram))
        item_pieces += [piece, swap(piece)]
    by_owner = run_sweep(table, user_prior, gram, item_pieces)

    fits = table[6, 2] > 0
    return lax.cond(
        fits, lambda done, *given: done, lambda done, *given: sweep_in_place(*given),
        by_owner, user_prior, item_factors, user_tiles, item_tiles, counts, live, gram_local,
    )


def solution(mesh):
    in_specs = (
        P(("blk", "grp"), None),
        P(("blk", "grp"), None),
        P(("blk", "grp")),
        P(("blk", "grp")),
        P(("blk", "grp"), None, None),
    )
    out_specs = P(("blk", "grp"), None)
    return jax.shard_map(body, mesh=mesh, in_specs=in_specs, out_specs=out_specs, check_vma=False)
```

```python
import functools

import jax
import jax.numpy as jnp
from jax import lax
from jax.experimental import pallas as pl
from jax.experimental.pallas import tpu as pltpu
from jax.sharding import PartitionSpec as P

ITERS = 3

ALPHA = 40.0
REG = 32.0
EPS = 1e-06

FAR_CAP = 14
COUNT_CAP = 24
NEAR_CAP = 8
ITEM_CAP = 16
LOADS = 128
SPAN = 2
VMEM_GRANT = 60 * 2**20
TOGETHER = 8


def fetch_tiles(item_factors, item_tiles, pairs, tile, rank):
    n_all = lax.axis_size(("blk", "grp"))
    tiles_held = item_factors.shape[0] // tile
    slots_each = max(2, pairs // n_all)
    owner = item_tiles // tiles_held
    local_slot = item_tiles % tiles_held
    position = jnp.arange(pairs, dtype=jnp.int32)
    earlier = (owner[None, :] == owner[:, None]) & (position[None, :] < position[:, None])
    order = jnp.sum(earlier.astype(jnp.int32), axis=1)
    requests = jnp.full((n_all, slots_each), -1, jnp.int32).at[owner, order].set(local_slot)
    wanted = lax.all_to_all(requests, ("blk", "grp"), split_axis=0, concat_axis=0, tiled=True)
    held = item_factors.reshape(tiles_held, tile, rank)
    picked = jnp.take(held, jnp.maximum(wanted, 0), axis=0)
    picked = jnp.where((wanted >= 0)[:, :, None, None], picked, jnp.zeros((), picked.dtype))
    arrived = lax.all_to_all(picked, ("blk", "grp"), split_axis=0, concat_axis=0, tiled=True)
    return arrived[owner, order]


def row_sum(left, right):
    return jnp.sum(left * right, axis=1, keepdims=True)


def sweep_in_place(user_prior, item_factors, user_tiles, item_tiles, counts, live, gram_local):
    pairs = counts.shape[0]
    tile = counts.shape[1]
    rank = item_factors.shape[1]
    n_grp = lax.axis_size("grp")
    own_rows = user_prior.shape[0]
    block_rows = own_rows * n_grp
    user_blocks = block_rows // tile
    span = min(32, pairs)
    gram = lax.psum(gram_local, ("blk", "grp"))
    pair_tiles = fetch_tiles(item_factors, item_tiles, pairs, tile, rank)
    rounds = (jnp.sum(live.astype(jnp.int32)) + span - 1) // span
    tile_ids = jnp.arange(user_blocks, dtype=jnp.int32)

    def accumulate(low_tiles, with_rhs):

        def one_round(index, totals):
            start = index * span
            users = lax.dynamic_slice_in_dim(user_tiles, start, span)
            factors = lax.dynamic_slice_in_dim(pair_tiles, start, span)
            counted = lax.dynamic_slice_in_dim(counts, start, span).astype(jnp.float32)
            selector = (tile_ids[:, None] == users[None, :]).astype(jnp.float32)
            users_low = jnp.take(low_tiles, users, axis=0)
            scores = jnp.einsum(
                "bur,bir->bui", users_low, factors, preferred_element_type=jnp.float32
            )
            scaled = (ALPHA * counted * scores).astype(jnp.bfloat16)
            back = jnp.einsum("bui,bir->bur", scaled, factors, preferred_element_type=jnp.float32)
            result = [
                totals[0]
                + jnp.einsum("tb,bur->tur", selector, back, precision=lax.Precision.HIGHEST)
            ]
            if with_rhs:
                confidence = jnp.where(counted > 0, 1.0 + ALPHA * counted, 0.0).astype(jnp.bfloat16)
                pulled = jnp.einsum(
                    "bui,bir->bur", confidence, factors, preferred_element_type=jnp.float32
                )
                result.append(
                    totals[1]
                    + jnp.einsum("tb,bur->tur", selector, pulled, precision=lax.Precision.HIGHEST)
                )
            return tuple(result)

        zeros = jnp.zeros((user_blocks, tile, rank), jnp.float32)
        start_state = (zeros, zeros) if with_rhs else (zeros,)
        totals = lax.fori_loop(0, rounds, one_round, start_state)
        return tuple((total.reshape(block_rows, rank) for total in totals))

    def gram_term(vectors):
        return jnp.dot(vectors, gram, precision=lax.Precision.HIGHEST) + REG * vectors

    low = lax.all_gather(user_prior.astype(jnp.bfloat16), "grp", axis=0, tiled=True)
    pair_part, rhs_part = accumulate(low.reshape(user_blocks, tile, rank), True)
    pair_share, rhs_share = (
        lax.psum_scatter(pair_part, "grp", scatter_dimension=0, tiled=True),
        lax.psum_scatter(rhs_part, "grp", scatter_dimension=0, tiled=True),
    )
    solution = user_prior
    residual = rhs_share - (gram_term(solution) + pair_share)
    direction = residual
    norm_now = row_sum(residual, residual)
    for step in range(ITERS):
        low = lax.all_gather(direction.astype(jnp.bfloat16), "grp", axis=0, tiled=True)
        (pair_part,) = accumulate(low.reshape(user_blocks, tile, rank), False)
        image = gram_term(direction) + lax.psum_scatter(
            pair_part, "grp", scatter_dimension=0, tiled=True
        )
        alpha = norm_now / (row_sum(direction, image) + EPS)
        solution = solution + alpha * direction
        residual = residual - alpha * image
        fresh = row_sum(residual, residual)
        direction = residual + fresh / (norm_now + EPS) * direction
        norm_now = fresh
    return solution


def bits_for(n):
    return (n - 1).bit_length()


def at_source(number, row, n_sources):
    return (row << bits_for(n_sources)) + number


def move_tile(sources, at, room, place):
    bits = bits_for(len(sources))
    row = lax.shift_right_logical(at, bits)
    which = at & ((1 << bits) - 1)

    def among(lo, hi):
        if hi - lo == 1:
            room[place] = sources[lo][row]
            return
        mid = (lo + hi) // 2
        pl.when(which < mid)(lambda: among(lo, mid))
        pl.when(which >= mid)(lambda: among(mid, hi))

    among(0, len(sources))


def sweep_kernel(plan, prior_ref, gram_ref, *refs):
    weights, factors, turned, low, image, residual, direction = refs[-7:]
    count_pieces, item_pieces, out_ref = refs[:2], refs[2:-8], refs[-8]
    tile, rank = factors.shape[1:]
    n_chunks = plan[6, 0]
    halves = (n_chunks + TOGETHER // 2 - 1) // (TOGETHER // 2)
    rounds = halves // 2

    def bring(place, carry):
        count_at = plan[3, place]
        item_at = plan[4, place]

        @pl.when(count_at > 0)
        def _():
            move_tile(count_pieces, count_at - 1, weights, place)
            move_tile(item_pieces, item_at, factors, place)

        @pl.when(count_at == 0)
        def _():
            weights[place] = jnp.zeros((tile, tile), weights.dtype)
            factors[place] = jnp.zeros((tile, rank), factors.dtype)

        return carry

    lax.fori_loop(0, halves * (TOGETHER // 2 * SPAN), bring, 0)

    def pair_images(with_rhs):
        image[...] = jnp.zeros_like(image)
        if with_rhs:
            residual[...] = jnp.zeros_like(residual)

        def some(first, n):
            shares = []
            for number in range(n):
                chunk = first + number
                rows = pl.ds(pl.multiple_of(plan[5, chunk] * tile, tile), tile)
                items = factors[pl.ds(chunk * SPAN, SPAN)].reshape(SPAN * tile, rank)
                scaled = jnp.concatenate(
                    [weights[chunk * SPAN + part].astype(jnp.float32) for part in range(SPAN)],
                    axis=1,
                )
                if with_rhs:
                    turned[chunk] = items.T
                scores = jnp.dot(low[rows, :], turned[chunk], preferred_element_type=jnp.float32)
                back = jnp.dot(
                    (scaled * scores).astype(jnp.bfloat16), items,
                    preferred_element_type=jnp.float32,
                )
                pulled = None
                if with_rhs:
                    confidence = jnp.where(scaled > 0, 1.0 + scaled, 0.0).astype(jnp.bfloat16)
                    pulled = jnp.dot(confidence, items, preferred_element_type=jnp.float32)
                shares.append((rows, back, pulled))
            for rows, back, pulled in shares:
                image[rows, :] += back
                if with_rhs:
                    residual[rows, :] += pulled

        def one_round(step, carry):
            some(step * TOGETHER, TOGETHER)
            return carry

        lax.fori_loop(0, rounds, one_round, 0)
        pl.when(halves % 2 == 1)(lambda: some(rounds * TOGETHER, TOGETHER // 2))

    def gram_term(vectors):
        return jnp.dot(
            vectors, gram_ref[...], precision=lax.Precision.HIGHEST,
            preferred_element_type=jnp.float32,
        ) + REG * vectors

    prior = prior_ref[...]
    low[...] = prior.astype(jnp.bfloat16)
    pair_images(True)
    first = residual[...] - (gram_term(prior) + image[...])
    residual[...] = first
    direction[...] = first
    out_ref[...] = prior
    norm_now = row_sum(first, first)
    for step in range(ITERS):
        heading = direction[...]
        low[...] = heading.astype(jnp.bfloat16)
        pair_images(False)
        shown = gram_term(heading) + image[...]
        alpha = norm_now / (row_sum(heading, shown) + EPS)
        out_ref[...] += alpha * heading
        if step < ITERS - 1:
            left = residual[...] - alpha * shown
            residual[...] = left
            fresh = row_sum(left, left)
            direction[...] = left + (fresh / (norm_now + EPS)) * heading
            norm_now = fresh


def run_sweep(plan, user_prior, gram, count_pieces, item_pieces):
    own_rows, rank = user_prior.shape
    tile = count_pieces[0].shape[1]
    pieces = [*count_pieces, *item_pieces]
    vmem = pl.BlockSpec(memory_space=pltpu.VMEM)
    return pl.pallas_call(
        sweep_kernel,
        out_shape=jax.ShapeDtypeStruct((own_rows, rank), jnp.float32),
        in_specs=[pl.BlockSpec(memory_space=pltpu.SMEM)] + [vmem] * (2 + len(pieces)),
        out_specs=vmem,
        scratch_shapes=[
            pltpu.VMEM((LOADS, tile, tile), jnp.bfloat16),
            pltpu.VMEM((LOADS, tile, rank), jnp.bfloat16),
            pltpu.VMEM((LOADS // SPAN, rank, SPAN * tile), jnp.bfloat16),
            pltpu.VMEM((own_rows, rank), jnp.bfloat16),
            pltpu.VMEM((own_rows, rank), jnp.float32),
            pltpu.VMEM((own_rows, rank), jnp.float32),
            pltpu.VMEM((own_rows, rank), jnp.float32),
        ],
        compiler_params=pltpu.CompilerParams(vmem_limit_bytes=32 * 2**20),
        name="sweep",
    )(plan, user_prior, gram, *pieces)


def pack_kernel(n_sources, n_outs, jobs, table, *refs):
    sources, refs = refs[:n_sources], refs[n_sources:]
    outs, rooms, written = refs[:n_outs], refs[n_outs:-1], refs[-1]
    copies = []
    for number, (lo, hi, row, start, length, out, first) in enumerate(jobs):

        def place(spot, carry, number=number, lo=lo, hi=hi, row=row, start=start):
            move_tile(sources[lo:hi], table[row, start + spot], rooms[number], spot)
            return carry

        lax.fori_loop(0, length, place, 0, unroll=2)
        target = outs[out].at[pl.ds(first, length)]
        copies.append(pltpu.make_async_copy(rooms[number], target, written.at[number]))
        copies[-1].start()
    for copy in copies:
        copy.wait()


def pack_tiles(name, table, sources, lengths, jobs):
    anywhere = pl.BlockSpec(memory_space=pl.ANY)
    kind = sources[0].dtype
    shape = sources[0].shape[1:]
    return pl.pallas_call(
        functools.partial(pack_kernel, len(sources), len(lengths), jobs),
        out_shape=[jax.ShapeDtypeStruct((n, *shape), kind) for n in lengths],
        in_specs=[pl.BlockSpec(memory_space=pltpu.SMEM)]
        + [pl.BlockSpec(memory_space=pltpu.VMEM)] * len(sources),
        out_specs=[anywhere] * len(lengths),
        scratch_shapes=[pltpu.VMEM((job[4], *shape), kind) for job in jobs]
        + [pltpu.SemaphoreType.DMA((len(jobs),))],
        compiler_params=pltpu.CompilerParams(vmem_limit_bytes=VMEM_GRANT),
        name=name,
    )(table, *sources)


def sum_with(value, axis, bit):
    size = lax.axis_size(axis)
    return value + lax.ppermute(value, axis, [(i, i ^ bit) for i in range(size)])


def iota(rows, columns, axis):
    return lax.broadcasted_iota(jnp.int32, (rows, columns), axis)


def dot_nt(left, right):
    return lax.dot_general(
        left.astype(jnp.bfloat16), right.astype(jnp.bfloat16), (((1,), (1,)), ((), ())),
        preferred_element_type=jnp.float32,
    )


def choose(key, hit, cells, *values):
    match = hit & (key == iota(cells, key.shape[1], 0))
    row = iota(8, key.shape[1], 0)
    digits = jnp.zeros((8, key.shape[1]), jnp.int32)
    for number, value in enumerate(values):
        digits = jnp.where(row == 2 * number, value & 31, digits)
        digits = jnp.where(row == 2 * number + 1, lax.shift_right_logical(value, 5), digits)
    found = dot_nt(digits.astype(jnp.float32), match.astype(jnp.float32)).astype(jnp.int32)
    return [
        found[2 * number:2 * number + 1] + 32 * found[2 * number + 1:2 * number + 2]
        for number in range(len(values))
    ]


def route_kernel(n_grp, pairs, own_tiles, tiles_held, spot, every_ref, out_ref):
    n_blk, n_entries = every_ref.shape
    width = out_ref.shape[1]
    n_chips = n_grp // 2
    user_blocks = n_grp * own_tiles
    all_chips = n_blk * n_chips
    pad = lambda n: -(-n // 8) * 8
    my_blk, my_grp = spot[0], spot[1]
    my_chip = lax.shift_right_logical(my_grp, 1)
    my_core = my_grp & 1
    index = iota(1, n_entries, 1)
    source = lax.shift_right_logical(index, bits_for(pairs))
    from_chip = lax.shift_right_logical(source, 1)
    one_hot = lambda key, n: key == iota(pad(n), n_entries, 0)

    def fields(packed):
        user = packed & (user_blocks - 1)
        packed = lax.shift_right_logical(packed, bits_for(user_blocks))
        live = (packed & 1) == 1
        item = lax.shift_right_logical(packed, 1)
        held = item & (2 * tiles_held - 1)
        chip = lax.shift_right_logical(item, bits_for(2 * tiles_held))
        return user, live, chip, held

    ids = iota(1, 2 * tiles_held, 1)
    fewer = iota(2 * tiles_held, 2 * tiles_held, 0) > iota(2 * tiles_held, 2 * tiles_held, 1)

    def needs(live, chip, held):
        on_chip = one_hot(chip, all_chips) & live
        on_tile = one_hot(held, 2 * tiles_held)
        needed = dot_nt(on_chip.astype(jnp.float32), on_tile.astype(jnp.float32)) > 0
        return on_chip, on_tile, needed, dot_nt(needed.astype(jnp.float32), fewer.astype(jnp.float32))

    excess = jnp.zeros((1, 1), jnp.float32)
    worst = lambda loads, room: jnp.max(loads, axis=(0, 1), keepdims=True) - room
    asked = jnp.zeros((1, width), jnp.int32)
    here = my_blk * n_chips + my_chip
    chip_row = iota(pad(all_chips), 2 * tiles_held, 0)
    for blk in range(n_blk):
        user, live, chip, held = fields(every_ref[blk:blk + 1, :])
        _, _, needed, ahead = needs(live, chip, held)
        away = lax.shift_right_logical(chip_row, bits_for(n_chips)) != blk
        asks = jnp.sum((needed & away).astype(jnp.float32), axis=1, keepdims=True)
        excess = jnp.maximum(excess, worst(asks, 2 * FAR_CAP))
        to_chip = lax.shift_right_logical(user, bits_for(own_tiles) + 1)
        to = one_hot(to_chip, n_chips).astype(jnp.float32)
        column = chip & (n_chips - 1)
        near = lax.shift_right_logical(chip, bits_for(n_chips)) == blk
        for key, inside, cap in (
            (from_chip, live, COUNT_CAP),
            (column, live & near, NEAR_CAP),
            (column, live & ~near, ITEM_CAP),
        ):
            loads = dot_nt((one_hot(key, n_chips) & inside).astype(jnp.float32), to)
            excess = jnp.maximum(excess, worst(loads, 2 * cap))
        loads = jnp.sum(
            (one_hot(user, user_blocks) & live).astype(jnp.int32), axis=1, keepdims=True
        )
        chunks = lax.shift_right_logical(loads + SPAN - 1, bits_for(SPAN)).astype(jnp.float32)
        owners = iota(pad(n_grp), pad(user_blocks), 1)
        owners = lax.shift_right_logical(owners, bits_for(own_tiles)) == iota(*owners.shape, 0)
        loads = jnp.dot(
            owners.astype(jnp.float32), jnp.broadcast_to(chunks, (chunks.shape[0], 128)),
            precision=lax.Precision.HIGHEST, preferred_element_type=jnp.float32,
        )
        excess = jnp.maximum(excess, worst(loads, LOADS // SPAN))

        mine = chip_row == here
        present = jnp.sum((needed & mine).astype(jnp.int32), axis=0, keepdims=True)
        place = jnp.sum(jnp.where(mine, ahead, 0.0), axis=0, keepdims=True).astype(jnp.int32)
        shift = (blk + n_blk - my_blk) & (n_blk - 1)
        spot_at = lax.shift_right_logical(place, 1)
        hit = (present > 0) & ((place & 1) == my_core) & (spot_at < FAR_CAP) & (shift > 0)
        value = at_source(
            lax.shift_right_logical(ids, bits_for(tiles_held)) ^ my_core, ids & (tiles_held - 1), 2
        )
        (found,) = choose((shift - 1) * FAR_CAP + spot_at, hit, width, value)
        asked = asked + found

    user, live, chip, held = fields(every_ref[pl.ds(my_blk, 1), :])
    on_chip, on_tile, _, ahead = needs(live, chip, held)
    places = jnp.dot(
        ahead.astype(jnp.bfloat16), on_tile.astype(jnp.float32).astype(jnp.bfloat16),
        preferred_element_type=jnp.float32,
    )
    far_place = jnp.sum(jnp.where(on_chip, places, 0.0), axis=0, keepdims=True).astype(jnp.int32)
    far_place = jnp.minimum(far_place, 2 * FAR_CAP - 1)
    owner = lax.shift_right_logical(user, bits_for(own_tiles))
    local_user = user & (own_tiles - 1)
    to_chip = lax.shift_right_logical(owner, 1)
    column = chip & (n_chips - 1)
    to_me = live & (owner == my_grp)
    shift = (my_blk + n_blk - lax.shift_right_logical(chip, bits_for(n_chips))) & (n_blk - 1)
    near, far = live & (shift == 0), live & (shift > 0)
    in_tile = one_hot(local_user, own_tiles) & to_me
    groups = [
        one_hot(from_chip, n_chips) & (live & (to_chip == my_chip)),
        one_hot(to_chip, n_chips) & (near & (column == my_chip)),
        one_hot(column, n_chips) & (near & (to_chip == my_chip)),
        one_hot(to_chip, n_chips) & (far & (column == my_chip)),
        one_hot(column, n_chips) & (far & (to_chip == my_chip)),
        in_tile,
    ]
    before = (iota(n_entries, n_entries, 0) < iota(n_entries, n_entries, 1)).astype(jnp.float32)
    before = before.astype(jnp.bfloat16)
    ranks = []
    for marks in groups:
        earlier = jnp.dot(
            marks.astype(jnp.float32).astype(jnp.bfloat16), before,
            preferred_element_type=jnp.float32,
        )
        earlier = jnp.sum(jnp.where(marks, earlier, 0.0), axis=0, keepdims=True)
        ranks.append(earlier.astype(jnp.int32))
    counts_back, near_out, near_back, far_out, far_back, user_rank = ranks

    half = lambda rank: lax.shift_right_logical(rank, 1)
    sent = lambda rank, cap: live & ((rank & 1) == my_core) & (half(rank) < cap)
    back = lambda rank, cap: jnp.minimum(half(rank), cap - 1)
    core = lambda rank: (rank & 1) ^ my_core
    out_ref[0:1, :] = jnp.zeros((1, width), jnp.int32)
    out_ref[1:2, :] = asked
    (out_ref[7:8, :],) = choose(
        to_chip * NEAR_CAP + half(near_out), near & (column == my_chip) & sent(near_out, NEAR_CAP),
        width,
        at_source(
            lax.shift_right_logical(held, bits_for(tiles_held)) ^ my_core, held & (tiles_held - 1), 2
        ),
    )
    (out_ref[2:3, :],) = choose(
        (to_chip ^ my_chip) * ITEM_CAP + half(far_out),
        far & (column == my_chip) & sent(far_out, ITEM_CAP), width,
        at_source(
            core(far_place) * (n_blk - 1) + shift - 1, half(far_place), 2 * (n_blk - 1)
        ),
    )

    loads = jnp.sum(in_tile.astype(jnp.int32), axis=1, keepdims=True)
    chunks = lax.shift_right_logical(loads + SPAN - 1, bits_for(SPAN)).astype(jnp.float32)
    rows = chunks.shape[0]
    ends = jnp.dot(
        (iota(rows, rows, 0) >= iota(rows, rows, 1)).astype(jnp.float32),
        jnp.broadcast_to(chunks, (rows, 128)),
        precision=lax.Precision.HIGHEST, preferred_element_type=jnp.float32,
    )
    firsts = ends[:, :1] - chunks
    room_at = jnp.sum(jnp.where(in_tile, firsts * SPAN, 0.0), axis=0, keepdims=True)
    room_at = room_at.astype(jnp.int32) + user_rank
    hit = to_me & (room_at < LOADS)
    count_at = at_source(
        core(counts_back), from_chip * COUNT_CAP + back(counts_back, COUNT_CAP), 2
    )
    n_sources = 2 + 2 * n_chips
    item_at = jnp.where(
        shift == 0,
        at_source(
            core(near_back), column * NEAR_CAP + back(near_back, NEAR_CAP), n_sources
        ),
        at_source(
            2 + (column ^ my_chip) * 2 + core(far_back), back(far_back, ITEM_CAP), n_sources
        ),
    )
    out_ref[3:4, :], out_ref[4:5, :] = choose(room_at, hit, width, count_at + 1, item_at)
    passed = (iota(rows, width, 1).astype(jnp.float32) >= ends[:, :1]) & (
        iota(rows, width, 0) < own_tiles - 1
    )
    out_ref[5:6, :] = jnp.sum(passed.astype(jnp.int32), axis=0, keepdims=True)
    total = ends[own_tiles - 1:own_tiles, :1].astype(jnp.int32)
    total = jnp.minimum(total, LOADS // SPAN)
    copies = jnp.sum(hit.astype(jnp.int32), axis=1, keepdims=True)
    at = iota(1, width, 1)
    fits = (excess <= 0.0).astype(jnp.int32)
    head = jnp.where(at == 0, total, jnp.where(at == 1, copies, jnp.where(at == 2, fits, 0)))
    out_ref[6:7, :] = head


def route_counts_kernel(n_grp, own_tiles, spot, entries_ref, out_ref):
    n_entries = entries_ref.shape[1]
    n_chips = n_grp // 2
    pairs = n_entries // 2
    my_core = spot[0]
    packed = entries_ref[...]
    user = packed & (n_grp * own_tiles - 1)
    live = (lax.shift_right_logical(packed, bits_for(n_grp * own_tiles)) & 1) == 1
    to_chip = lax.shift_right_logical(user, bits_for(own_tiles) + 1)
    marks = (to_chip == iota(-(-n_chips // 8) * 8, n_entries, 0)) & live
    before = (iota(n_entries, n_entries, 0) < iota(n_entries, n_entries, 1)).astype(jnp.float32)
    earlier = jnp.dot(
        marks.astype(jnp.float32).astype(jnp.bfloat16), before.astype(jnp.bfloat16),
        preferred_element_type=jnp.float32,
    )
    rank = jnp.sum(jnp.where(marks, earlier, 0.0), axis=0, keepdims=True).astype(jnp.int32)
    half = lax.shift_right_logical(rank, 1)
    index = iota(1, n_entries, 1)
    (chosen,) = choose(
        to_chip * COUNT_CAP + half, live & ((rank & 1) == my_core) & (half < COUNT_CAP),
        out_ref.shape[1],
        at_source(lax.shift_right_logical(index, bits_for(pairs)) ^ my_core, index & (pairs - 1), 2),
    )
    out_ref[...] = jnp.broadcast_to(chosen, out_ref.shape)


def route_counts(entries, my_core, n_grp, own_tiles):
    width = -(-n_grp // 2 * COUNT_CAP // 128) * 128
    vmem = pl.BlockSpec(memory_space=pltpu.VMEM)
    return pl.pallas_call(
        functools.partial(route_counts_kernel, n_grp, own_tiles),
        out_shape=jax.ShapeDtypeStruct((8, width), jnp.int32),
        in_specs=[pl.BlockSpec(memory_space=pltpu.SMEM), vmem],
        out_specs=vmem,
        compiler_params=pltpu.CompilerParams(vmem_limit_bytes=16 * 2**20),
        name="route_counts",
    )(jnp.reshape(my_core, (1,)).astype(jnp.int32), entries)


def route(every, my_blk, my_grp, n_grp, own_tiles, tiles_held):
    n_blk, n_entries = every.shape
    n_chips = n_grp // 2
    width = max((n_blk - 1) * FAR_CAP, n_chips * ITEM_CAP, LOADS)
    width = -(-width // 128) * 128
    vmem = pl.BlockSpec(memory_space=pltpu.VMEM)
    return pl.pallas_call(
        functools.partial(route_kernel, n_grp, n_entries // n_grp, own_tiles, tiles_held),
        out_shape=jax.ShapeDtypeStruct((8, width), jnp.int32),
        in_specs=[pl.BlockSpec(memory_space=pltpu.SMEM), vmem],
        out_specs=vmem,
        compiler_params=pltpu.CompilerParams(vmem_limit_bytes=16 * 2**20),
        name="route",
    )(jnp.stack([my_blk, my_grp]).astype(jnp.int32), every)


def scan_kernel(counts_ref, scaled_ref, most_ref):
    counts = counts_ref[...]
    scaled_ref[...] = (ALPHA * counts.astype(jnp.float32)).astype(jnp.bfloat16)
    most_ref[...] = jnp.max(counts, axis=1)


def scan_counts(counts):
    pairs, tile, columns = counts.shape
    block = 16
    return pl.pallas_call(
        scan_kernel,
        grid=(pairs // block,),
        out_shape=[
            jax.ShapeDtypeStruct(counts.shape, jnp.bfloat16),
            jax.ShapeDtypeStruct((pairs, columns), jnp.int32),
        ],
        in_specs=[pl.BlockSpec((block, tile, columns), lambda i: (i, 0, 0))],
        out_specs=[
            pl.BlockSpec((block, tile, columns), lambda i: (i, 0, 0)),
            pl.BlockSpec((block, columns), lambda i: (i, 0)),
        ],
        compiler_params=pltpu.CompilerParams(vmem_limit_bytes=16 * 2**20),
        name="scan_counts",
    )(counts)


def body(user_prior, item_factors, user_tiles, item_tiles, counts):
    pairs = counts.shape[0]
    tile = counts.shape[1]
    rank = item_factors.shape[1]
    n_blk = lax.axis_size("blk")
    n_grp = lax.axis_size("grp")
    n_all = n_blk * n_grp
    n_chips = n_grp // 2
    own_rows = user_prior.shape[0]
    own_tiles = own_rows // tile
    user_blocks = own_tiles * n_grp
    tiles_held = item_factors.shape[0] // tile
    my_blk = lax.axis_index("blk")
    my_grp = lax.axis_index("grp")
    my_chip = my_grp // 2
    my_core = my_grp % 2
    lanes = [[chip * 2 + core for chip in range(n_chips)] for core in range(2)]

    def swap(value):
        return lax.ppermute(value, "grp", [(i, i ^ 1) for i in range(n_grp)])

    def to_chips(value):
        return lax.all_to_all(
            value, "grp", split_axis=0, concat_axis=0, tiled=True, axis_index_groups=lanes
        )

    gram_local = lax.dot_general(
        item_factors, item_factors, (((0,), (0,)), ((), ())), preferred_element_type=jnp.float32
    )
    grp_bits, blk_bits = [[1 << n for n in range(bits_for(size))] for size in (n_grp, n_blk)]
    held = item_factors.reshape(tiles_held, tile, rank)
    held_mate = swap(held)
    scaled, column_most = scan_counts(counts)
    live = jnp.any(column_most > 0, axis=1)
    scaled_mate = swap(scaled)
    packed = (item_tiles * 2 + live.astype(jnp.int32)) * user_blocks + user_tiles
    every = lax.all_to_all(
        jnp.broadcast_to(packed, (n_all, pairs)), ("blk", "grp"), split_axis=0, concat_axis=0
    )
    packed_mate = swap(packed)
    first, second = jnp.where(my_core == 0, packed, packed_mate), jnp.where(my_core == 0, packed_mate, packed)
    entries = jnp.concatenate([first, second]).reshape(1, 2 * pairs)
    count_table = route_counts(entries, my_core, n_grp, own_tiles)
    jobs = [(0, 2, 0, chip * COUNT_CAP, COUNT_CAP, 0, chip * COUNT_CAP) for chip in range(n_chips)]
    (counts_out,) = pack_tiles(
        "pack_counts", count_table, [scaled, scaled_mate], [n_chips * COUNT_CAP], jobs
    )
    every, counts_out = lax.optimization_barrier((every, counts_out))
    counts_own = to_chips(counts_out)
    table = route(every.reshape(n_blk, n_grp * pairs), my_blk, my_grp, n_grp, own_tiles, tiles_held)
    gram = gram_local
    for bit in grp_bits[1:]:
        gram = sum_with(gram, "grp", bit)
    table, gram = lax.optimization_barrier((table, gram))

    jobs = [(0, 2, 1, shift * FAR_CAP, FAR_CAP, shift, 0) for shift in range(n_blk - 1)]
    for chip in range(n_chips):
        jobs.append((0, 2, 7, chip * NEAR_CAP, NEAR_CAP, n_blk - 1, chip * NEAR_CAP))
    lengths = [FAR_CAP] * (n_blk - 1) + [n_chips * NEAR_CAP]
    *far, near_out = pack_tiles("pack_first", table, [held, held_mate], lengths, jobs)
    far = [
        lax.ppermute(piece, "blk", [(i, (i + 1 + shift) % n_blk) for i in range(n_blk)])
        for shift, piece in enumerate(far)
    ]
    far_mate = [swap(piece) for piece in far]
    near_out, counts_own = lax.optimization_barrier((near_out, counts_own))
    counts_mate = swap(counts_own)
    near_own = to_chips(near_out)

    jobs = [(0, 2 * (n_blk - 1), 2, off * ITEM_CAP, ITEM_CAP, off, 0) for off in range(n_chips)]
    items_out = pack_tiles(
        "pack_items", table, [*far, *far_mate], [ITEM_CAP] * n_chips, jobs
    )
    gram, *items_out = lax.optimization_barrier((gram, *items_out))
    gram = sum_with(gram, "grp", grp_bits[0])
    for bit in blk_bits:
        gram = sum_with(gram, "blk", bit)
    item_pieces = []
    for off, piece in enumerate(items_out):
        if off:
            piece = lax.ppermute(piece, "grp", [(i, i ^ (2 * off)) for i in range(n_grp)])
        if off == 1:
            piece, near_own = lax.optimization_barrier((piece, near_own))
        if off == n_chips - 1:
            piece, gram = lax.optimization_barrier((piece, gram))
        item_pieces += [piece, swap(piece)]
    near = [near_own, swap(near_own)]
    by_owner = run_sweep(table, user_prior, gram, [counts_own, counts_mate], near + item_pieces)

    fits = table[6, 2] > 0
    return lax.cond(
        fits, lambda done, *given: done, lambda done, *given: sweep_in_place(*given),
        by_owner, user_prior, item_factors, user_tiles, item_tiles, counts, live, gram_local,
    )


def solution(mesh):
    in_specs = (
        P(("blk", "grp"), None),
        P(("blk", "grp"), None),
        P(("blk", "grp")),
        P(("blk", "grp")),
        P(("blk", "grp"), None, None),
    )
    out_specs = P(("blk", "grp"), None)
    return jax.shard_map(body, mesh=mesh, in_specs=in_specs, out_specs=out_specs, check_vma=False)
```

```python
import functools

import jax
import jax.numpy as jnp
from jax import lax
from jax.experimental import pallas as pl
from jax.experimental.pallas import tpu as pltpu
from jax.sharding import PartitionSpec as P

ITERS = 3

ALPHA = 40.0
REG = 32.0
EPS = 1e-06

FAR_CAP = 14
COUNT_CAP = 24
NEAR_CAP = 8
ITEM_CAP = 16
LOADS = 128
SPAN = 2
VMEM_GRANT = 60 * 2**20
TOGETHER = 8


def fetch_tiles(item_factors, item_tiles, pairs, tile, rank):
    n_all = lax.axis_size(("blk", "grp"))
    tiles_held = item_factors.shape[0] // tile
    slots_each = max(2, pairs // n_all)
    owner = item_tiles // tiles_held
    local_slot = item_tiles % tiles_held
    position = jnp.arange(pairs, dtype=jnp.int32)
    earlier = (owner[None, :] == owner[:, None]) & (position[None, :] < position[:, None])
    order = jnp.sum(earlier.astype(jnp.int32), axis=1)
    requests = jnp.full((n_all, slots_each), -1, jnp.int32).at[owner, order].set(local_slot)
    wanted = lax.all_to_all(requests, ("blk", "grp"), split_axis=0, concat_axis=0, tiled=True)
    held = item_factors.reshape(tiles_held, tile, rank)
    picked = jnp.take(held, jnp.maximum(wanted, 0), axis=0)
    picked = jnp.where((wanted >= 0)[:, :, None, None], picked, jnp.zeros((), picked.dtype))
    arrived = lax.all_to_all(picked, ("blk", "grp"), split_axis=0, concat_axis=0, tiled=True)
    return arrived[owner, order]


def row_sum(left, right):
    return jnp.sum(left * right, axis=1, keepdims=True)


def sweep_in_place(user_prior, item_factors, user_tiles, item_tiles, counts, live, gram_local):
    pairs = counts.shape[0]
    tile = counts.shape[1]
    rank = item_factors.shape[1]
    n_grp = lax.axis_size("grp")
    own_rows = user_prior.shape[0]
    block_rows = own_rows * n_grp
    user_blocks = block_rows // tile
    span = min(32, pairs)
    gram = lax.psum(gram_local, ("blk", "grp"))
    pair_tiles = fetch_tiles(item_factors, item_tiles, pairs, tile, rank)
    rounds = (jnp.sum(live.astype(jnp.int32)) + span - 1) // span
    tile_ids = jnp.arange(user_blocks, dtype=jnp.int32)

    def accumulate(low_tiles, with_rhs):

        def one_round(index, totals):
            start = index * span
            users = lax.dynamic_slice_in_dim(user_tiles, start, span)
            factors = lax.dynamic_slice_in_dim(pair_tiles, start, span)
            counted = lax.dynamic_slice_in_dim(counts, start, span).astype(jnp.float32)
            selector = (tile_ids[:, None] == users[None, :]).astype(jnp.float32)
            users_low = jnp.take(low_tiles, users, axis=0)
            scores = jnp.einsum(
                "bur,bir->bui", users_low, factors, preferred_element_type=jnp.float32
            )
            scaled = (ALPHA * counted * scores).astype(jnp.bfloat16)
            back = jnp.einsum("bui,bir->bur", scaled, factors, preferred_element_type=jnp.float32)
            result = [
                totals[0]
                + jnp.einsum("tb,bur->tur", selector, back, precision=lax.Precision.HIGHEST)
            ]
            if with_rhs:
                confidence = jnp.where(counted > 0, 1.0 + ALPHA * counted, 0.0).astype(jnp.bfloat16)
                pulled = jnp.einsum(
                    "bui,bir->bur", confidence, factors, preferred_element_type=jnp.float32
                )
                result.append(
                    totals[1]
                    + jnp.einsum("tb,bur->tur", selector, pulled, precision=lax.Precision.HIGHEST)
                )
            return tuple(result)

        zeros = jnp.zeros((user_blocks, tile, rank), jnp.float32)
        start_state = (zeros, zeros) if with_rhs else (zeros,)
        totals = lax.fori_loop(0, rounds, one_round, start_state)
        return tuple((total.reshape(block_rows, rank) for total in totals))

    def gram_term(vectors):
        return jnp.dot(vectors, gram, precision=lax.Precision.HIGHEST) + REG * vectors

    low = lax.all_gather(user_prior.astype(jnp.bfloat16), "grp", axis=0, tiled=True)
    pair_part, rhs_part = accumulate(low.reshape(user_blocks, tile, rank), True)
    pair_share, rhs_share = (
        lax.psum_scatter(pair_part, "grp", scatter_dimension=0, tiled=True),
        lax.psum_scatter(rhs_part, "grp", scatter_dimension=0, tiled=True),
    )
    solution = user_prior
    residual = rhs_share - (gram_term(solution) + pair_share)
    direction = residual
    norm_now = row_sum(residual, residual)
    for step in range(ITERS):
        low = lax.all_gather(direction.astype(jnp.bfloat16), "grp", axis=0, tiled=True)
        (pair_part,) = accumulate(low.reshape(user_blocks, tile, rank), False)
        image = gram_term(direction) + lax.psum_scatter(
            pair_part, "grp", scatter_dimension=0, tiled=True
        )
        alpha = norm_now / (row_sum(direction, image) + EPS)
        solution = solution + alpha * direction
        residual = residual - alpha * image
        fresh = row_sum(residual, residual)
        direction = residual + fresh / (norm_now + EPS) * direction
        norm_now = fresh
    return solution


def bits_for(n):
    return (n - 1).bit_length()


def at_source(number, row, n_sources):
    return (row << bits_for(n_sources)) + number


def move_tile(sources, at, room, place):
    bits = bits_for(len(sources))
    row = lax.shift_right_logical(at, bits)
    which = at & ((1 << bits) - 1)

    def among(lo, hi):
        if hi - lo == 1:
            room[place] = sources[lo][row]
            return
        mid = (lo + hi) // 2
        pl.when(which < mid)(lambda: among(lo, mid))
        pl.when(which >= mid)(lambda: among(mid, hi))

    among(0, len(sources))


def sweep_kernel(plan, prior_ref, gram_ref, *refs):
    weights, factors, turned, low, image, residual, direction = refs[-7:]
    count_pieces, item_pieces, out_ref = refs[:2], refs[2:-8], refs[-8]
    tile, rank = factors.shape[1:]
    n_chunks = plan[6, 0]
    halves = (n_chunks + TOGETHER // 2 - 1) // (TOGETHER // 2)
    rounds = halves // 2

    def bring(place, carry):
        count_at = plan[3, place]
        item_at = plan[4, place]

        @pl.when(count_at > 0)
        def _():
            move_tile(count_pieces, count_at - 1, weights, place)
            move_tile(item_pieces, item_at, factors, place)

        @pl.when(count_at == 0)
        def _():
            weights[place] = jnp.zeros((tile, tile), weights.dtype)
            factors[place] = jnp.zeros((tile, rank), factors.dtype)

        return carry

    lax.fori_loop(0, halves * (TOGETHER // 2 * SPAN), bring, 0)

    def pair_images(with_rhs):
        image[...] = jnp.zeros_like(image)
        if with_rhs:
            residual[...] = jnp.zeros_like(residual)

        def some(first, n):
            shares = []
            for number in range(n):
                chunk = first + number
                rows = pl.ds(pl.multiple_of(plan[5, chunk] * tile, tile), tile)
                items = factors[pl.ds(chunk * SPAN, SPAN)].reshape(SPAN * tile, rank)
                scaled = jnp.concatenate(
                    [weights[chunk * SPAN + part].astype(jnp.float32) for part in range(SPAN)],
                    axis=1,
                )
                if with_rhs:
                    turned[chunk] = items.T
                scores = jnp.dot(low[rows, :], turned[chunk], preferred_element_type=jnp.float32)
                back = jnp.dot(
                    (scaled * scores).astype(jnp.bfloat16), items,
                    preferred_element_type=jnp.float32,
                )
                pulled = None
                if with_rhs:
                    confidence = jnp.where(scaled > 0, 1.0 + scaled, 0.0).astype(jnp.bfloat16)
                    pulled = jnp.dot(confidence, items, preferred_element_type=jnp.float32)
                shares.append((rows, back, pulled))
            for rows, back, pulled in shares:
                image[rows, :] += back
                if with_rhs:
                    residual[rows, :] += pulled

        def one_round(step, carry):
            some(step * TOGETHER, TOGETHER)
            return carry

        lax.fori_loop(0, rounds, one_round, 0)
        pl.when(halves % 2 == 1)(lambda: some(rounds * TOGETHER, TOGETHER // 2))

    def gram_term(vectors):
        return jnp.dot(
            vectors, gram_ref[...], precision=lax.Precision.HIGHEST,
            preferred_element_type=jnp.float32,
        ) + REG * vectors

    prior = prior_ref[...]
    low[...] = prior.astype(jnp.bfloat16)
    pair_images(True)
    first = residual[...] - (gram_term(prior) + image[...])
    residual[...] = first
    direction[...] = first
    out_ref[...] = prior
    norm_now = row_sum(first, first)
    for step in range(ITERS):
        heading = direction[...]
        low[...] = heading.astype(jnp.bfloat16)
        pair_images(False)
        shown = gram_term(heading) + image[...]
        alpha = norm_now / (row_sum(heading, shown) + EPS)
        out_ref[...] += alpha * heading
        if step < ITERS - 1:
            left = residual[...] - alpha * shown
            residual[...] = left
            fresh = row_sum(left, left)
            direction[...] = left + (fresh / (norm_now + EPS)) * heading
            norm_now = fresh


def run_sweep(plan, user_prior, gram, count_pieces, item_pieces):
    own_rows, rank = user_prior.shape
    tile = count_pieces[0].shape[1]
    pieces = [*count_pieces, *item_pieces]
    vmem = pl.BlockSpec(memory_space=pltpu.VMEM)
    return pl.pallas_call(
        sweep_kernel,
        out_shape=jax.ShapeDtypeStruct((own_rows, rank), jnp.float32),
        in_specs=[pl.BlockSpec(memory_space=pltpu.SMEM)] + [vmem] * (2 + len(pieces)),
        out_specs=vmem,
        scratch_shapes=[
            pltpu.VMEM((LOADS, tile, tile), jnp.bfloat16),
            pltpu.VMEM((LOADS, tile, rank), jnp.bfloat16),
            pltpu.VMEM((LOADS // SPAN, rank, SPAN * tile), jnp.bfloat16),
            pltpu.VMEM((own_rows, rank), jnp.bfloat16),
            pltpu.VMEM((own_rows, rank), jnp.float32),
            pltpu.VMEM((own_rows, rank), jnp.float32),
            pltpu.VMEM((own_rows, rank), jnp.float32),
        ],
        compiler_params=pltpu.CompilerParams(vmem_limit_bytes=32 * 2**20),
        name="sweep",
    )(plan, user_prior, gram, *pieces)


def pack_kernel(n_sources, n_outs, jobs, table, *refs):
    sources, refs = refs[:n_sources], refs[n_sources:]
    outs, rooms, written = refs[:n_outs], refs[n_outs:-1], refs[-1]
    copies = []
    for number, (lo, hi, row, start, length, out, first) in enumerate(jobs):

        def place(spot, carry, number=number, lo=lo, hi=hi, row=row, start=start):
            move_tile(sources[lo:hi], table[row, start + spot], rooms[number], spot)
            return carry

        lax.fori_loop(0, length, place, 0, unroll=2)
        target = outs[out].at[pl.ds(first, length)]
        copies.append(pltpu.make_async_copy(rooms[number], target, written.at[number]))
        copies[-1].start()
    for copy in copies:
        copy.wait()


def pack_tiles(name, table, sources, lengths, jobs):
    anywhere = pl.BlockSpec(memory_space=pl.ANY)
    kind = sources[0].dtype
    shape = sources[0].shape[1:]
    return pl.pallas_call(
        functools.partial(pack_kernel, len(sources), len(lengths), jobs),
        out_shape=[jax.ShapeDtypeStruct((n, *shape), kind) for n in lengths],
        in_specs=[pl.BlockSpec(memory_space=pltpu.SMEM)]
        + [pl.BlockSpec(memory_space=pltpu.VMEM)] * len(sources),
        out_specs=[anywhere] * len(lengths),
        scratch_shapes=[pltpu.VMEM((job[4], *shape), kind) for job in jobs]
        + [pltpu.SemaphoreType.DMA((len(jobs),))],
        compiler_params=pltpu.CompilerParams(vmem_limit_bytes=VMEM_GRANT),
        name=name,
    )(table, *sources)


def sum_with(value, axis, bit):
    size = lax.axis_size(axis)
    return value + lax.ppermute(value, axis, [(i, i ^ bit) for i in range(size)])


def iota(rows, columns, axis):
    return lax.broadcasted_iota(jnp.int32, (rows, columns), axis)


def dot_nt(left, right):
    return lax.dot_general(
        left.astype(jnp.bfloat16), right.astype(jnp.bfloat16), (((1,), (1,)), ((), ())),
        preferred_element_type=jnp.float32,
    )


def choose(key, hit, cells, *values):
    match = hit & (key == iota(cells, key.shape[1], 0))
    row = iota(8, key.shape[1], 0)
    digits = jnp.zeros((8, key.shape[1]), jnp.int32)
    for number, value in enumerate(values):
        digits = jnp.where(row == 2 * number, value & 31, digits)
        digits = jnp.where(row == 2 * number + 1, lax.shift_right_logical(value, 5), digits)
    found = dot_nt(digits.astype(jnp.float32), match.astype(jnp.float32)).astype(jnp.int32)
    return [
        found[2 * number:2 * number + 1] + 32 * found[2 * number + 1:2 * number + 2]
        for number in range(len(values))
    ]


def route_kernel(n_grp, pairs, own_tiles, tiles_held, spot, every_ref, out_ref):
    n_blk, n_entries = every_ref.shape
    width = out_ref.shape[1]
    n_chips = n_grp // 2
    user_blocks = n_grp * own_tiles
    all_chips = n_blk * n_chips
    pad = lambda n: -(-n // 8) * 8
    my_blk, my_grp = spot[0], spot[1]
    my_chip = lax.shift_right_logical(my_grp, 1)
    my_core = my_grp & 1
    index = iota(1, n_entries, 1)
    source = lax.shift_right_logical(index, bits_for(pairs))
    from_chip = lax.shift_right_logical(source, 1)
    one_hot = lambda key, n: key == iota(pad(n), n_entries, 0)

    def fields(packed):
        user = packed & (user_blocks - 1)
        packed = lax.shift_right_logical(packed, bits_for(user_blocks))
        live = (packed & 1) == 1
        item = lax.shift_right_logical(packed, 1)
        held = item & (2 * tiles_held - 1)
        chip = lax.shift_right_logical(item, bits_for(2 * tiles_held))
        return user, live, chip, held

    ids = iota(1, 2 * tiles_held, 1)
    fewer = iota(2 * tiles_held, 2 * tiles_held, 0) > iota(2 * tiles_held, 2 * tiles_held, 1)

    def needs(live, chip, held):
        on_chip = one_hot(chip, all_chips) & live
        on_tile = one_hot(held, 2 * tiles_held)
        needed = dot_nt(on_chip.astype(jnp.float32), on_tile.astype(jnp.float32)) > 0
        return on_chip, on_tile, needed, dot_nt(needed.astype(jnp.float32), fewer.astype(jnp.float32))

    excess = jnp.zeros((1, 1), jnp.float32)
    worst = lambda loads, room: jnp.max(loads, axis=(0, 1), keepdims=True) - room
    asked = jnp.zeros((1, width), jnp.int32)
    here = my_blk * n_chips + my_chip
    chip_row = iota(pad(all_chips), 2 * tiles_held, 0)
    for blk in range(n_blk):
        user, live, chip, held = fields(every_ref[blk:blk + 1, :])
        _, _, needed, ahead = needs(live, chip, held)
        away = lax.shift_right_logical(chip_row, bits_for(n_chips)) != blk
        asks = jnp.sum((needed & away).astype(jnp.float32), axis=1, keepdims=True)
        excess = jnp.maximum(excess, worst(asks, 2 * FAR_CAP))
        to_chip = lax.shift_right_logical(user, bits_for(own_tiles) + 1)
        to = one_hot(to_chip, n_chips).astype(jnp.float32)
        column = chip & (n_chips - 1)
        near = lax.shift_right_logical(chip, bits_for(n_chips)) == blk
        for key, inside, cap in (
            (from_chip, live, COUNT_CAP),
            (column, live & near, NEAR_CAP),
            (column, live & ~near, ITEM_CAP),
        ):
            loads = dot_nt((one_hot(key, n_chips) & inside).astype(jnp.float32), to)
            excess = jnp.maximum(excess, worst(loads, 2 * cap))
        loads = jnp.sum(
            (one_hot(user, user_blocks) & live).astype(jnp.int32), axis=1, keepdims=True
        )
        chunks = lax.shift_right_logical(loads + SPAN - 1, bits_for(SPAN)).astype(jnp.float32)
        owners = iota(pad(n_grp), pad(user_blocks), 1)
        owners = lax.shift_right_logical(owners, bits_for(own_tiles)) == iota(*owners.shape, 0)
        loads = jnp.dot(
            owners.astype(jnp.float32), jnp.broadcast_to(chunks, (chunks.shape[0], 128)),
            precision=lax.Precision.HIGHEST, preferred_element_type=jnp.float32,
        )
        excess = jnp.maximum(excess, worst(loads, LOADS // SPAN))

        mine = chip_row == here
        present = jnp.sum((needed & mine).astype(jnp.int32), axis=0, keepdims=True)
        place = jnp.sum(jnp.where(mine, ahead, 0.0), axis=0, keepdims=True).astype(jnp.int32)
        shift = (blk + n_blk - my_blk) & (n_blk - 1)
        spot_at = lax.shift_right_logical(place, 1)
        hit = (present > 0) & ((place & 1) == my_core) & (spot_at < FAR_CAP) & (shift > 0)
        value = at_source(
            lax.shift_right_logical(ids, bits_for(tiles_held)) ^ my_core, ids & (tiles_held - 1), 2
        )
        (found,) = choose((shift - 1) * FAR_CAP + spot_at, hit, width, value)
        asked = asked + found

    user, live, chip, held = fields(every_ref[pl.ds(my_blk, 1), :])
    on_chip, on_tile, _, ahead = needs(live, chip, held)
    places = jnp.dot(
        ahead.astype(jnp.bfloat16), on_tile.astype(jnp.float32).astype(jnp.bfloat16),
        preferred_element_type=jnp.float32,
    )
    far_place = jnp.sum(jnp.where(on_chip, places, 0.0), axis=0, keepdims=True).astype(jnp.int32)
    far_place = jnp.minimum(far_place, 2 * FAR_CAP - 1)
    owner = lax.shift_right_logical(user, bits_for(own_tiles))
    local_user = user & (own_tiles - 1)
    to_chip = lax.shift_right_logical(owner, 1)
    column = chip & (n_chips - 1)
    to_me = live & (owner == my_grp)
    shift = (my_blk + n_blk - lax.shift_right_logical(chip, bits_for(n_chips))) & (n_blk - 1)
    near, far = live & (shift == 0), live & (shift > 0)
    in_tile = one_hot(local_user, own_tiles) & to_me
    groups = [
        one_hot(from_chip, n_chips) & (live & (to_chip == my_chip)),
        one_hot(to_chip, n_chips) & (near & (column == my_chip)),
        one_hot(column, n_chips) & (near & (to_chip == my_chip)),
        one_hot(to_chip, n_chips) & (far & (column == my_chip)),
        one_hot(column, n_chips) & (far & (to_chip == my_chip)),
        in_tile,
    ]
    before = (iota(n_entries, n_entries, 0) < iota(n_entries, n_entries, 1)).astype(jnp.float32)
    before = before.astype(jnp.bfloat16)
    ranks = []
    for marks in groups:
        earlier = jnp.dot(
            marks.astype(jnp.float32).astype(jnp.bfloat16), before,
            preferred_element_type=jnp.float32,
        )
        earlier = jnp.sum(jnp.where(marks, earlier, 0.0), axis=0, keepdims=True)
        ranks.append(earlier.astype(jnp.int32))
    counts_back, near_out, near_back, far_out, far_back, user_rank = ranks

    half = lambda rank: lax.shift_right_logical(rank, 1)
    sent = lambda rank, cap: live & ((rank & 1) == my_core) & (half(rank) < cap)
    back = lambda rank, cap: jnp.minimum(half(rank), cap - 1)
    core = lambda rank: (rank & 1) ^ my_core
    out_ref[0:1, :] = jnp.zeros((1, width), jnp.int32)
    out_ref[1:2, :] = asked
    (out_ref[7:8, :],) = choose(
        to_chip * NEAR_CAP + half(near_out), near & (column == my_chip) & sent(near_out, NEAR_CAP),
        width,
        at_source(
            lax.shift_right_logical(held, bits_for(tiles_held)) ^ my_core, held & (tiles_held - 1), 2
        ),
    )
    (out_ref[2:3, :],) = choose(
        (to_chip ^ my_chip) * ITEM_CAP + half(far_out),
        far & (column == my_chip) & sent(far_out, ITEM_CAP), width,
        at_source(
            core(far_place) * (n_blk - 1) + shift - 1, half(far_place), 2 * (n_blk - 1)
        ),
    )

    loads = jnp.sum(in_tile.astype(jnp.int32), axis=1, keepdims=True)
    chunks = lax.shift_right_logical(loads + SPAN - 1, bits_for(SPAN)).astype(jnp.float32)
    rows = chunks.shape[0]
    ends = jnp.dot(
        (iota(rows, rows, 0) >= iota(rows, rows, 1)).astype(jnp.float32),
        jnp.broadcast_to(chunks, (rows, 128)),
        precision=lax.Precision.HIGHEST, preferred_element_type=jnp.float32,
    )
    firsts = ends[:, :1] - chunks
    room_at = jnp.sum(jnp.where(in_tile, firsts * SPAN, 0.0), axis=0, keepdims=True)
    room_at = room_at.astype(jnp.int32) + user_rank
    hit = to_me & (room_at < LOADS)
    count_at = at_source(
        core(counts_back), from_chip * COUNT_CAP + back(counts_back, COUNT_CAP), 2
    )
    n_sources = 2 + 2 * n_chips
    item_at = jnp.where(
        shift == 0,
        at_source(
            core(near_back), column * NEAR_CAP + back(near_back, NEAR_CAP), n_sources
        ),
        at_source(
            2 + (column ^ my_chip) * 2 + core(far_back), back(far_back, ITEM_CAP), n_sources
        ),
    )
    out_ref[3:4, :], out_ref[4:5, :] = choose(room_at, hit, width, count_at + 1, item_at)
    passed = (iota(rows, width, 1).astype(jnp.float32) >= ends[:, :1]) & (
        iota(rows, width, 0) < own_tiles - 1
    )
    out_ref[5:6, :] = jnp.sum(passed.astype(jnp.int32), axis=0, keepdims=True)
    total = ends[own_tiles - 1:own_tiles, :1].astype(jnp.int32)
    total = jnp.minimum(total, LOADS // SPAN)
    copies = jnp.sum(hit.astype(jnp.int32), axis=1, keepdims=True)
    at = iota(1, width, 1)
    fits = (excess <= 0.0).astype(jnp.int32)
    head = jnp.where(at == 0, total, jnp.where(at == 1, copies, jnp.where(at == 2, fits, 0)))
    out_ref[6:7, :] = head


def route_counts_kernel(n_grp, own_tiles, spot, entries_ref, out_ref):
    n_entries = entries_ref.shape[1]
    n_chips = n_grp // 2
    pairs = n_entries // 2
    my_core = spot[0]
    packed = entries_ref[...]
    user = packed & (n_grp * own_tiles - 1)
    live = (lax.shift_right_logical(packed, bits_for(n_grp * own_tiles)) & 1) == 1
    to_chip = lax.shift_right_logical(user, bits_for(own_tiles) + 1)
    marks = (to_chip == iota(-(-n_chips // 8) * 8, n_entries, 0)) & live
    before = (iota(n_entries, n_entries, 0) < iota(n_entries, n_entries, 1)).astype(jnp.float32)
    earlier = jnp.dot(
        marks.astype(jnp.float32).astype(jnp.bfloat16), before.astype(jnp.bfloat16),
        preferred_element_type=jnp.float32,
    )
    rank = jnp.sum(jnp.where(marks, earlier, 0.0), axis=0, keepdims=True).astype(jnp.int32)
    half = lax.shift_right_logical(rank, 1)
    index = iota(1, n_entries, 1)
    (chosen,) = choose(
        to_chip * COUNT_CAP + half, live & ((rank & 1) == my_core) & (half < COUNT_CAP),
        out_ref.shape[1],
        at_source(lax.shift_right_logical(index, bits_for(pairs)) ^ my_core, index & (pairs - 1), 2),
    )
    out_ref[...] = jnp.broadcast_to(chosen, out_ref.shape)


def route_counts(entries, my_core, n_grp, own_tiles):
    width = -(-n_grp // 2 * COUNT_CAP // 128) * 128
    vmem = pl.BlockSpec(memory_space=pltpu.VMEM)
    return pl.pallas_call(
        functools.partial(route_counts_kernel, n_grp, own_tiles),
        out_shape=jax.ShapeDtypeStruct((8, width), jnp.int32),
        in_specs=[pl.BlockSpec(memory_space=pltpu.SMEM), vmem],
        out_specs=vmem,
        compiler_params=pltpu.CompilerParams(vmem_limit_bytes=16 * 2**20),
        name="route_counts",
    )(jnp.reshape(my_core, (1,)).astype(jnp.int32), entries)


def route(every, my_blk, my_grp, n_grp, own_tiles, tiles_held):
    n_blk, n_entries = every.shape
    n_chips = n_grp // 2
    width = max((n_blk - 1) * FAR_CAP, n_chips * ITEM_CAP, LOADS)
    width = -(-width // 128) * 128
    vmem = pl.BlockSpec(memory_space=pltpu.VMEM)
    return pl.pallas_call(
        functools.partial(route_kernel, n_grp, n_entries // n_grp, own_tiles, tiles_held),
        out_shape=jax.ShapeDtypeStruct((8, width), jnp.int32),
        in_specs=[pl.BlockSpec(memory_space=pltpu.SMEM), vmem],
        out_specs=vmem,
        compiler_params=pltpu.CompilerParams(vmem_limit_bytes=16 * 2**20),
        name="route",
    )(jnp.stack([my_blk, my_grp]).astype(jnp.int32), every)


def scan_kernel(counts_ref, scaled_ref, most_ref):
    counts = counts_ref[...]
    scaled_ref[...] = (ALPHA * counts.astype(jnp.float32)).astype(jnp.bfloat16)
    most_ref[...] = jnp.max(counts, axis=1)


def scan_counts(counts):
    pairs, tile, columns = counts.shape
    block = 16
    return pl.pallas_call(
        scan_kernel,
        grid=(pairs // block,),
        out_shape=[
            jax.ShapeDtypeStruct(counts.shape, jnp.bfloat16),
            jax.ShapeDtypeStruct((pairs, columns), jnp.int32),
        ],
        in_specs=[pl.BlockSpec((block, tile, columns), lambda i: (i, 0, 0))],
        out_specs=[
            pl.BlockSpec((block, tile, columns), lambda i: (i, 0, 0)),
            pl.BlockSpec((block, columns), lambda i: (i, 0)),
        ],
        compiler_params=pltpu.CompilerParams(vmem_limit_bytes=16 * 2**20),
        name="scan_counts",
    )(counts)


def body(user_prior, item_factors, user_tiles, item_tiles, counts):
    pairs = counts.shape[0]
    tile = counts.shape[1]
    rank = item_factors.shape[1]
    n_blk = lax.axis_size("blk")
    n_grp = lax.axis_size("grp")
    n_all = n_blk * n_grp
    n_chips = n_grp // 2
    own_rows = user_prior.shape[0]
    own_tiles = own_rows // tile
    user_blocks = own_tiles * n_grp
    tiles_held = item_factors.shape[0] // tile
    my_blk = lax.axis_index("blk")
    my_grp = lax.axis_index("grp")
    my_chip = my_grp // 2
    my_core = my_grp % 2
    lanes = [[chip * 2 + core for chip in range(n_chips)] for core in range(2)]

    def swap(value):
        return lax.ppermute(value, "grp", [(i, i ^ 1) for i in range(n_grp)])

    def to_chips(value):
        return lax.all_to_all(
            value, "grp", split_axis=0, concat_axis=0, tiled=True, axis_index_groups=lanes
        )

    gram_local = lax.dot_general(
        item_factors, item_factors, (((0,), (0,)), ((), ())), preferred_element_type=jnp.float32
    )
    grp_bits, blk_bits = [[1 << n for n in range(bits_for(size))] for size in (n_grp, n_blk)]
    held = item_factors.reshape(tiles_held, tile, rank)
    held_mate = swap(held)
    scaled, column_most = scan_counts(counts)
    live = jnp.any(column_most > 0, axis=1)
    scaled_mate = swap(scaled)
    packed = (item_tiles * 2 + live.astype(jnp.int32)) * user_blocks + user_tiles
    every = lax.all_to_all(
        jnp.broadcast_to(packed, (n_all, pairs)), ("blk", "grp"), split_axis=0, concat_axis=0
    )
    packed_mate = swap(packed)
    first, second = jnp.where(my_core == 0, packed, packed_mate), jnp.where(my_core == 0, packed_mate, packed)
    entries = jnp.concatenate([first, second]).reshape(1, 2 * pairs)
    count_table = route_counts(entries, my_core, n_grp, own_tiles)
    jobs = [(0, 2, 0, chip * COUNT_CAP, COUNT_CAP, 0, chip * COUNT_CAP) for chip in range(n_chips)]
    (counts_out,) = pack_tiles(
        "pack_counts", count_table, [scaled, scaled_mate], [n_chips * COUNT_CAP], jobs
    )
    gram = gram_local
    for bit in grp_bits[1:]:
        gram = sum_with(gram, "grp", bit)
    every, counts_out, gram = lax.optimization_barrier((every, counts_out, gram))
    counts_own = to_chips(counts_out)
    table = route(every.reshape(n_blk, n_grp * pairs), my_blk, my_grp, n_grp, own_tiles, tiles_held)

    jobs = [(0, 2, 1, shift * FAR_CAP, FAR_CAP, shift, 0) for shift in range(n_blk - 1)]
    for chip in range(n_chips):
        jobs.append((0, 2, 7, chip * NEAR_CAP, NEAR_CAP, n_blk - 1, chip * NEAR_CAP))
    lengths = [FAR_CAP] * (n_blk - 1) + [n_chips * NEAR_CAP]
    *far, near_out = pack_tiles("pack_first", table, [held, held_mate], lengths, jobs)
    far = [
        lax.ppermute(piece, "blk", [(i, (i + 1 + shift) % n_blk) for i in range(n_blk)])
        for shift, piece in enumerate(far)
    ]
    far_mate = [swap(piece) for piece in far]
    near_out, counts_own = lax.optimization_barrier((near_out, counts_own))
    counts_mate = swap(counts_own)
    near_own = to_chips(near_out)

    jobs = [(0, 2 * (n_blk - 1), 2, off * ITEM_CAP, ITEM_CAP, off, 0) for off in range(n_chips)]
    items_out = pack_tiles(
        "pack_items", table, [*far, *far_mate], [ITEM_CAP] * n_chips, jobs
    )
    gram, *items_out = lax.optimization_barrier((gram, *items_out))
    gram = sum_with(gram, "grp", grp_bits[0])
    for bit in blk_bits:
        gram = sum_with(gram, "blk", bit)
    item_pieces = []
    for off, piece in enumerate(items_out):
        if off:
            piece = lax.ppermute(piece, "grp", [(i, i ^ (2 * off)) for i in range(n_grp)])
        if off == 1:
            piece, near_own = lax.optimization_barrier((piece, near_own))
        if off == n_chips - 1:
            piece, gram = lax.optimization_barrier((piece, gram))
        item_pieces += [piece, swap(piece)]
    near = [near_own, swap(near_own)]
    by_owner = run_sweep(table, user_prior, gram, [counts_own, counts_mate], near + item_pieces)

    fits = table[6, 2] > 0
    return lax.cond(
        fits, lambda done, *given: done, lambda done, *given: sweep_in_place(*given),
        by_owner, user_prior, item_factors, user_tiles, item_tiles, counts, live, gram_local,
    )


def solution(mesh):
    in_specs = (
        P(("blk", "grp"), None),
        P(("blk", "grp"), None),
        P(("blk", "grp")),
        P(("blk", "grp")),
        P(("blk", "grp"), None, None),
    )
    out_specs = P(("blk", "grp"), None)
    return jax.shard_map(body, mesh=mesh, in_specs=in_specs, out_specs=out_specs, check_vma=False)
```

```python
import functools

import jax
import jax.numpy as jnp
from jax import lax
from jax.experimental import pallas as pl
from jax.experimental.pallas import tpu as pltpu
from jax.sharding import PartitionSpec as P

ITERS = 3

ALPHA = 40.0
REG = 32.0
EPS = 1e-06

FAR_CAP = 14
COUNT_CAP = 24
ITEM_CAP = 20
LOADS = 128
SPAN = 2
VMEM_GRANT = 60 * 2**20
TOGETHER = 8


def fetch_tiles(item_factors, item_tiles, pairs, tile, rank):
    n_all = lax.axis_size(("blk", "grp"))
    tiles_held = item_factors.shape[0] // tile
    slots_each = max(2, pairs // n_all)
    owner = item_tiles // tiles_held
    local_slot = item_tiles % tiles_held
    position = jnp.arange(pairs, dtype=jnp.int32)
    earlier = (owner[None, :] == owner[:, None]) & (position[None, :] < position[:, None])
    order = jnp.sum(earlier.astype(jnp.int32), axis=1)
    requests = jnp.full((n_all, slots_each), -1, jnp.int32).at[owner, order].set(local_slot)
    wanted = lax.all_to_all(requests, ("blk", "grp"), split_axis=0, concat_axis=0, tiled=True)
    held = item_factors.reshape(tiles_held, tile, rank)
    picked = jnp.take(held, jnp.maximum(wanted, 0), axis=0)
    picked = jnp.where((wanted >= 0)[:, :, None, None], picked, jnp.zeros((), picked.dtype))
    arrived = lax.all_to_all(picked, ("blk", "grp"), split_axis=0, concat_axis=0, tiled=True)
    return arrived[owner, order]


def row_sum(left, right):
    return jnp.sum(left * right, axis=1, keepdims=True)


def sweep_in_place(user_prior, item_factors, user_tiles, item_tiles, counts, live, gram_local):
    pairs = counts.shape[0]
    tile = counts.shape[1]
    rank = item_factors.shape[1]
    n_grp = lax.axis_size("grp")
    own_rows = user_prior.shape[0]
    block_rows = own_rows * n_grp
    user_blocks = block_rows // tile
    span = min(32, pairs)
    gram = lax.psum(gram_local, ("blk", "grp"))
    pair_tiles = fetch_tiles(item_factors, item_tiles, pairs, tile, rank)
    rounds = (jnp.sum(live.astype(jnp.int32)) + span - 1) // span
    tile_ids = jnp.arange(user_blocks, dtype=jnp.int32)

    def accumulate(low_tiles, with_rhs):

        def one_round(index, totals):
            start = index * span
            users = lax.dynamic_slice_in_dim(user_tiles, start, span)
            factors = lax.dynamic_slice_in_dim(pair_tiles, start, span)
            counted = lax.dynamic_slice_in_dim(counts, start, span).astype(jnp.float32)
            selector = (tile_ids[:, None] == users[None, :]).astype(jnp.float32)
            users_low = jnp.take(low_tiles, users, axis=0)
            scores = jnp.einsum(
                "bur,bir->bui", users_low, factors, preferred_element_type=jnp.float32
            )
            scaled = (ALPHA * counted * scores).astype(jnp.bfloat16)
            back = jnp.einsum("bui,bir->bur", scaled, factors, preferred_element_type=jnp.float32)
            result = [
                totals[0]
                + jnp.einsum("tb,bur->tur", selector, back, precision=lax.Precision.HIGHEST)
            ]
            if with_rhs:
                confidence = jnp.where(counted > 0, 1.0 + ALPHA * counted, 0.0).astype(jnp.bfloat16)
                pulled = jnp.einsum(
                    "bui,bir->bur", confidence, factors, preferred_element_type=jnp.float32
                )
                result.append(
                    totals[1]
                    + jnp.einsum("tb,bur->tur", selector, pulled, precision=lax.Precision.HIGHEST)
                )
            return tuple(result)

        zeros = jnp.zeros((user_blocks, tile, rank), jnp.float32)
        start_state = (zeros, zeros) if with_rhs else (zeros,)
        totals = lax.fori_loop(0, rounds, one_round, start_state)
        return tuple((total.reshape(block_rows, rank) for total in totals))

    def gram_term(vectors):
        return jnp.dot(vectors, gram, precision=lax.Precision.HIGHEST) + REG * vectors

    low = lax.all_gather(user_prior.astype(jnp.bfloat16), "grp", axis=0, tiled=True)
    pair_part, rhs_part = accumulate(low.reshape(user_blocks, tile, rank), True)
    pair_share, rhs_share = (
        lax.psum_scatter(pair_part, "grp", scatter_dimension=0, tiled=True),
        lax.psum_scatter(rhs_part, "grp", scatter_dimension=0, tiled=True),
    )
    solution = user_prior
    residual = rhs_share - (gram_term(solution) + pair_share)
    direction = residual
    norm_now = row_sum(residual, residual)
    for step in range(ITERS):
        low = lax.all_gather(direction.astype(jnp.bfloat16), "grp", axis=0, tiled=True)
        (pair_part,) = accumulate(low.reshape(user_blocks, tile, rank), False)
        image = gram_term(direction) + lax.psum_scatter(
            pair_part, "grp", scatter_dimension=0, tiled=True
        )
        alpha = norm_now / (row_sum(direction, image) + EPS)
        solution = solution + alpha * direction
        residual = residual - alpha * image
        fresh = row_sum(residual, residual)
        direction = residual + fresh / (norm_now + EPS) * direction
        norm_now = fresh
    return solution


def bits_for(n):
    return (n - 1).bit_length()


def at_source(number, row, n_sources):
    return (row << bits_for(n_sources)) + number


def move_tile(sources, at, room, place):
    bits = bits_for(len(sources))
    row = lax.shift_right_logical(at, bits)
    which = at & ((1 << bits) - 1)

    def among(lo, hi):
        if hi - lo == 1:
            room[place] = sources[lo][row]
            return
        mid = (lo + hi) // 2
        pl.when(which < mid)(lambda: among(lo, mid))
        pl.when(which >= mid)(lambda: among(mid, hi))

    among(0, len(sources))


def sweep_kernel(plan, prior_ref, gram_ref, *refs):
    weights, factors, turned, low, image, residual, direction = refs[-7:]
    count_pieces, item_pieces, out_ref = refs[:2], refs[2:-8], refs[-8]
    tile, rank = factors.shape[1:]
    n_chunks = plan[6, 0]
    halves = (n_chunks + TOGETHER // 2 - 1) // (TOGETHER // 2)
    rounds = halves // 2

    def bring(place, carry):
        count_at = plan[3, place]
        item_at = plan[4, place]

        @pl.when(count_at > 0)
        def _():
            move_tile(count_pieces, count_at - 1, weights, place)
            move_tile(item_pieces, item_at, factors, place)

        @pl.when(count_at == 0)
        def _():
            weights[place] = jnp.zeros((tile, tile), weights.dtype)
            factors[place] = jnp.zeros((tile, rank), factors.dtype)

        return carry

    lax.fori_loop(0, halves * (TOGETHER // 2 * SPAN), bring, 0)

    def pair_images(with_rhs):
        image[...] = jnp.zeros_like(image)
        if with_rhs:
            residual[...] = jnp.zeros_like(residual)

        def some(first, n):
            shares = []
            for number in range(n):
                chunk = first + number
                rows = pl.ds(pl.multiple_of(plan[5, chunk] * tile, tile), tile)
                items = factors[pl.ds(chunk * SPAN, SPAN)].reshape(SPAN * tile, rank)
                scaled = jnp.concatenate(
                    [weights[chunk * SPAN + part].astype(jnp.float32) for part in range(SPAN)],
                    axis=1,
                )
                if with_rhs:
                    turned[chunk] = items.T
                scores = jnp.dot(low[rows, :], turned[chunk], preferred_element_type=jnp.float32)
                back = jnp.dot(
                    (scaled * scores).astype(jnp.bfloat16), items,
                    preferred_element_type=jnp.float32,
                )
                pulled = None
                if with_rhs:
                    confidence = jnp.where(scaled > 0, 1.0 + scaled, 0.0).astype(jnp.bfloat16)
                    pulled = jnp.dot(confidence, items, preferred_element_type=jnp.float32)
                shares.append((rows, back, pulled))
            for rows, back, pulled in shares:
                image[rows, :] += back
                if with_rhs:
                    residual[rows, :] += pulled

        def one_round(step, carry):
            some(step * TOGETHER, TOGETHER)
            return carry

        lax.fori_loop(0, rounds, one_round, 0)
        pl.when(halves % 2 == 1)(lambda: some(rounds * TOGETHER, TOGETHER // 2))

    def gram_term(vectors):
        return jnp.dot(
            vectors, gram_ref[...], precision=lax.Precision.HIGHEST,
            preferred_element_type=jnp.float32,
        ) + REG * vectors

    prior = prior_ref[...]
    low[...] = prior.astype(jnp.bfloat16)
    pair_images(True)
    first = residual[...] - (gram_term(prior) + image[...])
    residual[...] = first
    direction[...] = first
    out_ref[...] = prior
    norm_now = row_sum(first, first)
    for step in range(ITERS):
        heading = direction[...]
        low[...] = heading.astype(jnp.bfloat16)
        pair_images(False)
        shown = gram_term(heading) + image[...]
        alpha = norm_now / (row_sum(heading, shown) + EPS)
        out_ref[...] += alpha * heading
        if step < ITERS - 1:
            left = residual[...] - alpha * shown
            residual[...] = left
            fresh = row_sum(left, left)
            direction[...] = left + (fresh / (norm_now + EPS)) * heading
            norm_now = fresh


def run_sweep(plan, user_prior, gram, count_pieces, item_pieces):
    own_rows, rank = user_prior.shape
    tile = count_pieces[0].shape[1]
    pieces = [*count_pieces, *item_pieces]
    vmem = pl.BlockSpec(memory_space=pltpu.VMEM)
    return pl.pallas_call(
        sweep_kernel,
        out_shape=jax.ShapeDtypeStruct((own_rows, rank), jnp.float32),
        in_specs=[pl.BlockSpec(memory_space=pltpu.SMEM)] + [vmem] * (2 + len(pieces)),
        out_specs=vmem,
        scratch_shapes=[
            pltpu.VMEM((LOADS, tile, tile), jnp.bfloat16),
            pltpu.VMEM((LOADS, tile, rank), jnp.bfloat16),
            pltpu.VMEM((LOADS // SPAN, rank, SPAN * tile), jnp.bfloat16),
            pltpu.VMEM((own_rows, rank), jnp.bfloat16),
            pltpu.VMEM((own_rows, rank), jnp.float32),
            pltpu.VMEM((own_rows, rank), jnp.float32),
            pltpu.VMEM((own_rows, rank), jnp.float32),
        ],
        compiler_params=pltpu.CompilerParams(vmem_limit_bytes=32 * 2**20),
        name="sweep",
    )(plan, user_prior, gram, *pieces)


def pack_kernel(n_sources, n_outs, jobs, table, *refs):
    sources, refs = refs[:n_sources], refs[n_sources:]
    outs, rooms, written = refs[:n_outs], refs[n_outs:-1], refs[-1]
    copies = []
    for number, (lo, hi, row, start, length, out, first) in enumerate(jobs):

        def place(spot, carry, number=number, lo=lo, hi=hi, row=row, start=start):
            move_tile(sources[lo:hi], table[row, start + spot], rooms[number], spot)
            return carry

        lax.fori_loop(0, length, place, 0, unroll=2)
        target = outs[out].at[pl.ds(first, length)]
        copies.append(pltpu.make_async_copy(rooms[number], target, written.at[number]))
        copies[-1].start()
    for copy in copies:
        copy.wait()


def pack_tiles(name, table, sources, lengths, jobs):
    anywhere = pl.BlockSpec(memory_space=pl.ANY)
    kind = sources[0].dtype
    shape = sources[0].shape[1:]
    return pl.pallas_call(
        functools.partial(pack_kernel, len(sources), len(lengths), jobs),
        out_shape=[jax.ShapeDtypeStruct((n, *shape), kind) for n in lengths],
        in_specs=[pl.BlockSpec(memory_space=pltpu.SMEM)]
        + [pl.BlockSpec(memory_space=pltpu.VMEM)] * len(sources),
        out_specs=[anywhere] * len(lengths),
        scratch_shapes=[pltpu.VMEM((job[4], *shape), kind) for job in jobs]
        + [pltpu.SemaphoreType.DMA((len(jobs),))],
        compiler_params=pltpu.CompilerParams(vmem_limit_bytes=VMEM_GRANT),
        name=name,
    )(table, *sources)


def sum_with(value, axis, bit):
    size = lax.axis_size(axis)
    return value + lax.ppermute(value, axis, [(i, i ^ bit) for i in range(size)])


def iota(rows, columns, axis):
    return lax.broadcasted_iota(jnp.int32, (rows, columns), axis)


def dot_nt(left, right):
    return lax.dot_general(
        left.astype(jnp.bfloat16), right.astype(jnp.bfloat16), (((1,), (1,)), ((), ())),
        preferred_element_type=jnp.float32,
    )


def choose(key, hit, cells, *values):
    match = hit & (key == iota(cells, key.shape[1], 0))
    row = iota(8, key.shape[1], 0)
    digits = jnp.zeros((8, key.shape[1]), jnp.int32)
    for number, value in enumerate(values):
        digits = jnp.where(row == 2 * number, value & 31, digits)
        digits = jnp.where(row == 2 * number + 1, lax.shift_right_logical(value, 5), digits)
    found = dot_nt(digits.astype(jnp.float32), match.astype(jnp.float32)).astype(jnp.int32)
    return [
        found[2 * number:2 * number + 1] + 32 * found[2 * number + 1:2 * number + 2]
        for number in range(len(values))
    ]


def route_kernel(n_grp, pairs, own_tiles, tiles_held, spot, every_ref, out_ref):
    n_blk, n_entries = every_ref.shape
    width = out_ref.shape[1]
    n_chips = n_grp // 2
    user_blocks = n_grp * own_tiles
    all_chips = n_blk * n_chips
    pad = lambda n: -(-n // 8) * 8
    my_blk, my_grp = spot[0], spot[1]
    my_chip = lax.shift_right_logical(my_grp, 1)
    my_core = my_grp & 1
    index = iota(1, n_entries, 1)
    source = lax.shift_right_logical(index, bits_for(pairs))
    from_chip = lax.shift_right_logical(source, 1)
    one_hot = lambda key, n: key == iota(pad(n), n_entries, 0)

    def fields(packed):
        user = packed & (user_blocks - 1)
        packed = lax.shift_right_logical(packed, bits_for(user_blocks))
        live = (packed & 1) == 1
        item = lax.shift_right_logical(packed, 1)
        held = item & (2 * tiles_held - 1)
        chip = lax.shift_right_logical(item, bits_for(2 * tiles_held))
        return user, live, chip, held

    ids = iota(1, 2 * tiles_held, 1)
    fewer = iota(2 * tiles_held, 2 * tiles_held, 0) > iota(2 * tiles_held, 2 * tiles_held, 1)

    def needs(live, chip, held):
        on_chip = one_hot(chip, all_chips) & live
        on_tile = one_hot(held, 2 * tiles_held)
        needed = dot_nt(on_chip.astype(jnp.float32), on_tile.astype(jnp.float32)) > 0
        return on_chip, on_tile, needed, dot_nt(needed.astype(jnp.float32), fewer.astype(jnp.float32))

    excess = jnp.zeros((1, 1), jnp.float32)
    worst = lambda loads, room: jnp.max(loads, axis=(0, 1), keepdims=True) - room
    asked = jnp.zeros((1, width), jnp.int32)
    here = my_blk * n_chips + my_chip
    chip_row = iota(pad(all_chips), 2 * tiles_held, 0)
    for blk in range(n_blk):
        user, live, chip, held = fields(every_ref[blk:blk + 1, :])
        _, _, needed, ahead = needs(live, chip, held)
        away = lax.shift_right_logical(chip_row, bits_for(n_chips)) != blk
        asks = jnp.sum((needed & away).astype(jnp.float32), axis=1, keepdims=True)
        excess = jnp.maximum(excess, worst(asks, 2 * FAR_CAP))
        to_chip = lax.shift_right_logical(user, bits_for(own_tiles) + 1)
        to = one_hot(to_chip, n_chips).astype(jnp.float32)
        column = chip & (n_chips - 1)
        for key, cap in ((from_chip, COUNT_CAP), (column, ITEM_CAP)):
            loads = dot_nt((one_hot(key, n_chips) & live).astype(jnp.float32), to)
            excess = jnp.maximum(excess, worst(loads, 2 * cap))
        loads = jnp.sum(
            (one_hot(user, user_blocks) & live).astype(jnp.int32), axis=1, keepdims=True
        )
        chunks = lax.shift_right_logical(loads + SPAN - 1, bits_for(SPAN)).astype(jnp.float32)
        owners = iota(pad(n_grp), pad(user_blocks), 1)
        owners = lax.shift_right_logical(owners, bits_for(own_tiles)) == iota(*owners.shape, 0)
        loads = jnp.dot(
            owners.astype(jnp.float32), jnp.broadcast_to(chunks, (chunks.shape[0], 128)),
            precision=lax.Precision.HIGHEST, preferred_element_type=jnp.float32,
        )
        excess = jnp.maximum(excess, worst(loads, LOADS // SPAN))

        mine = chip_row == here
        present = jnp.sum((needed & mine).astype(jnp.int32), axis=0, keepdims=True)
        place = jnp.sum(jnp.where(mine, ahead, 0.0), axis=0, keepdims=True).astype(jnp.int32)
        shift = (blk + n_blk - my_blk) & (n_blk - 1)
        spot_at = lax.shift_right_logical(place, 1)
        hit = (present > 0) & ((place & 1) == my_core) & (spot_at < FAR_CAP) & (shift > 0)
        value = at_source(
            lax.shift_right_logical(ids, bits_for(tiles_held)) ^ my_core, ids & (tiles_held - 1), 2
        )
        (found,) = choose((shift - 1) * FAR_CAP + spot_at, hit, width, value)
        asked = asked + found

    user, live, chip, held = fields(every_ref[pl.ds(my_blk, 1), :])
    on_chip, on_tile, _, ahead = needs(live, chip, held)
    places = jnp.dot(
        ahead.astype(jnp.bfloat16), on_tile.astype(jnp.float32).astype(jnp.bfloat16),
        preferred_element_type=jnp.float32,
    )
    far_place = jnp.sum(jnp.where(on_chip, places, 0.0), axis=0, keepdims=True).astype(jnp.int32)
    far_place = jnp.minimum(far_place, 2 * FAR_CAP - 1)
    owner = lax.shift_right_logical(user, bits_for(own_tiles))
    local_user = user & (own_tiles - 1)
    to_chip = lax.shift_right_logical(owner, 1)
    column = chip & (n_chips - 1)
    to_me = live & (owner == my_grp)
    shift = (my_blk + n_blk - lax.shift_right_logical(chip, bits_for(n_chips))) & (n_blk - 1)
    in_tile = one_hot(local_user, own_tiles) & to_me
    groups = [
        one_hot(from_chip, n_chips) & (live & (to_chip == my_chip)),
        one_hot(to_chip, n_chips) & (live & (column == my_chip)),
        one_hot(column, n_chips) & (live & (to_chip == my_chip)),
        in_tile,
    ]
    before = (iota(n_entries, n_entries, 0) < iota(n_entries, n_entries, 1)).astype(jnp.float32)
    before = before.astype(jnp.bfloat16)
    ranks = []
    for marks in groups:
        earlier = jnp.dot(
            marks.astype(jnp.float32).astype(jnp.bfloat16), before,
            preferred_element_type=jnp.float32,
        )
        earlier = jnp.sum(jnp.where(marks, earlier, 0.0), axis=0, keepdims=True)
        ranks.append(earlier.astype(jnp.int32))
    counts_back, items_out, items_back, user_rank = ranks

    half = lambda rank: lax.shift_right_logical(rank, 1)
    sent = lambda rank, cap: live & ((rank & 1) == my_core) & (half(rank) < cap)
    back = lambda rank, cap: jnp.minimum(half(rank), cap - 1)
    core = lambda rank: (rank & 1) ^ my_core
    out_ref[0:1, :] = jnp.zeros((1, width), jnp.int32)
    out_ref[1:2, :] = asked
    lane = jnp.where(
        shift == 0, lax.shift_right_logical(held, bits_for(tiles_held)) ^ my_core, core(far_place)
    )
    (out_ref[2:3, :],) = choose(
        (to_chip ^ my_chip) * ITEM_CAP + half(items_out),
        (column == my_chip) & sent(items_out, ITEM_CAP), width,
        at_source(
            lane * n_blk + shift,
            jnp.where(shift == 0, held & (tiles_held - 1), half(far_place)), 2 * n_blk,
        ),
    )
    out_ref[7:8, :] = jnp.zeros((1, width), jnp.int32)

    loads = jnp.sum(in_tile.astype(jnp.int32), axis=1, keepdims=True)
    chunks = lax.shift_right_logical(loads + SPAN - 1, bits_for(SPAN)).astype(jnp.float32)
    rows = chunks.shape[0]
    ends = jnp.dot(
        (iota(rows, rows, 0) >= iota(rows, rows, 1)).astype(jnp.float32),
        jnp.broadcast_to(chunks, (rows, 128)),
        precision=lax.Precision.HIGHEST, preferred_element_type=jnp.float32,
    )
    firsts = ends[:, :1] - chunks
    room_at = jnp.sum(jnp.where(in_tile, firsts * SPAN, 0.0), axis=0, keepdims=True)
    room_at = room_at.astype(jnp.int32) + user_rank
    hit = to_me & (room_at < LOADS)
    count_at = at_source(
        core(counts_back), from_chip * COUNT_CAP + back(counts_back, COUNT_CAP), 2
    )
    item_at = at_source(
        (column ^ my_chip) * 2 + core(items_back), back(items_back, ITEM_CAP), 2 * n_chips
    )
    out_ref[3:4, :], out_ref[4:5, :] = choose(room_at, hit, width, count_at + 1, item_at)
    passed = (iota(rows, width, 1).astype(jnp.float32) >= ends[:, :1]) & (
        iota(rows, width, 0) < own_tiles - 1
    )
    out_ref[5:6, :] = jnp.sum(passed.astype(jnp.int32), axis=0, keepdims=True)
    total = ends[own_tiles - 1:own_tiles, :1].astype(jnp.int32)
    total = jnp.minimum(total, LOADS // SPAN)
    copies = jnp.sum(hit.astype(jnp.int32), axis=1, keepdims=True)
    at = iota(1, width, 1)
    fits = (excess <= 0.0).astype(jnp.int32)
    head = jnp.where(at == 0, total, jnp.where(at == 1, copies, jnp.where(at == 2, fits, 0)))
    out_ref[6:7, :] = head


def route_counts_kernel(n_grp, own_tiles, spot, entries_ref, out_ref):
    n_entries = entries_ref.shape[1]
    n_chips = n_grp // 2
    pairs = n_entries // 2
    my_core = spot[0]
    packed = entries_ref[...]
    user = packed & (n_grp * own_tiles - 1)
    live = (lax.shift_right_logical(packed, bits_for(n_grp * own_tiles)) & 1) == 1
    to_chip = lax.shift_right_logical(user, bits_for(own_tiles) + 1)
    marks = (to_chip == iota(-(-n_chips // 8) * 8, n_entries, 0)) & live
    before = (iota(n_entries, n_entries, 0) < iota(n_entries, n_entries, 1)).astype(jnp.float32)
    earlier = jnp.dot(
        marks.astype(jnp.float32).astype(jnp.bfloat16), before.astype(jnp.bfloat16),
        preferred_element_type=jnp.float32,
    )
    rank = jnp.sum(jnp.where(marks, earlier, 0.0), axis=0, keepdims=True).astype(jnp.int32)
    half = lax.shift_right_logical(rank, 1)
    index = iota(1, n_entries, 1)
    (chosen,) = choose(
        to_chip * COUNT_CAP + half, live & ((rank & 1) == my_core) & (half < COUNT_CAP),
        out_ref.shape[1],
        at_source(lax.shift_right_logical(index, bits_for(pairs)) ^ my_core, index & (pairs - 1), 2),
    )
    out_ref[...] = jnp.broadcast_to(chosen, out_ref.shape)


def route_counts(entries, my_core, n_grp, own_tiles):
    width = -(-n_grp // 2 * COUNT_CAP // 128) * 128
    vmem = pl.BlockSpec(memory_space=pltpu.VMEM)
    return pl.pallas_call(
        functools.partial(route_counts_kernel, n_grp, own_tiles),
        out_shape=jax.ShapeDtypeStruct((8, width), jnp.int32),
        in_specs=[pl.BlockSpec(memory_space=pltpu.SMEM), vmem],
        out_specs=vmem,
        compiler_params=pltpu.CompilerParams(vmem_limit_bytes=16 * 2**20),
        name="route_counts",
    )(jnp.reshape(my_core, (1,)).astype(jnp.int32), entries)


def route(every, my_blk, my_grp, n_grp, own_tiles, tiles_held):
    n_blk, n_entries = every.shape
    n_chips = n_grp // 2
    width = max((n_blk - 1) * FAR_CAP, n_chips * ITEM_CAP, LOADS)
    width = -(-width // 128) * 128
    vmem = pl.BlockSpec(memory_space=pltpu.VMEM)
    return pl.pallas_call(
        functools.partial(route_kernel, n_grp, n_entries // n_grp, own_tiles, tiles_held),
        out_shape=jax.ShapeDtypeStruct((8, width), jnp.int32),
        in_specs=[pl.BlockSpec(memory_space=pltpu.SMEM), vmem],
        out_specs=vmem,
        compiler_params=pltpu.CompilerParams(vmem_limit_bytes=16 * 2**20),
        name="route",
    )(jnp.stack([my_blk, my_grp]).astype(jnp.int32), every)


def scan_kernel(counts_ref, scaled_ref, most_ref):
    counts = counts_ref[...]
    scaled_ref[...] = (ALPHA * counts.astype(jnp.float32)).astype(jnp.bfloat16)
    most_ref[...] = jnp.max(counts, axis=1)


def scan_counts(counts):
    pairs, tile, columns = counts.shape
    block = 16
    return pl.pallas_call(
        scan_kernel,
        grid=(pairs // block,),
        out_shape=[
            jax.ShapeDtypeStruct(counts.shape, jnp.bfloat16),
            jax.ShapeDtypeStruct((pairs, columns), jnp.int32),
        ],
        in_specs=[pl.BlockSpec((block, tile, columns), lambda i: (i, 0, 0))],
        out_specs=[
            pl.BlockSpec((block, tile, columns), lambda i: (i, 0, 0)),
            pl.BlockSpec((block, columns), lambda i: (i, 0)),
        ],
        compiler_params=pltpu.CompilerParams(vmem_limit_bytes=16 * 2**20),
        name="scan_counts",
    )(counts)


def body(user_prior, item_factors, user_tiles, item_tiles, counts):
    pairs = counts.shape[0]
    tile = counts.shape[1]
    rank = item_factors.shape[1]
    n_blk = lax.axis_size("blk")
    n_grp = lax.axis_size("grp")
    n_all = n_blk * n_grp
    n_chips = n_grp // 2
    own_rows = user_prior.shape[0]
    own_tiles = own_rows // tile
    user_blocks = own_tiles * n_grp
    tiles_held = item_factors.shape[0] // tile
    my_blk = lax.axis_index("blk")
    my_grp = lax.axis_index("grp")
    my_chip = my_grp // 2
    my_core = my_grp % 2
    lanes = [[chip * 2 + core for chip in range(n_chips)] for core in range(2)]

    def swap(value):
        return lax.ppermute(value, "grp", [(i, i ^ 1) for i in range(n_grp)])

    def to_chips(value):
        return lax.all_to_all(
            value, "grp", split_axis=0, concat_axis=0, tiled=True, axis_index_groups=lanes
        )

    gram_local = lax.dot_general(
        item_factors, item_factors, (((0,), (0,)), ((), ())), preferred_element_type=jnp.float32
    )
    grp_bits, blk_bits = [[1 << n for n in range(bits_for(size))] for size in (n_grp, n_blk)]
    held = item_factors.reshape(tiles_held, tile, rank)
    held_mate = swap(held)
    scaled, column_most = scan_counts(counts)
    live = jnp.any(column_most > 0, axis=1)
    scaled_mate = swap(scaled)
    packed = (item_tiles * 2 + live.astype(jnp.int32)) * user_blocks + user_tiles
    every = lax.all_to_all(
        jnp.broadcast_to(packed, (n_all, pairs)), ("blk", "grp"), split_axis=0, concat_axis=0
    )
    packed_mate = swap(packed)
    first, second = jnp.where(my_core == 0, packed, packed_mate), jnp.where(my_core == 0, packed_mate, packed)
    entries = jnp.concatenate([first, second]).reshape(1, 2 * pairs)
    count_table = route_counts(entries, my_core, n_grp, own_tiles)
    jobs = [(0, 2, 0, chip * COUNT_CAP, COUNT_CAP, 0, chip * COUNT_CAP) for chip in range(n_chips)]
    (counts_out,) = pack_tiles(
        "pack_counts", count_table, [scaled, scaled_mate], [n_chips * COUNT_CAP], jobs
    )
    gram = gram_local
    for bit in grp_bits[1:]:
        gram = sum_with(gram, "grp", bit)
    every, counts_out, gram = lax.optimization_barrier((every, counts_out, gram))
    counts_own = to_chips(counts_out)
    table = route(every.reshape(n_blk, n_grp * pairs), my_blk, my_grp, n_grp, own_tiles, tiles_held)

    jobs = [(0, 2, 1, shift * FAR_CAP, FAR_CAP, shift, 0) for shift in range(n_blk - 1)]
    far = pack_tiles("pack_first", table, [held, held_mate], [FAR_CAP] * (n_blk - 1), jobs)
    far = [
        lax.ppermute(piece, "blk", [(i, (i + 1 + shift) % n_blk) for i in range(n_blk)])
        for shift, piece in enumerate(far)
    ]
    far_mate = [swap(piece) for piece in far]

    jobs = [(0, 2 * n_blk, 2, off * ITEM_CAP, ITEM_CAP, off, 0) for off in range(n_chips)]
    items_out = pack_tiles(
        "pack_items", table, [held, *far, held_mate, *far_mate], [ITEM_CAP] * n_chips, jobs
    )
    counts_own, gram, *items_out = lax.optimization_barrier((counts_own, gram, *items_out))
    counts_mate = swap(counts_own)
    gram = sum_with(gram, "grp", grp_bits[0])
    for bit in blk_bits:
        gram = sum_with(gram, "blk", bit)
    item_pieces = []
    for off, piece in enumerate(items_out):
        if off:
            piece = lax.ppermute(piece, "grp", [(i, i ^ (2 * off)) for i in range(n_grp)])
        if off == n_chips - 1:
            piece, gram = lax.optimization_barrier((piece, gram))
        item_pieces += [piece, swap(piece)]
    by_owner = run_sweep(table, user_prior, gram, [counts_own, counts_mate], item_pieces)

    fits = table[6, 2] > 0
    return lax.cond(
        fits, lambda done, *given: done, lambda done, *given: sweep_in_place(*given),
        by_owner, user_prior, item_factors, user_tiles, item_tiles, counts, live, gram_local,
    )


def solution(mesh):
    in_specs = (
        P(("blk", "grp"), None),
        P(("blk", "grp"), None),
        P(("blk", "grp")),
        P(("blk", "grp")),
        P(("blk", "grp"), None, None),
    )
    out_specs = P(("blk", "grp"), None)
    return jax.shard_map(body, mesh=mesh, in_specs=in_specs, out_specs=out_specs, check_vma=False)
```

```python
import functools

import jax
import jax.numpy as jnp
from jax import lax
from jax.experimental import pallas as pl
from jax.experimental.pallas import tpu as pltpu
from jax.sharding import PartitionSpec as P

ITERS = 3

ALPHA = 40.0
REG = 32.0
EPS = 1e-06

FAR_CAP = 14
COUNT_CAP = 24
ITEM_CAP = 20
LOADS = 128
SPAN = 2
VMEM_GRANT = 60 * 2**20
TOGETHER = 8


def fetch_tiles(item_factors, item_tiles, pairs, tile, rank):
    n_all = lax.axis_size(("blk", "grp"))
    tiles_held = item_factors.shape[0] // tile
    slots_each = max(2, pairs // n_all)
    owner = item_tiles // tiles_held
    local_slot = item_tiles % tiles_held
    position = jnp.arange(pairs, dtype=jnp.int32)
    earlier = (owner[None, :] == owner[:, None]) & (position[None, :] < position[:, None])
    order = jnp.sum(earlier.astype(jnp.int32), axis=1)
    requests = jnp.full((n_all, slots_each), -1, jnp.int32).at[owner, order].set(local_slot)
    wanted = lax.all_to_all(requests, ("blk", "grp"), split_axis=0, concat_axis=0, tiled=True)
    held = item_factors.reshape(tiles_held, tile, rank)
    picked = jnp.take(held, jnp.maximum(wanted, 0), axis=0)
    picked = jnp.where((wanted >= 0)[:, :, None, None], picked, jnp.zeros((), picked.dtype))
    arrived = lax.all_to_all(picked, ("blk", "grp"), split_axis=0, concat_axis=0, tiled=True)
    return arrived[owner, order]


def row_sum(left, right):
    return jnp.sum(left * right, axis=1, keepdims=True)


def sweep_in_place(user_prior, item_factors, user_tiles, item_tiles, counts, live, gram_local):
    pairs = counts.shape[0]
    tile = counts.shape[1]
    rank = item_factors.shape[1]
    n_grp = lax.axis_size("grp")
    own_rows = user_prior.shape[0]
    block_rows = own_rows * n_grp
    user_blocks = block_rows // tile
    span = min(32, pairs)
    gram = lax.psum(gram_local, ("blk", "grp"))
    pair_tiles = fetch_tiles(item_factors, item_tiles, pairs, tile, rank)
    rounds = (jnp.sum(live.astype(jnp.int32)) + span - 1) // span
    tile_ids = jnp.arange(user_blocks, dtype=jnp.int32)

    def accumulate(low_tiles, with_rhs):

        def one_round(index, totals):
            start = index * span
            users = lax.dynamic_slice_in_dim(user_tiles, start, span)
            factors = lax.dynamic_slice_in_dim(pair_tiles, start, span)
            counted = lax.dynamic_slice_in_dim(counts, start, span).astype(jnp.float32)
            selector = (tile_ids[:, None] == users[None, :]).astype(jnp.float32)
            users_low = jnp.take(low_tiles, users, axis=0)
            scores = jnp.einsum(
                "bur,bir->bui", users_low, factors, preferred_element_type=jnp.float32
            )
            scaled = (ALPHA * counted * scores).astype(jnp.bfloat16)
            back = jnp.einsum("bui,bir->bur", scaled, factors, preferred_element_type=jnp.float32)
            result = [
                totals[0]
                + jnp.einsum("tb,bur->tur", selector, back, precision=lax.Precision.HIGHEST)
            ]
            if with_rhs:
                confidence = jnp.where(counted > 0, 1.0 + ALPHA * counted, 0.0).astype(jnp.bfloat16)
                pulled = jnp.einsum(
                    "bui,bir->bur", confidence, factors, preferred_element_type=jnp.float32
                )
                result.append(
                    totals[1]
                    + jnp.einsum("tb,bur->tur", selector, pulled, precision=lax.Precision.HIGHEST)
                )
            return tuple(result)

        zeros = jnp.zeros((user_blocks, tile, rank), jnp.float32)
        start_state = (zeros, zeros) if with_rhs else (zeros,)
        totals = lax.fori_loop(0, rounds, one_round, start_state)
        return tuple((total.reshape(block_rows, rank) for total in totals))

    def gram_term(vectors):
        return jnp.dot(vectors, gram, precision=lax.Precision.HIGHEST) + REG * vectors

    low = lax.all_gather(user_prior.astype(jnp.bfloat16), "grp", axis=0, tiled=True)
    pair_part, rhs_part = accumulate(low.reshape(user_blocks, tile, rank), True)
    pair_share, rhs_share = (
        lax.psum_scatter(pair_part, "grp", scatter_dimension=0, tiled=True),
        lax.psum_scatter(rhs_part, "grp", scatter_dimension=0, tiled=True),
    )
    solution = user_prior
    residual = rhs_share - (gram_term(solution) + pair_share)
    direction = residual
    norm_now = row_sum(residual, residual)
    for step in range(ITERS):
        low = lax.all_gather(direction.astype(jnp.bfloat16), "grp", axis=0, tiled=True)
        (pair_part,) = accumulate(low.reshape(user_blocks, tile, rank), False)
        image = gram_term(direction) + lax.psum_scatter(
            pair_part, "grp", scatter_dimension=0, tiled=True
        )
        alpha = norm_now / (row_sum(direction, image) + EPS)
        solution = solution + alpha * direction
        residual = residual - alpha * image
        fresh = row_sum(residual, residual)
        direction = residual + fresh / (norm_now + EPS) * direction
        norm_now = fresh
    return solution


def bits_for(n):
    return (n - 1).bit_length()


def at_source(number, row, n_sources):
    return (row << bits_for(n_sources)) + number


def move_tile(sources, at, room, place):
    bits = bits_for(len(sources))
    row = lax.shift_right_logical(at, bits)
    which = at & ((1 << bits) - 1)

    def among(lo, hi):
        if hi - lo == 1:
            room[place] = sources[lo][row]
            return
        mid = (lo + hi) // 2
        pl.when(which < mid)(lambda: among(lo, mid))
        pl.when(which >= mid)(lambda: among(mid, hi))

    among(0, len(sources))


def sweep_kernel(plan, prior_ref, gram_ref, *refs):
    weights, factors, turned, low, image, residual, direction = refs[-7:]
    count_pieces, item_pieces, out_ref = refs[:2], refs[2:-8], refs[-8]
    tile, rank = factors.shape[1:]
    n_chunks = plan[6, 0]
    halves = (n_chunks + TOGETHER // 2 - 1) // (TOGETHER // 2)
    rounds = halves // 2

    def bring(place, carry):
        count_at = plan[3, place]
        item_at = plan[4, place]

        @pl.when(count_at > 0)
        def _():
            move_tile(count_pieces, count_at - 1, weights, place)
            move_tile(item_pieces, item_at, factors, place)

        @pl.when(count_at == 0)
        def _():
            weights[place] = jnp.zeros((tile, tile), weights.dtype)
            factors[place] = jnp.zeros((tile, rank), factors.dtype)

        return carry

    lax.fori_loop(0, halves * (TOGETHER // 2 * SPAN), bring, 0)

    def pair_images(with_rhs):
        image[...] = jnp.zeros_like(image)
        if with_rhs:
            residual[...] = jnp.zeros_like(residual)

        def some(first, n):
            shares = []
            for number in range(n):
                chunk = first + number
                rows = pl.ds(pl.multiple_of(plan[5, chunk] * tile, tile), tile)
                items = factors[pl.ds(chunk * SPAN, SPAN)].reshape(SPAN * tile, rank)
                scaled = jnp.concatenate(
                    [weights[chunk * SPAN + part].astype(jnp.float32) for part in range(SPAN)],
                    axis=1,
                )
                if with_rhs:
                    turned[chunk] = items.T
                scores = jnp.dot(low[rows, :], turned[chunk], preferred_element_type=jnp.float32)
                back = jnp.dot(
                    (scaled * scores).astype(jnp.bfloat16), items,
                    preferred_element_type=jnp.float32,
                )
                pulled = None
                if with_rhs:
                    confidence = jnp.where(scaled > 0, 1.0 + scaled, 0.0).astype(jnp.bfloat16)
                    pulled = jnp.dot(confidence, items, preferred_element_type=jnp.float32)
                shares.append((rows, back, pulled))
            for rows, back, pulled in shares:
                image[rows, :] += back
                if with_rhs:
                    residual[rows, :] += pulled

        def one_round(step, carry):
            some(step * TOGETHER, TOGETHER)
            return carry

        lax.fori_loop(0, rounds, one_round, 0)
        pl.when(halves % 2 == 1)(lambda: some(rounds * TOGETHER, TOGETHER // 2))

    def gram_term(vectors):
        return jnp.dot(
            vectors, gram_ref[...], precision=lax.Precision.HIGHEST,
            preferred_element_type=jnp.float32,
        ) + REG * vectors

    prior = prior_ref[...]
    low[...] = prior.astype(jnp.bfloat16)
    pair_images(True)
    first = residual[...] - (gram_term(prior) + image[...])
    residual[...] = first
    direction[...] = first
    out_ref[...] = prior
    norm_now = row_sum(first, first)
    for step in range(ITERS):
        heading = direction[...]
        low[...] = heading.astype(jnp.bfloat16)
        pair_images(False)
        shown = gram_term(heading) + image[...]
        alpha = norm_now / (row_sum(heading, shown) + EPS)
        out_ref[...] += alpha * heading
        if step < ITERS - 1:
            left = residual[...] - alpha * shown
            residual[...] = left
            fresh = row_sum(left, left)
            direction[...] = left + (fresh / (norm_now + EPS)) * heading
            norm_now = fresh


def run_sweep(plan, user_prior, gram, count_pieces, item_pieces):
    own_rows, rank = user_prior.shape
    tile = count_pieces[0].shape[1]
    pieces = [*count_pieces, *item_pieces]
    vmem = pl.BlockSpec(memory_space=pltpu.VMEM)
    return pl.pallas_call(
        sweep_kernel,
        out_shape=jax.ShapeDtypeStruct((own_rows, rank), jnp.float32),
        in_specs=[pl.BlockSpec(memory_space=pltpu.SMEM)] + [vmem] * (2 + len(pieces)),
        out_specs=vmem,
        scratch_shapes=[
            pltpu.VMEM((LOADS, tile, tile), jnp.bfloat16),
            pltpu.VMEM((LOADS, tile, rank), jnp.bfloat16),
            pltpu.VMEM((LOADS // SPAN, rank, SPAN * tile), jnp.bfloat16),
            pltpu.VMEM((own_rows, rank), jnp.bfloat16),
            pltpu.VMEM((own_rows, rank), jnp.float32),
            pltpu.VMEM((own_rows, rank), jnp.float32),
            pltpu.VMEM((own_rows, rank), jnp.float32),
        ],
        compiler_params=pltpu.CompilerParams(vmem_limit_bytes=32 * 2**20),
        name="sweep",
    )(plan, user_prior, gram, *pieces)


def pack_kernel(order, n_outs, jobs, table, *refs):
    sources = [refs[order.index(number)] for number in range(len(order))]
    refs = refs[len(order):]
    outs, rooms, written = refs[:n_outs], refs[n_outs:-1], refs[-1]
    copies = []
    for number, (lo, hi, row, start, length, out, first) in enumerate(jobs):

        def place(spot, carry, number=number, lo=lo, hi=hi, row=row, start=start):
            move_tile(sources[lo:hi], table[row, start + spot], rooms[number], spot)
            return carry

        lax.fori_loop(0, length, place, 0, unroll=2)
        target = outs[out].at[pl.ds(first, length)]
        copies.append(pltpu.make_async_copy(rooms[number], target, written.at[number]))
        copies[-1].start()
    for copy in copies:
        copy.wait()


def pack_tiles(name, table, sources, lengths, jobs, order=None):
    anywhere = pl.BlockSpec(memory_space=pl.ANY)
    order = list(order or range(len(sources)))
    kind = sources[0].dtype
    shape = sources[0].shape[1:]
    return pl.pallas_call(
        functools.partial(pack_kernel, order, len(lengths), jobs),
        out_shape=[jax.ShapeDtypeStruct((n, *shape), kind) for n in lengths],
        in_specs=[pl.BlockSpec(memory_space=pltpu.SMEM)]
        + [pl.BlockSpec(memory_space=pltpu.VMEM)] * len(sources),
        out_specs=[anywhere] * len(lengths),
        scratch_shapes=[pltpu.VMEM((job[4], *shape), kind) for job in jobs]
        + [pltpu.SemaphoreType.DMA((len(jobs),))],
        compiler_params=pltpu.CompilerParams(vmem_limit_bytes=VMEM_GRANT),
        name=name,
    )(table, *[sources[number] for number in order])


def sum_with(value, axis, bit):
    size = lax.axis_size(axis)
    return value + lax.ppermute(value, axis, [(i, i ^ bit) for i in range(size)])


def iota(rows, columns, axis):
    return lax.broadcasted_iota(jnp.int32, (rows, columns), axis)


def dot_nt(left, right):
    return lax.dot_general(
        left.astype(jnp.bfloat16), right.astype(jnp.bfloat16), (((1,), (1,)), ((), ())),
        preferred_element_type=jnp.float32,
    )


def choose(key, hit, cells, *values):
    match = hit & (key == iota(cells, key.shape[1], 0))
    row = iota(8, key.shape[1], 0)
    digits = jnp.zeros((8, key.shape[1]), jnp.int32)
    for number, value in enumerate(values):
        digits = jnp.where(row == 2 * number, value & 31, digits)
        digits = jnp.where(row == 2 * number + 1, lax.shift_right_logical(value, 5), digits)
    found = dot_nt(digits.astype(jnp.float32), match.astype(jnp.float32)).astype(jnp.int32)
    return [
        found[2 * number:2 * number + 1] + 32 * found[2 * number + 1:2 * number + 2]
        for number in range(len(values))
    ]


def route_kernel(n_grp, pairs, own_tiles, tiles_held, spot, every_ref, out_ref):
    n_blk, n_entries = every_ref.shape
    width = out_ref.shape[1]
    n_chips = n_grp // 2
    user_blocks = n_grp * own_tiles
    all_chips = n_blk * n_chips
    pad = lambda n: -(-n // 8) * 8
    my_blk, my_grp = spot[0], spot[1]
    my_chip = lax.shift_right_logical(my_grp, 1)
    my_core = my_grp & 1
    index = iota(1, n_entries, 1)
    source = lax.shift_right_logical(index, bits_for(pairs))
    from_chip = lax.shift_right_logical(source, 1)
    one_hot = lambda key, n: key == iota(pad(n), n_entries, 0)

    def fields(packed):
        user = packed & (user_blocks - 1)
        packed = lax.shift_right_logical(packed, bits_for(user_blocks))
        live = (packed & 1) == 1
        item = lax.shift_right_logical(packed, 1)
        held = item & (2 * tiles_held - 1)
        chip = lax.shift_right_logical(item, bits_for(2 * tiles_held))
        return user, live, chip, held

    ids = iota(1, 2 * tiles_held, 1)
    fewer = iota(2 * tiles_held, 2 * tiles_held, 0) > iota(2 * tiles_held, 2 * tiles_held, 1)

    def needs(live, chip, held):
        on_chip = one_hot(chip, all_chips) & live
        on_tile = one_hot(held, 2 * tiles_held)
        needed = dot_nt(on_chip.astype(jnp.float32), on_tile.astype(jnp.float32)) > 0
        return on_chip, on_tile, needed, dot_nt(needed.astype(jnp.float32), fewer.astype(jnp.float32))

    excess = jnp.zeros((1, 1), jnp.float32)
    worst = lambda loads, room: jnp.max(loads, axis=(0, 1), keepdims=True) - room
    asked = jnp.zeros((1, width), jnp.int32)
    here = my_blk * n_chips + my_chip
    chip_row = iota(pad(all_chips), 2 * tiles_held, 0)
    for blk in range(n_blk):
        user, live, chip, held = fields(every_ref[blk:blk + 1, :])
        _, _, needed, ahead = needs(live, chip, held)
        away = lax.shift_right_logical(chip_row, bits_for(n_chips)) != blk
        asks = jnp.sum((needed & away).astype(jnp.float32), axis=1, keepdims=True)
        excess = jnp.maximum(excess, worst(asks, 2 * FAR_CAP))
        to_chip = lax.shift_right_logical(user, bits_for(own_tiles) + 1)
        to = one_hot(to_chip, n_chips).astype(jnp.float32)
        column = chip & (n_chips - 1)
        for key, cap in ((from_chip, COUNT_CAP), (column, ITEM_CAP)):
            loads = dot_nt((one_hot(key, n_chips) & live).astype(jnp.float32), to)
            excess = jnp.maximum(excess, worst(loads, 2 * cap))
        loads = jnp.sum(
            (one_hot(user, user_blocks) & live).astype(jnp.int32), axis=1, keepdims=True
        )
        chunks = lax.shift_right_logical(loads + SPAN - 1, bits_for(SPAN)).astype(jnp.float32)
        owners = iota(pad(n_grp), pad(user_blocks), 1)
        owners = lax.shift_right_logical(owners, bits_for(own_tiles)) == iota(*owners.shape, 0)
        loads = jnp.dot(
            owners.astype(jnp.float32), jnp.broadcast_to(chunks, (chunks.shape[0], 128)),
            precision=lax.Precision.HIGHEST, preferred_element_type=jnp.float32,
        )
        excess = jnp.maximum(excess, worst(loads, LOADS // SPAN))

        mine = chip_row == here
        present = jnp.sum((needed & mine).astype(jnp.int32), axis=0, keepdims=True)
        place = jnp.sum(jnp.where(mine, ahead, 0.0), axis=0, keepdims=True).astype(jnp.int32)
        shift = (blk + n_blk - my_blk) & (n_blk - 1)
        spot_at = lax.shift_right_logical(place, 1)
        hit = (present > 0) & ((place & 1) == my_core) & (spot_at < FAR_CAP) & (shift > 0)
        value = at_source(
            lax.shift_right_logical(ids, bits_for(tiles_held)) ^ my_core, ids & (tiles_held - 1), 2
        )
        (found,) = choose((shift - 1) * FAR_CAP + spot_at, hit, width, value)
        asked = asked + found

    user, live, chip, held = fields(every_ref[pl.ds(my_blk, 1), :])
    on_chip, on_tile, _, ahead = needs(live, chip, held)
    places = jnp.dot(
        ahead.astype(jnp.bfloat16), on_tile.astype(jnp.float32).astype(jnp.bfloat16),
        preferred_element_type=jnp.float32,
    )
    far_place = jnp.sum(jnp.where(on_chip, places, 0.0), axis=0, keepdims=True).astype(jnp.int32)
    far_place = jnp.minimum(far_place, 2 * FAR_CAP - 1)
    owner = lax.shift_right_logical(user, bits_for(own_tiles))
    local_user = user & (own_tiles - 1)
    to_chip = lax.shift_right_logical(owner, 1)
    column = chip & (n_chips - 1)
    to_me = live & (owner == my_grp)
    shift = (my_blk + n_blk - lax.shift_right_logical(chip, bits_for(n_chips))) & (n_blk - 1)
    in_tile = one_hot(local_user, own_tiles) & to_me
    groups = [
        one_hot(from_chip, n_chips) & (live & (to_chip == my_chip)),
        one_hot(to_chip, n_chips) & (live & (column == my_chip)),
        one_hot(column, n_chips) & (live & (to_chip == my_chip)),
        in_tile,
    ]
    before = (iota(n_entries, n_entries, 0) < iota(n_entries, n_entries, 1)).astype(jnp.float32)
    before = before.astype(jnp.bfloat16)
    ranks = []
    for marks in groups:
        earlier = jnp.dot(
            marks.astype(jnp.float32).astype(jnp.bfloat16), before,
            preferred_element_type=jnp.float32,
        )
        earlier = jnp.sum(jnp.where(marks, earlier, 0.0), axis=0, keepdims=True)
        ranks.append(earlier.astype(jnp.int32))
    counts_back, items_out, items_back, user_rank = ranks

    half = lambda rank: lax.shift_right_logical(rank, 1)
    sent = lambda rank, cap: live & ((rank & 1) == my_core) & (half(rank) < cap)
    back = lambda rank, cap: jnp.minimum(half(rank), cap - 1)
    core = lambda rank: (rank & 1) ^ my_core
    out_ref[0:1, :] = jnp.zeros((1, width), jnp.int32)
    out_ref[1:2, :] = asked
    lane = jnp.where(
        shift == 0, lax.shift_right_logical(held, bits_for(tiles_held)) ^ my_core, core(far_place)
    )
    (out_ref[2:3, :],) = choose(
        (to_chip ^ my_chip) * ITEM_CAP + half(items_out),
        (column == my_chip) & sent(items_out, ITEM_CAP), width,
        at_source(
            lane * n_blk + shift,
            jnp.where(shift == 0, held & (tiles_held - 1), half(far_place)), 2 * n_blk,
        ),
    )
    out_ref[7:8, :] = jnp.zeros((1, width), jnp.int32)

    loads = jnp.sum(in_tile.astype(jnp.int32), axis=1, keepdims=True)
    chunks = lax.shift_right_logical(loads + SPAN - 1, bits_for(SPAN)).astype(jnp.float32)
    rows = chunks.shape[0]
    ends = jnp.dot(
        (iota(rows, rows, 0) >= iota(rows, rows, 1)).astype(jnp.float32),
        jnp.broadcast_to(chunks, (rows, 128)),
        precision=lax.Precision.HIGHEST, preferred_element_type=jnp.float32,
    )
    firsts = ends[:, :1] - chunks
    room_at = jnp.sum(jnp.where(in_tile, firsts * SPAN, 0.0), axis=0, keepdims=True)
    room_at = room_at.astype(jnp.int32) + user_rank
    hit = to_me & (room_at < LOADS)
    count_at = at_source(
        core(counts_back), from_chip * COUNT_CAP + back(counts_back, COUNT_CAP), 2
    )
    item_at = at_source(
        (column ^ my_chip) * 2 + core(items_back), back(items_back, ITEM_CAP), 2 * n_chips
    )
    out_ref[3:4, :], out_ref[4:5, :] = choose(room_at, hit, width, count_at + 1, item_at)
    passed = (iota(rows, width, 1).astype(jnp.float32) >= ends[:, :1]) & (
        iota(rows, width, 0) < own_tiles - 1
    )
    out_ref[5:6, :] = jnp.sum(passed.astype(jnp.int32), axis=0, keepdims=True)
    total = ends[own_tiles - 1:own_tiles, :1].astype(jnp.int32)
    total = jnp.minimum(total, LOADS // SPAN)
    copies = jnp.sum(hit.astype(jnp.int32), axis=1, keepdims=True)
    at = iota(1, width, 1)
    fits = (excess <= 0.0).astype(jnp.int32)
    head = jnp.where(at == 0, total, jnp.where(at == 1, copies, jnp.where(at == 2, fits, 0)))
    out_ref[6:7, :] = head


def route_counts_kernel(n_grp, own_tiles, spot, entries_ref, out_ref):
    n_entries = entries_ref.shape[1]
    n_chips = n_grp // 2
    pairs = n_entries // 2
    my_core = spot[0]
    packed = entries_ref[...]
    user = packed & (n_grp * own_tiles - 1)
    live = (lax.shift_right_logical(packed, bits_for(n_grp * own_tiles)) & 1) == 1
    to_chip = lax.shift_right_logical(user, bits_for(own_tiles) + 1)
    marks = (to_chip == iota(-(-n_chips // 8) * 8, n_entries, 0)) & live
    before = (iota(n_entries, n_entries, 0) < iota(n_entries, n_entries, 1)).astype(jnp.float32)
    earlier = jnp.dot(
        marks.astype(jnp.float32).astype(jnp.bfloat16), before.astype(jnp.bfloat16),
        preferred_element_type=jnp.float32,
    )
    rank = jnp.sum(jnp.where(marks, earlier, 0.0), axis=0, keepdims=True).astype(jnp.int32)
    half = lax.shift_right_logical(rank, 1)
    index = iota(1, n_entries, 1)
    (chosen,) = choose(
        to_chip * COUNT_CAP + half, live & ((rank & 1) == my_core) & (half < COUNT_CAP),
        out_ref.shape[1],
        at_source(lax.shift_right_logical(index, bits_for(pairs)) ^ my_core, index & (pairs - 1), 2),
    )
    out_ref[...] = jnp.broadcast_to(chosen, out_ref.shape)


def route_counts(entries, my_core, n_grp, own_tiles):
    width = -(-n_grp // 2 * COUNT_CAP // 128) * 128
    vmem = pl.BlockSpec(memory_space=pltpu.VMEM)
    return pl.pallas_call(
        functools.partial(route_counts_kernel, n_grp, own_tiles),
        out_shape=jax.ShapeDtypeStruct((8, width), jnp.int32),
        in_specs=[pl.BlockSpec(memory_space=pltpu.SMEM), vmem],
        out_specs=vmem,
        compiler_params=pltpu.CompilerParams(vmem_limit_bytes=16 * 2**20),
        name="route_counts",
    )(jnp.reshape(my_core, (1,)).astype(jnp.int32), entries)


def route(every, my_blk, my_grp, n_grp, own_tiles, tiles_held):
    n_blk, n_entries = every.shape
    n_chips = n_grp // 2
    width = max((n_blk - 1) * FAR_CAP, n_chips * ITEM_CAP, LOADS)
    width = -(-width // 128) * 128
    vmem = pl.BlockSpec(memory_space=pltpu.VMEM)
    return pl.pallas_call(
        functools.partial(route_kernel, n_grp, n_entries // n_grp, own_tiles, tiles_held),
        out_shape=jax.ShapeDtypeStruct((8, width), jnp.int32),
        in_specs=[pl.BlockSpec(memory_space=pltpu.SMEM), vmem],
        out_specs=vmem,
        compiler_params=pltpu.CompilerParams(vmem_limit_bytes=16 * 2**20),
        name="route",
    )(jnp.stack([my_blk, my_grp]).astype(jnp.int32), every)


def scan_kernel(counts_ref, scaled_ref, most_ref):
    counts = counts_ref[...]
    scaled_ref[...] = (ALPHA * counts.astype(jnp.float32)).astype(jnp.bfloat16)
    most_ref[...] = jnp.max(counts, axis=1)


def scan_counts(counts):
    pairs, tile, columns = counts.shape
    block = 16
    return pl.pallas_call(
        scan_kernel,
        grid=(pairs // block,),
        out_shape=[
            jax.ShapeDtypeStruct(counts.shape, jnp.bfloat16),
            jax.ShapeDtypeStruct((pairs, columns), jnp.int32),
        ],
        in_specs=[pl.BlockSpec((block, tile, columns), lambda i: (i, 0, 0))],
        out_specs=[
            pl.BlockSpec((block, tile, columns), lambda i: (i, 0, 0)),
            pl.BlockSpec((block, columns), lambda i: (i, 0)),
        ],
        compiler_params=pltpu.CompilerParams(vmem_limit_bytes=16 * 2**20),
        name="scan_counts",
    )(counts)


def body(user_prior, item_factors, user_tiles, item_tiles, counts):
    pairs = counts.shape[0]
    tile = counts.shape[1]
    rank = item_factors.shape[1]
    n_blk = lax.axis_size("blk")
    n_grp = lax.axis_size("grp")
    n_all = n_blk * n_grp
    n_chips = n_grp // 2
    own_rows = user_prior.shape[0]
    own_tiles = own_rows // tile
    user_blocks = own_tiles * n_grp
    tiles_held = item_factors.shape[0] // tile
    my_blk = lax.axis_index("blk")
    my_grp = lax.axis_index("grp")
    my_chip = my_grp // 2
    my_core = my_grp % 2
    lanes = [[chip * 2 + core for chip in range(n_chips)] for core in range(2)]

    def swap(value):
        return lax.ppermute(value, "grp", [(i, i ^ 1) for i in range(n_grp)])

    def to_chips(value):
        return lax.all_to_all(
            value, "grp", split_axis=0, concat_axis=0, tiled=True, axis_index_groups=lanes
        )

    gram_local = lax.dot_general(
        item_factors, item_factors, (((0,), (0,)), ((), ())), preferred_element_type=jnp.float32
    )
    grp_bits, blk_bits = [[1 << n for n in range(bits_for(size))] for size in (n_grp, n_blk)]
    held = item_factors.reshape(tiles_held, tile, rank)
    held_mate = swap(held)
    scaled, column_most = scan_counts(counts)
    live = jnp.any(column_most > 0, axis=1)
    scaled_mate = swap(scaled)
    packed = (item_tiles * 2 + live.astype(jnp.int32)) * user_blocks + user_tiles
    every = lax.all_to_all(
        jnp.broadcast_to(packed, (n_all, pairs)), ("blk", "grp"), split_axis=0, concat_axis=0
    )
    packed_mate = swap(packed)
    first, second = jnp.where(my_core == 0, packed, packed_mate), jnp.where(my_core == 0, packed_mate, packed)
    entries = jnp.concatenate([first, second]).reshape(1, 2 * pairs)
    count_table = route_counts(entries, my_core, n_grp, own_tiles)
    jobs = [(0, 2, 0, chip * COUNT_CAP, COUNT_CAP, 0, chip * COUNT_CAP) for chip in range(n_chips)]
    (counts_out,) = pack_tiles(
        "pack_counts", count_table, [scaled, scaled_mate], [n_chips * COUNT_CAP], jobs
    )
    gram = gram_local
    for bit in grp_bits[1:]:
        gram = sum_with(gram, "grp", bit)
    every, counts_out, gram = lax.optimization_barrier((every, counts_out, gram))
    counts_own = to_chips(counts_out)
    table = route(every.reshape(n_blk, n_grp * pairs), my_blk, my_grp, n_grp, own_tiles, tiles_held)

    jobs = [(0, 2, 1, shift * FAR_CAP, FAR_CAP, shift, 0) for shift in range(n_blk - 1)]
    far = pack_tiles("pack_first", table, [held, held_mate], [FAR_CAP] * (n_blk - 1), jobs)
    far = [
        lax.ppermute(piece, "blk", [(i, (i + 1 + shift) % n_blk) for i in range(n_blk)])
        for shift, piece in enumerate(far)
    ]
    far_mate = [swap(piece) for piece in far]

    by_way = sorted(range(1, n_blk), key=lambda shift: min(shift, n_blk - shift))
    jobs = [(0, 2 * n_blk, 2, off * ITEM_CAP, ITEM_CAP, off, 0) for off in range(n_chips)]
    items_out = pack_tiles(
        "pack_items", table, [held, *far, held_mate, *far_mate], [ITEM_CAP] * n_chips, jobs,
        [0, *by_way, n_blk, *(n_blk + shift for shift in by_way)],
    )
    counts_own, gram, *items_out = lax.optimization_barrier((counts_own, gram, *items_out))
    counts_mate = swap(counts_own)
    gram = sum_with(gram, "grp", grp_bits[0])
    for bit in blk_bits:
        gram = sum_with(gram, "blk", bit)
    item_pieces = []
    for off, piece in enumerate(items_out):
        if off:
            piece = lax.ppermute(piece, "grp", [(i, i ^ (2 * off)) for i in range(n_grp)])
        if off == n_chips - 1:
            piece, gram = lax.optimization_barrier((piece, gram))
        item_pieces += [piece, swap(piece)]
    by_owner = run_sweep(table, user_prior, gram, [counts_own, counts_mate], item_pieces)

    fits = table[6, 2] > 0
    return lax.cond(
        fits, lambda done, *given: done, lambda done, *given: sweep_in_place(*given),
        by_owner, user_prior, item_factors, user_tiles, item_tiles, counts, live, gram_local,
    )


def solution(mesh):
    in_specs = (
        P(("blk", "grp"), None),
        P(("blk", "grp"), None),
        P(("blk", "grp")),
        P(("blk", "grp")),
        P(("blk", "grp"), None, None),
    )
    out_specs = P(("blk", "grp"), None)
    return jax.shard_map(body, mesh=mesh, in_specs=in_specs, out_specs=out_specs, check_vma=False)
```
